32 devices in a mesh: dp: 4 (over y, core), row: 2 (over x), col: 4 (over z).
Axes of the slice: x: 2, y: 2, z: 4, core: 2. Of those that a mesh axis runs over, the one named last changes fastest.
Arguments:
- block_input: bfloat16 [8192, 2048], P(('dp', 'row'), 'col'), may hold values from -7.2 to 7.2
- cotangent: bfloat16 [8192, 2048], P(('dp', 'row'), 'col'), may hold values from -7.2 to 7.2
- segments: int32 [4, 2048], P('dp'), may hold values from 0 to 3, never falling along the last dimension, each value on 1 to 1024 neighbouring positions
- norm_gains: float32 [2, 2048], P(None, 'col'), may hold values from 0.5 to 1.5
- w_query: float32 [2048, 2048], P('col', 'row'), may hold values from -0.125 to 0.125
- w_keyvalue: float32 [2048, 512], P('col'), may hold values from -0.125 to 0.125
- w_output: float32 [2048, 2048], P('row', 'col'), may hold values from -1 to 1
- w_gateup: float32 [2048, 2, 5632], P('col', None, 'row'), may hold values from -0.125 to 0.125
- w_down: float32 [5632, 2048], P('row', 'col'), may hold values from -0.078125 to 0.078125
- gains_moment: float32 [2, 2048], P(None, 'col'), may hold values from -64 to 64
- gains_square: float32 [2, 2048], P(None, 'col'), may hold values from 4.096 to 65.536
- query_moment: float32 [2048, 2048], P('col', 'row'), may hold values from -128 to 128
- query_square: float32 [2048, 2048], P('col', 'row'), may hold values from 16.384 to 262.144
- keyvalue_moment: float32 [2048, 512], P('col'), may hold values from -160 to 160
- keyvalue_square: float32 [2048, 512], P('col'), may hold values from 32.768 to 524.288
- output_moment: float32 [2048, 2048], P('row', 'col'), may hold values from -6 to 6
- output_square: float32 [2048, 2048], P('row', 'col'), may hold values from 0.04096 to 0.65536
- gateup_moment: float32 [2048, 2, 5632], P('col', None, 'row'), may hold values from -20 to 20
- gateup_square: float32 [2048, 2, 5632], P('col', None, 'row'), may hold values from 0.4096 to 6.5536
- down_moment: float32 [5632, 2048], P('row', 'col'), may hold values from -40 to 40
- down_square: float32 [5632, 2048], P('row', 'col'), may hold values from 1.6384 to 26.2144
Outputs:
- layer_output: bfloat16 [8192, 2048], P(('dp', 'row'), 'col')
- input_grad: float32 [8192, 2048], P(('dp', 'row'), 'col')
- new_gains_moment: float32 [2, 2048], P(None, 'col')
- new_gains_square: float32 [2, 2048], P(None, 'col')
- new_gains: float32 [2, 2048], P(None, 'col')
- new_query_moment: float32 [2048, 2048], P('col', 'row')
- new_query_square: float32 [2048, 2048], P('col', 'row')
- new_query: float32 [2048, 2048], P('col', 'row')
- new_keyvalue_moment: float32 [2048, 512], P('col')
- new_keyvalue_square: float32 [2048, 512], P('col')
- new_keyvalue: float32 [2048, 512], P('col')
- new_output_moment: float32 [2048, 2048], P('row', 'col')
- new_output_square: float32 [2048, 2048], P('row', 'col')
- new_output: float32 [2048, 2048], P('row', 'col')
- new_gateup_moment: float32 [2048, 2, 5632], P('col', None, 'row')
- new_gateup_square: float32 [2048, 2, 5632], P('col', None, 'row')
- new_gateup: float32 [2048, 2, 5632], P('col', None, 'row')
- new_down_moment: float32 [5632, 2048], P('row', 'col')
- new_down_square: float32 [5632, 2048], P('row', 'col')
- new_down: float32 [5632, 2048], P('row', 'col')
The draws below stay inside these ranges and needn't reach their ends.
All inputs are finite; a program needn't handle non-finite values.
Results may differ from the reference program's by a relative error of at most 0.025.
Values may be sent and summed in bfloat16 or wider, within the bound.
No kernel may reach another device: no remote copies, remote signals or barrier semaphores. Data moves between devices by JAX's collectives and lax.ppermute only.
A program may use at most 448 MiB of HBM per device.

```python
import math
import jax
import jax.numpy as jnp
import numpy as np
from jax import lax

D = 2048
HEADS = 32
KV_HEADS = 4
HEAD_DIM = 64
FF = 5632
LEN = 2048
DOCS = 4
STEP = 10
SEQS = 4
TOKENS = 8192
DOC_MOST = 1024
N_DP = 4
N_ROW = 2


def apply_ramp(samples, along_axis, low_end, high_end):
    count = samples.shape[along_axis]
    ramp = low_end + (high_end - low_end) * jnp.arange(count, dtype=jnp.float32) / max(count - 1, 1)
    if along_axis == 0:
        return samples * ramp[:, None]
    return samples * ramp[None, :]


def draw_block_input(key, part):
    key = jax.random.fold_in(key, 11)
    samples = jax.random.truncated_normal(key, -4.0, 4.0, (TOKENS, D), jnp.float32)
    return apply_ramp(samples, 1, 0.6, 1.8).astype(jnp.bfloat16)


def draw_cotangent(key, part):
    key = jax.random.fold_in(key, 23)
    samples = jax.random.truncated_normal(key, -4.0, 4.0, (TOKENS, D), jnp.float32)
    return apply_ramp(samples, 0, 0.6, 1.8).astype(jnp.bfloat16)


def levels(own_key, shape, shards, least, high):
    gain, own = 1.0, jax.random.fold_in(own_key, 6)
    for dim, shards_of in shards:
        draws = jnp.exp(jax.random.uniform(jax.random.fold_in(own, dim), (shards_of,), jnp.float32, least / len(shards), high / len(shards)))
        gain = gain * jnp.repeat(draws, shape[dim] // shards_of).reshape([-1 if axis == dim else 1 for axis in range(len(shape))])
    return gain


def profile(number_of, total, most, lean):
    weights = [(1 << 20) // math.isqrt(standing ** lean) + 1 for standing in range(2, number_of + 1)]
    spare, counts = total - most - (number_of - 1), [1] * (number_of - 1)
    while spare > 0:
        free = [i for i in range(number_of - 1) if counts[i] < most]
        pool, budget = sum([weights[i] for i in free]), spare
        for i in free:
            extra = min(most - counts[i], max(1, budget * weights[i] // pool), spare)
            counts[i] = counts[i] + extra
            spare = spare - extra
    return np.array([most] + counts)


def uneven_parts(stream_key, number_of, total, reach, lean):
    if number_of == 2:
        one = jax.random.randint(stream_key, (), max(1, total - reach), min(reach, total - 1) + 1)
        return jnp.stack([one, total - one])
    tallies = jnp.asarray(profile(number_of, total, reach, lean), jnp.int32)
    pairs = (number_of - 1) // 2
    giver, taker = tallies[1:1 + 2 * pairs:2], tallies[2:2 + 2 * pairs:2]
    margin = jnp.minimum(giver - 1, reach - taker)
    moved = jax.random.randint(jax.random.fold_in(stream_key, 1), (pairs,), 0, 1 << 20) % (margin + 1)
    tallies = tallies.at[1:1 + 2 * pairs:2].set(giver - moved).at[2:2 + 2 * pairs:2].set(taker + moved)
    return tallies[jax.random.permutation(jax.random.fold_in(stream_key, 2), number_of)]


def gaussian(stream_key, shape, scale, reach, shards=(), held_as=jnp.bfloat16):
    level = levels(stream_key, shape, shards, -0.22, 0.18) if shards else 1.0
    array = jax.random.normal(stream_key, shape, jnp.float32) * scale * level
    return jnp.minimum(jnp.maximum(array, -reach), reach).astype(held_as)


def setup_inputs(seed: int = 0) -> dict:
    streams_of = jax.random.split(jax.random.key(seed), 22)
    return {
        "block_input": draw_block_input(jax.random.fold_in(streams_of[21], 71), 0),
        "cotangent": draw_cotangent(jax.random.fold_in(streams_of[21], 71), 0),
        "segments": jax.vmap(lambda own: jnp.searchsorted(jnp.cumsum(uneven_parts(own, DOCS, LEN, DOC_MOST, 0)), jnp.arange(LEN), side="right"))(jax.random.split(streams_of[2], SEQS)).reshape((SEQS, LEN)).astype(jnp.int32),
        "norm_gains": jnp.clip(1.0 + 0.1 * jax.random.normal(streams_of[3], (2, D), jnp.float32), 0.5, 1.5),
        "w_query": gaussian(streams_of[4], (D, HEADS * HEAD_DIM), D ** -0.5, 0.125, ((0, 4), (1, 2)), jnp.float32),
        "w_keyvalue": gaussian(streams_of[5], (D, 2 * KV_HEADS * HEAD_DIM), D ** -0.5, 0.125, ((0, 4),), jnp.float32),
        "w_output": gaussian(streams_of[6], (HEADS * HEAD_DIM, D), (HEADS * HEAD_DIM // 64) ** -0.5, 1.0, ((0, 2), (1, 4)), jnp.float32),
        "w_gateup": gaussian(streams_of[7], (D, 2, FF), D ** -0.5, 0.125, ((0, 4), (2, 2)), jnp.float32),
        "w_down": gaussian(streams_of[8], (FF, D), FF ** -0.5, 0.078125, ((0, 2), (1, 4)), jnp.float32),
        "gains_moment": gaussian(streams_of[9], (2, D), (0.11 * TOKENS ** 0.5), 64.0, ((1, 4),), jnp.float32),
        "gains_square": jnp.clip(jnp.exp(math.log(65.536) - 2.7725887 * jax.random.uniform(streams_of[10], (2, D), jnp.float32) ** levels(streams_of[10], (2, D), ((1, 4),), -0.2, 0.2)), 4.096, 65.536),
        "query_moment": gaussian(streams_of[11], (D, HEADS * HEAD_DIM), (0.11 * (4 * TOKENS) ** 0.5), 128.0, ((0, 4), (1, 2)), jnp.float32),
        "query_square": jnp.clip(jnp.exp(math.log(262.144) - 2.7725887 * jax.random.uniform(streams_of[12], (D, HEADS * HEAD_DIM), jnp.float32) ** levels(streams_of[12], (D, HEADS * HEAD_DIM), ((0, 4), (1, 2)), -0.2, 0.2)), 16.384, 262.144),
        "keyvalue_moment": gaussian(streams_of[13], (D, 2 * KV_HEADS * HEAD_DIM), (0.11 * (8 * TOKENS) ** 0.5), 160.0, ((0, 4),), jnp.float32),
        "keyvalue_square": jnp.clip(jnp.exp(math.log(524.288) - 2.7725887 * jax.random.uniform(streams_of[14], (D, 2 * KV_HEADS * HEAD_DIM), jnp.float32) ** levels(streams_of[14], (D, 2 * KV_HEADS * HEAD_DIM), ((0, 4),), -0.2, 0.2)), 32.768, 524.288),
        "output_moment": gaussian(streams_of[15], (HEADS * HEAD_DIM, D), (0.11 * (0.01 * TOKENS) ** 0.5), 6.0, ((0, 2), (1, 4)), jnp.float32),
        "output_square": jnp.clip(jnp.exp(math.log(0.65536) - 2.7725887 * jax.random.uniform(streams_of[16], (HEADS * HEAD_DIM, D), jnp.float32) ** levels(streams_of[16], (HEADS * HEAD_DIM, D), ((0, 2), (1, 4)), -0.2, 0.2)), 0.04096, 0.65536),
        "gateup_moment": gaussian(streams_of[17], (D, 2, FF), (0.11 * (0.1 * TOKENS) ** 0.5), 20.0, ((0, 4), (2, 2)), jnp.float32),
        "gateup_square": jnp.clip(jnp.exp(math.log(6.5536) - 2.7725887 * jax.random.uniform(streams_of[18], (D, 2, FF), jnp.float32) ** levels(streams_of[18], (D, 2, FF), ((0, 4), (2, 2)), -0.2, 0.2)), 0.4096, 6.5536),
        "down_moment": gaussian(streams_of[19], (FF, D), (0.11 * (0.4 * TOKENS) ** 0.5), 40.0, ((0, 2), (1, 4)), jnp.float32),
        "down_square": jnp.clip(jnp.exp(math.log(26.2144) - 2.7725887 * jax.random.uniform(streams_of[20], (FF, D), jnp.float32) ** levels(streams_of[20], (FF, D), ((0, 2), (1, 4)), -0.2, 0.2)), 1.6384, 26.2144),
    }


@jax.custom_vjp
def low(v):
    return lax.optimization_barrier(v.astype(jnp.bfloat16)).astype(jnp.float32)

@jax.custom_vjp
def low_back(v):
    return v

def low_keep(v):
    return (low(v), None)

def low_pass(kept, grad):
    return (grad,)

def back_keep(v):
    return (v, None)

def back_low(kept, grad):
    return (low(grad),)
low.defvjp(low_keep, low_pass)
low_back.defvjp(back_keep, back_low)
EPSILON = 1e-05
BETA_ONE = 0.9
BETA_TWO = 0.999
ADAM_EPS = 1e-08
MASKED = -1e+30
HIGHEST = lax.Precision.HIGHEST

def matmul(left_side, right_side):
    return jnp.dot(left_side, right_side, precision=HIGHEST, preferred_element_type=jnp.float32)

def rms_scale(values, gain_row):
    return values * lax.rsqrt(lax.optimization_barrier(jnp.mean(values * values, axis=-1, keepdims=True)) + EPSILON) * gain_row

def rotate(values, cosine, sine_table):
    half_dim = values.shape[-1] // 2
    turned = jnp.concatenate([-values[..., half_dim:], values[..., :half_dim]], axis=-1)
    return values * cosine + turned * sine_table

def angles(segment_ids):
    length = segment_ids.shape[0]
    places = jnp.arange(length, dtype=jnp.int32)
    starts = jnp.concatenate([jnp.ones((1,), jnp.bool_), segment_ids[1:] != segment_ids[:-1]])
    doc_start = lax.cummax(jnp.where(starts, places, 0), axis=0)
    offsets = (places - doc_start).astype(jnp.float32)
    frequency = 10000.0 ** (-2.0 * jnp.arange(HEAD_DIM // 2, dtype=jnp.float32) / HEAD_DIM)
    phases = offsets[:, None] * frequency[None, :]
    phases = jnp.concatenate([phases, phases], axis=1)
    return (jnp.cos(phases), jnp.sin(phases))

def attend(queries, keys_rot, values_low, segment_ids):
    length = queries.shape[0]
    per_group = queries.shape[1]
    block_rows = min(512, length)
    count_blocks = length // block_rows
    places = jnp.arange(length, dtype=jnp.int32)
    score_scale = HEAD_DIM ** (-0.5)

    def one_block(operands):
        query_block, query_places, query_segs = operands
        scores = jnp.einsum('bjcd,kcd->cjbk', query_block, keys_rot, precision=HIGHEST) * score_scale
        scores = low_back(scores)
        allowed = (segment_ids[None, :] == query_segs[:, None]) & (places[None, :] <= query_places[:, None])
        scores = jnp.where(allowed[None, None], scores, MASKED)
        row_peak = lax.optimization_barrier(jnp.max(scores, axis=-1, keepdims=True))
        weights = jnp.exp(scores - row_peak)
        weights = low(weights / lax.optimization_barrier(jnp.sum(weights, axis=-1, keepdims=True)))
        return jnp.einsum('cjbk,kcd->bjcd', weights, values_low, precision=HIGHEST)
    outputs = lax.map(jax.checkpoint(one_block), (queries.reshape(count_blocks, block_rows, per_group, KV_HEADS, HEAD_DIM), places.reshape(count_blocks, block_rows), segment_ids.reshape(count_blocks, block_rows)))
    return outputs.reshape(length, per_group * KV_HEADS * HEAD_DIM)

def sequence_forward(x_seq, segment_ids, norm_gains, w_query, w_keyvalue, w_output, w_gateup, w_down):
    length = x_seq.shape[0]
    group_heads = HEADS // N_ROW
    per_group = group_heads // KV_HEADS
    cosine, sine_table = angles(segment_ids)
    normed = low(rms_scale(x_seq, norm_gains[0]))
    query_sum = low_back(matmul(normed, w_query)).reshape(length, HEADS, HEAD_DIM)
    pair_sum = matmul(normed, w_keyvalue).reshape(length, KV_HEADS, 2, HEAD_DIM)
    queries = low(rotate(query_sum, cosine[:, None], sine_table[:, None]))
    pieces = []
    for group_index in range(N_ROW):
        keys_rot = low(rotate(low_back(pair_sum[:, :, 0]), cosine[:, None], sine_table[:, None]))
        values_low = low(low_back(pair_sum[:, :, 1]))
        group_queries = queries[:, group_index * group_heads:(group_index + 1) * group_heads]
        group_queries = group_queries.reshape(length, per_group, KV_HEADS, HEAD_DIM)
        pieces.append(attend(group_queries, keys_rot, values_low, segment_ids))
    mixed = low(low_back(jnp.concatenate(pieces, axis=1)))
    middle = x_seq + low_back(matmul(mixed, w_output))
    normed_two = low(rms_scale(middle, norm_gains[1]))
    gate_sum = low_back(matmul(normed_two, w_gateup[:, 0]))
    upward = low_back(matmul(normed_two, w_gateup[:, 1]))
    hidden = low(low_back(jax.nn.silu(gate_sum) * upward))
    return middle + low_back(matmul(hidden, w_down))

def adamw_step(weight, gradient, moment, square, step_rate, decay_rate):
    moment_new = BETA_ONE * moment + (1.0 - BETA_ONE) * gradient
    square_new = BETA_TWO * square + (1.0 - BETA_TWO) * gradient * gradient
    fixed_one = moment_new / (1.0 - BETA_ONE ** STEP)
    fixed_two = square_new / (1.0 - BETA_TWO ** STEP)
    weight_new = weight - step_rate * (fixed_one / (jnp.sqrt(fixed_two) + ADAM_EPS) + decay_rate * weight)
    return (moment_new, square_new, weight_new)

def reference(block_input, cotangent, segments, norm_gains, w_query, w_keyvalue, w_output, w_gateup, w_down, gains_moment, gains_square, query_moment, query_square, keyvalue_moment, keyvalue_square, output_moment, output_square, gateup_moment, gateup_square, down_moment, down_square):
    inputs = block_input.astype(jnp.float32).reshape(N_DP, LEN, D)

    def whole(inputs, norm_gains, w_query, w_keyvalue, w_output, w_gateup, w_down):
        rounded = [low(w_query), low(w_keyvalue), low(w_output), low(w_gateup), low(w_down)]

        def per_sequence(operands):
            return sequence_forward(operands[0], operands[1], norm_gains, rounded[0], rounded[1], rounded[2], rounded[3], rounded[4])
        return lax.map(per_sequence, (inputs, segments))
    outputs, pull_back = jax.vjp(whole, inputs, norm_gains, w_query, w_keyvalue, w_output, w_gateup, w_down)
    gradients = pull_back(cotangent.astype(jnp.float32).reshape(N_DP, LEN, D))
    gains_new = adamw_step(norm_gains, gradients[1], gains_moment, gains_square, 0.6, 0.0)
    query_new = adamw_step(w_query, gradients[2], query_moment, query_square, D ** (-0.5), 0.1)
    keyvalue_new = adamw_step(w_keyvalue, gradients[3], keyvalue_moment, keyvalue_square, D ** (-0.5), 0.1)
    output_new = adamw_step(w_output, gradients[4], output_moment, output_square, (HEADS * HEAD_DIM // 64) ** (-0.5), 0.1)
    gateup_new = adamw_step(w_gateup, gradients[5], gateup_moment, gateup_square, D ** (-0.5), 0.1)
    down_new = adamw_step(w_down, gradients[6], down_moment, down_square, FF ** (-0.5), 0.1)
    return (outputs.reshape(TOKENS, D).astype(jnp.bfloat16), gradients[0].reshape(TOKENS, D), gains_new[0], gains_new[1], gains_new[2], query_new[0], query_new[1], query_new[2], keyvalue_new[0], keyvalue_new[1], keyvalue_new[2], output_new[0], output_new[1], output_new[2], gateup_new[0], gateup_new[1], gateup_new[2], down_new[0], down_new[1], down_new[2])
```

```python
import functools

import jax
import jax.numpy as jnp
from jax import lax
from jax.experimental import pallas as pl
from jax.experimental.pallas import tpu as pltpu
from jax.sharding import Mesh, PartitionSpec as P

D = 2048
HEADS = 32
KV_HEADS = 4
HEAD_DIM = 64
FF = 5632
STEP = 10

EPSILON = 1e-05
BETA_ONE = 0.9
BETA_TWO = 0.999
ADAM_EPS = 1e-08
MASKED = -1e30
SCORE_SCALE = HEAD_DIM ** (-0.5)
LANES = 128
VMEM_LIMIT = 48 * 1024 * 1024


def dot_nn(left, right):
    return lax.dot_general(left, right, (((1,), (0,)), ((), ())), preferred_element_type=jnp.float32)


def dot_nt(left, right):
    return lax.dot_general(left, right, (((1,), (1,)), ((), ())), preferred_element_type=jnp.float32)


def dot_tn(left, right):
    return lax.dot_general(left, right, (((0,), (0,)), ((), ())), preferred_element_type=jnp.float32)


def adamw_step(weight, gradient, moment, square, step_rate, decay_rate):
    moment_new = BETA_ONE * moment + (1.0 - BETA_ONE) * gradient
    square_new = BETA_TWO * square + (1.0 - BETA_TWO) * gradient * gradient
    fixed_one = moment_new / (1.0 - BETA_ONE**STEP)
    fixed_two = square_new / (1.0 - BETA_TWO**STEP)
    weight_new = weight - step_rate * (
        fixed_one / (jnp.sqrt(fixed_two) + ADAM_EPS) + decay_rate * weight
    )
    return (moment_new, square_new, weight_new)


def document_starts(segment_ids):
    places = jnp.arange(segment_ids.shape[0], dtype=jnp.int32)
    starts = jnp.concatenate([jnp.ones((1,), jnp.bool_), segment_ids[1:] != segment_ids[:-1]])
    return lax.cummax(jnp.where(starts, places, 0), axis=0)


def turn(values):
    lane = lax.broadcasted_iota(jnp.int32, values.shape, 1)
    ahead = pltpu.roll(values, LANES - HEAD_DIM // 2, 1)
    behind = pltpu.roll(values, HEAD_DIM // 2, 1)
    return jnp.where(lane % HEAD_DIM < HEAD_DIM // 2, -ahead, behind)


def project_kernel(rows_ref, weight_ref, cos_ref, sin_ref, query_ref, pair_ref):
    sums = dot_nn(rows_ref[...], weight_ref[...])
    cosine, sine = cos_ref[...], sin_ref[...]
    width = query_ref.shape[1]
    lane = lax.broadcasted_iota(jnp.int32, cosine.shape, 1)
    for start in range(0, width, LANES):
        part = sums[:, start : start + LANES]
        turned = (part * cosine + turn(part) * sine).astype(jnp.bfloat16)
        query_ref[:, start : start + LANES] = turned * jnp.bfloat16(SCORE_SCALE)
    for which in range(2):
        part = sums[:, width + which * LANES : width + (which + 1) * LANES]
        is_key = (lane < HEAD_DIM) if which == 0 else (lane >= HEAD_DIM)
        turned = jnp.where(is_key, part * cosine + turn(part) * sine, part)
        pair_ref[:, which * LANES : (which + 1) * LANES] = turned.astype(jnp.bfloat16)


def project(rows, weight, cosine, sine, width, block):
    count = rows.shape[0] // block
    total = weight.shape[1]
    return pl.pallas_call(
        project_kernel,
        grid=(count,),
        in_specs=[
            pl.BlockSpec((block, rows.shape[1]), lambda i: (i, 0)),
            pl.BlockSpec(weight.shape, lambda i: (0, 0)),
            pl.BlockSpec((block, LANES), lambda i: (i, 0)),
            pl.BlockSpec((block, LANES), lambda i: (i, 0)),
        ],
        out_specs=[
            pl.BlockSpec((block, width), lambda i: (i, 0)),
            pl.BlockSpec((block, total - width), lambda i: (i, 0)),
        ],
        out_shape=[
            jax.ShapeDtypeStruct((rows.shape[0], width), jnp.bfloat16),
            jax.ShapeDtypeStruct((rows.shape[0], total - width), jnp.bfloat16),
        ],
        compiler_params=pltpu.CompilerParams(vmem_limit_bytes=VMEM_LIMIT),
        cost_estimate=pl.CostEstimate(
            flops=2 * rows.shape[0] * rows.shape[1] * total,
            bytes_accessed=rows.size * 2 + weight.size * 2,
            transcendentals=0,
        ),
        name="project",
    )(rows, weight, cosine, sine)


def stack_heads(values):
    return jnp.concatenate(
        [values[:, start : start + LANES] for start in range(0, values.shape[1], LANES)], axis=0
    )


def block_of(meta_ref, chunk, step, parts, lines):
    base = chunk * (2 + parts)
    key_block = meta_ref[base + 1] - step
    slot = meta_ref[base + 2 + key_block // lines]
    own_line = meta_ref[pl.num_programs(0) * (2 + parts)]
    shift = lax.rem(own_line - lax.rem(key_block, lines) + lines, lines)
    return (key_block, slot, shift)


def attend_kernel(parts, lines, meta_ref, query_ref, *refs):
    pair_refs, (info_ref, out_ref, log_ref, held) = (refs[:lines], refs[lines:])
    chunk = pl.program_id(0)
    block = query_ref.shape[0]
    heads = query_ref.shape[1] // LANES

    @pl.when(chunk == 0)
    def _():
        for line in range(lines):
            held[line] = pair_refs[line][...]

    stacked = stack_heads(query_ref[...])
    lane = lax.broadcasted_iota(jnp.int32, stacked.shape, 1)
    place = jnp.concatenate([info_ref[0, 0:1, :]] * heads, axis=1)
    start = jnp.concatenate([info_ref[0, 1:2, :]] * heads, axis=1)
    base = chunk * (2 + parts)
    steps = meta_ref[base + 1] - meta_ref[base] + 1
    width = heads * block
    outs = []
    for which in range(2):
        is_key = (lane < HEAD_DIM) if which == 0 else (lane >= HEAD_DIM)
        queries = jnp.where(is_key, stacked, jnp.zeros_like(stacked))

        def body(step, carry):
            peak, total, mixed = carry
            key_block, slot, shift = block_of(meta_ref, chunk, step, parts, lines)
            pair = held[shift, slot, :, which * LANES : (which + 1) * LANES]
            scores = dot_nt(pair, queries)
            key_place = key_block * block + lax.broadcasted_iota(jnp.int32, (block, width), 0)
            scores = jnp.where((key_place <= place) & (key_place >= start), scores, MASKED)
            new_peak = jnp.maximum(peak, jnp.max(scores, axis=0, keepdims=True))
            weights = jnp.exp(scores - new_peak)
            shrink = jnp.exp(peak - new_peak)
            total = total * shrink + jnp.sum(weights, axis=0, keepdims=True)
            mixed = mixed * shrink + dot_tn(pair, weights.astype(jnp.bfloat16))
            return (new_peak, total, mixed)

        peak, total, mixed = lax.fori_loop(
            0,
            steps,
            body,
            (
                jnp.full((1, width), MASKED, jnp.float32),
                jnp.zeros((1, width), jnp.float32),
                jnp.zeros((LANES, width), jnp.float32),
            ),
        )
        log_ref[0, which : which + 1, :] = peak + jnp.log(total)
        outs.append(mixed / total)
    joined = jnp.concatenate([outs[1][:HEAD_DIM], outs[0][HEAD_DIM:]], axis=0)
    rows = joined.T.astype(jnp.bfloat16)
    for head in range(heads):
        out_ref[:, head * LANES : (head + 1) * LANES] = rows[head * block : (head + 1) * block]


def attend(meta, queries, pairs, info, parts):
    chunks, block = (info.shape[0], info.shape[2])
    width = queries.shape[1]
    heads = width // LANES
    lines = len(pairs)
    shape = (chunks, block, 2 * LANES)
    steps = 3 * chunks
    return pl.pallas_call(
        functools.partial(attend_kernel, parts, lines),
        grid_spec=pltpu.PrefetchScalarGridSpec(
            num_scalar_prefetch=1,
            grid=(chunks,),
            in_specs=[pl.BlockSpec((block, width), lambda i, m: (i, 0))]
            + [pl.BlockSpec(shape, lambda i, m: (0, 0, 0))] * lines
            + [pl.BlockSpec((1, 2, block), lambda i, m: (i, 0, 0))],
            out_specs=[
                pl.BlockSpec((block, width), lambda i, m: (i, 0)),
                pl.BlockSpec((1, 2, heads * block), lambda i, m: (i, 0, 0)),
            ],
            scratch_shapes=[pltpu.VMEM((lines,) + shape, jnp.bfloat16)],
        ),
        out_shape=[
            jax.ShapeDtypeStruct(queries.shape, jnp.bfloat16),
            jax.ShapeDtypeStruct((chunks, 2, heads * block), jnp.float32),
        ],
        compiler_params=pltpu.CompilerParams(vmem_limit_bytes=VMEM_LIMIT),
        cost_estimate=pl.CostEstimate(
            flops=steps * 2 * 2 * 2 * heads * block * block * LANES,
            bytes_accessed=queries.size * 4 + lines * pairs[0].size * 2,
            transcendentals=steps * 2 * heads * block * block,
        ),
        name="attend",
    )(meta, queries, *[pair.reshape(shape) for pair in pairs], info)


def attend_back_kernel(parts, lines, meta_ref, query_ref, *refs):
    pair_refs = refs[:lines]
    grad_ref, mixed_ref, log_ref, info_ref, cos_ref, sin_ref = refs[lines : lines + 6]
    query_out = refs[lines + 6]
    pair_outs = refs[lines + 7 : lines + 7 + lines]
    held, sums = refs[lines + 7 + lines :]
    chunk = pl.program_id(0)
    block = query_ref.shape[0]
    heads = query_ref.shape[1] // LANES

    @pl.when(chunk == 0)
    def _():
        for line in range(lines):
            held[line] = pair_refs[line][...]
        sums[...] = jnp.zeros_like(sums)

    stacked = stack_heads(query_ref[...])
    stacked_grad = stack_heads(grad_ref[...])
    product = stacked_grad.astype(jnp.float32) * stack_heads(mixed_ref[...]).astype(jnp.float32)
    lane = lax.broadcasted_iota(jnp.int32, stacked.shape, 1)
    place = jnp.concatenate([info_ref[0, 0:1, :]] * heads, axis=1)
    start = jnp.concatenate([info_ref[0, 1:2, :]] * heads, axis=1)
    base = chunk * (2 + parts)
    steps = meta_ref[base + 1] - meta_ref[base] + 1
    width = heads * block
    grads = []
    for which in range(2):
        is_key = (lane < HEAD_DIM) if which == 0 else (lane >= HEAD_DIM)
        queries = jnp.where(is_key, stacked, jnp.zeros_like(stacked))
        grad = jnp.where(is_key, jnp.zeros_like(stacked_grad), stacked_grad)
        own = jnp.where(is_key, 0.0, product)
        centre = lax.dot_general(
            jnp.ones((8, LANES), jnp.float32),
            own,
            (((1,), (1,)), ((), ())),
            precision=lax.Precision.HIGHEST,
            preferred_element_type=jnp.float32,
        )[0:1]
        logs = log_ref[0, which : which + 1, :]

        def body(step, grad_query):
            key_block, slot, shift = block_of(meta_ref, chunk, step, parts, lines)
            columns = slice(which * LANES, (which + 1) * LANES)
            pair = held[shift, slot, :, columns]
            scores = dot_nt(pair, queries)
            key_place = key_block * block + lax.broadcasted_iota(jnp.int32, (block, width), 0)
            scores = jnp.where((key_place <= place) & (key_place >= start), scores, MASKED)
            weights = jnp.exp(scores - logs)
            grad_scores = (weights * (dot_nt(pair, grad) - centre)).astype(jnp.bfloat16)
            sums[shift, slot, :, columns] += dot_nn(grad_scores, queries) + dot_nn(
                weights.astype(jnp.bfloat16), grad
            )
            return grad_query + dot_tn(pair, grad_scores)

        grads.append(lax.fori_loop(0, steps, body, jnp.zeros((LANES, width), jnp.float32)))
    joined = jnp.concatenate([grads[0][:HEAD_DIM], grads[1][HEAD_DIM:]], axis=0)
    rows = joined.T * SCORE_SCALE
    cosine, sine = cos_ref[...], sin_ref[...]
    for head in range(heads):
        part = rows[head * block : (head + 1) * block]
        back = part * cosine - turn(part) * sine
        query_out[:, head * LANES : (head + 1) * LANES] = back.astype(jnp.bfloat16)

    @pl.when(chunk == pl.num_programs(0) - 1)
    def _():
        for line in range(lines):
            pair_outs[line][...] = sums[line].astype(jnp.bfloat16)


def attend_back(meta, queries, pairs, grad_mixed, mixed, logs, info, cosine, sine, parts):
    chunks, block = (info.shape[0], info.shape[2])
    width = queries.shape[1]
    heads = width // LANES
    lines = len(pairs)
    shape = (chunks, block, 2 * LANES)
    steps = 3 * chunks
    wide = pl.BlockSpec((block, width), lambda i, m: (i, 0))
    table = pl.BlockSpec((block, LANES), lambda i, m: (i, 0))
    whole = pl.BlockSpec(shape, lambda i, m: (0, 0, 0))
    outs = pl.pallas_call(
        functools.partial(attend_back_kernel, parts, lines),
        grid_spec=pltpu.PrefetchScalarGridSpec(
            num_scalar_prefetch=1,
            grid=(chunks,),
            in_specs=[wide]
            + [whole] * lines
            + [
                wide,
                wide,
                pl.BlockSpec((1, 2, heads * block), lambda i, m: (i, 0, 0)),
                pl.BlockSpec((1, 2, block), lambda i, m: (i, 0, 0)),
                table,
                table,
            ],
            out_specs=[wide] + [whole] * lines,
            scratch_shapes=[
                pltpu.VMEM((lines,) + shape, jnp.bfloat16),
                pltpu.VMEM((lines,) + shape, jnp.float32),
            ],
        ),
        out_shape=[jax.ShapeDtypeStruct(queries.shape, jnp.bfloat16)]
        + [jax.ShapeDtypeStruct(shape, jnp.bfloat16)] * lines,
        compiler_params=pltpu.CompilerParams(vmem_limit_bytes=VMEM_LIMIT),
        cost_estimate=pl.CostEstimate(
            flops=steps * 2 * 5 * 2 * heads * block * block * LANES,
            bytes_accessed=queries.size * 8 + 2 * lines * pairs[0].size * 2,
            transcendentals=steps * 2 * heads * block * block,
        ),
        name="attend_back",
    )(
        meta,
        queries,
        *[pair.reshape(shape) for pair in pairs],
        grad_mixed,
        mixed,
        logs,
        info,
        cosine,
        sine,
    )
    return (outs[0], [out.reshape(chunks * block, 2 * LANES) for out in outs[1:]])


def pair_back_kernel(*refs):
    *part_refs, cos_ref, sin_ref, out_ref = refs
    cosine, sine = cos_ref[...], sin_ref[...]
    lane = lax.broadcasted_iota(jnp.int32, cosine.shape, 1)
    for which in range(2):
        columns = slice(which * LANES, (which + 1) * LANES)
        total = part_refs[0][:, columns].astype(jnp.float32)
        for ref in part_refs[1:]:
            total = total + ref[:, columns].astype(jnp.float32)
        is_key = (lane < HEAD_DIM) if which == 0 else (lane >= HEAD_DIM)
        total = jnp.where(is_key, total * cosine - turn(total) * sine, total)
        out_ref[:, columns] = total.astype(jnp.bfloat16)


def pair_back(parts, cosine, sine, block):
    rows, columns = parts[0].shape
    tile = pl.BlockSpec((block, columns), lambda i: (i, 0))
    table = pl.BlockSpec((block, LANES), lambda i: (i, 0))
    return pl.pallas_call(
        pair_back_kernel,
        grid=(rows // block,),
        in_specs=[tile] * len(parts) + [table, table],
        out_specs=tile,
        out_shape=jax.ShapeDtypeStruct((rows, columns), jnp.bfloat16),
        compiler_params=pltpu.CompilerParams(vmem_limit_bytes=VMEM_LIMIT),
        name="pair_back",
    )(*parts, cosine, sine)


def on_device(
    sizes,
    block_input,
    cotangent,
    segments,
    norm_gains,
    w_query,
    w_keyvalue,
    w_output,
    w_gateup,
    w_down,
    gains_moment,
    gains_square,
    query_moment,
    query_square,
    keyvalue_moment,
    keyvalue_square,
    output_moment,
    output_square,
    gateup_moment,
    gateup_square,
    down_moment,
    down_square,
):
    rows_on, lines = sizes
    y, core, row, line = [lax.axis_index(name) for name in ("y", "core", "row", "col")]
    length = segments.shape[1]
    block = block_input.shape[0] // lines
    wide = block_input.shape[1]
    half = wide // 2
    slots = 2 * rows_on
    per_row = w_query.shape[1] // (KV_HEADS * HEAD_DIM)
    query_width = per_row * LANES
    hidden_here = w_gateup.shape[2] // 2

    def shift(value, axis, size, by):
        return lax.ppermute(value, axis, [(i, (i + by) % size) for i in range(size)])

    def other_y(value):
        return lax.ppermute(value, "y", [(0, 1), (1, 0)])

    def place_of(y_at, core_at, row_at):
        return (y_at * 2 + core_at) * rows_on + row_at

    first_pairs, second_pairs = ([], [])
    for y_at in range(2):
        for core_at in range(2):
            for row_at in range(rows_on):
                over_row = (
                    place_of(y_at, core_at, row_at),
                    place_of(y_at, core_at, (row_at + 1) % rows_on),
                )
                over_y = (place_of(y_at, core_at, row_at), place_of(1 - y_at, core_at, row_at))
                first_pairs.append(over_row if core_at == 0 else over_y)
                second_pairs.append(over_y if core_at == 0 else over_row)
    near = ("y", "core", "row")

    def gather_tokens(own):
        if rows_on == 2:
            first = lax.ppermute(own, near, first_pairs)
            second = lax.ppermute(own, near, second_pairs)
            third = lax.ppermute(first, near, second_pairs)
            return jnp.concatenate([own, first, second, third], axis=0)
        parts = [own] + [shift(own, "row", rows_on, by) for by in range(1, rows_on)]
        return jnp.concatenate(parts + [other_y(part) for part in parts], axis=0)

    def reduce_tokens(partial):
        parts = [partial[i * block : (i + 1) * block] for i in range(slots)]
        if rows_on == 2:
            third = lax.ppermute(parts[3], near, second_pairs)
            second = lax.ppermute(parts[2], near, second_pairs)
            first = parts[1].astype(jnp.float32) + third.astype(jnp.float32)
            first = lax.ppermute(first.astype(jnp.bfloat16), near, first_pairs)
            own = parts[0].astype(jnp.float32) + second.astype(jnp.float32)
            return own + first.astype(jnp.float32)
        sums = [
            parts[i].astype(jnp.float32) + other_y(parts[rows_on + i]).astype(jnp.float32)
            for i in range(rows_on)
        ]
        total = sums[0]
        for by in range(1, rows_on):
            moved = shift(sums[by].astype(jnp.bfloat16), "row", rows_on, -by)
            total = total + moved.astype(jnp.float32)
        return total

    if rows_on == 2:
        slot_y = [y, jnp.where(core == 0, y, 1 - y), jnp.where(core == 0, 1 - y, y), 1 - y]
        slot_row = [row, jnp.where(core == 0, 1 - row, row), jnp.where(core == 0, row, 1 - row), 1 - row]
    else:
        slot_y = [y] * rows_on + [1 - y] * rows_on
        slot_row = [(row - by) % rows_on for by in range(rows_on)] * 2

    def pick(parts, index):
        return lax.dynamic_index_in_dim(jnp.stack(parts), index, 0, keepdims=False)

    def tokens_from_features(values):
        parts = []
        for by in range(lines):
            part = lax.dynamic_slice_in_dim(values, ((line + by) % lines) * block, block, 0)
            parts.append(part if by == 0 else shift(part, "col", lines, by))
        blocks = [pick(parts, (line - at) % lines) for at in range(lines)]
        return jnp.concatenate([b[:, :half] for b in blocks] + [b[:, half:] for b in blocks], axis=1)

    def features_from_tokens(values):
        blocks = [
            jnp.concatenate(
                [
                    values[:, at * half : (at + 1) * half],
                    values[:, D // 2 + at * half : D // 2 + (at + 1) * half],
                ],
                axis=1,
            )
            for at in range(lines)
        ]
        parts = []
        for by in range(lines):
            part = pick(blocks, (line + by) % lines)
            parts.append(part if by == 0 else shift(part, "col", lines, by))
        return jnp.concatenate([pick(parts, (line - at) % lines) for at in range(lines)], axis=0)

    def half_rows(values):
        return lax.dynamic_slice_in_dim(values, core * half, half, 0)

    def half_columns(values):
        return lax.dynamic_slice_in_dim(values, core * half, half, 1)

    def gather_weight(piece):
        return lax.all_gather(piece, ("core", "col"), axis=0, tiled=True)

    query_rows = half_rows(w_query).astype(jnp.bfloat16)
    pair_rows = half_rows(w_keyvalue).astype(jnp.bfloat16)

    def joint_of(at):
        pieces = [
            query_rows[:, (2 * j + at) * LANES : (2 * j + at + 1) * LANES] for j in range(per_row)
        ]
        pair = pair_rows[:, at * 2 * LANES : (at + 1) * 2 * LANES]
        pieces += [
            pair[:, :LANES],
            pair[:, LANES + HEAD_DIM :],
            pair[:, LANES : LANES + HEAD_DIM],
        ]
        return jnp.concatenate(pieces, axis=1)

    joint_weight = gather_weight(jnp.where(y == 0, joint_of(0), joint_of(1)))
    output_columns = half_columns(w_output).astype(jnp.bfloat16)

    def output_of(at):
        pieces = []
        for j in range(per_row):
            base = (2 * j + at) * LANES
            pieces += [
                output_columns[base + HEAD_DIM : base + LANES],
                output_columns[base : base + HEAD_DIM],
            ]
        return jnp.concatenate(pieces, axis=0)

    output_weight = gather_weight(jnp.where(y == 0, output_of(0), output_of(1)).T)
    gateup_piece = lax.dynamic_slice(
        w_gateup, (core * half, 0, y * hidden_here), (half, 2, hidden_here)
    ).astype(jnp.bfloat16)
    gateup_weight = gather_weight(
        jnp.concatenate([gateup_piece[:, 0], gateup_piece[:, 1]], axis=1)
    )
    down_piece = lax.dynamic_slice(
        w_down, (y * hidden_here, core * half), (hidden_here, half)
    ).astype(jnp.bfloat16)
    down_weight = gather_weight(down_piece.T)

    gain_parts = [norm_gains] + [shift(norm_gains, "col", lines, by) for by in range(1, lines)]
    gain_blocks = [pick(gain_parts, (line - at) % lines) for at in range(lines)]
    gains = jnp.concatenate(
        [b[:, :half] for b in gain_blocks] + [b[:, half:] for b in gain_blocks], axis=1
    )

    own_starts = document_starts(segments[0])
    other_starts = document_starts(other_y(segments)[0])
    frequency = 10000.0 ** (-2.0 * jnp.arange(HEAD_DIM // 2, dtype=jnp.float32) / HEAD_DIM)
    starts, places, meta = ([], [], [])
    for slot in range(slots):
        begin = slot_row[slot] * (lines * block) + line * block
        of_chunk = lax.dynamic_slice_in_dim(
            jnp.where(slot_y[slot] == y, own_starts, other_starts), begin, block, 0
        )
        starts.append(of_chunk)
        places.append(begin + jnp.arange(block, dtype=jnp.int32))
        meta += [of_chunk[0] // block, begin // block]
        for row_at in range(rows_on):
            found = jnp.int32(0)
            for other in range(slots):
                same = (slot_y[other] == slot_y[slot]) & (slot_row[other] == row_at)
                found = found + jnp.where(same, other, 0)
            meta.append(found)
    meta = jnp.stack([jnp.asarray(m, jnp.int32) for m in meta + [line]])
    starts, places = (jnp.stack(starts), jnp.stack(places))
    info = jnp.stack([places, starts], axis=1)
    offsets = (places - starts).astype(jnp.float32).reshape(-1)
    phases = offsets[:, None] * jnp.tile(frequency, LANES // (HEAD_DIM // 2))[None, :]
    cosine, sine = (jnp.cos(phases), jnp.sin(phases))

    residual_low = tokens_from_features(block_input)
    residual = residual_low.astype(jnp.float32)
    scale_one = lax.rsqrt(jnp.mean(residual * residual, axis=1, keepdims=True) + EPSILON)
    normed_one = gather_tokens((residual * scale_one * gains[0]).astype(jnp.bfloat16))
    queries, pair = project(normed_one, joint_weight, cosine, sine, query_width, block)
    pairs = [pair] + [shift(pair, "col", lines, by) for by in range(1, lines)]
    mixed, logs = attend(meta, queries, pairs, info, rows_on)
    attn_sum = reduce_tokens(dot_nt(mixed, output_weight).astype(jnp.bfloat16))
    middle = residual + attn_sum
    scale_two = lax.rsqrt(jnp.mean(middle * middle, axis=1, keepdims=True) + EPSILON)
    normed_two = gather_tokens((middle * scale_two * gains[1]).astype(jnp.bfloat16))
    pair_sum = dot_nn(normed_two, gateup_weight)
    gate_sum, upward = (pair_sum[:, :hidden_here], pair_sum[:, hidden_here:])
    sigmoid_gate = jax.nn.sigmoid(gate_sum)
    silu_gate = gate_sum * sigmoid_gate
    hidden = (silu_gate * upward).astype(jnp.bfloat16)

    cot_low = tokens_from_features(cotangent)
    cot = gather_tokens(cot_low)
    grad_hidden = dot_nn(cot, down_weight)
    grad_gate = grad_hidden * upward * sigmoid_gate * (1.0 + gate_sum * (1.0 - sigmoid_gate))
    grad_pair = jnp.concatenate(
        [grad_gate.astype(jnp.bfloat16), (grad_hidden * silu_gate).astype(jnp.bfloat16)], axis=1
    )
    grad_normed_two = reduce_tokens(dot_nt(grad_pair, gateup_weight).astype(jnp.bfloat16))

    def norm_back(values, scale, grad_normed, gain):
        scaled = grad_normed * gain
        total = jnp.sum(scaled * values, axis=1, keepdims=True)
        return scale * scaled - values * (scale**3 * total / D)

    grad_middle = cot_low.astype(jnp.float32) + norm_back(
        middle, scale_two, grad_normed_two, gains[1]
    )
    gain_two = jnp.sum(grad_normed_two * middle * scale_two, axis=0)

    ffn_sum = reduce_tokens(dot_nt(hidden, down_weight).astype(jnp.bfloat16))
    layer_output = features_from_tokens((middle + ffn_sum).astype(jnp.bfloat16))

    def scatter_grad(gradient):
        return lax.psum_scatter(
            gradient.astype(jnp.bfloat16), ("core", "col"), scatter_dimension=0, tiled=True
        )

    def collect(piece):
        whole = lax.all_gather(piece, ("y", "core"), axis=0, tiled=True)
        return (whole[:wide].astype(jnp.float32), whole[wide:].astype(jnp.float32))

    grad_down = collect(scatter_grad(dot_tn(cot, hidden)))
    grad_gateup = collect(scatter_grad(dot_tn(normed_two, grad_pair)))

    back = gather_tokens(grad_middle.astype(jnp.bfloat16))
    grad_mixed = dot_nn(back, output_weight).astype(jnp.bfloat16)
    grad_output = collect(scatter_grad(dot_tn(back, mixed)))
    grad_query, grad_parts = attend_back(
        meta, queries, pairs, grad_mixed, mixed, logs, info, cosine, sine, rows_on
    )
    grad_parts = [grad_parts[0]] + [
        shift(grad_parts[by], "col", lines, -by) for by in range(1, lines)
    ]
    grad_keyvalue = pair_back(grad_parts, cosine, sine, block)
    grad_joint = jnp.concatenate([grad_query, grad_keyvalue], axis=1)
    grad_normed_one = reduce_tokens(dot_nt(grad_joint, joint_weight).astype(jnp.bfloat16))
    input_grad = grad_middle + norm_back(residual, scale_one, grad_normed_one, gains[0])
    gain_one = jnp.sum(grad_normed_one * residual * scale_one, axis=0)
    input_grad = features_from_tokens(input_grad.astype(jnp.bfloat16)).astype(jnp.float32)
    joint_piece = scatter_grad(dot_tn(normed_one, grad_joint))
    pair_piece = joint_piece[:, query_width:]
    pair_total = pair_piece.astype(jnp.float32)
    for by in range(1, rows_on):
        pair_total = pair_total + shift(pair_piece, "row", rows_on, by).astype(jnp.float32)
    joint_piece = jnp.concatenate(
        [joint_piece[:, :query_width], pair_total.astype(jnp.bfloat16)], axis=1
    )
    grad_joint_sum = collect(joint_piece)

    gain_sums = jnp.stack([gain_one, gain_two])
    blocks = [
        jnp.concatenate(
            [
                gain_sums[:, at * half : (at + 1) * half],
                gain_sums[:, D // 2 + at * half : D // 2 + (at + 1) * half],
            ],
            axis=1,
        )
        for at in range(lines)
    ]
    grad_gains = blocks_total = pick(blocks, line)
    for by in range(1, lines):
        grad_gains = grad_gains + shift(pick(blocks, (line + by) % lines), "col", lines, by)
    for axis, size in (("core", 2), ("y", 2), ("row", rows_on)):
        blocks_total = grad_gains
        for by in range(1, size):
            grad_gains = grad_gains + shift(blocks_total, axis, size, by)

    gains_new = adamw_step(norm_gains, grad_gains, gains_moment, gains_square, 0.6, 0.0)
    query_grad = jnp.concatenate(
        [
            grad_joint_sum[at][:, j * LANES : (j + 1) * LANES]
            for j in range(per_row)
            for at in range(2)
        ],
        axis=1,
    )
    pair_grad = jnp.concatenate(
        [
            piece
            for at in range(2)
            for piece in (
                grad_joint_sum[at][:, query_width : query_width + LANES],
                grad_joint_sum[at][:, query_width + LANES + HEAD_DIM :],
                grad_joint_sum[at][:, query_width + LANES : query_width + LANES + HEAD_DIM],
            )
        ],
        axis=1,
    )
    turned = [grad_output[at].T for at in range(2)]
    output_grad = jnp.concatenate(
        [
            turned[at][j * LANES + part : j * LANES + part + HEAD_DIM]
            for j in range(per_row)
            for at in range(2)
            for part in (HEAD_DIM, 0)
        ],
        axis=0,
    )
    gateup_grad = jnp.concatenate(
        [grad_gateup[at].reshape(wide, 2, hidden_here) for at in range(2)], axis=2
    )
    down_grad = jnp.concatenate([grad_down[at].T for at in range(2)], axis=0)
    query_new = adamw_step(w_query, query_grad, query_moment, query_square, D ** (-0.5), 0.1)
    keyvalue_new = adamw_step(
        w_keyvalue, pair_grad, keyvalue_moment, keyvalue_square, D ** (-0.5), 0.1
    )
    output_new = adamw_step(
        w_output, output_grad, output_moment, output_square, (HEADS * HEAD_DIM // 64) ** (-0.5), 0.1
    )
    gateup_new = adamw_step(w_gateup, gateup_grad, gateup_moment, gateup_square, D ** (-0.5), 0.1)
    down_new = adamw_step(w_down, down_grad, down_moment, down_square, FF ** (-0.5), 0.1)
    return (
        layer_output,
        input_grad,
        *gains_new,
        *query_new,
        *keyvalue_new,
        *output_new,
        *gateup_new,
        *down_new,
    )


def solution(mesh):
    dp, rows_on, lines = (mesh.shape["dp"], mesh.shape["row"], mesh.shape["col"])
    split = Mesh(mesh.devices.reshape(dp // 2, 2, rows_on, lines), ("y", "core", "row", "col"))
    tokens = P(("y", "core", "row"), "col")
    narrow, wide = (P("col", "row"), P("row", "col"))
    gains, pair, gateup = (P(None, "col"), P("col", None), P("col", None, "row"))
    return jax.shard_map(
        functools.partial(on_device, (rows_on, lines)),
        mesh=split,
        in_specs=(
            tokens,
            tokens,
            P(("y", "core"), None),
            gains,
            narrow,
            pair,
            wide,
            gateup,
            wide,
            gains,
            gains,
            narrow,
            narrow,
            pair,
            pair,
            wide,
            wide,
            gateup,
            gateup,
            wide,
            wide,
        ),
        out_specs=(tokens, tokens)
        + (gains,) * 3
        + (narrow,) * 3
        + (pair,) * 3
        + (wide,) * 3
        + (gateup,) * 3
        + (wide,) * 3,
        check_vma=False,
    )
```

```python
import functools

import jax
import jax.numpy as jnp
from jax import lax
from jax.experimental import pallas as pl
from jax.experimental.pallas import tpu as pltpu
from jax.sharding import Mesh, PartitionSpec as P

D = 2048
HEADS = 32
KV_HEADS = 4
HEAD_DIM = 64
FF = 5632
STEP = 10

EPSILON = 1e-05
BETA_ONE = 0.9
BETA_TWO = 0.999
ADAM_EPS = 1e-08
MASKED = -1e30
SCORE_SCALE = HEAD_DIM ** (-0.5)
LANES = 128
VMEM_LIMIT = 48 * 1024 * 1024


def dot_nn(left, right):
    return lax.dot_general(left, right, (((1,), (0,)), ((), ())), preferred_element_type=jnp.float32)


def dot_nt(left, right):
    return lax.dot_general(left, right, (((1,), (1,)), ((), ())), preferred_element_type=jnp.float32)


def dot_tn(left, right):
    return lax.dot_general(left, right, (((0,), (0,)), ((), ())), preferred_element_type=jnp.float32)


def adamw_step(weight, gradient, moment, square, step_rate, decay_rate):
    moment_new = BETA_ONE * moment + (1.0 - BETA_ONE) * gradient
    square_new = BETA_TWO * square + (1.0 - BETA_TWO) * gradient * gradient
    fixed_one = moment_new / (1.0 - BETA_ONE**STEP)
    fixed_two = square_new / (1.0 - BETA_TWO**STEP)
    weight_new = weight - step_rate * (
        fixed_one / (jnp.sqrt(fixed_two) + ADAM_EPS) + decay_rate * weight
    )
    return (moment_new, square_new, weight_new)


def document_starts(segment_ids):
    places = jnp.arange(segment_ids.shape[0], dtype=jnp.int32)
    starts = jnp.concatenate([jnp.ones((1,), jnp.bool_), segment_ids[1:] != segment_ids[:-1]])
    return lax.cummax(jnp.where(starts, places, 0), axis=0)


def turn(values):
    lane = lax.broadcasted_iota(jnp.int32, values.shape, 1)
    ahead = pltpu.roll(values, LANES - HEAD_DIM // 2, 1)
    behind = pltpu.roll(values, HEAD_DIM // 2, 1)
    return jnp.where(lane % HEAD_DIM < HEAD_DIM // 2, -ahead, behind)


def project_kernel(rows_ref, weight_ref, cos_ref, sin_ref, query_ref, pair_ref):
    sums = dot_nn(rows_ref[...], weight_ref[...])
    cosine, sine = cos_ref[...], sin_ref[...]
    width = query_ref.shape[1]
    lane = lax.broadcasted_iota(jnp.int32, cosine.shape, 1)
    for start in range(0, width, LANES):
        part = sums[:, start : start + LANES]
        turned = (part * cosine + turn(part) * sine).astype(jnp.bfloat16)
        query_ref[:, start : start + LANES] = turned * jnp.bfloat16(SCORE_SCALE)
    for which in range(2):
        part = sums[:, width + which * LANES : width + (which + 1) * LANES]
        is_key = (lane < HEAD_DIM) if which == 0 else (lane >= HEAD_DIM)
        turned = jnp.where(is_key, part * cosine + turn(part) * sine, part)
        pair_ref[:, which * LANES : (which + 1) * LANES] = turned.astype(jnp.bfloat16)


def project(rows, weight, cosine, sine, width, block):
    count = rows.shape[0] // block
    total = weight.shape[1]
    return pl.pallas_call(
        project_kernel,
        grid=(count,),
        in_specs=[
            pl.BlockSpec((block, rows.shape[1]), lambda i: (i, 0)),
            pl.BlockSpec(weight.shape, lambda i: (0, 0)),
            pl.BlockSpec((block, LANES), lambda i: (i, 0)),
            pl.BlockSpec((block, LANES), lambda i: (i, 0)),
        ],
        out_specs=[
            pl.BlockSpec((block, width), lambda i: (i, 0)),
            pl.BlockSpec((block, total - width), lambda i: (i, 0)),
        ],
        out_shape=[
            jax.ShapeDtypeStruct((rows.shape[0], width), jnp.bfloat16),
            jax.ShapeDtypeStruct((rows.shape[0], total - width), jnp.bfloat16),
        ],
        compiler_params=pltpu.CompilerParams(vmem_limit_bytes=VMEM_LIMIT),
        cost_estimate=pl.CostEstimate(
            flops=2 * rows.shape[0] * rows.shape[1] * total,
            bytes_accessed=rows.size * 2 + weight.size * 2,
            transcendentals=0,
        ),
        name="project",
    )(rows, weight, cosine, sine)


def stack_heads(values):
    return jnp.concatenate(
        [values[:, start : start + LANES] for start in range(0, values.shape[1], LANES)], axis=0
    )


def block_of(meta_ref, chunk, step, parts, lines):
    base = chunk * (2 + parts)
    key_block = meta_ref[base + 1] - step
    slot = meta_ref[base + 2 + key_block // lines]
    own_line = meta_ref[pl.num_programs(0) * (2 + parts)]
    shift = lax.rem(own_line - lax.rem(key_block, lines) + lines, lines)
    return (key_block, slot, shift)


def attend_kernel(parts, lines, meta_ref, query_ref, *refs):
    pair_refs, (info_ref, out_ref, log_ref, held) = (refs[:lines], refs[lines:])
    chunk = pl.program_id(0)
    block = query_ref.shape[0]
    heads = query_ref.shape[1] // LANES

    @pl.when(chunk == 0)
    def _():
        for line in range(lines):
            held[line] = pair_refs[line][...]

    stacked = stack_heads(query_ref[...])
    lane = lax.broadcasted_iota(jnp.int32, stacked.shape, 1)
    place = jnp.concatenate([info_ref[0, 0:1, :]] * heads, axis=1)
    start = jnp.concatenate([info_ref[0, 1:2, :]] * heads, axis=1)
    base = chunk * (2 + parts)
    steps = meta_ref[base + 1] - meta_ref[base] + 1
    width = heads * block
    outs = []
    for which in range(2):
        is_key = (lane < HEAD_DIM) if which == 0 else (lane >= HEAD_DIM)
        queries = jnp.where(is_key, stacked, jnp.zeros_like(stacked))

        def body(step, carry):
            peak, total, mixed = carry
            key_block, slot, shift = block_of(meta_ref, chunk, step, parts, lines)
            pair = held[shift, slot, :, which * LANES : (which + 1) * LANES]
            scores = dot_nt(pair, queries)
            key_place = key_block * block + lax.broadcasted_iota(jnp.int32, (block, width), 0)
            scores = jnp.where((key_place <= place) & (key_place >= start), scores, MASKED)
            new_peak = jnp.maximum(peak, jnp.max(scores, axis=0, keepdims=True))
            weights = jnp.exp(scores - new_peak)
            shrink = jnp.exp(peak - new_peak)
            total = total * shrink + jnp.sum(weights, axis=0, keepdims=True)
            mixed = mixed * shrink + dot_tn(pair, weights.astype(jnp.bfloat16))
            return (new_peak, total, mixed)

        peak, total, mixed = lax.fori_loop(
            0,
            steps,
            body,
            (
                jnp.full((1, width), MASKED, jnp.float32),
                jnp.zeros((1, width), jnp.float32),
                jnp.zeros((LANES, width), jnp.float32),
            ),
        )
        log_ref[0, which : which + 1, :] = peak + jnp.log(total)
        outs.append(mixed / total)
    joined = jnp.concatenate([outs[1][:HEAD_DIM], outs[0][HEAD_DIM:]], axis=0)
    rows = joined.T.astype(jnp.bfloat16)
    for head in range(heads):
        out_ref[:, head * LANES : (head + 1) * LANES] = rows[head * block : (head + 1) * block]


def attend(meta, queries, pairs, info, parts):
    chunks, block = (info.shape[0], info.shape[2])
    width = queries.shape[1]
    heads = width // LANES
    lines = len(pairs)
    shape = (chunks, block, 2 * LANES)
    steps = 3 * chunks
    return pl.pallas_call(
        functools.partial(attend_kernel, parts, lines),
        grid_spec=pltpu.PrefetchScalarGridSpec(
            num_scalar_prefetch=1,
            grid=(chunks,),
            in_specs=[pl.BlockSpec((block, width), lambda i, m: (i, 0))]
            + [pl.BlockSpec(shape, lambda i, m: (0, 0, 0))] * lines
            + [pl.BlockSpec((1, 2, block), lambda i, m: (i, 0, 0))],
            out_specs=[
                pl.BlockSpec((block, width), lambda i, m: (i, 0)),
                pl.BlockSpec((1, 2, heads * block), lambda i, m: (i, 0, 0)),
            ],
            scratch_shapes=[pltpu.VMEM((lines,) + shape, jnp.bfloat16)],
        ),
        out_shape=[
            jax.ShapeDtypeStruct(queries.shape, jnp.bfloat16),
            jax.ShapeDtypeStruct((chunks, 2, heads * block), jnp.float32),
        ],
        compiler_params=pltpu.CompilerParams(vmem_limit_bytes=VMEM_LIMIT),
        cost_estimate=pl.CostEstimate(
            flops=steps * 2 * 2 * 2 * heads * block * block * LANES,
            bytes_accessed=queries.size * 4 + lines * pairs[0].size * 2,
            transcendentals=steps * 2 * heads * block * block,
        ),
        name="attend",
    )(meta, queries, *[pair.reshape(shape) for pair in pairs], info)


def attend_back_kernel(parts, lines, meta_ref, query_ref, *refs):
    pair_refs = refs[:lines]
    grad_ref, mixed_ref, log_ref, info_ref, cos_ref, sin_ref = refs[lines : lines + 6]
    query_out = refs[lines + 6]
    pair_outs = refs[lines + 7 : lines + 7 + lines]
    held, sums = refs[lines + 7 + lines :]
    chunk = pl.program_id(0)
    block = query_ref.shape[0]
    heads = query_ref.shape[1] // LANES

    @pl.when(chunk == 0)
    def _():
        for line in range(lines):
            held[line] = pair_refs[line][...]
        sums[...] = jnp.zeros_like(sums)

    stacked = stack_heads(query_ref[...])
    stacked_grad = stack_heads(grad_ref[...])
    product = stacked_grad.astype(jnp.float32) * stack_heads(mixed_ref[...]).astype(jnp.float32)
    lane = lax.broadcasted_iota(jnp.int32, stacked.shape, 1)
    place = jnp.concatenate([info_ref[0, 0:1, :]] * heads, axis=1)
    start = jnp.concatenate([info_ref[0, 1:2, :]] * heads, axis=1)
    base = chunk * (2 + parts)
    steps = meta_ref[base + 1] - meta_ref[base] + 1
    width = heads * block
    grads = []
    for which in range(2):
        is_key = (lane < HEAD_DIM) if which == 0 else (lane >= HEAD_DIM)
        queries = jnp.where(is_key, stacked, jnp.zeros_like(stacked))
        grad = jnp.where(is_key, jnp.zeros_like(stacked_grad), stacked_grad)
        own = jnp.where(is_key, 0.0, product)
        centre = lax.dot_general(
            jnp.ones((8, LANES), jnp.float32),
            own,
            (((1,), (1,)), ((), ())),
            precision=lax.Precision.HIGHEST,
            preferred_element_type=jnp.float32,
        )[0:1]
        logs = log_ref[0, which : which + 1, :]

        def body(step, grad_query):
            key_block, slot, shift = block_of(meta_ref, chunk, step, parts, lines)
            columns = slice(which * LANES, (which + 1) * LANES)
            pair = held[shift, slot, :, columns]
            scores = dot_nt(pair, queries)
            key_place = key_block * block + lax.broadcasted_iota(jnp.int32, (block, width), 0)
            scores = jnp.where((key_place <= place) & (key_place >= start), scores, MASKED)
            weights = jnp.exp(scores - logs)
            grad_scores = (weights * (dot_nt(pair, grad) - centre)).astype(jnp.bfloat16)
            sums[shift, slot, :, columns] += dot_nn(grad_scores, queries) + dot_nn(
                weights.astype(jnp.bfloat16), grad
            )
            return grad_query + dot_tn(pair, grad_scores)

        grads.append(lax.fori_loop(0, steps, body, jnp.zeros((LANES, width), jnp.float32)))
    joined = jnp.concatenate([grads[0][:HEAD_DIM], grads[1][HEAD_DIM:]], axis=0)
    rows = joined.T * SCORE_SCALE
    cosine, sine = cos_ref[...], sin_ref[...]
    for head in range(heads):
        part = rows[head * block : (head + 1) * block]
        back = part * cosine - turn(part) * sine
        query_out[:, head * LANES : (head + 1) * LANES] = back.astype(jnp.bfloat16)

    @pl.when(chunk == pl.num_programs(0) - 1)
    def _():
        for line in range(lines):
            pair_outs[line][...] = sums[line].astype(jnp.bfloat16)


def attend_back(meta, queries, pairs, grad_mixed, mixed, logs, info, cosine, sine, parts):
    chunks, block = (info.shape[0], info.shape[2])
    width = queries.shape[1]
    heads = width // LANES
    lines = len(pairs)
    shape = (chunks, block, 2 * LANES)
    steps = 3 * chunks
    wide = pl.BlockSpec((block, width), lambda i, m: (i, 0))
    table = pl.BlockSpec((block, LANES), lambda i, m: (i, 0))
    whole = pl.BlockSpec(shape, lambda i, m: (0, 0, 0))
    outs = pl.pallas_call(
        functools.partial(attend_back_kernel, parts, lines),
        grid_spec=pltpu.PrefetchScalarGridSpec(
            num_scalar_prefetch=1,
            grid=(chunks,),
            in_specs=[wide]
            + [whole] * lines
            + [
                wide,
                wide,
                pl.BlockSpec((1, 2, heads * block), lambda i, m: (i, 0, 0)),
                pl.BlockSpec((1, 2, block), lambda i, m: (i, 0, 0)),
                table,
                table,
            ],
            out_specs=[wide] + [whole] * lines,
            scratch_shapes=[
                pltpu.VMEM((lines,) + shape, jnp.bfloat16),
                pltpu.VMEM((lines,) + shape, jnp.float32),
            ],
        ),
        out_shape=[jax.ShapeDtypeStruct(queries.shape, jnp.bfloat16)]
        + [jax.ShapeDtypeStruct(shape, jnp.bfloat16)] * lines,
        compiler_params=pltpu.CompilerParams(vmem_limit_bytes=VMEM_LIMIT),
        cost_estimate=pl.CostEstimate(
            flops=steps * 2 * 5 * 2 * heads * block * block * LANES,
            bytes_accessed=queries.size * 8 + 2 * lines * pairs[0].size * 2,
            transcendentals=steps * 2 * heads * block * block,
        ),
        name="attend_back",
    )(
        meta,
        queries,
        *[pair.reshape(shape) for pair in pairs],
        grad_mixed,
        mixed,
        logs,
        info,
        cosine,
        sine,
    )
    return (outs[0], [out.reshape(chunks * block, 2 * LANES) for out in outs[1:]])


def pair_back_kernel(*refs):
    *part_refs, cos_ref, sin_ref, out_ref = refs
    cosine, sine = cos_ref[...], sin_ref[...]
    lane = lax.broadcasted_iota(jnp.int32, cosine.shape, 1)
    for which in range(2):
        columns = slice(which * LANES, (which + 1) * LANES)
        total = part_refs[0][:, columns].astype(jnp.float32)
        for ref in part_refs[1:]:
            total = total + ref[:, columns].astype(jnp.float32)
        is_key = (lane < HEAD_DIM) if which == 0 else (lane >= HEAD_DIM)
        total = jnp.where(is_key, total * cosine - turn(total) * sine, total)
        out_ref[:, columns] = total.astype(jnp.bfloat16)


def pair_back(parts, cosine, sine, block):
    rows, columns = parts[0].shape
    tile = pl.BlockSpec((block, columns), lambda i: (i, 0))
    table = pl.BlockSpec((block, LANES), lambda i: (i, 0))
    return pl.pallas_call(
        pair_back_kernel,
        grid=(rows // block,),
        in_specs=[tile] * len(parts) + [table, table],
        out_specs=tile,
        out_shape=jax.ShapeDtypeStruct((rows, columns), jnp.bfloat16),
        compiler_params=pltpu.CompilerParams(vmem_limit_bytes=VMEM_LIMIT),
        name="pair_back",
    )(*parts, cosine, sine)


def on_device(
    sizes,
    block_input,
    cotangent,
    segments,
    norm_gains,
    w_query,
    w_keyvalue,
    w_output,
    w_gateup,
    w_down,
    gains_moment,
    gains_square,
    query_moment,
    query_square,
    keyvalue_moment,
    keyvalue_square,
    output_moment,
    output_square,
    gateup_moment,
    gateup_square,
    down_moment,
    down_square,
):
    rows_on, lines = sizes
    y, core, row, line = [lax.axis_index(name) for name in ("y", "core", "row", "col")]
    length = segments.shape[1]
    block = block_input.shape[0] // lines
    wide = block_input.shape[1]
    half = wide // 2
    slots = 2 * rows_on
    per_row = w_query.shape[1] // (KV_HEADS * HEAD_DIM)
    query_width = per_row * LANES
    hidden_here = w_gateup.shape[2] // 2

    def shift(value, axis, size, by):
        return lax.ppermute(value, axis, [(i, (i + by) % size) for i in range(size)])

    def other_core(value):
        return lax.ppermute(value, "core", [(0, 1), (1, 0)])

    def other_y(value):
        return lax.ppermute(value, "y", [(0, 1), (1, 0)])

    def place_of(y_at, core_at, row_at):
        return (y_at * 2 + core_at) * rows_on + row_at

    first_pairs, second_pairs = ([], [])
    for y_at in range(2):
        for core_at in range(2):
            for row_at in range(rows_on):
                over_row = (
                    place_of(y_at, core_at, row_at),
                    place_of(y_at, core_at, (row_at + 1) % rows_on),
                )
                over_y = (place_of(y_at, core_at, row_at), place_of(1 - y_at, core_at, row_at))
                first_pairs.append(over_row if core_at == 0 else over_y)
                second_pairs.append(over_y if core_at == 0 else over_row)
    near = ("y", "core", "row")

    def gather_tokens(own):
        if rows_on == 2:
            first = lax.ppermute(own, near, first_pairs)
            second = lax.ppermute(own, near, second_pairs)
            third = lax.ppermute(first, near, second_pairs)
            return jnp.concatenate([own, first, second, third], axis=0)
        parts = [own] + [shift(own, "row", rows_on, by) for by in range(1, rows_on)]
        return jnp.concatenate(parts + [other_y(part) for part in parts], axis=0)

    def reduce_tokens(left, right, beside=()):
        def rows_of(first, last):
            return dot_nt(left[first * block : last * block], right).astype(jnp.bfloat16)

        done = []
        if rows_on == 2:
            far = rows_of(2, 4)
            third = lax.ppermute(far[block:], near, second_pairs)
            second = lax.ppermute(far[:block], near, second_pairs)
            close = rows_of(0, 2)
            if beside:
                done = beside[0]()
                third, second, *done = lax.optimization_barrier((third, second, *done))
            first = close[block:].astype(jnp.float32) + third.astype(jnp.float32)
            first = lax.ppermute(first.astype(jnp.bfloat16), near, first_pairs)
            own = close[:block].astype(jnp.float32) + second.astype(jnp.float32)
            return (own + first.astype(jnp.float32), done)
        partial = rows_of(0, slots)
        parts = [partial[i * block : (i + 1) * block] for i in range(slots)]
        if beside:
            done = beside[0]()
        sums = [
            parts[i].astype(jnp.float32) + other_y(parts[rows_on + i]).astype(jnp.float32)
            for i in range(rows_on)
        ]
        total = sums[0]
        for by in range(1, rows_on):
            moved = shift(sums[by].astype(jnp.bfloat16), "row", rows_on, -by)
            total = total + moved.astype(jnp.float32)
        return (total, done)

    if rows_on == 2:
        slot_y = [y, jnp.where(core == 0, y, 1 - y), jnp.where(core == 0, 1 - y, y), 1 - y]
        slot_row = [row, jnp.where(core == 0, 1 - row, row), jnp.where(core == 0, row, 1 - row), 1 - row]
    else:
        slot_y = [y] * rows_on + [1 - y] * rows_on
        slot_row = [(row - by) % rows_on for by in range(rows_on)] * 2

    def pick(parts, index):
        return lax.dynamic_index_in_dim(jnp.stack(parts), index, 0, keepdims=False)

    def tokens_from_features(values):
        parts = []
        for by in range(lines):
            part = lax.dynamic_slice_in_dim(values, ((line + by) % lines) * block, block, 0)
            parts.append(part if by == 0 else shift(part, "col", lines, by))
        blocks = [pick(parts, (line - at) % lines) for at in range(lines)]
        return jnp.concatenate([b[:, :half] for b in blocks] + [b[:, half:] for b in blocks], axis=1)

    def features_from_tokens(values):
        blocks = [
            jnp.concatenate(
                [
                    values[:, at * half : (at + 1) * half],
                    values[:, D // 2 + at * half : D // 2 + (at + 1) * half],
                ],
                axis=1,
            )
            for at in range(lines)
        ]
        parts = []
        for by in range(lines):
            part = pick(blocks, (line + by) % lines)
            parts.append(part if by == 0 else shift(part, "col", lines, by))
        return jnp.concatenate([pick(parts, (line - at) % lines) for at in range(lines)], axis=0)

    def half_rows(values):
        return lax.dynamic_slice_in_dim(values, core * half, half, 0)

    def half_columns(values):
        return lax.dynamic_slice_in_dim(values, core * half, half, 1)

    def gather_weight(piece):
        return lax.all_gather(piece, ("core", "col"), axis=0, tiled=True)

    query_rows = half_rows(w_query).astype(jnp.bfloat16)
    pair_rows = half_rows(w_keyvalue).astype(jnp.bfloat16)

    def joint_of(at):
        pieces = [
            query_rows[:, (2 * j + at) * LANES : (2 * j + at + 1) * LANES] for j in range(per_row)
        ]
        pair = pair_rows[:, at * 2 * LANES : (at + 1) * 2 * LANES]
        pieces += [
            pair[:, :LANES],
            pair[:, LANES + HEAD_DIM :],
            pair[:, LANES : LANES + HEAD_DIM],
        ]
        return jnp.concatenate(pieces, axis=1)

    joint_weight = gather_weight(jnp.where(y == 0, joint_of(0), joint_of(1)))
    output_columns = half_columns(w_output).astype(jnp.bfloat16)

    def output_of(at):
        pieces = []
        for j in range(per_row):
            base = (2 * j + at) * LANES
            pieces += [
                output_columns[base + HEAD_DIM : base + LANES],
                output_columns[base : base + HEAD_DIM],
            ]
        return jnp.concatenate(pieces, axis=0)

    output_weight = gather_weight(jnp.where(y == 0, output_of(0), output_of(1)).T)
    gateup_piece = lax.dynamic_slice(
        w_gateup, (core * half, 0, y * hidden_here), (half, 2, hidden_here)
    ).astype(jnp.bfloat16)
    gateup_weight = gather_weight(
        jnp.concatenate([gateup_piece[:, 0], gateup_piece[:, 1]], axis=1)
    )
    down_piece = lax.dynamic_slice(
        w_down, (y * hidden_here, core * half), (hidden_here, half)
    ).astype(jnp.bfloat16)
    down_weight = gather_weight(down_piece.T)

    gain_parts = [norm_gains] + [shift(norm_gains, "col", lines, by) for by in range(1, lines)]
    gain_blocks = [pick(gain_parts, (line - at) % lines) for at in range(lines)]
    gains = jnp.concatenate(
        [b[:, :half] for b in gain_blocks] + [b[:, half:] for b in gain_blocks], axis=1
    )

    own_starts = document_starts(segments[0])
    other_starts = document_starts(other_y(segments)[0])
    frequency = 10000.0 ** (-2.0 * jnp.arange(HEAD_DIM // 2, dtype=jnp.float32) / HEAD_DIM)
    starts, places, meta = ([], [], [])
    for slot in range(slots):
        begin = slot_row[slot] * (lines * block) + line * block
        of_chunk = lax.dynamic_slice_in_dim(
            jnp.where(slot_y[slot] == y, own_starts, other_starts), begin, block, 0
        )
        starts.append(of_chunk)
        places.append(begin + jnp.arange(block, dtype=jnp.int32))
        meta += [of_chunk[0] // block, begin // block]
        for row_at in range(rows_on):
            found = jnp.int32(0)
            for other in range(slots):
                same = (slot_y[other] == slot_y[slot]) & (slot_row[other] == row_at)
                found = found + jnp.where(same, other, 0)
            meta.append(found)
    meta = jnp.stack([jnp.asarray(m, jnp.int32) for m in meta + [line]])
    starts, places = (jnp.stack(starts), jnp.stack(places))
    info = jnp.stack([places, starts], axis=1)
    offsets = (places - starts).astype(jnp.float32).reshape(-1)
    phases = offsets[:, None] * jnp.tile(frequency, LANES // (HEAD_DIM // 2))[None, :]
    cosine, sine = (jnp.cos(phases), jnp.sin(phases))

    residual_low = tokens_from_features(block_input)
    residual = residual_low.astype(jnp.float32)
    scale_one = lax.rsqrt(jnp.mean(residual * residual, axis=1, keepdims=True) + EPSILON)
    normed_one = gather_tokens((residual * scale_one * gains[0]).astype(jnp.bfloat16))
    queries, pair = project(normed_one, joint_weight, cosine, sine, query_width, block)
    pairs = [pair] + [shift(pair, "col", lines, by) for by in range(1, lines)]
    late_cotangent, *pairs = lax.optimization_barrier((cotangent, *pairs))
    cot_low = tokens_from_features(late_cotangent)
    cot = gather_tokens(cot_low)
    mixed, logs = attend(meta, queries, pairs, info, rows_on)
    attn_sum, _ = reduce_tokens(mixed, output_weight)
    middle = residual + attn_sum
    scale_two = lax.rsqrt(jnp.mean(middle * middle, axis=1, keepdims=True) + EPSILON)
    normed_two = gather_tokens((middle * scale_two * gains[1]).astype(jnp.bfloat16))
    pair_sum = dot_nn(normed_two, gateup_weight)
    gate_sum, upward = (pair_sum[:, :hidden_here], pair_sum[:, hidden_here:])
    sigmoid_gate = jax.nn.sigmoid(gate_sum)
    silu_gate = gate_sum * sigmoid_gate
    hidden = (silu_gate * upward).astype(jnp.bfloat16)

    grad_hidden = dot_nn(cot, down_weight)
    grad_gate = grad_hidden * upward * sigmoid_gate * (1.0 + gate_sum * (1.0 - sigmoid_gate))
    grad_pair = jnp.concatenate(
        [grad_gate.astype(jnp.bfloat16), (grad_hidden * silu_gate).astype(jnp.bfloat16)], axis=1
    )

    def other_half(rows, grad):
        rows = lax.dynamic_slice_in_dim(rows, (1 - core) * (D // 2), D // 2, 1)
        return dot_tn(rows, grad).astype(jnp.bfloat16)

    def scatter_grad(rows, grad, received):
        rows = lax.dynamic_slice_in_dim(rows, core * (D // 2), D // 2, 1)
        total = dot_tn(rows, grad) + received.astype(jnp.float32)
        return lax.psum_scatter(
            total.astype(jnp.bfloat16), "col", scatter_dimension=0, tiled=True
        )

    def collect(piece):
        whole = lax.all_gather(piece, ("y", "core"), axis=0, tiled=True)
        return (whole[:wide], whole[wide:])

    grad_normed_two, (gateup_other, down_other) = reduce_tokens(
        grad_pair,
        gateup_weight,
        [lambda: [other_half(normed_two, grad_pair), other_half(cot, hidden)]],
    )
    gateup_other, down_other = (other_core(gateup_other), other_core(down_other))
    gateup_piece = scatter_grad(normed_two, grad_pair, gateup_other)
    down_piece = scatter_grad(cot, hidden, down_other)

    def norm_back(values, scale, grad_normed, gain):
        scaled = grad_normed * gain
        total = jnp.sum(scaled * values, axis=1, keepdims=True)
        return scale * scaled - values * (scale**3 * total / D)

    grad_middle = cot_low.astype(jnp.float32) + norm_back(
        middle, scale_two, grad_normed_two, gains[1]
    )
    gain_two = jnp.sum(grad_normed_two * middle * scale_two, axis=0)

    back = gather_tokens(grad_middle.astype(jnp.bfloat16))
    back, late_hidden = lax.optimization_barrier((back, hidden))
    ffn_sum, _ = reduce_tokens(late_hidden, down_weight)
    layer_output = features_from_tokens((middle + ffn_sum).astype(jnp.bfloat16))
    grad_mixed = dot_nn(back, output_weight).astype(jnp.bfloat16)
    output_piece = scatter_grad(back, mixed, other_core(other_half(back, mixed)))
    grad_query, grad_parts = attend_back(
        meta, queries, pairs, grad_mixed, mixed, logs, info, cosine, sine, rows_on
    )
    grad_parts = [grad_parts[0]] + [
        shift(grad_parts[by], "col", lines, -by) for by in range(1, lines)
    ]
    grad_keyvalue = pair_back(grad_parts, cosine, sine, block)
    grad_joint = jnp.concatenate([grad_query, grad_keyvalue], axis=1)
    grad_normed_one, (joint_other,) = reduce_tokens(
        grad_joint, joint_weight, [lambda: [other_half(normed_one, grad_joint)]]
    )
    joint_piece = scatter_grad(normed_one, grad_joint, other_core(joint_other))
    input_grad = grad_middle + norm_back(residual, scale_one, grad_normed_one, gains[0])
    gain_one = jnp.sum(grad_normed_one * residual * scale_one, axis=0)
    input_grad = features_from_tokens(input_grad.astype(jnp.bfloat16)).astype(jnp.float32)
    pair_piece = joint_piece[:, query_width:]
    pair_total = pair_piece.astype(jnp.float32)
    for by in range(1, rows_on):
        pair_total = pair_total + shift(pair_piece, "row", rows_on, by).astype(jnp.float32)
    joint_piece = jnp.concatenate(
        [joint_piece[:, :query_width], pair_total.astype(jnp.bfloat16)], axis=1
    )
    grad_down, grad_gateup, grad_output, grad_joint_sum = (
        collect(down_piece),
        collect(gateup_piece),
        collect(output_piece),
        collect(joint_piece),
    )

    gain_sums = jnp.stack([gain_one, gain_two])
    blocks = [
        jnp.concatenate(
            [
                gain_sums[:, at * half : (at + 1) * half],
                gain_sums[:, D // 2 + at * half : D // 2 + (at + 1) * half],
            ],
            axis=1,
        )
        for at in range(lines)
    ]
    grad_gains = blocks_total = pick(blocks, line)
    for by in range(1, lines):
        grad_gains = grad_gains + shift(pick(blocks, (line + by) % lines), "col", lines, by)
    for axis, size in (("core", 2), ("y", 2), ("row", rows_on)):
        blocks_total = grad_gains
        for by in range(1, size):
            grad_gains = grad_gains + shift(blocks_total, axis, size, by)

    gains_new = adamw_step(norm_gains, grad_gains, gains_moment, gains_square, 0.6, 0.0)
    query_grad = jnp.concatenate(
        [
            grad_joint_sum[at][:, j * LANES : (j + 1) * LANES]
            for j in range(per_row)
            for at in range(2)
        ],
        axis=1,
    )
    pair_grad = jnp.concatenate(
        [
            piece
            for at in range(2)
            for piece in (
                grad_joint_sum[at][:, query_width : query_width + LANES],
                grad_joint_sum[at][:, query_width + LANES + HEAD_DIM :],
                grad_joint_sum[at][:, query_width + LANES : query_width + LANES + HEAD_DIM],
            )
        ],
        axis=1,
    )
    turned = [grad_output[at].T for at in range(2)]
    output_grad = jnp.concatenate(
        [
            turned[at][j * LANES + part : j * LANES + part + HEAD_DIM]
            for j in range(per_row)
            for at in range(2)
            for part in (HEAD_DIM, 0)
        ],
        axis=0,
    )
    gateup_grad = jnp.concatenate(
        [grad_gateup[at].reshape(wide, 2, hidden_here) for at in range(2)], axis=2
    )
    down_grad = jnp.concatenate([grad_down[at].T for at in range(2)], axis=0)
    query_grad, pair_grad, output_grad, gateup_grad, down_grad = [
        lax.optimization_barrier(grad).astype(jnp.float32)
        for grad in (query_grad, pair_grad, output_grad, gateup_grad, down_grad)
    ]
    query_new = adamw_step(w_query, query_grad, query_moment, query_square, D ** (-0.5), 0.1)
    keyvalue_new = adamw_step(
        w_keyvalue, pair_grad, keyvalue_moment, keyvalue_square, D ** (-0.5), 0.1
    )
    output_new = adamw_step(
        w_output, output_grad, output_moment, output_square, (HEADS * HEAD_DIM // 64) ** (-0.5), 0.1
    )
    gateup_new = adamw_step(w_gateup, gateup_grad, gateup_moment, gateup_square, D ** (-0.5), 0.1)
    down_new = adamw_step(w_down, down_grad, down_moment, down_square, FF ** (-0.5), 0.1)
    return (
        layer_output,
        input_grad,
        *gains_new,
        *query_new,
        *keyvalue_new,
        *output_new,
        *gateup_new,
        *down_new,
    )


def solution(mesh):
    dp, rows_on, lines = (mesh.shape["dp"], mesh.shape["row"], mesh.shape["col"])
    split = Mesh(mesh.devices.reshape(dp // 2, 2, rows_on, lines), ("y", "core", "row", "col"))
    tokens = P(("y", "core", "row"), "col")
    narrow, wide = (P("col", "row"), P("row", "col"))
    gains, pair, gateup = (P(None, "col"), P("col", None), P("col", None, "row"))
    return jax.shard_map(
        functools.partial(on_device, (rows_on, lines)),
        mesh=split,
        in_specs=(
            tokens,
            tokens,
            P(("y", "core"), None),
            gains,
            narrow,
            pair,
            wide,
            gateup,
            wide,
            gains,
            gains,
            narrow,
            narrow,
            pair,
            pair,
            wide,
            wide,
            gateup,
            gateup,
            wide,
            wide,
        ),
        out_specs=(tokens, tokens)
        + (gains,) * 3
        + (narrow,) * 3
        + (pair,) * 3
        + (wide,) * 3
        + (gateup,) * 3
        + (wide,) * 3,
        check_vma=False,
    )
```

```python
import functools

import jax
import jax.numpy as jnp
from jax import lax
from jax.experimental import pallas as pl
from jax.experimental.pallas import tpu as pltpu
from jax.sharding import Mesh, PartitionSpec as P

D = 2048
HEADS = 32
KV_HEADS = 4
HEAD_DIM = 64
FF = 5632
STEP = 10

EPSILON = 1e-05
BETA_ONE = 0.9
BETA_TWO = 0.999
ADAM_EPS = 1e-08
MASKED = -1e30
SCORE_SCALE = HEAD_DIM ** (-0.5)
LANES = 128
VMEM_LIMIT = 48 * 1024 * 1024


def dot_nn(left, right):
    return lax.dot_general(left, right, (((1,), (0,)), ((), ())), preferred_element_type=jnp.float32)


def dot_nt(left, right):
    return lax.dot_general(left, right, (((1,), (1,)), ((), ())), preferred_element_type=jnp.float32)


def dot_tn(left, right):
    return lax.dot_general(left, right, (((0,), (0,)), ((), ())), preferred_element_type=jnp.float32)


def adamw_step(weight, gradient, moment, square, step_rate, decay_rate):
    moment_new = BETA_ONE * moment + (1.0 - BETA_ONE) * gradient
    square_new = BETA_TWO * square + (1.0 - BETA_TWO) * gradient * gradient
    fixed_one = moment_new / (1.0 - BETA_ONE**STEP)
    fixed_two = square_new / (1.0 - BETA_TWO**STEP)
    weight_new = weight - step_rate * (
        fixed_one / (jnp.sqrt(fixed_two) + ADAM_EPS) + decay_rate * weight
    )
    return (moment_new, square_new, weight_new)


def document_starts(segment_ids):
    places = jnp.arange(segment_ids.shape[0], dtype=jnp.int32)
    starts = jnp.concatenate([jnp.ones((1,), jnp.bool_), segment_ids[1:] != segment_ids[:-1]])
    return lax.cummax(jnp.where(starts, places, 0), axis=0)


def turn(values):
    lane = lax.broadcasted_iota(jnp.int32, values.shape, 1)
    ahead = pltpu.roll(values, LANES - HEAD_DIM // 2, 1)
    behind = pltpu.roll(values, HEAD_DIM // 2, 1)
    return jnp.where(lane % HEAD_DIM < HEAD_DIM // 2, -ahead, behind)


def project_kernel(rows_ref, weight_ref, cos_ref, sin_ref, query_ref, pair_ref):
    sums = dot_nn(rows_ref[...], weight_ref[...])
    cosine, sine = cos_ref[...], sin_ref[...]
    width = query_ref.shape[1]
    lane = lax.broadcasted_iota(jnp.int32, cosine.shape, 1)
    for start in range(0, width, LANES):
        part = sums[:, start : start + LANES]
        turned = (part * cosine + turn(part) * sine).astype(jnp.bfloat16)
        query_ref[:, start : start + LANES] = turned * jnp.bfloat16(SCORE_SCALE)
    for which in range(2):
        part = sums[:, width + which * LANES : width + (which + 1) * LANES]
        is_key = (lane < HEAD_DIM) if which == 0 else (lane >= HEAD_DIM)
        turned = jnp.where(is_key, part * cosine + turn(part) * sine, part)
        pair_ref[:, which * LANES : (which + 1) * LANES] = turned.astype(jnp.bfloat16)


def project(rows, weight, cosine, sine, width, block):
    count = rows.shape[0] // block
    total = weight.shape[1]
    return pl.pallas_call(
        project_kernel,
        grid=(count,),
        in_specs=[
            pl.BlockSpec((block, rows.shape[1]), lambda i: (i, 0)),
            pl.BlockSpec(weight.shape, lambda i: (0, 0)),
            pl.BlockSpec((block, LANES), lambda i: (i, 0)),
            pl.BlockSpec((block, LANES), lambda i: (i, 0)),
        ],
        out_specs=[
            pl.BlockSpec((block, width), lambda i: (i, 0)),
            pl.BlockSpec((block, total - width), lambda i: (i, 0)),
        ],
        out_shape=[
            jax.ShapeDtypeStruct((rows.shape[0], width), jnp.bfloat16),
            jax.ShapeDtypeStruct((rows.shape[0], total - width), jnp.bfloat16),
        ],
        compiler_params=pltpu.CompilerParams(vmem_limit_bytes=VMEM_LIMIT),
        cost_estimate=pl.CostEstimate(
            flops=2 * rows.shape[0] * rows.shape[1] * total,
            bytes_accessed=rows.size * 2 + weight.size * 2,
            transcendentals=0,
        ),
        name="project",
    )(rows, weight, cosine, sine)


def stack_heads(values):
    return jnp.concatenate(
        [values[:, start : start + LANES] for start in range(0, values.shape[1], LANES)], axis=0
    )


def block_of(meta_ref, chunk, step, parts, lines):
    base = chunk * (2 + parts)
    key_block = meta_ref[base + 1] - step
    slot = meta_ref[base + 2 + key_block // lines]
    own_line = meta_ref[pl.num_programs(0) * (2 + parts)]
    line = lax.rem(key_block, lines)
    return (key_block, slot, line, lax.rem(own_line - line + lines, lines))


def attend_kernel(parts, lines, meta_ref, query_ref, pair_ref, info_ref, out_ref, log_ref):
    chunk = pl.program_id(0)
    block = query_ref.shape[0]
    heads = query_ref.shape[1] // LANES
    stacked = stack_heads(query_ref[...])
    lane = lax.broadcasted_iota(jnp.int32, stacked.shape, 1)
    place = jnp.concatenate([info_ref[0, 0:1, :]] * heads, axis=1)
    start = jnp.concatenate([info_ref[0, 1:2, :]] * heads, axis=1)
    base = chunk * (2 + parts)
    steps = meta_ref[base + 1] - meta_ref[base] + 1
    width = heads * block
    outs = []
    for which in range(2):
        is_key = (lane < HEAD_DIM) if which == 0 else (lane >= HEAD_DIM)
        queries = jnp.where(is_key, stacked, jnp.zeros_like(stacked))

        def body(step, carry):
            peak, total, mixed = carry
            key_block, slot, at, _ = block_of(meta_ref, chunk, step, parts, lines)
            pair = pair_ref[at, slot, :, which * LANES : (which + 1) * LANES]
            scores = dot_nt(pair, queries)
            key_place = key_block * block + lax.broadcasted_iota(jnp.int32, (block, width), 0)
            scores = jnp.where((key_place <= place) & (key_place >= start), scores, MASKED)
            new_peak = jnp.maximum(peak, jnp.max(scores, axis=0, keepdims=True))
            weights = jnp.exp(scores - new_peak)
            shrink = jnp.exp(peak - new_peak)
            total = total * shrink + jnp.sum(weights, axis=0, keepdims=True)
            mixed = mixed * shrink + dot_tn(pair, weights.astype(jnp.bfloat16))
            return (new_peak, total, mixed)

        peak, total, mixed = lax.fori_loop(
            0,
            steps,
            body,
            (
                jnp.full((1, width), MASKED, jnp.float32),
                jnp.zeros((1, width), jnp.float32),
                jnp.zeros((LANES, width), jnp.float32),
            ),
        )
        log_ref[0, which : which + 1, :] = peak + jnp.log(total)
        outs.append(mixed / total)
    joined = jnp.concatenate([outs[1][:HEAD_DIM], outs[0][HEAD_DIM:]], axis=0)
    rows = joined.T.astype(jnp.bfloat16)
    for head in range(heads):
        out_ref[:, head * LANES : (head + 1) * LANES] = rows[head * block : (head + 1) * block]


def attend(meta, queries, pairs, info, parts):
    chunks, block = (info.shape[0], info.shape[2])
    width = queries.shape[1]
    heads = width // LANES
    lines = pairs.shape[0]
    steps = 3 * chunks
    return pl.pallas_call(
        functools.partial(attend_kernel, parts, lines),
        grid_spec=pltpu.PrefetchScalarGridSpec(
            num_scalar_prefetch=1,
            grid=(chunks,),
            in_specs=[
                pl.BlockSpec((block, width), lambda i, m: (i, 0)),
                pl.BlockSpec(pairs.shape, lambda i, m: (0, 0, 0, 0)),
                pl.BlockSpec((1, 2, block), lambda i, m: (i, 0, 0)),
            ],
            out_specs=[
                pl.BlockSpec((block, width), lambda i, m: (i, 0)),
                pl.BlockSpec((1, 2, heads * block), lambda i, m: (i, 0, 0)),
            ],
        ),
        out_shape=[
            jax.ShapeDtypeStruct(queries.shape, jnp.bfloat16),
            jax.ShapeDtypeStruct((chunks, 2, heads * block), jnp.float32),
        ],
        compiler_params=pltpu.CompilerParams(vmem_limit_bytes=VMEM_LIMIT),
        cost_estimate=pl.CostEstimate(
            flops=steps * 2 * 2 * 2 * heads * block * block * LANES,
            bytes_accessed=queries.size * 4 + pairs.size * 2,
            transcendentals=steps * 2 * heads * block * block,
        ),
        name="attend",
    )(meta, queries, pairs, info)


def attend_back_kernel(parts, lines, meta_ref, query_ref, *refs):
    pair_ref, grad_ref, mixed_ref, log_ref, info_ref, cos_ref, sin_ref, query_out = refs[:8]
    pair_outs = refs[8 : 8 + lines]
    sums = refs[8 + lines]
    chunk = pl.program_id(0)
    block = query_ref.shape[0]
    heads = query_ref.shape[1] // LANES

    @pl.when(chunk == 0)
    def _():
        sums[...] = jnp.zeros_like(sums)

    stacked = stack_heads(query_ref[...])
    stacked_grad = stack_heads(grad_ref[...])
    product = stacked_grad.astype(jnp.float32) * stack_heads(mixed_ref[...]).astype(jnp.float32)
    lane = lax.broadcasted_iota(jnp.int32, stacked.shape, 1)
    place = jnp.concatenate([info_ref[0, 0:1, :]] * heads, axis=1)
    start = jnp.concatenate([info_ref[0, 1:2, :]] * heads, axis=1)
    base = chunk * (2 + parts)
    steps = meta_ref[base + 1] - meta_ref[base] + 1
    width = heads * block
    grads = []
    for which in range(2):
        is_key = (lane < HEAD_DIM) if which == 0 else (lane >= HEAD_DIM)
        queries = jnp.where(is_key, stacked, jnp.zeros_like(stacked))
        grad = jnp.where(is_key, jnp.zeros_like(stacked_grad), stacked_grad)
        own = jnp.where(is_key, 0.0, product)
        centre = lax.dot_general(
            jnp.ones((8, LANES), jnp.float32),
            own,
            (((1,), (1,)), ((), ())),
            precision=lax.Precision.HIGHEST,
            preferred_element_type=jnp.float32,
        )[0:1]
        logs = log_ref[0, which : which + 1, :]

        def body(step, grad_query):
            key_block, slot, at, shift = block_of(meta_ref, chunk, step, parts, lines)
            columns = slice(which * LANES, (which + 1) * LANES)
            pair = pair_ref[at, slot, :, columns]
            scores = dot_nt(pair, queries)
            key_place = key_block * block + lax.broadcasted_iota(jnp.int32, (block, width), 0)
            scores = jnp.where((key_place <= place) & (key_place >= start), scores, MASKED)
            weights = jnp.exp(scores - logs)
            grad_scores = (weights * (dot_nt(pair, grad) - centre)).astype(jnp.bfloat16)
            sums[shift, slot, :, columns] += dot_nn(grad_scores, queries) + dot_nn(
                weights.astype(jnp.bfloat16), grad
            )
            return grad_query + dot_tn(pair, grad_scores)

        grads.append(lax.fori_loop(0, steps, body, jnp.zeros((LANES, width), jnp.float32)))
    joined = jnp.concatenate([grads[0][:HEAD_DIM], grads[1][HEAD_DIM:]], axis=0)
    rows = joined.T * SCORE_SCALE
    cosine, sine = cos_ref[...], sin_ref[...]
    for head in range(heads):
        part = rows[head * block : (head + 1) * block]
        back = part * cosine - turn(part) * sine
        query_out[:, head * LANES : (head + 1) * LANES] = back.astype(jnp.bfloat16)

    @pl.when(chunk == pl.num_programs(0) - 1)
    def _():
        for line in range(lines):
            pair_outs[line][...] = sums[line].astype(jnp.bfloat16)


def attend_back(meta, queries, pairs, grad_mixed, mixed, logs, info, cosine, sine, parts):
    chunks, block = (info.shape[0], info.shape[2])
    width = queries.shape[1]
    heads = width // LANES
    lines = pairs.shape[0]
    shape = pairs.shape[1:]
    steps = 3 * chunks
    wide = pl.BlockSpec((block, width), lambda i, m: (i, 0))
    table = pl.BlockSpec((block, LANES), lambda i, m: (i, 0))
    whole = pl.BlockSpec(shape, lambda i, m: (0, 0, 0))
    outs = pl.pallas_call(
        functools.partial(attend_back_kernel, parts, lines),
        grid_spec=pltpu.PrefetchScalarGridSpec(
            num_scalar_prefetch=1,
            grid=(chunks,),
            in_specs=[
                wide,
                pl.BlockSpec(pairs.shape, lambda i, m: (0, 0, 0, 0)),
                wide,
                wide,
                pl.BlockSpec((1, 2, heads * block), lambda i, m: (i, 0, 0)),
                pl.BlockSpec((1, 2, block), lambda i, m: (i, 0, 0)),
                table,
                table,
            ],
            out_specs=[wide] + [whole] * lines,
            scratch_shapes=[pltpu.VMEM(pairs.shape, jnp.float32)],
        ),
        out_shape=[jax.ShapeDtypeStruct(queries.shape, jnp.bfloat16)]
        + [jax.ShapeDtypeStruct(shape, jnp.bfloat16)] * lines,
        compiler_params=pltpu.CompilerParams(vmem_limit_bytes=VMEM_LIMIT),
        cost_estimate=pl.CostEstimate(
            flops=steps * 2 * 5 * 2 * heads * block * block * LANES,
            bytes_accessed=queries.size * 8 + 2 * pairs.size * 2,
            transcendentals=steps * 2 * heads * block * block,
        ),
        name="attend_back",
    )(
        meta,
        queries,
        pairs,
        grad_mixed,
        mixed,
        logs,
        info,
        cosine,
        sine,
    )
    return (outs[0], [out.reshape(chunks * block, 2 * LANES) for out in outs[1:]])


def pair_back_kernel(*refs):
    *part_refs, cos_ref, sin_ref, out_ref = refs
    cosine, sine = cos_ref[...], sin_ref[...]
    lane = lax.broadcasted_iota(jnp.int32, cosine.shape, 1)
    for which in range(2):
        columns = slice(which * LANES, (which + 1) * LANES)
        total = part_refs[0][:, columns].astype(jnp.float32)
        for ref in part_refs[1:]:
            total = total + ref[:, columns].astype(jnp.float32)
        is_key = (lane < HEAD_DIM) if which == 0 else (lane >= HEAD_DIM)
        total = jnp.where(is_key, total * cosine - turn(total) * sine, total)
        out_ref[:, columns] = total.astype(jnp.bfloat16)


def pair_back(parts, cosine, sine, block):
    rows, columns = parts[0].shape
    tile = pl.BlockSpec((block, columns), lambda i: (i, 0))
    table = pl.BlockSpec((block, LANES), lambda i: (i, 0))
    return pl.pallas_call(
        pair_back_kernel,
        grid=(rows // block,),
        in_specs=[tile] * len(parts) + [table, table],
        out_specs=tile,
        out_shape=jax.ShapeDtypeStruct((rows, columns), jnp.bfloat16),
        compiler_params=pltpu.CompilerParams(vmem_limit_bytes=VMEM_LIMIT),
        name="pair_back",
    )(*parts, cosine, sine)


def on_device(
    sizes,
    block_input,
    cotangent,
    segments,
    norm_gains,
    w_query,
    w_keyvalue,
    w_output,
    w_gateup,
    w_down,
    gains_moment,
    gains_square,
    query_moment,
    query_square,
    keyvalue_moment,
    keyvalue_square,
    output_moment,
    output_square,
    gateup_moment,
    gateup_square,
    down_moment,
    down_square,
):
    rows_on, lines = sizes
    y, core, row, line = [lax.axis_index(name) for name in ("y", "core", "row", "col")]
    length = segments.shape[1]
    block = block_input.shape[0] // lines
    wide = block_input.shape[1]
    half = wide // 2
    slots = 2 * rows_on
    per_row = w_query.shape[1] // (KV_HEADS * HEAD_DIM)
    query_width = per_row * LANES
    hidden_here = w_gateup.shape[2] // 2

    def shift(value, axis, size, by):
        return lax.ppermute(value, axis, [(i, (i + by) % size) for i in range(size)])

    def other_core(value):
        return lax.ppermute(value, "core", [(0, 1), (1, 0)])

    def other_y(value):
        return lax.ppermute(value, "y", [(0, 1), (1, 0)])

    def place_of(y_at, core_at, row_at):
        return (y_at * 2 + core_at) * rows_on + row_at

    first_pairs, second_pairs = ([], [])
    for y_at in range(2):
        for core_at in range(2):
            for row_at in range(rows_on):
                over_row = (
                    place_of(y_at, core_at, row_at),
                    place_of(y_at, core_at, (row_at + 1) % rows_on),
                )
                over_y = (place_of(y_at, core_at, row_at), place_of(1 - y_at, core_at, row_at))
                first_pairs.append(over_row if core_at == 0 else over_y)
                second_pairs.append(over_y if core_at == 0 else over_row)
    near = ("y", "core", "row")

    def gather_tokens(own):
        if rows_on == 2:
            first = lax.ppermute(own, near, first_pairs)
            second = lax.ppermute(own, near, second_pairs)
            third = lax.ppermute(first, near, second_pairs)
            return [own, first, second, third]
        parts = [own] + [shift(own, "row", rows_on, by) for by in range(1, rows_on)]
        return parts + [other_y(part) for part in parts]

    def reduce_tokens(left, right, beside=()):
        def rows_of(first, last):
            return dot_nt(left[first * block : last * block], right).astype(jnp.bfloat16)

        done = []
        if rows_on == 2:
            far = rows_of(2, 4)
            third = lax.ppermute(far[block:], near, second_pairs)
            second = lax.ppermute(far[:block], near, second_pairs)
            close = rows_of(0, 2)
            if beside:
                done = beside[0]()
                third, second, *done = lax.optimization_barrier((third, second, *done))
            first = close[block:].astype(jnp.float32) + third.astype(jnp.float32)
            first = lax.ppermute(first.astype(jnp.bfloat16), near, first_pairs)
            own = close[:block].astype(jnp.float32) + second.astype(jnp.float32)
            return (own + first.astype(jnp.float32), done)
        partial = rows_of(0, slots)
        parts = [partial[i * block : (i + 1) * block] for i in range(slots)]
        if beside:
            done = beside[0]()
        sums = [
            parts[i].astype(jnp.float32) + other_y(parts[rows_on + i]).astype(jnp.float32)
            for i in range(rows_on)
        ]
        total = sums[0]
        for by in range(1, rows_on):
            moved = shift(sums[by].astype(jnp.bfloat16), "row", rows_on, -by)
            total = total + moved.astype(jnp.float32)
        return (total, done)

    if rows_on == 2:
        slot_y = [y, jnp.where(core == 0, y, 1 - y), jnp.where(core == 0, 1 - y, y), 1 - y]
        slot_row = [row, jnp.where(core == 0, 1 - row, row), jnp.where(core == 0, row, 1 - row), 1 - row]
    else:
        slot_y = [y] * rows_on + [1 - y] * rows_on
        slot_row = [(row - by) % rows_on for by in range(rows_on)] * 2

    def pick(parts, index):
        return lax.dynamic_index_in_dim(jnp.stack(parts), index, 0, keepdims=False)

    def tokens_from_features(values):
        parts = []
        for by in range(lines):
            part = lax.dynamic_slice_in_dim(values, ((line + by) % lines) * block, block, 0)
            parts.append(part if by == 0 else shift(part, "col", lines, by))
        blocks = [pick(parts, (line - at) % lines) for at in range(lines)]
        return jnp.concatenate([b[:, :half] for b in blocks] + [b[:, half:] for b in blocks], axis=1)

    def features_from_tokens(values):
        blocks = [
            jnp.concatenate(
                [
                    values[:, at * half : (at + 1) * half],
                    values[:, D // 2 + at * half : D // 2 + (at + 1) * half],
                ],
                axis=1,
            )
            for at in range(lines)
        ]
        parts = []
        for by in range(lines):
            part = pick(blocks, (line + by) % lines)
            parts.append(part if by == 0 else shift(part, "col", lines, by))
        return jnp.concatenate([pick(parts, (line - at) % lines) for at in range(lines)], axis=0)

    def half_rows(values):
        return lax.dynamic_slice_in_dim(values, core * half, half, 0)

    def half_columns(values):
        return lax.dynamic_slice_in_dim(values, core * half, half, 1)

    def gather_weight(piece):
        return lax.all_gather(piece, ("core", "col"), axis=0, tiled=True)

    query_rows = half_rows(w_query).astype(jnp.bfloat16)
    pair_rows = half_rows(w_keyvalue).astype(jnp.bfloat16)

    def joint_of(at):
        pieces = [
            query_rows[:, (2 * j + at) * LANES : (2 * j + at + 1) * LANES] for j in range(per_row)
        ]
        pair = pair_rows[:, at * 2 * LANES : (at + 1) * 2 * LANES]
        pieces += [
            pair[:, :LANES],
            pair[:, LANES + HEAD_DIM :],
            pair[:, LANES : LANES + HEAD_DIM],
        ]
        return jnp.concatenate(pieces, axis=1)

    joint_mine = jnp.where(y == 0, joint_of(0), joint_of(1))
    output_columns = half_columns(w_output).astype(jnp.bfloat16)

    def output_of(at):
        pieces = []
        for j in range(per_row):
            base = (2 * j + at) * LANES
            pieces += [
                output_columns[base + HEAD_DIM : base + LANES],
                output_columns[base : base + HEAD_DIM],
            ]
        return jnp.concatenate(pieces, axis=0)

    output_mine = jnp.where(y == 0, output_of(0), output_of(1)).T
    gateup_mine = lax.dynamic_slice(
        w_gateup, (core * half, 0, y * hidden_here), (half, 2, hidden_here)
    ).astype(jnp.bfloat16)
    gateup_mine = jnp.concatenate([gateup_mine[:, 0], gateup_mine[:, 1]], axis=1)
    down_mine = lax.dynamic_slice(
        w_down, (y * hidden_here, core * half), (hidden_here, half)
    ).astype(jnp.bfloat16).T

    gain_parts = [norm_gains] + [shift(norm_gains, "col", lines, by) for by in range(1, lines)]
    gain_blocks = [pick(gain_parts, (line - at) % lines) for at in range(lines)]
    gains = jnp.concatenate(
        [b[:, :half] for b in gain_blocks] + [b[:, half:] for b in gain_blocks], axis=1
    )

    own_starts = document_starts(segments[0])
    other_starts = document_starts(other_y(segments)[0])
    frequency = 10000.0 ** (-2.0 * jnp.arange(HEAD_DIM // 2, dtype=jnp.float32) / HEAD_DIM)
    starts, places, meta = ([], [], [])
    for slot in range(slots):
        begin = slot_row[slot] * (lines * block) + line * block
        of_chunk = lax.dynamic_slice_in_dim(
            jnp.where(slot_y[slot] == y, own_starts, other_starts), begin, block, 0
        )
        starts.append(of_chunk)
        places.append(begin + jnp.arange(block, dtype=jnp.int32))
        meta += [of_chunk[0] // block, begin // block]
        for row_at in range(rows_on):
            found = jnp.int32(0)
            for other in range(slots):
                same = (slot_y[other] == slot_y[slot]) & (slot_row[other] == row_at)
                found = found + jnp.where(same, other, 0)
            meta.append(found)
    meta = jnp.stack([jnp.asarray(m, jnp.int32) for m in meta + [line]])
    starts, places = (jnp.stack(starts), jnp.stack(places))
    info = jnp.stack([places, starts], axis=1)
    offsets = (places - starts).astype(jnp.float32).reshape(-1)
    phases = offsets[:, None] * jnp.tile(frequency, LANES // (HEAD_DIM // 2))[None, :]
    cosine, sine = (jnp.cos(phases), jnp.sin(phases))

    residual_low = tokens_from_features(block_input)
    residual_low, joint_mine, output_mine = lax.optimization_barrier(
        (residual_low, joint_mine, output_mine)
    )
    joint_weight = gather_weight(joint_mine)
    residual = residual_low.astype(jnp.float32)
    scale_one = lax.rsqrt(jnp.mean(residual * residual, axis=1, keepdims=True) + EPSILON)
    normed_parts = gather_tokens((residual * scale_one * gains[0]).astype(jnp.bfloat16))
    queries, pair = zip(
        *[
            project(
                part,
                joint_weight,
                cosine[i * block : (i + 1) * block],
                sine[i * block : (i + 1) * block],
                query_width,
                block,
            )
            for i, part in enumerate(normed_parts)
        ]
    )
    queries = jnp.concatenate(queries, axis=0)
    pairs = lax.all_gather(jnp.stack(pair), "col", axis=0, tiled=False)
    output_weight = gather_weight(output_mine)
    pairs, gateup_mine, down_mine = lax.optimization_barrier((pairs, gateup_mine, down_mine))
    gateup_weight = gather_weight(gateup_mine)
    down_weight = gather_weight(down_mine)
    mixed, logs = attend(meta, queries, pairs, info, rows_on)
    attn_sum, _ = reduce_tokens(mixed, output_weight)
    attn_sum, late_cotangent = lax.optimization_barrier((attn_sum, cotangent))
    cot_low = tokens_from_features(late_cotangent)
    middle = residual + attn_sum
    scale_two = lax.rsqrt(jnp.mean(middle * middle, axis=1, keepdims=True) + EPSILON)
    normed_two = gather_tokens((middle * scale_two * gains[1]).astype(jnp.bfloat16))
    *normed_two, cot_low = lax.optimization_barrier((*normed_two, cot_low))
    normed_two = jnp.concatenate(normed_two, axis=0)
    cot = jnp.concatenate(gather_tokens(cot_low), axis=0)
    pair_sum = dot_nn(normed_two, gateup_weight)
    gate_sum, upward = (pair_sum[:, :hidden_here], pair_sum[:, hidden_here:])
    sigmoid_gate = jax.nn.sigmoid(gate_sum)
    silu_gate = gate_sum * sigmoid_gate
    hidden = (silu_gate * upward).astype(jnp.bfloat16)

    grad_hidden = dot_nn(cot, down_weight)
    grad_gate = grad_hidden * upward * sigmoid_gate * (1.0 + gate_sum * (1.0 - sigmoid_gate))
    grad_pair = jnp.concatenate(
        [grad_gate.astype(jnp.bfloat16), (grad_hidden * silu_gate).astype(jnp.bfloat16)], axis=1
    )

    def other_half(rows, grad):
        rows = lax.dynamic_slice_in_dim(rows, (1 - core) * (D // 2), D // 2, 1)
        return dot_tn(rows, grad).astype(jnp.bfloat16)

    def scatter_grad(rows, grad, received):
        rows = lax.dynamic_slice_in_dim(rows, core * (D // 2), D // 2, 1)
        total = dot_tn(rows, grad) + received.astype(jnp.float32)
        return lax.psum_scatter(
            total.astype(jnp.bfloat16), "col", scatter_dimension=0, tiled=True
        )

    def collect(piece):
        whole = lax.all_gather(piece, ("y", "core"), axis=0, tiled=True)
        return (whole[:wide], whole[wide:])

    grad_normed_two, (gateup_other, down_other) = reduce_tokens(
        grad_pair,
        gateup_weight,
        [lambda: [other_half(normed_two, grad_pair), other_half(cot, hidden)]],
    )
    gateup_other, down_other = (other_core(gateup_other), other_core(down_other))
    gateup_piece = scatter_grad(normed_two, grad_pair, gateup_other)
    down_piece = scatter_grad(cot, hidden, down_other)

    def norm_back(values, scale, grad_normed, gain):
        scaled = grad_normed * gain
        total = jnp.sum(scaled * values, axis=1, keepdims=True)
        return scale * scaled - values * (scale**3 * total / D)

    grad_middle = cot_low.astype(jnp.float32) + norm_back(
        middle, scale_two, grad_normed_two, gains[1]
    )
    gain_two = jnp.sum(grad_normed_two * middle * scale_two, axis=0)

    back = jnp.concatenate(gather_tokens(grad_middle.astype(jnp.bfloat16)), axis=0)
    back, late_hidden = lax.optimization_barrier((back, hidden))
    ffn_sum, _ = reduce_tokens(late_hidden, down_weight)
    grad_mixed = dot_nn(back, output_weight).astype(jnp.bfloat16)
    output_piece = scatter_grad(back, mixed, other_core(other_half(back, mixed)))
    grad_query, grad_parts = attend_back(
        meta, queries, pairs, grad_mixed, mixed, logs, info, cosine, sine, rows_on
    )
    grad_parts = [grad_parts[0]] + [
        shift(grad_parts[by], "col", lines, -by) for by in range(1, lines)
    ]
    grad_keyvalue = pair_back(grad_parts, cosine, sine, block)
    grad_joint = jnp.concatenate([grad_query, grad_keyvalue], axis=1)
    normed_one = jnp.concatenate(normed_parts, axis=0)
    grad_normed_one, (joint_other, gateup_piece, down_piece, ffn_sum) = reduce_tokens(
        grad_joint,
        joint_weight,
        [lambda: [other_half(normed_one, grad_joint), gateup_piece, down_piece, ffn_sum]],
    )
    layer_output = features_from_tokens((middle + ffn_sum).astype(jnp.bfloat16))
    joint_piece = scatter_grad(normed_one, grad_joint, other_core(joint_other))
    input_grad = grad_middle + norm_back(residual, scale_one, grad_normed_one, gains[0])
    gain_one = jnp.sum(grad_normed_one * residual * scale_one, axis=0)
    input_grad, layer_output = lax.optimization_barrier(
        (input_grad.astype(jnp.bfloat16), layer_output)
    )
    input_grad = features_from_tokens(input_grad).astype(jnp.float32)
    pair_piece = joint_piece[:, query_width:]
    pair_total = pair_piece.astype(jnp.float32)
    for by in range(1, rows_on):
        pair_total = pair_total + shift(pair_piece, "row", rows_on, by).astype(jnp.float32)
    joint_piece = jnp.concatenate(
        [joint_piece[:, :query_width], pair_total.astype(jnp.bfloat16)], axis=1
    )
    grad_down, grad_gateup, grad_output, grad_joint_sum = (
        collect(down_piece),
        collect(gateup_piece),
        collect(output_piece),
        collect(joint_piece),
    )

    gain_sums = jnp.stack([gain_one, gain_two])
    blocks = [
        jnp.concatenate(
            [
                gain_sums[:, at * half : (at + 1) * half],
                gain_sums[:, D // 2 + at * half : D // 2 + (at + 1) * half],
            ],
            axis=1,
        )
        for at in range(lines)
    ]
    grad_gains = blocks_total = pick(blocks, line)
    for by in range(1, lines):
        grad_gains = grad_gains + shift(pick(blocks, (line + by) % lines), "col", lines, by)
    for axis, size in (("core", 2), ("y", 2), ("row", rows_on)):
        blocks_total = grad_gains
        for by in range(1, size):
            grad_gains = grad_gains + shift(blocks_total, axis, size, by)

    gains_new = adamw_step(norm_gains, grad_gains, gains_moment, gains_square, 0.6, 0.0)
    query_grad = jnp.concatenate(
        [
            grad_joint_sum[at][:, j * LANES : (j + 1) * LANES]
            for j in range(per_row)
            for at in range(2)
        ],
        axis=1,
    )
    pair_grad = jnp.concatenate(
        [
            piece
            for at in range(2)
            for piece in (
                grad_joint_sum[at][:, query_width : query_width + LANES],
                grad_joint_sum[at][:, query_width + LANES + HEAD_DIM :],
                grad_joint_sum[at][:, query_width + LANES : query_width + LANES + HEAD_DIM],
            )
        ],
        axis=1,
    )
    turned = [grad_output[at].T for at in range(2)]
    output_grad = jnp.concatenate(
        [
            turned[at][j * LANES + part : j * LANES + part + HEAD_DIM]
            for j in range(per_row)
            for at in range(2)
            for part in (HEAD_DIM, 0)
        ],
        axis=0,
    )
    gateup_grad = jnp.concatenate(
        [grad_gateup[at].reshape(wide, 2, hidden_here) for at in range(2)], axis=2
    )
    down_grad = jnp.concatenate([grad_down[at].T for at in range(2)], axis=0)
    query_grad, pair_grad, output_grad, gateup_grad, down_grad = [
        lax.optimization_barrier(grad).astype(jnp.float32)
        for grad in (query_grad, pair_grad, output_grad, gateup_grad, down_grad)
    ]
    query_new = adamw_step(w_query, query_grad, query_moment, query_square, D ** (-0.5), 0.1)
    keyvalue_new = adamw_step(
        w_keyvalue, pair_grad, keyvalue_moment, keyvalue_square, D ** (-0.5), 0.1
    )
    output_new = adamw_step(
        w_output, output_grad, output_moment, output_square, (HEADS * HEAD_DIM // 64) ** (-0.5), 0.1
    )
    gateup_new = adamw_step(w_gateup, gateup_grad, gateup_moment, gateup_square, D ** (-0.5), 0.1)
    down_new = adamw_step(w_down, down_grad, down_moment, down_square, FF ** (-0.5), 0.1)
    return (
        layer_output,
        input_grad,
        *gains_new,
        *query_new,
        *keyvalue_new,
        *output_new,
        *gateup_new,
        *down_new,
    )


def solution(mesh):
    dp, rows_on, lines = (mesh.shape["dp"], mesh.shape["row"], mesh.shape["col"])
    split = Mesh(mesh.devices.reshape(dp // 2, 2, rows_on, lines), ("y", "core", "row", "col"))
    tokens = P(("y", "core", "row"), "col")
    narrow, wide = (P("col", "row"), P("row", "col"))
    gains, pair, gateup = (P(None, "col"), P("col", None), P("col", None, "row"))
    return jax.shard_map(
        functools.partial(on_device, (rows_on, lines)),
        mesh=split,
        in_specs=(
            tokens,
            tokens,
            P(("y", "core"), None),
            gains,
            narrow,
            pair,
            wide,
            gateup,
            wide,
            gains,
            gains,
            narrow,
            narrow,
            pair,
            pair,
            wide,
            wide,
            gateup,
            gateup,
            wide,
            wide,
        ),
        out_specs=(tokens, tokens)
        + (gains,) * 3
        + (narrow,) * 3
        + (pair,) * 3
        + (wide,) * 3
        + (gateup,) * 3
        + (wide,) * 3,
        check_vma=False,
    )
```

```python
import functools

import jax
import jax.numpy as jnp
from jax import lax
from jax.experimental import pallas as pl
from jax.experimental.pallas import tpu as pltpu
from jax.sharding import Mesh, PartitionSpec as P

D = 2048
HEADS = 32
KV_HEADS = 4
HEAD_DIM = 64
FF = 5632
STEP = 10

EPSILON = 1e-05
BETA_ONE = 0.9
BETA_TWO = 0.999
ADAM_EPS = 1e-08
MASKED = -1e30
SCORE_SCALE = HEAD_DIM ** (-0.5)
LANES = 128
VMEM_LIMIT = 48 * 1024 * 1024


def dot_nn(left, right):
    return lax.dot_general(left, right, (((1,), (0,)), ((), ())), preferred_element_type=jnp.float32)


def dot_nt(left, right):
    return lax.dot_general(left, right, (((1,), (1,)), ((), ())), preferred_element_type=jnp.float32)


def dot_tn(left, right):
    return lax.dot_general(left, right, (((0,), (0,)), ((), ())), preferred_element_type=jnp.float32)


def adamw_step(weight, gradient, moment, square, step_rate, decay_rate):
    moment_new = BETA_ONE * moment + (1.0 - BETA_ONE) * gradient
    square_new = BETA_TWO * square + (1.0 - BETA_TWO) * gradient * gradient
    fixed_one = moment_new / (1.0 - BETA_ONE**STEP)
    fixed_two = square_new / (1.0 - BETA_TWO**STEP)
    weight_new = weight - step_rate * (
        fixed_one / (jnp.sqrt(fixed_two) + ADAM_EPS) + decay_rate * weight
    )
    return (moment_new, square_new, weight_new)


def document_starts(segment_ids):
    places = jnp.arange(segment_ids.shape[0], dtype=jnp.int32)
    starts = jnp.concatenate([jnp.ones((1,), jnp.bool_), segment_ids[1:] != segment_ids[:-1]])
    return lax.cummax(jnp.where(starts, places, 0), axis=0)


def turn(values):
    lane = lax.broadcasted_iota(jnp.int32, values.shape, 1)
    ahead = pltpu.roll(values, LANES - HEAD_DIM // 2, 1)
    behind = pltpu.roll(values, HEAD_DIM // 2, 1)
    return jnp.where(lane % HEAD_DIM < HEAD_DIM // 2, -ahead, behind)


def project_kernel(rows_ref, weight_ref, cos_ref, sin_ref, query_ref, pair_ref):
    sums = dot_nn(rows_ref[...], weight_ref[...])
    cosine, sine = cos_ref[...], sin_ref[...]
    width = query_ref.shape[1]
    lane = lax.broadcasted_iota(jnp.int32, cosine.shape, 1)
    for start in range(0, width, LANES):
        part = sums[:, start : start + LANES]
        turned = (part * cosine + turn(part) * sine).astype(jnp.bfloat16)
        query_ref[:, start : start + LANES] = turned * jnp.bfloat16(SCORE_SCALE)
    for which in range(2):
        part = sums[:, width + which * LANES : width + (which + 1) * LANES]
        is_key = (lane < HEAD_DIM) if which == 0 else (lane >= HEAD_DIM)
        turned = jnp.where(is_key, part * cosine + turn(part) * sine, part)
        pair_ref[:, which * LANES : (which + 1) * LANES] = turned.astype(jnp.bfloat16)


def project(rows, weight, cosine, sine, width, block):
    count = rows.shape[0] // block
    total = weight.shape[1]
    return pl.pallas_call(
        project_kernel,
        grid=(count,),
        in_specs=[
            pl.BlockSpec((block, rows.shape[1]), lambda i: (i, 0)),
            pl.BlockSpec(weight.shape, lambda i: (0, 0)),
            pl.BlockSpec((block, LANES), lambda i: (i, 0)),
            pl.BlockSpec((block, LANES), lambda i: (i, 0)),
        ],
        out_specs=[
            pl.BlockSpec((block, width), lambda i: (i, 0)),
            pl.BlockSpec((block, total - width), lambda i: (i, 0)),
        ],
        out_shape=[
            jax.ShapeDtypeStruct((rows.shape[0], width), jnp.bfloat16),
            jax.ShapeDtypeStruct((rows.shape[0], total - width), jnp.bfloat16),
        ],
        compiler_params=pltpu.CompilerParams(vmem_limit_bytes=VMEM_LIMIT),
        cost_estimate=pl.CostEstimate(
            flops=2 * rows.shape[0] * rows.shape[1] * total,
            bytes_accessed=rows.size * 2 + weight.size * 2,
            transcendentals=0,
        ),
        name="project",
    )(rows, weight, cosine, sine)


def stack_heads(values):
    return jnp.concatenate(
        [values[:, start : start + LANES] for start in range(0, values.shape[1], LANES)], axis=0
    )


def block_of(meta_ref, chunk, step, parts, lines):
    base = chunk * (2 + parts)
    key_block = meta_ref[base + 1] - step
    slot = meta_ref[base + 2 + key_block // lines]
    own_line = meta_ref[pl.num_programs(0) * (2 + parts)]
    line = lax.rem(key_block, lines)
    return (key_block, slot, line, lax.rem(own_line - line + lines, lines))


def attend_kernel(parts, lines, meta_ref, query_ref, pair_ref, info_ref, out_ref, log_ref):
    chunk = pl.program_id(0)
    block = query_ref.shape[0]
    heads = query_ref.shape[1] // LANES
    stacked = stack_heads(query_ref[...])
    lane = lax.broadcasted_iota(jnp.int32, stacked.shape, 1)
    place = jnp.concatenate([info_ref[0, 0:1, :]] * heads, axis=1)
    start = jnp.concatenate([info_ref[0, 1:2, :]] * heads, axis=1)
    base = chunk * (2 + parts)
    steps = meta_ref[base + 1] - meta_ref[base] + 1
    width = heads * block
    outs = []
    for which in range(2):
        is_key = (lane < HEAD_DIM) if which == 0 else (lane >= HEAD_DIM)
        queries = jnp.where(is_key, stacked, jnp.zeros_like(stacked))

        def body(step, carry):
            peak, total, mixed = carry
            key_block, slot, at, _ = block_of(meta_ref, chunk, step, parts, lines)
            pair = pair_ref[at, slot, :, which * LANES : (which + 1) * LANES]
            scores = dot_nt(pair, queries)
            key_place = key_block * block + lax.broadcasted_iota(jnp.int32, (block, width), 0)
            scores = jnp.where((key_place <= place) & (key_place >= start), scores, MASKED)
            new_peak = jnp.maximum(peak, jnp.max(scores, axis=0, keepdims=True))
            weights = jnp.exp(scores - new_peak)
            shrink = jnp.exp(peak - new_peak)
            total = total * shrink + jnp.sum(weights, axis=0, keepdims=True)
            mixed = mixed * shrink + dot_tn(pair, weights.astype(jnp.bfloat16))
            return (new_peak, total, mixed)

        peak, total, mixed = lax.fori_loop(
            0,
            steps,
            body,
            (
                jnp.full((1, width), MASKED, jnp.float32),
                jnp.zeros((1, width), jnp.float32),
                jnp.zeros((LANES, width), jnp.float32),
            ),
        )
        log_ref[0, which : which + 1, :] = peak + jnp.log(total)
        outs.append(mixed / total)
    joined = jnp.concatenate([outs[1][:HEAD_DIM], outs[0][HEAD_DIM:]], axis=0)
    rows = joined.T.astype(jnp.bfloat16)
    for head in range(heads):
        out_ref[:, head * LANES : (head + 1) * LANES] = rows[head * block : (head + 1) * block]


def attend(meta, queries, pairs, info, parts):
    chunks, block = (info.shape[0], info.shape[2])
    width = queries.shape[1]
    heads = width // LANES
    lines = pairs.shape[0]
    steps = 3 * chunks
    return pl.pallas_call(
        functools.partial(attend_kernel, parts, lines),
        grid_spec=pltpu.PrefetchScalarGridSpec(
            num_scalar_prefetch=1,
            grid=(chunks,),
            in_specs=[
                pl.BlockSpec((block, width), lambda i, m: (i, 0)),
                pl.BlockSpec(pairs.shape, lambda i, m: (0, 0, 0, 0)),
                pl.BlockSpec((1, 2, block), lambda i, m: (i, 0, 0)),
            ],
            out_specs=[
                pl.BlockSpec((block, width), lambda i, m: (i, 0)),
                pl.BlockSpec((1, 2, heads * block), lambda i, m: (i, 0, 0)),
            ],
        ),
        out_shape=[
            jax.ShapeDtypeStruct(queries.shape, jnp.bfloat16),
            jax.ShapeDtypeStruct((chunks, 2, heads * block), jnp.float32),
        ],
        compiler_params=pltpu.CompilerParams(vmem_limit_bytes=VMEM_LIMIT),
        cost_estimate=pl.CostEstimate(
            flops=steps * 2 * 2 * 2 * heads * block * block * LANES,
            bytes_accessed=queries.size * 4 + pairs.size * 2,
            transcendentals=steps * 2 * heads * block * block,
        ),
        name="attend",
    )(meta, queries, pairs, info)


def attend_back_kernel(parts, lines, meta_ref, query_ref, *refs):
    pair_ref, grad_ref, mixed_ref, log_ref, info_ref, cos_ref, sin_ref, query_out = refs[:8]
    pair_outs = refs[8 : 8 + lines]
    sums = refs[8 + lines]
    chunk = pl.program_id(0)
    block = query_ref.shape[0]
    heads = query_ref.shape[1] // LANES

    @pl.when(chunk == 0)
    def _():
        sums[...] = jnp.zeros_like(sums)

    stacked = stack_heads(query_ref[...])
    stacked_grad = stack_heads(grad_ref[...])
    product = stacked_grad.astype(jnp.float32) * stack_heads(mixed_ref[...]).astype(jnp.float32)
    lane = lax.broadcasted_iota(jnp.int32, stacked.shape, 1)
    place = jnp.concatenate([info_ref[0, 0:1, :]] * heads, axis=1)
    start = jnp.concatenate([info_ref[0, 1:2, :]] * heads, axis=1)
    base = chunk * (2 + parts)
    steps = meta_ref[base + 1] - meta_ref[base] + 1
    width = heads * block
    grads = []
    for which in range(2):
        is_key = (lane < HEAD_DIM) if which == 0 else (lane >= HEAD_DIM)
        queries = jnp.where(is_key, stacked, jnp.zeros_like(stacked))
        grad = jnp.where(is_key, jnp.zeros_like(stacked_grad), stacked_grad)
        own = jnp.where(is_key, 0.0, product)
        centre = lax.dot_general(
            jnp.ones((8, LANES), jnp.float32),
            own,
            (((1,), (1,)), ((), ())),
            precision=lax.Precision.HIGHEST,
            preferred_element_type=jnp.float32,
        )[0:1]
        logs = log_ref[0, which : which + 1, :]

        def body(step, grad_query):
            key_block, slot, at, shift = block_of(meta_ref, chunk, step, parts, lines)
            columns = slice(which * LANES, (which + 1) * LANES)
            pair = pair_ref[at, slot, :, columns]
            scores = dot_nt(pair, queries)
            key_place = key_block * block + lax.broadcasted_iota(jnp.int32, (block, width), 0)
            scores = jnp.where((key_place <= place) & (key_place >= start), scores, MASKED)
            weights = jnp.exp(scores - logs)
            grad_scores = (weights * (dot_nt(pair, grad) - centre)).astype(jnp.bfloat16)
            sums[shift, slot, :, columns] += dot_nn(grad_scores, queries) + dot_nn(
                weights.astype(jnp.bfloat16), grad
            )
            return grad_query + dot_tn(pair, grad_scores)

        grads.append(lax.fori_loop(0, steps, body, jnp.zeros((LANES, width), jnp.float32)))
    joined = jnp.concatenate([grads[0][:HEAD_DIM], grads[1][HEAD_DIM:]], axis=0)
    rows = joined.T * SCORE_SCALE
    cosine, sine = cos_ref[...], sin_ref[...]
    for head in range(heads):
        part = rows[head * block : (head + 1) * block]
        back = part * cosine - turn(part) * sine
        query_out[:, head * LANES : (head + 1) * LANES] = back.astype(jnp.bfloat16)

    @pl.when(chunk == pl.num_programs(0) - 1)
    def _():
        for line in range(lines):
            pair_outs[line][...] = sums[line].astype(jnp.bfloat16)


def attend_back(meta, queries, pairs, grad_mixed, mixed, logs, info, cosine, sine, parts):
    chunks, block = (info.shape[0], info.shape[2])
    width = queries.shape[1]
    heads = width // LANES
    lines = pairs.shape[0]
    shape = pairs.shape[1:]
    steps = 3 * chunks
    wide = pl.BlockSpec((block, width), lambda i, m: (i, 0))
    table = pl.BlockSpec((block, LANES), lambda i, m: (i, 0))
    whole = pl.BlockSpec(shape, lambda i, m: (0, 0, 0))
    outs = pl.pallas_call(
        functools.partial(attend_back_kernel, parts, lines),
        grid_spec=pltpu.PrefetchScalarGridSpec(
            num_scalar_prefetch=1,
            grid=(chunks,),
            in_specs=[
                wide,
                pl.BlockSpec(pairs.shape, lambda i, m: (0, 0, 0, 0)),
                wide,
                wide,
                pl.BlockSpec((1, 2, heads * block), lambda i, m: (i, 0, 0)),
                pl.BlockSpec((1, 2, block), lambda i, m: (i, 0, 0)),
                table,
                table,
            ],
            out_specs=[wide] + [whole] * lines,
            scratch_shapes=[pltpu.VMEM(pairs.shape, jnp.float32)],
        ),
        out_shape=[jax.ShapeDtypeStruct(queries.shape, jnp.bfloat16)]
        + [jax.ShapeDtypeStruct(shape, jnp.bfloat16)] * lines,
        compiler_params=pltpu.CompilerParams(vmem_limit_bytes=VMEM_LIMIT),
        cost_estimate=pl.CostEstimate(
            flops=steps * 2 * 5 * 2 * heads * block * block * LANES,
            bytes_accessed=queries.size * 8 + 2 * pairs.size * 2,
            transcendentals=steps * 2 * heads * block * block,
        ),
        name="attend_back",
    )(
        meta,
        queries,
        pairs,
        grad_mixed,
        mixed,
        logs,
        info,
        cosine,
        sine,
    )
    return (outs[0], [out.reshape(chunks * block, 2 * LANES) for out in outs[1:]])


def pair_back_kernel(*refs):
    *part_refs, cos_ref, sin_ref, out_ref = refs
    cosine, sine = cos_ref[...], sin_ref[...]
    lane = lax.broadcasted_iota(jnp.int32, cosine.shape, 1)
    for which in range(2):
        columns = slice(which * LANES, (which + 1) * LANES)
        total = part_refs[0][:, columns].astype(jnp.float32)
        for ref in part_refs[1:]:
            total = total + ref[:, columns].astype(jnp.float32)
        is_key = (lane < HEAD_DIM) if which == 0 else (lane >= HEAD_DIM)
        total = jnp.where(is_key, total * cosine - turn(total) * sine, total)
        out_ref[:, columns] = total.astype(jnp.bfloat16)


def pair_back(parts, cosine, sine, block):
    rows, columns = parts[0].shape
    tile = pl.BlockSpec((block, columns), lambda i: (i, 0))
    table = pl.BlockSpec((block, LANES), lambda i: (i, 0))
    return pl.pallas_call(
        pair_back_kernel,
        grid=(rows // block,),
        in_specs=[tile] * len(parts) + [table, table],
        out_specs=tile,
        out_shape=jax.ShapeDtypeStruct((rows, columns), jnp.bfloat16),
        compiler_params=pltpu.CompilerParams(vmem_limit_bytes=VMEM_LIMIT),
        name="pair_back",
    )(*parts, cosine, sine)


def update(refs, index, gradient, rate):
    weight, moment, square = [ref[index] for ref in refs[:3]]
    moment_new, square_new, weight_new = adamw_step(weight, gradient, moment, square, rate, 0.1)
    for ref, value in zip(refs[3:], (moment_new, square_new, weight_new)):
        ref[index] = value


def chosen(meta_ref, grad_refs, at, rows, columns):
    own_y = meta_ref[0] == at
    first = pl.program_id(0) == 0
    near = jnp.where(first, grad_refs[0][rows, columns], grad_refs[2][rows, columns])
    far = jnp.where(first, grad_refs[1][rows, columns], grad_refs[3][rows, columns])
    return jnp.where(own_y, near, far).astype(jnp.float32)


def joint_update_kernel(meta_ref, *refs):
    grad_refs, query_refs, pair_refs = (refs[:4], refs[4:7] + refs[10:13], refs[7:10] + refs[13:16])
    groups = query_refs[0].shape[1] // (2 * LANES)
    every = slice(None)
    for at in range(2):
        for j in range(groups):
            gradient = chosen(meta_ref, grad_refs, at, every, slice(j * LANES, (j + 1) * LANES))
            place = slice((2 * j + at) * LANES, (2 * j + at + 1) * LANES)
            update(query_refs, (every, place), gradient, D ** (-0.5))
        for which in range(2):
            start = (groups + which) * LANES
            gradient = chosen(meta_ref, grad_refs, at, every, slice(start, start + LANES))
            if which == 1:
                gradient = pltpu.roll(gradient, HEAD_DIM, 1)
            place = slice((2 * at + which) * LANES, (2 * at + which + 1) * LANES)
            update(pair_refs, (every, place), gradient, D ** (-0.5))


def joint_update(meta, grads, query, pair):
    half = grads[0].shape[0]

    def rows_of(array):
        return pl.BlockSpec((half, array.shape[1]), lambda i, m: ((m[1] + i) % 2, 0))

    whole = pl.BlockSpec(grads[0].shape, lambda i, m: (0, 0))
    blocks = [rows_of(array) for array in (*query, *pair)]
    return pl.pallas_call(
        joint_update_kernel,
        grid_spec=pltpu.PrefetchScalarGridSpec(
            num_scalar_prefetch=1, grid=(2,), in_specs=[whole] * 4 + blocks, out_specs=blocks
        ),
        out_shape=[jax.ShapeDtypeStruct(array.shape, array.dtype) for array in (*query, *pair)],
        compiler_params=pltpu.CompilerParams(vmem_limit_bytes=VMEM_LIMIT),
        cost_estimate=pl.CostEstimate(
            flops=20 * (query[0].size + pair[0].size),
            bytes_accessed=24 * (query[0].size + pair[0].size),
            transcendentals=0,
        ),
        name="joint_update",
    )(meta, *grads, *query, *pair)


def turned_update_kernel(rate, swapped, meta_ref, *refs):
    grad_refs, weight_refs, token_ref = (refs[:4], refs[4:10], refs[10])
    at = pl.program_id(1)
    width = grad_refs[0].shape[1]
    every = slice(None)
    for j, start in enumerate(range(0, width, LANES)):
        strip = slice(start, min(start + LANES, width))
        gradient = chosen(meta_ref, grad_refs, at, every, strip).T
        if swapped:
            gradient = jnp.concatenate([gradient[HEAD_DIM:], gradient[:HEAD_DIM]], axis=0)
            index = (j, 0)
        else:
            index = (strip, every)
        update(weight_refs, index, gradient, rate)
    token_ref[...] = jnp.zeros_like(token_ref)


def turned_update(meta, grads, weights, rate, swapped):
    half, width = grads[0].shape
    shape = weights[0].shape
    if swapped:
        weights = [w.reshape(width // LANES, 2, LANES, shape[1]) for w in weights]
        block = pl.BlockSpec(
            (width // LANES, 1, LANES, half), lambda i, at, m: (0, at, 0, (m[1] + i) % 2)
        )
    else:
        block = pl.BlockSpec((width, half), lambda i, at, m: (at, (m[1] + i) % 2))
    outs = pl.pallas_call(
        functools.partial(turned_update_kernel, rate, swapped),
        grid_spec=pltpu.PrefetchScalarGridSpec(
            num_scalar_prefetch=1,
            grid=(2, 2),
            in_specs=[pl.BlockSpec(grads[0].shape, lambda i, at, m: (0, 0))] * 4 + [block] * 3,
            out_specs=[block] * 3 + [pl.BlockSpec((8, LANES), lambda i, at, m: (0, 0))],
        ),
        out_shape=[jax.ShapeDtypeStruct(weights[0].shape, jnp.float32)] * 3
        + [jax.ShapeDtypeStruct((8, LANES), jnp.float32)],
        compiler_params=pltpu.CompilerParams(vmem_limit_bytes=VMEM_LIMIT),
        cost_estimate=pl.CostEstimate(
            flops=20 * weights[0].size, bytes_accessed=24 * weights[0].size, transcendentals=0
        ),
        name="turned_update",
    )(meta, *grads, *weights)
    return ([out.reshape(shape) for out in outs[:3]], outs[3])


def on_device(
    sizes,
    block_input,
    cotangent,
    segments,
    norm_gains,
    w_query,
    w_keyvalue,
    w_output,
    w_gateup,
    w_down,
    gains_moment,
    gains_square,
    query_moment,
    query_square,
    keyvalue_moment,
    keyvalue_square,
    output_moment,
    output_square,
    gateup_moment,
    gateup_square,
    down_moment,
    down_square,
):
    rows_on, lines = sizes
    y, core, row, line = [lax.axis_index(name) for name in ("y", "core", "row", "col")]
    length = segments.shape[1]
    block = block_input.shape[0] // lines
    wide = block_input.shape[1]
    half = wide // 2
    slots = 2 * rows_on
    per_row = w_query.shape[1] // (KV_HEADS * HEAD_DIM)
    query_width = per_row * LANES
    hidden_here = w_gateup.shape[2] // 2

    def shift(value, axis, size, by):
        return lax.ppermute(value, axis, [(i, (i + by) % size) for i in range(size)])

    def other_core(value):
        return lax.ppermute(value, "core", [(0, 1), (1, 0)])

    def other_y(value):
        return lax.ppermute(value, "y", [(0, 1), (1, 0)])

    def place_of(y_at, core_at, row_at):
        return (y_at * 2 + core_at) * rows_on + row_at

    first_pairs, second_pairs = ([], [])
    for y_at in range(2):
        for core_at in range(2):
            for row_at in range(rows_on):
                over_row = (
                    place_of(y_at, core_at, row_at),
                    place_of(y_at, core_at, (row_at + 1) % rows_on),
                )
                over_y = (place_of(y_at, core_at, row_at), place_of(1 - y_at, core_at, row_at))
                first_pairs.append(over_row if core_at == 0 else over_y)
                second_pairs.append(over_y if core_at == 0 else over_row)
    near = ("y", "core", "row")

    def gather_tokens(own):
        if rows_on == 2:
            first = lax.ppermute(own, near, first_pairs)
            second = lax.ppermute(own, near, second_pairs)
            third = lax.ppermute(first, near, second_pairs)
            return [own, first, second, third]
        parts = [own] + [shift(own, "row", rows_on, by) for by in range(1, rows_on)]
        return parts + [other_y(part) for part in parts]

    def reduce_tokens(terms, after_close=None, after_first=None):
        def rows_of(first, last):
            total = 0.0
            for left, right in terms:
                total = total + dot_nt(left[first * block : last * block], right)
            return total.astype(jnp.bfloat16)

        if rows_on == 2:
            far = rows_of(2, 4)
            third = lax.ppermute(far[block:], near, second_pairs)
            second = lax.ppermute(far[:block], near, second_pairs)
            close = rows_of(0, 2)
            early = after_close(close) if after_close else None
            first = (close[block:].astype(jnp.float32) + third.astype(jnp.float32)).astype(jnp.bfloat16)
            late = after_first(first) if after_first else None
            first = lax.ppermute(first, near, first_pairs)
            own = close[:block].astype(jnp.float32) + second.astype(jnp.float32)
            return (own + first.astype(jnp.float32), early, late)
        partial = rows_of(0, slots)
        early = after_close(partial) if after_close else None
        parts = [partial[i * block : (i + 1) * block] for i in range(slots)]
        sums = [
            parts[i].astype(jnp.float32) + other_y(parts[rows_on + i]).astype(jnp.float32)
            for i in range(rows_on)
        ]
        late = after_first(sums[0]) if after_first else None
        total = sums[0]
        for by in range(1, rows_on):
            moved = shift(sums[by].astype(jnp.bfloat16), "row", rows_on, -by)
            total = total + moved.astype(jnp.float32)
        return (total, early, late)

    def tied(key, *values):
        return lax.optimization_barrier((key, *values))[1:]

    if rows_on == 2:
        slot_y = [y, jnp.where(core == 0, y, 1 - y), jnp.where(core == 0, 1 - y, y), 1 - y]
        slot_row = [row, jnp.where(core == 0, 1 - row, row), jnp.where(core == 0, row, 1 - row), 1 - row]
    else:
        slot_y = [y] * rows_on + [1 - y] * rows_on
        slot_row = [(row - by) % rows_on for by in range(rows_on)] * 2

    def pick(parts, index):
        return lax.dynamic_index_in_dim(jnp.stack(parts), index, 0, keepdims=False)

    def tokens_from_features(values):
        parts = []
        for by in range(lines):
            part = lax.dynamic_slice_in_dim(values, ((line + by) % lines) * block, block, 0)
            parts.append(part if by == 0 else shift(part, "col", lines, by))
        blocks = [pick(parts, (line - at) % lines) for at in range(lines)]
        return jnp.concatenate([b[:, :half] for b in blocks] + [b[:, half:] for b in blocks], axis=1)

    def features_from_tokens(values):
        blocks = [
            jnp.concatenate(
                [
                    values[:, at * half : (at + 1) * half],
                    values[:, D // 2 + at * half : D // 2 + (at + 1) * half],
                ],
                axis=1,
            )
            for at in range(lines)
        ]
        parts = []
        for by in range(lines):
            part = pick(blocks, (line + by) % lines)
            parts.append(part if by == 0 else shift(part, "col", lines, by))
        return jnp.concatenate([pick(parts, (line - at) % lines) for at in range(lines)], axis=0)

    def half_rows(values):
        return lax.dynamic_slice_in_dim(values, core * half, half, 0)

    def half_columns(values):
        return lax.dynamic_slice_in_dim(values, core * half, half, 1)

    def gather_weight(piece):
        return lax.all_gather(piece, ("core", "col"), axis=0, tiled=True)

    query_rows = half_rows(w_query).astype(jnp.bfloat16)
    pair_rows = half_rows(w_keyvalue).astype(jnp.bfloat16)

    def joint_of(at):
        pieces = [
            query_rows[:, (2 * j + at) * LANES : (2 * j + at + 1) * LANES] for j in range(per_row)
        ]
        pair = pair_rows[:, at * 2 * LANES : (at + 1) * 2 * LANES]
        pieces += [
            pair[:, :LANES],
            pair[:, LANES + HEAD_DIM :],
            pair[:, LANES : LANES + HEAD_DIM],
        ]
        return jnp.concatenate(pieces, axis=1)

    joint_mine = jnp.where(y == 0, joint_of(0), joint_of(1))
    output_columns = half_columns(w_output).astype(jnp.bfloat16)

    def output_of(at):
        pieces = []
        for j in range(per_row):
            base = (2 * j + at) * LANES
            pieces += [
                output_columns[base + HEAD_DIM : base + LANES],
                output_columns[base : base + HEAD_DIM],
            ]
        return jnp.concatenate(pieces, axis=0)

    output_mine = jnp.where(y == 0, output_of(0), output_of(1)).T
    gateup_mine = lax.dynamic_slice(
        w_gateup, (core * half, 0, y * hidden_here), (half, 2, hidden_here)
    ).astype(jnp.bfloat16)
    gateup_mine = jnp.concatenate([gateup_mine[:, 0], gateup_mine[:, 1]], axis=1)
    down_mine = lax.dynamic_slice(
        w_down, (y * hidden_here, core * half), (hidden_here, half)
    ).astype(jnp.bfloat16).T

    gain_parts = [norm_gains] + [shift(norm_gains, "col", lines, by) for by in range(1, lines)]
    gain_blocks = [pick(gain_parts, (line - at) % lines) for at in range(lines)]
    gains = jnp.concatenate(
        [b[:, :half] for b in gain_blocks] + [b[:, half:] for b in gain_blocks], axis=1
    )

    own_starts = document_starts(segments[0])
    other_starts = document_starts(other_y(segments)[0])
    frequency = 10000.0 ** (-2.0 * jnp.arange(HEAD_DIM // 2, dtype=jnp.float32) / HEAD_DIM)
    starts, places, meta = ([], [], [])
    for slot in range(slots):
        begin = slot_row[slot] * (lines * block) + line * block
        of_chunk = lax.dynamic_slice_in_dim(
            jnp.where(slot_y[slot] == y, own_starts, other_starts), begin, block, 0
        )
        starts.append(of_chunk)
        places.append(begin + jnp.arange(block, dtype=jnp.int32))
        meta += [of_chunk[0] // block, begin // block]
        for row_at in range(rows_on):
            found = jnp.int32(0)
            for other in range(slots):
                same = (slot_y[other] == slot_y[slot]) & (slot_row[other] == row_at)
                found = found + jnp.where(same, other, 0)
            meta.append(found)
    meta = jnp.stack([jnp.asarray(m, jnp.int32) for m in meta + [line]])
    starts, places = (jnp.stack(starts), jnp.stack(places))
    info = jnp.stack([places, starts], axis=1)
    offsets = (places - starts).astype(jnp.float32).reshape(-1)
    phases = offsets[:, None] * jnp.tile(frequency, LANES // (HEAD_DIM // 2))[None, :]
    cosine, sine = (jnp.cos(phases), jnp.sin(phases))

    residual_low = tokens_from_features(block_input)
    residual_low, joint_mine, output_mine = lax.optimization_barrier(
        (residual_low, joint_mine, output_mine)
    )
    first_weight = gather_weight(jnp.concatenate([joint_mine, output_mine], axis=1))
    joint_width = joint_mine.shape[1]
    joint_weight, output_weight = (first_weight[:, :joint_width], first_weight[:, joint_width:])
    residual = residual_low.astype(jnp.float32)
    scale_one = lax.rsqrt(jnp.mean(residual * residual, axis=1, keepdims=True) + EPSILON)
    normed_parts = gather_tokens((residual * scale_one * gains[0]).astype(jnp.bfloat16))
    queries, pair = zip(
        *[
            project(
                part,
                joint_weight,
                cosine[i * block : (i + 1) * block],
                sine[i * block : (i + 1) * block],
                query_width,
                block,
            )
            for i, part in enumerate(normed_parts)
        ]
    )
    queries = jnp.concatenate(queries, axis=0)
    pairs = lax.all_gather(jnp.stack(pair), "col", axis=0, tiled=False)
    pairs, gateup_mine, down_mine = lax.optimization_barrier((pairs, gateup_mine, down_mine))
    gateup_weight = gather_weight(gateup_mine)
    down_weight = gather_weight(down_mine)
    mixed, logs = attend(meta, queries, pairs, info, rows_on)
    attn_sum, _, _ = reduce_tokens([(mixed, output_weight)])
    (late_cotangent,) = tied(attn_sum, cotangent)
    cot_low = tokens_from_features(late_cotangent)
    middle = residual + attn_sum
    scale_two = lax.rsqrt(jnp.mean(middle * middle, axis=1, keepdims=True) + EPSILON)
    normed_two = gather_tokens((middle * scale_two * gains[1]).astype(jnp.bfloat16))
    (cot_low,) = tied(normed_two[-1], cot_low)
    normed_two = jnp.concatenate(normed_two, axis=0)
    cot = jnp.concatenate(gather_tokens(cot_low), axis=0)
    pair_sum = dot_nn(normed_two, gateup_weight)
    gate_sum, upward = (pair_sum[:, :hidden_here], pair_sum[:, hidden_here:])
    sigmoid_gate = jax.nn.sigmoid(gate_sum)
    silu_gate = gate_sum * sigmoid_gate
    hidden = (silu_gate * upward).astype(jnp.bfloat16)

    grad_hidden = dot_nn(cot, down_weight)
    grad_gate = grad_hidden * upward * sigmoid_gate * (1.0 + gate_sum * (1.0 - sigmoid_gate))
    grad_gate = grad_gate.astype(jnp.bfloat16)
    grad_up = (grad_hidden * silu_gate).astype(jnp.bfloat16)

    def other_half(rows, grad):
        rows = lax.dynamic_slice_in_dim(rows, (1 - core) * (D // 2), D // 2, 1)
        return dot_tn(rows, grad).astype(jnp.bfloat16)

    def own_half(rows, grad, received):
        rows = lax.dynamic_slice_in_dim(rows, core * (D // 2), D // 2, 1)
        total = dot_tn(rows, grad) + received.astype(jnp.float32)
        return total.astype(jnp.bfloat16)

    def scatter(total):
        return lax.psum_scatter(total, "col", scatter_dimension=0, tiled=True)

    def collect(piece):
        near_y = other_y(piece)
        return [piece, near_y, other_core(piece), other_core(near_y)]

    def down_work(close):
        rows, grad = tied(close, cot, hidden)
        received = other_core(other_half(rows, grad))
        return scatter(own_half(rows, grad, received))

    def gate_work(first):
        rows, grad, grad_next = tied(first, normed_two, grad_gate, grad_up)
        return (
            other_core(other_half(rows, grad)),
            other_core(other_half(rows, grad_next)),
        )

    grad_normed_two, down_piece, (gate_other, up_other) = reduce_tokens(
        [
            (grad_gate, gateup_weight[:, :hidden_here]),
            (grad_up, gateup_weight[:, hidden_here:]),
        ],
        down_work,
        gate_work,
    )

    def norm_back(values, scale, grad_normed, gain):
        scaled = grad_normed * gain
        total = jnp.sum(scaled * values, axis=1, keepdims=True)
        return scale * scaled - values * (scale**3 * total / D)

    grad_middle = cot_low.astype(jnp.float32) + norm_back(
        middle, scale_two, grad_normed_two, gains[1]
    )
    gain_two = jnp.sum(grad_normed_two * middle * scale_two, axis=0)

    grad_middle_low = grad_middle.astype(jnp.bfloat16)
    rows, grad, grad_next = tied(grad_middle_low, normed_two, grad_gate, grad_up)
    gate_piece = scatter(own_half(rows, grad, gate_other))
    up_total = own_half(rows, grad_next, up_other)
    back = jnp.concatenate(gather_tokens(grad_middle_low), axis=0)
    (late_hidden,) = tied(back, hidden)
    ffn_sum, _, _ = reduce_tokens([(late_hidden, down_weight)])
    grad_mixed = dot_nn(back, output_weight).astype(jnp.bfloat16)
    grad_query, grad_parts = attend_back(
        meta, queries, pairs, grad_mixed, mixed, logs, info, cosine, sine, rows_on
    )
    grad_parts = [grad_parts[0]] + [
        shift(grad_parts[by], "col", lines, -by) for by in range(1, lines)
    ]
    meta_core = jnp.stack([y, core]).astype(jnp.int32)
    down_new, down_done = turned_update(
        meta_core, collect(down_piece), [w_down, down_moment, down_square], FF ** (-0.5), False
    )
    *grad_parts, up_total, back, mixed, _, _, gate_piece = lax.optimization_barrier(
        (*grad_parts, up_total, back, mixed, down_done, ffn_sum, gate_piece)
    )
    up_piece = scatter(up_total)
    output_piece = scatter(own_half(back, mixed, other_core(other_half(back, mixed))))
    grad_keyvalue = pair_back(grad_parts, cosine, sine, block)
    grad_joint = jnp.concatenate([grad_query, grad_keyvalue], axis=1)
    normed_one = jnp.concatenate(normed_parts, axis=0)

    def joint_work(close):
        rows, grad = tied(close, normed_one, grad_joint)
        return scatter(own_half(rows, grad, other_core(other_half(rows, grad))))

    grad_normed_one, joint_piece, _ = reduce_tokens([(grad_joint, joint_weight)], joint_work)
    layer_output = features_from_tokens((middle + ffn_sum).astype(jnp.bfloat16))
    input_grad = grad_middle + norm_back(residual, scale_one, grad_normed_one, gains[0])
    gain_one = jnp.sum(grad_normed_one * residual * scale_one, axis=0)
    input_grad, layer_output = lax.optimization_barrier(
        (input_grad.astype(jnp.bfloat16), layer_output)
    )
    input_grad = features_from_tokens(input_grad).astype(jnp.float32)
    pair_piece = joint_piece[:, query_width:]
    pair_total = pair_piece.astype(jnp.float32)
    for by in range(1, rows_on):
        pair_total = pair_total + shift(pair_piece, "row", rows_on, by).astype(jnp.float32)
    joint_piece = jnp.concatenate(
        [joint_piece[:, :query_width], pair_total.astype(jnp.bfloat16)], axis=1
    )
    joint_new = joint_update(
        meta_core,
        collect(joint_piece),
        [w_query, query_moment, query_square],
        [w_keyvalue, keyvalue_moment, keyvalue_square],
    )
    output_new, _ = turned_update(
        meta_core,
        collect(output_piece),
        [w_output, output_moment, output_square],
        (HEADS * HEAD_DIM // 64) ** (-0.5),
        True,
    )

    gain_sums = jnp.stack([gain_one, gain_two])
    blocks = [
        jnp.concatenate(
            [
                gain_sums[:, at * half : (at + 1) * half],
                gain_sums[:, D // 2 + at * half : D // 2 + (at + 1) * half],
            ],
            axis=1,
        )
        for at in range(lines)
    ]
    grad_gains = pick(blocks, line)
    for by in range(1, lines):
        grad_gains = grad_gains + shift(pick(blocks, (line + by) % lines), "col", lines, by)
    for axis, size in (("core", 2), ("y", 2), ("row", rows_on)):
        blocks_total = grad_gains
        for by in range(1, size):
            grad_gains = grad_gains + shift(blocks_total, axis, size, by)

    gains_new = adamw_step(norm_gains, grad_gains, gains_moment, gains_square, 0.6, 0.0)

    def arranged(piece):
        shards = collect(piece)
        at = [
            [pick(shards, jnp.where(y == y_at, 0, 1) + jnp.where(core == c_at, 0, 2)) for y_at in range(2)]
            for c_at in range(2)
        ]
        return jnp.concatenate([jnp.concatenate(row_of, axis=1) for row_of in at], axis=0)

    gateup_grad = jnp.stack([arranged(gate_piece), arranged(up_piece)], axis=1)
    gateup_grad = lax.optimization_barrier(gateup_grad.astype(jnp.float32))
    gateup_new = adamw_step(w_gateup, gateup_grad, gateup_moment, gateup_square, D ** (-0.5), 0.1)
    return (
        layer_output,
        input_grad,
        *gains_new,
        *joint_new,
        *output_new,
        *gateup_new,
        *down_new,
    )


def solution(mesh):
    dp, rows_on, lines = (mesh.shape["dp"], mesh.shape["row"], mesh.shape["col"])
    split = Mesh(mesh.devices.reshape(dp // 2, 2, rows_on, lines), ("y", "core", "row", "col"))
    tokens = P(("y", "core", "row"), "col")
    narrow, wide = (P("col", "row"), P("row", "col"))
    gains, pair, gateup = (P(None, "col"), P("col", None), P("col", None, "row"))
    return jax.shard_map(
        functools.partial(on_device, (rows_on, lines)),
        mesh=split,
        in_specs=(
            tokens,
            tokens,
            P(("y", "core"), None),
            gains,
            narrow,
            pair,
            wide,
            gateup,
            wide,
            gains,
            gains,
            narrow,
            narrow,
            pair,
            pair,
            wide,
            wide,
            gateup,
            gateup,
            wide,
            wide,
        ),
        out_specs=(tokens, tokens)
        + (gains,) * 3
        + (narrow,) * 3
        + (pair,) * 3
        + (wide,) * 3
        + (gateup,) * 3
        + (wide,) * 3,
        check_vma=False,
    )
```

```python
import functools

import jax
import jax.numpy as jnp
from jax import lax
from jax.experimental import pallas as pl
from jax.experimental.pallas import tpu as pltpu
from jax.sharding import Mesh, PartitionSpec as P

D = 2048
HEADS = 32
KV_HEADS = 4
HEAD_DIM = 64
FF = 5632
STEP = 10

EPSILON = 1e-05
BETA_ONE = 0.9
BETA_TWO = 0.999
ADAM_EPS = 1e-08
MASKED = -1e30
SCORE_SCALE = HEAD_DIM ** (-0.5)
LANES = 128
VMEM_LIMIT = 48 * 1024 * 1024


def dot_nn(left, right):
    return lax.dot_general(left, right, (((1,), (0,)), ((), ())), preferred_element_type=jnp.float32)


def dot_nt(left, right):
    return lax.dot_general(left, right, (((1,), (1,)), ((), ())), preferred_element_type=jnp.float32)


def dot_tn(left, right):
    return lax.dot_general(left, right, (((0,), (0,)), ((), ())), preferred_element_type=jnp.float32)


def adamw_step(weight, gradient, moment, square, step_rate, decay_rate):
    moment_new = BETA_ONE * moment + (1.0 - BETA_ONE) * gradient
    square_new = BETA_TWO * square + (1.0 - BETA_TWO) * gradient * gradient
    fixed_one = moment_new / (1.0 - BETA_ONE**STEP)
    fixed_two = square_new / (1.0 - BETA_TWO**STEP)
    weight_new = weight - step_rate * (
        fixed_one / (jnp.sqrt(fixed_two) + ADAM_EPS) + decay_rate * weight
    )
    return (moment_new, square_new, weight_new)


def document_starts(segment_ids):
    places = jnp.arange(segment_ids.shape[0], dtype=jnp.int32)
    starts = jnp.concatenate([jnp.ones((1,), jnp.bool_), segment_ids[1:] != segment_ids[:-1]])
    return lax.cummax(jnp.where(starts, places, 0), axis=0)


def turn(values):
    lane = lax.broadcasted_iota(jnp.int32, values.shape, 1)
    ahead = pltpu.roll(values, LANES - HEAD_DIM // 2, 1)
    behind = pltpu.roll(values, HEAD_DIM // 2, 1)
    return jnp.where(lane % HEAD_DIM < HEAD_DIM // 2, -ahead, behind)


def project_kernel(rows_ref, weight_ref, cos_ref, sin_ref, query_ref, pair_ref):
    sums = dot_nn(rows_ref[...], weight_ref[...])
    cosine, sine = cos_ref[...], sin_ref[...]
    width = query_ref.shape[1]
    lane = lax.broadcasted_iota(jnp.int32, cosine.shape, 1)
    for start in range(0, width, LANES):
        part = sums[:, start : start + LANES]
        turned = (part * cosine + turn(part) * sine).astype(jnp.bfloat16)
        query_ref[:, start : start + LANES] = turned * jnp.bfloat16(SCORE_SCALE)
    for which in range(2):
        part = sums[:, width + which * LANES : width + (which + 1) * LANES]
        is_key = (lane < HEAD_DIM) if which == 0 else (lane >= HEAD_DIM)
        turned = jnp.where(is_key, part * cosine + turn(part) * sine, part)
        pair_ref[:, which * LANES : (which + 1) * LANES] = turned.astype(jnp.bfloat16)


def project(rows, weight, total, cosine, sine, width, block):
    count = rows.shape[0] // block
    return pl.pallas_call(
        project_kernel,
        grid=(count,),
        in_specs=[
            pl.BlockSpec((block, rows.shape[1]), lambda i: (i, 0)),
            pl.BlockSpec((weight.shape[0], total), lambda i: (0, 0)),
            pl.BlockSpec((block, LANES), lambda i: (i, 0)),
            pl.BlockSpec((block, LANES), lambda i: (i, 0)),
        ],
        out_specs=[
            pl.BlockSpec((block, width), lambda i: (i, 0)),
            pl.BlockSpec((block, total - width), lambda i: (i, 0)),
        ],
        out_shape=[
            jax.ShapeDtypeStruct((rows.shape[0], width), jnp.bfloat16),
            jax.ShapeDtypeStruct((rows.shape[0], total - width), jnp.bfloat16),
        ],
        compiler_params=pltpu.CompilerParams(vmem_limit_bytes=VMEM_LIMIT),
        cost_estimate=pl.CostEstimate(
            flops=2 * rows.shape[0] * rows.shape[1] * total,
            bytes_accessed=rows.size * 2 + weight.shape[0] * total * 2,
            transcendentals=0,
        ),
        name="project",
    )(rows, weight, cosine, sine)


def stack_heads(values):
    return jnp.concatenate(
        [values[:, start : start + LANES] for start in range(0, values.shape[1], LANES)], axis=0
    )


def block_of(meta_ref, chunk, step, parts, lines):
    base = chunk * (2 + parts)
    key_block = meta_ref[base + 1] - step
    slot = meta_ref[base + 2 + key_block // lines]
    own_line = meta_ref[pl.num_programs(0) * (2 + parts)]
    line = lax.rem(key_block, lines)
    return (key_block, slot, line, lax.rem(own_line - line + lines, lines))


def attend_kernel(parts, lines, meta_ref, query_ref, pair_ref, info_ref, out_ref, log_ref):
    chunk = pl.program_id(0)
    block = query_ref.shape[0]
    heads = query_ref.shape[1] // LANES
    stacked = stack_heads(query_ref[...])
    lane = lax.broadcasted_iota(jnp.int32, stacked.shape, 1)
    place = jnp.concatenate([info_ref[0, 0:1, :]] * heads, axis=1)
    start = jnp.concatenate([info_ref[0, 1:2, :]] * heads, axis=1)
    base = chunk * (2 + parts)
    steps = meta_ref[base + 1] - meta_ref[base] + 1
    width = heads * block
    outs = []
    for which in range(2):
        is_key = (lane < HEAD_DIM) if which == 0 else (lane >= HEAD_DIM)
        queries = jnp.where(is_key, stacked, jnp.zeros_like(stacked))

        def body(step, carry):
            peak, total, mixed = carry
            key_block, slot, at, _ = block_of(meta_ref, chunk, step, parts, lines)
            pair = pair_ref[at, slot, :, which * LANES : (which + 1) * LANES]
            scores = dot_nt(pair, queries)
            key_place = key_block * block + lax.broadcasted_iota(jnp.int32, (block, width), 0)
            scores = jnp.where((key_place <= place) & (key_place >= start), scores, MASKED)
            new_peak = jnp.maximum(peak, jnp.max(scores, axis=0, keepdims=True))
            weights = jnp.exp(scores - new_peak)
            shrink = jnp.exp(peak - new_peak)
            total = total * shrink + jnp.sum(weights, axis=0, keepdims=True)
            mixed = mixed * shrink + dot_tn(pair, weights.astype(jnp.bfloat16))
            return (new_peak, total, mixed)

        peak, total, mixed = lax.fori_loop(
            0,
            steps,
            body,
            (
                jnp.full((1, width), MASKED, jnp.float32),
                jnp.zeros((1, width), jnp.float32),
                jnp.zeros((LANES, width), jnp.float32),
            ),
        )
        log_ref[0, which : which + 1, :] = peak + jnp.log(total)
        outs.append(mixed / total)
    joined = jnp.concatenate([outs[1][:HEAD_DIM], outs[0][HEAD_DIM:]], axis=0)
    rows = joined.T.astype(jnp.bfloat16)
    for head in range(heads):
        out_ref[:, head * LANES : (head + 1) * LANES] = rows[head * block : (head + 1) * block]


def attend(meta, queries, pairs, info, parts):
    chunks, block = (info.shape[0], info.shape[2])
    width = queries.shape[1]
    heads = width // LANES
    lines = pairs.shape[0]
    steps = 3 * chunks
    return pl.pallas_call(
        functools.partial(attend_kernel, parts, lines),
        grid_spec=pltpu.PrefetchScalarGridSpec(
            num_scalar_prefetch=1,
            grid=(chunks,),
            in_specs=[
                pl.BlockSpec((block, width), lambda i, m: (i, 0)),
                pl.BlockSpec(pairs.shape, lambda i, m: (0, 0, 0, 0)),
                pl.BlockSpec((1, 2, block), lambda i, m: (i, 0, 0)),
            ],
            out_specs=[
                pl.BlockSpec((block, width), lambda i, m: (i, 0)),
                pl.BlockSpec((1, 2, heads * block), lambda i, m: (i, 0, 0)),
            ],
        ),
        out_shape=[
            jax.ShapeDtypeStruct(queries.shape, jnp.bfloat16),
            jax.ShapeDtypeStruct((chunks, 2, heads * block), jnp.float32),
        ],
        compiler_params=pltpu.CompilerParams(vmem_limit_bytes=VMEM_LIMIT),
        cost_estimate=pl.CostEstimate(
            flops=steps * 2 * 2 * 2 * heads * block * block * LANES,
            bytes_accessed=queries.size * 4 + pairs.size * 2,
            transcendentals=steps * 2 * heads * block * block,
        ),
        name="attend",
    )(meta, queries, pairs, info)


def attend_back_kernel(parts, lines, meta_ref, query_ref, *refs):
    pair_ref, grad_ref, mixed_ref, log_ref, info_ref, cos_ref, sin_ref, query_out = refs[:8]
    pair_outs = refs[8 : 8 + lines]
    sums = refs[8 + lines]
    chunk = pl.program_id(0)
    block = query_ref.shape[0]
    heads = query_ref.shape[1] // LANES

    @pl.when(chunk == 0)
    def _():
        sums[...] = jnp.zeros_like(sums)

    stacked = stack_heads(query_ref[...])
    stacked_grad = stack_heads(grad_ref[...])
    product = stacked_grad.astype(jnp.float32) * stack_heads(mixed_ref[...]).astype(jnp.float32)
    lane = lax.broadcasted_iota(jnp.int32, stacked.shape, 1)
    place = jnp.concatenate([info_ref[0, 0:1, :]] * heads, axis=1)
    start = jnp.concatenate([info_ref[0, 1:2, :]] * heads, axis=1)
    base = chunk * (2 + parts)
    steps = meta_ref[base + 1] - meta_ref[base] + 1
    width = heads * block
    grads = []
    for which in range(2):
        is_key = (lane < HEAD_DIM) if which == 0 else (lane >= HEAD_DIM)
        queries = jnp.where(is_key, stacked, jnp.zeros_like(stacked))
        grad = jnp.where(is_key, jnp.zeros_like(stacked_grad), stacked_grad)
        own = jnp.where(is_key, 0.0, product)
        centre = lax.dot_general(
            jnp.ones((8, LANES), jnp.float32),
            own,
            (((1,), (1,)), ((), ())),
            precision=lax.Precision.HIGHEST,
            preferred_element_type=jnp.float32,
        )[0:1]
        logs = log_ref[0, which : which + 1, :]

        def body(step, grad_query):
            key_block, slot, at, shift = block_of(meta_ref, chunk, step, parts, lines)
            columns = slice(which * LANES, (which + 1) * LANES)
            pair = pair_ref[at, slot, :, columns]
            scores = dot_nt(pair, queries)
            key_place = key_block * block + lax.broadcasted_iota(jnp.int32, (block, width), 0)
            scores = jnp.where((key_place <= place) & (key_place >= start), scores, MASKED)
            weights = jnp.exp(scores - logs)
            grad_scores = (weights * (dot_nt(pair, grad) - centre)).astype(jnp.bfloat16)
            sums[shift, slot, :, columns] += dot_nn(grad_scores, queries) + dot_nn(
                weights.astype(jnp.bfloat16), grad
            )
            return grad_query + dot_tn(pair, grad_scores)

        grads.append(lax.fori_loop(0, steps, body, jnp.zeros((LANES, width), jnp.float32)))
    joined = jnp.concatenate([grads[0][:HEAD_DIM], grads[1][HEAD_DIM:]], axis=0)
    rows = joined.T * SCORE_SCALE
    cosine, sine = cos_ref[...], sin_ref[...]
    for head in range(heads):
        part = rows[head * block : (head + 1) * block]
        back = part * cosine - turn(part) * sine
        query_out[:, head * LANES : (head + 1) * LANES] = back.astype(jnp.bfloat16)

    @pl.when(chunk == pl.num_programs(0) - 1)
    def _():
        for line in range(lines):
            pair_outs[line][...] = sums[line].astype(jnp.bfloat16)


def attend_back(meta, queries, pairs, grad_mixed, mixed, logs, info, cosine, sine, parts):
    chunks, block = (info.shape[0], info.shape[2])
    width = queries.shape[1]
    heads = width // LANES
    lines = pairs.shape[0]
    shape = pairs.shape[1:]
    steps = 3 * chunks
    wide = pl.BlockSpec((block, width), lambda i, m: (i, 0))
    table = pl.BlockSpec((block, LANES), lambda i, m: (i, 0))
    whole = pl.BlockSpec(shape, lambda i, m: (0, 0, 0))
    outs = pl.pallas_call(
        functools.partial(attend_back_kernel, parts, lines),
        grid_spec=pltpu.PrefetchScalarGridSpec(
            num_scalar_prefetch=1,
            grid=(chunks,),
            in_specs=[
                wide,
                pl.BlockSpec(pairs.shape, lambda i, m: (0, 0, 0, 0)),
                wide,
                wide,
                pl.BlockSpec((1, 2, heads * block), lambda i, m: (i, 0, 0)),
                pl.BlockSpec((1, 2, block), lambda i, m: (i, 0, 0)),
                table,
                table,
            ],
            out_specs=[wide] + [whole] * lines,
            scratch_shapes=[pltpu.VMEM(pairs.shape, jnp.float32)],
        ),
        out_shape=[jax.ShapeDtypeStruct(queries.shape, jnp.bfloat16)]
        + [jax.ShapeDtypeStruct(shape, jnp.bfloat16)] * lines,
        compiler_params=pltpu.CompilerParams(vmem_limit_bytes=VMEM_LIMIT),
        cost_estimate=pl.CostEstimate(
            flops=steps * 2 * 5 * 2 * heads * block * block * LANES,
            bytes_accessed=queries.size * 8 + 2 * pairs.size * 2,
            transcendentals=steps * 2 * heads * block * block,
        ),
        name="attend_back",
    )(
        meta,
        queries,
        pairs,
        grad_mixed,
        mixed,
        logs,
        info,
        cosine,
        sine,
    )
    return (outs[0], [out.reshape(chunks * block, 2 * LANES) for out in outs[1:]])


def pair_back_kernel(*refs):
    *part_refs, cos_ref, sin_ref, out_ref = refs
    cosine, sine = cos_ref[...], sin_ref[...]
    lane = lax.broadcasted_iota(jnp.int32, cosine.shape, 1)
    for which in range(2):
        columns = slice(which * LANES, (which + 1) * LANES)
        total = part_refs[0][:, columns].astype(jnp.float32)
        for ref in part_refs[1:]:
            total = total + ref[:, columns].astype(jnp.float32)
        is_key = (lane < HEAD_DIM) if which == 0 else (lane >= HEAD_DIM)
        total = jnp.where(is_key, total * cosine - turn(total) * sine, total)
        out_ref[:, columns] = total.astype(jnp.bfloat16)


def pair_back(parts, cosine, sine, block):
    rows, columns = parts[0].shape
    tile = pl.BlockSpec((block, columns), lambda i: (i, 0))
    table = pl.BlockSpec((block, LANES), lambda i: (i, 0))
    return pl.pallas_call(
        pair_back_kernel,
        grid=(rows // block,),
        in_specs=[tile] * len(parts) + [table, table],
        out_specs=tile,
        out_shape=jax.ShapeDtypeStruct((rows, columns), jnp.bfloat16),
        compiler_params=pltpu.CompilerParams(vmem_limit_bytes=VMEM_LIMIT),
        name="pair_back",
    )(*parts, cosine, sine)


def update(refs, index, gradient, rate):
    weight, moment, square = [ref[index] for ref in refs[:3]]
    moment_new, square_new, weight_new = adamw_step(weight, gradient, moment, square, rate, 0.1)
    for ref, value in zip(refs[3:], (moment_new, square_new, weight_new)):
        ref[index] = value


def chosen(meta_ref, grad_refs, at, rows, columns):
    own_y = meta_ref[0] == at
    first = pl.program_id(0) == 0
    near = jnp.where(first, grad_refs[0][rows, columns], grad_refs[2][rows, columns])
    far = jnp.where(first, grad_refs[1][rows, columns], grad_refs[3][rows, columns])
    return jnp.where(own_y, near, far).astype(jnp.float32)


def joint_update_kernel(meta_ref, *refs):
    grad_refs, query_refs, pair_refs = (refs[:4], refs[4:7] + refs[10:13], refs[7:10] + refs[13:16])
    groups = query_refs[0].shape[1] // (2 * LANES)
    every = slice(None)
    for at in range(2):
        for j in range(groups):
            gradient = chosen(meta_ref, grad_refs, at, every, slice(j * LANES, (j + 1) * LANES))
            place = slice((2 * j + at) * LANES, (2 * j + at + 1) * LANES)
            update(query_refs, (every, place), gradient, D ** (-0.5))
        for which in range(2):
            start = (groups + which) * LANES
            gradient = chosen(meta_ref, grad_refs, at, every, slice(start, start + LANES))
            if which == 1:
                gradient = pltpu.roll(gradient, HEAD_DIM, 1)
            place = slice((2 * at + which) * LANES, (2 * at + which + 1) * LANES)
            update(pair_refs, (every, place), gradient, D ** (-0.5))


def joint_update(meta, grads, query, pair):
    half = grads[0].shape[0]

    def rows_of(array):
        return pl.BlockSpec((half, array.shape[1]), lambda i, m: ((m[1] + i) % 2, 0))

    whole = pl.BlockSpec(grads[0].shape, lambda i, m: (0, 0))
    blocks = [rows_of(array) for array in (*query, *pair)]
    return pl.pallas_call(
        joint_update_kernel,
        grid_spec=pltpu.PrefetchScalarGridSpec(
            num_scalar_prefetch=1, grid=(2,), in_specs=[whole] * 4 + blocks, out_specs=blocks
        ),
        out_shape=[jax.ShapeDtypeStruct(array.shape, array.dtype) for array in (*query, *pair)],
        compiler_params=pltpu.CompilerParams(vmem_limit_bytes=VMEM_LIMIT),
        cost_estimate=pl.CostEstimate(
            flops=20 * (query[0].size + pair[0].size),
            bytes_accessed=24 * (query[0].size + pair[0].size),
            transcendentals=0,
        ),
        name="joint_update",
    )(meta, *grads, *query, *pair)


def turned_update_kernel(rate, swapped, meta_ref, *refs):
    grad_refs, weight_refs, token_ref = (refs[:4], refs[4:10], refs[10])
    at = pl.program_id(1)
    width = grad_refs[0].shape[1]
    every = slice(None)
    for j, start in enumerate(range(0, width, LANES)):
        strip = slice(start, min(start + LANES, width))
        gradient = chosen(meta_ref, grad_refs, at, every, strip).T
        if swapped:
            gradient = jnp.concatenate([gradient[HEAD_DIM:], gradient[:HEAD_DIM]], axis=0)
            index = (j, 0)
        else:
            index = (strip, every)
        update(weight_refs, index, gradient, rate)
    token_ref[...] = jnp.zeros_like(token_ref)


def turned_update(meta, grads, weights, rate, swapped):
    half, width = grads[0].shape
    shape = weights[0].shape
    if swapped:
        weights = [w.reshape(width // LANES, 2, LANES, shape[1]) for w in weights]
        block = pl.BlockSpec(
            (width // LANES, 1, LANES, half), lambda i, at, m: (0, at, 0, (m[1] + i) % 2)
        )
    else:
        block = pl.BlockSpec((width, half), lambda i, at, m: (at, (m[1] + i) % 2))
    outs = pl.pallas_call(
        functools.partial(turned_update_kernel, rate, swapped),
        grid_spec=pltpu.PrefetchScalarGridSpec(
            num_scalar_prefetch=1,
            grid=(2, 2),
            in_specs=[pl.BlockSpec(grads[0].shape, lambda i, at, m: (0, 0))] * 4 + [block] * 3,
            out_specs=[block] * 3 + [pl.BlockSpec((8, LANES), lambda i, at, m: (0, 0))],
        ),
        out_shape=[jax.ShapeDtypeStruct(weights[0].shape, jnp.float32)] * 3
        + [jax.ShapeDtypeStruct((8, LANES), jnp.float32)],
        compiler_params=pltpu.CompilerParams(vmem_limit_bytes=VMEM_LIMIT),
        cost_estimate=pl.CostEstimate(
            flops=20 * weights[0].size, bytes_accessed=24 * weights[0].size, transcendentals=0
        ),
        name="turned_update",
    )(meta, *grads, *weights)
    return ([out.reshape(shape) for out in outs[:3]], outs[3])


def gateup_update_kernel(meta_ref, *refs):
    gate_refs, up_refs, weight_refs, token_ref = (refs[:4], refs[4:8], refs[8:14], refs[14])
    every = slice(None)
    gate, up = [
        jnp.concatenate([chosen(meta_ref, grads, at, every, every) for at in range(2)], axis=1)
        for grads in (gate_refs, up_refs)
    ]
    update(weight_refs, every, jnp.stack([gate, up], axis=1), D ** (-0.5))
    token_ref[...] = jnp.zeros_like(token_ref)


def gateup_update(meta, gates, ups, weights, rows):
    half, width = gates[0].shape
    shape = weights[0].shape
    tiles = half // rows
    grad = pl.BlockSpec((rows, width), lambda i, j, m: (j, 0))
    block = pl.BlockSpec(
        (rows, 2, shape[2]), lambda i, j, m: (((m[1] + i) % 2) * tiles + j, 0, 0)
    )
    outs = pl.pallas_call(
        gateup_update_kernel,
        grid_spec=pltpu.PrefetchScalarGridSpec(
            num_scalar_prefetch=1,
            grid=(2, tiles),
            in_specs=[grad] * 8 + [block] * 3,
            out_specs=[block] * 3 + [pl.BlockSpec((8, LANES), lambda i, j, m: (0, 0))],
        ),
        out_shape=[jax.ShapeDtypeStruct(shape, jnp.float32)] * 3
        + [jax.ShapeDtypeStruct((8, LANES), jnp.float32)],
        compiler_params=pltpu.CompilerParams(vmem_limit_bytes=VMEM_LIMIT),
        cost_estimate=pl.CostEstimate(
            flops=20 * weights[0].size, bytes_accessed=28 * weights[0].size, transcendentals=0
        ),
        name="gateup_update",
    )(meta, *gates, *ups, *weights)
    return (outs[:3], outs[3])


def on_device(
    sizes,
    block_input,
    cotangent,
    segments,
    norm_gains,
    w_query,
    w_keyvalue,
    w_output,
    w_gateup,
    w_down,
    gains_moment,
    gains_square,
    query_moment,
    query_square,
    keyvalue_moment,
    keyvalue_square,
    output_moment,
    output_square,
    gateup_moment,
    gateup_square,
    down_moment,
    down_square,
):
    rows_on, lines = sizes
    y, core, row, line = [lax.axis_index(name) for name in ("y", "core", "row", "col")]
    length = segments.shape[1]
    block = block_input.shape[0] // lines
    wide = block_input.shape[1]
    half = wide // 2
    slots = 2 * rows_on
    per_row = w_query.shape[1] // (KV_HEADS * HEAD_DIM)
    query_width = per_row * LANES
    hidden_here = w_gateup.shape[2] // 2

    def shift(value, axis, size, by):
        return lax.ppermute(value, axis, [(i, (i + by) % size) for i in range(size)])

    def other_core(value):
        return lax.ppermute(value, "core", [(0, 1), (1, 0)])

    def other_y(value):
        return lax.ppermute(value, "y", [(0, 1), (1, 0)])

    def place_of(y_at, core_at, row_at):
        return (y_at * 2 + core_at) * rows_on + row_at

    first_pairs, second_pairs = ([], [])
    for y_at in range(2):
        for core_at in range(2):
            for row_at in range(rows_on):
                over_row = (
                    place_of(y_at, core_at, row_at),
                    place_of(y_at, core_at, (row_at + 1) % rows_on),
                )
                over_y = (place_of(y_at, core_at, row_at), place_of(1 - y_at, core_at, row_at))
                first_pairs.append(over_row if core_at == 0 else over_y)
                second_pairs.append(over_y if core_at == 0 else over_row)
    near = ("y", "core", "row")

    def gather_tokens(own):
        if rows_on == 2:
            first = lax.ppermute(own, near, first_pairs)
            second = lax.ppermute(own, near, second_pairs)
            third = lax.ppermute(first, near, second_pairs)
            return [own, first, second, third]
        parts = [own] + [shift(own, "row", rows_on, by) for by in range(1, rows_on)]
        return parts + [other_y(part) for part in parts]

    def reduce_tokens(terms, after_close=None, after_first=None, before_last=None):
        def rows_of(first, last):
            total = 0.0
            for left, right in terms:
                total = total + dot_nt(left[first * block : last * block], right)
            return total.astype(jnp.bfloat16)

        if rows_on == 2:
            far = rows_of(2, 4)
            third = lax.ppermute(far[block:], near, second_pairs)
            second = lax.ppermute(far[:block], near, second_pairs)
            close = rows_of(0, 2)
            early = after_close(close) if after_close else None
            key = (close[block:].astype(jnp.float32) + third.astype(jnp.float32)).astype(jnp.bfloat16)
            first = lax.ppermute(key, near, first_pairs)
            late = after_first(key, early) if after_first else None
            needed = before_last(early, late) if before_last else []
            first = lax.optimization_barrier((first, *needed))[0]
            own = close[:block].astype(jnp.float32) + second.astype(jnp.float32)
            return (own + first.astype(jnp.float32), early, late, key)
        partial = rows_of(0, slots)
        early = after_close(partial) if after_close else None
        parts = [partial[i * block : (i + 1) * block] for i in range(slots)]
        sums = [
            parts[i].astype(jnp.float32) + other_y(parts[rows_on + i]).astype(jnp.float32)
            for i in range(rows_on)
        ]
        key = sums[0]
        late = after_first(key, early) if after_first else None
        total = sums[0]
        for by in range(1, rows_on):
            moved = shift(sums[by].astype(jnp.bfloat16), "row", rows_on, -by)
            total = total + moved.astype(jnp.float32)
        return (total, early, late, key)

    def tied(key, *values):
        return lax.optimization_barrier((key, *values))[1:]

    if rows_on == 2:
        slot_y = [y, jnp.where(core == 0, y, 1 - y), jnp.where(core == 0, 1 - y, y), 1 - y]
        slot_row = [row, jnp.where(core == 0, 1 - row, row), jnp.where(core == 0, row, 1 - row), 1 - row]
    else:
        slot_y = [y] * rows_on + [1 - y] * rows_on
        slot_row = [(row - by) % rows_on for by in range(rows_on)] * 2

    def pick(parts, index):
        return lax.dynamic_index_in_dim(jnp.stack(parts), index, 0, keepdims=False)

    def tokens_sent(values):
        parts = []
        for by in range(lines):
            part = lax.dynamic_slice_in_dim(values, ((line + by) % lines) * block, block, 0)
            parts.append(part if by == 0 else shift(part, "col", lines, by))
        return parts

    def tokens_of(parts):
        blocks = [pick(parts, (line - at) % lines) for at in range(lines)]
        return jnp.concatenate([b[:, :half] for b in blocks] + [b[:, half:] for b in blocks], axis=1)

    def features_from_tokens(values):
        blocks = [
            jnp.concatenate(
                [
                    values[:, at * half : (at + 1) * half],
                    values[:, D // 2 + at * half : D // 2 + (at + 1) * half],
                ],
                axis=1,
            )
            for at in range(lines)
        ]
        parts = []
        for by in range(lines):
            part = pick(blocks, (line + by) % lines)
            parts.append(part if by == 0 else shift(part, "col", lines, by))
        return jnp.concatenate([pick(parts, (line - at) % lines) for at in range(lines)], axis=0)

    def half_rows(values):
        return lax.dynamic_slice_in_dim(values, core * half, half, 0)

    def half_columns(values):
        return lax.dynamic_slice_in_dim(values, core * half, half, 1)

    def gather_weight(piece):
        return lax.all_gather(piece, ("core", "col"), axis=0, tiled=True)

    query_rows = half_rows(w_query).astype(jnp.bfloat16)
    pair_rows = half_rows(w_keyvalue).astype(jnp.bfloat16)

    def joint_of(at):
        pieces = [
            query_rows[:, (2 * j + at) * LANES : (2 * j + at + 1) * LANES] for j in range(per_row)
        ]
        pair = pair_rows[:, at * 2 * LANES : (at + 1) * 2 * LANES]
        pieces += [
            pair[:, :LANES],
            pair[:, LANES + HEAD_DIM :],
            pair[:, LANES : LANES + HEAD_DIM],
        ]
        return jnp.concatenate(pieces, axis=1)

    joint_mine = jnp.where(y == 0, joint_of(0), joint_of(1))
    output_columns = half_columns(w_output).astype(jnp.bfloat16)

    def output_of(at):
        pieces = []
        for j in range(per_row):
            base = (2 * j + at) * LANES
            pieces += [
                output_columns[base + HEAD_DIM : base + LANES],
                output_columns[base : base + HEAD_DIM],
            ]
        return jnp.concatenate(pieces, axis=0)

    output_mine = jnp.where(y == 0, output_of(0), output_of(1)).T
    gateup_mine = lax.dynamic_slice(
        w_gateup, (core * half, 0, y * hidden_here), (half, 2, hidden_here)
    ).astype(jnp.bfloat16)
    gateup_mine = jnp.concatenate([gateup_mine[:, 0], gateup_mine[:, 1]], axis=1)
    down_mine = lax.dynamic_slice(
        w_down, (y * hidden_here, core * half), (hidden_here, half)
    ).astype(jnp.bfloat16).T

    gain_parts = [norm_gains] + [shift(norm_gains, "col", lines, by) for by in range(1, lines)]
    gain_blocks = [pick(gain_parts, (line - at) % lines) for at in range(lines)]
    gains = jnp.concatenate(
        [b[:, :half] for b in gain_blocks] + [b[:, half:] for b in gain_blocks], axis=1
    )

    own_starts = document_starts(segments[0])
    other_starts = document_starts(other_y(segments)[0])
    frequency = 10000.0 ** (-2.0 * jnp.arange(HEAD_DIM // 2, dtype=jnp.float32) / HEAD_DIM)
    starts, places, meta = ([], [], [])
    for slot in range(slots):
        begin = slot_row[slot] * (lines * block) + line * block
        of_chunk = lax.dynamic_slice_in_dim(
            jnp.where(slot_y[slot] == y, own_starts, other_starts), begin, block, 0
        )
        starts.append(of_chunk)
        places.append(begin + jnp.arange(block, dtype=jnp.int32))
        meta += [of_chunk[0] // block, begin // block]
        for row_at in range(rows_on):
            found = jnp.int32(0)
            for other in range(slots):
                same = (slot_y[other] == slot_y[slot]) & (slot_row[other] == row_at)
                found = found + jnp.where(same, other, 0)
            meta.append(found)
    meta = jnp.stack([jnp.asarray(m, jnp.int32) for m in meta + [line]])
    starts, places = (jnp.stack(starts), jnp.stack(places))
    info = jnp.stack([places, starts], axis=1)
    offsets = (places - starts).astype(jnp.float32).reshape(-1)
    phases = offsets[:, None] * jnp.tile(frequency, LANES // (HEAD_DIM // 2))[None, :]
    cosine, sine = (jnp.cos(phases), jnp.sin(phases))

    residual_low = tokens_of(tokens_sent(block_input))
    residual_low, joint_mine, output_mine = lax.optimization_barrier(
        (residual_low, joint_mine, output_mine)
    )
    first_weight = gather_weight(jnp.concatenate([joint_mine, output_mine], axis=1))
    joint_width = joint_mine.shape[1]
    joint_weight, output_weight = (first_weight[:, :joint_width], first_weight[:, joint_width:])
    residual = residual_low.astype(jnp.float32)
    scale_one = lax.rsqrt(jnp.mean(residual * residual, axis=1, keepdims=True) + EPSILON)
    normed_parts = gather_tokens((residual * scale_one * gains[0]).astype(jnp.bfloat16))
    queries, pair = zip(
        *[
            project(
                part,
                first_weight,
                joint_width,
                cosine[i * block : (i + 1) * block],
                sine[i * block : (i + 1) * block],
                query_width,
                block,
            )
            for i, part in enumerate(normed_parts)
        ]
    )
    queries = jnp.concatenate(queries, axis=0)
    pairs = lax.all_gather(jnp.stack(pair), "col", axis=0, tiled=False)
    pairs, gateup_mine, down_mine = lax.optimization_barrier((pairs, gateup_mine, down_mine))
    gateup_weight = gather_weight(gateup_mine)
    down_weight = gather_weight(down_mine)
    mixed, logs = attend(meta, queries, pairs, info, rows_on)
    attn_sum, _, _, _ = reduce_tokens([(mixed, output_weight)])
    (late_cotangent,) = tied(attn_sum, cotangent)
    cot_parts = tokens_sent(late_cotangent)
    middle = residual + attn_sum
    scale_two = lax.rsqrt(jnp.mean(middle * middle, axis=1, keepdims=True) + EPSILON)
    normed_two = gather_tokens((middle * scale_two * gains[1]).astype(jnp.bfloat16))
    cot_low = tokens_of(tied(normed_two[-1], *cot_parts))
    normed_two = jnp.concatenate(normed_two, axis=0)
    cot = jnp.concatenate(gather_tokens(cot_low), axis=0)
    pair_sum = dot_nn(normed_two, gateup_weight)
    gate_sum, upward = (pair_sum[:, :hidden_here], pair_sum[:, hidden_here:])
    sigmoid_gate = jax.nn.sigmoid(gate_sum)
    silu_gate = gate_sum * sigmoid_gate
    hidden = (silu_gate * upward).astype(jnp.bfloat16)

    grad_hidden = dot_nn(cot, down_weight)
    grad_gate = grad_hidden * upward * sigmoid_gate * (1.0 + gate_sum * (1.0 - sigmoid_gate))
    grad_gate = grad_gate.astype(jnp.bfloat16)
    grad_up = (grad_hidden * silu_gate).astype(jnp.bfloat16)

    def other_half(rows, grad):
        rows = lax.dynamic_slice_in_dim(rows, (1 - core) * (D // 2), D // 2, 1)
        return dot_tn(rows, grad).astype(jnp.bfloat16)

    def own_half(rows, grad, received):
        rows = lax.dynamic_slice_in_dim(rows, core * (D // 2), D // 2, 1)
        total = dot_tn(rows, grad) + received.astype(jnp.float32)
        return total.astype(jnp.bfloat16)

    def scatter(total):
        return lax.psum_scatter(total, "col", scatter_dimension=0, tiled=True)

    def collect(piece):
        near_y = other_y(piece)
        return [piece, near_y, other_core(piece), other_core(near_y)]

    def others(key, rows, *grads):
        rows, *grads = tied(key, rows, *grads)
        return [other_core(other_half(rows, grad)) for grad in grads]

    def owns(key, rows, grads, received):
        rows, *values = tied(key, rows, *grads, *received)
        count = len(grads)
        return [own_half(rows, g, r) for g, r in zip(values[:count], values[count:])]

    grad_normed_two, _, (gate_total, up_total), _ = reduce_tokens(
        [
            (grad_gate, gateup_weight[:, :hidden_here]),
            (grad_up, gateup_weight[:, hidden_here:]),
        ],
        lambda close: others(close, normed_two, grad_gate, grad_up),
        lambda key, early: owns(key, normed_two, (grad_gate, grad_up), early),
        lambda early, late: late,
    )
    gate_piece, up_piece = (scatter(gate_total), scatter(up_total))

    def norm_back(values, scale, grad_normed, gain):
        scaled = grad_normed * gain
        total = jnp.sum(scaled * values, axis=1, keepdims=True)
        return scale * scaled - values * (scale**3 * total / D)

    grad_middle = cot_low.astype(jnp.float32) + norm_back(
        middle, scale_two, grad_normed_two, gains[1]
    )
    gain_two = jnp.sum(grad_normed_two * middle * scale_two, axis=0)

    grad_middle_low = grad_middle.astype(jnp.bfloat16)
    back = jnp.concatenate(gather_tokens(grad_middle_low), axis=0)
    grad_mixed = dot_nn(back, output_weight).astype(jnp.bfloat16)
    grad_query, grad_parts = attend_back(
        meta, queries, pairs, grad_mixed, mixed, logs, info, cosine, sine, rows_on
    )
    grad_parts = [grad_parts[0]] + [
        shift(grad_parts[by], "col", lines, -by) for by in range(1, lines)
    ]
    (late_hidden,) = tied(grad_query, hidden)
    ffn_sum, _, _, ffn_key = reduce_tokens([(late_hidden, down_weight)])
    down_other = others(grad_query, cot, hidden)
    output_other = others(grad_query, back, mixed)
    down_total = own_half(cot, hidden, *down_other)
    output_total = own_half(back, mixed, *output_other)
    *grad_parts, down_total, output_total, _ = lax.optimization_barrier(
        (*grad_parts, down_total, output_total, ffn_key)
    )
    down_piece, output_piece = (scatter(down_total), scatter(output_total))
    meta_core = jnp.stack([y, core]).astype(jnp.int32)
    gateup_new, gateup_done = gateup_update(
        meta_core,
        collect(gate_piece),
        collect(up_piece),
        [w_gateup, gateup_moment, gateup_square],
        32,
    )
    grad_keyvalue = pair_back(grad_parts, cosine, sine, block)
    grad_joint = jnp.concatenate([grad_query, grad_keyvalue], axis=1)
    normed_one = jnp.concatenate(normed_parts, axis=0)

    grad_normed_one, _, (joint_total,), _ = reduce_tokens(
        [(grad_joint, joint_weight)],
        lambda close: others(close, normed_one, grad_joint),
        lambda key, early: owns(key, normed_one, (grad_joint,), early),
        lambda early, late: [*late, gateup_done],
    )
    joint_piece = scatter(joint_total)
    layer_output = features_from_tokens((middle + ffn_sum).astype(jnp.bfloat16))
    input_grad = grad_middle + norm_back(residual, scale_one, grad_normed_one, gains[0])
    gain_one = jnp.sum(grad_normed_one * residual * scale_one, axis=0)
    input_grad, layer_output = lax.optimization_barrier(
        (input_grad.astype(jnp.bfloat16), layer_output)
    )
    input_grad = features_from_tokens(input_grad).astype(jnp.float32)
    pair_piece = joint_piece[:, query_width:]
    pair_total = pair_piece.astype(jnp.float32)
    for by in range(1, rows_on):
        pair_total = pair_total + shift(pair_piece, "row", rows_on, by).astype(jnp.float32)
    joint_piece = jnp.concatenate(
        [joint_piece[:, :query_width], pair_total.astype(jnp.bfloat16)], axis=1
    )
    down_new, _ = turned_update(
        meta_core, collect(down_piece), [w_down, down_moment, down_square], FF ** (-0.5), False
    )
    joint_new = joint_update(
        meta_core,
        collect(joint_piece),
        [w_query, query_moment, query_square],
        [w_keyvalue, keyvalue_moment, keyvalue_square],
    )
    output_new, _ = turned_update(
        meta_core,
        collect(output_piece),
        [w_output, output_moment, output_square],
        (HEADS * HEAD_DIM // 64) ** (-0.5),
        True,
    )

    gain_sums = jnp.stack([gain_one, gain_two])
    blocks = [
        jnp.concatenate(
            [
                gain_sums[:, at * half : (at + 1) * half],
                gain_sums[:, D // 2 + at * half : D // 2 + (at + 1) * half],
            ],
            axis=1,
        )
        for at in range(lines)
    ]
    grad_gains = pick(blocks, line)
    for by in range(1, lines):
        grad_gains = grad_gains + shift(pick(blocks, (line + by) % lines), "col", lines, by)
    for axis, size in (("core", 2), ("y", 2), ("row", rows_on)):
        blocks_total = grad_gains
        for by in range(1, size):
            grad_gains = grad_gains + shift(blocks_total, axis, size, by)

    gains_new = adamw_step(norm_gains, grad_gains, gains_moment, gains_square, 0.6, 0.0)
    return (
        layer_output,
        input_grad,
        *gains_new,
        *joint_new,
        *output_new,
        *gateup_new,
        *down_new,
    )


def solution(mesh):
    dp, rows_on, lines = (mesh.shape["dp"], mesh.shape["row"], mesh.shape["col"])
    split = Mesh(mesh.devices.reshape(dp // 2, 2, rows_on, lines), ("y", "core", "row", "col"))
    tokens = P(("y", "core", "row"), "col")
    narrow, wide = (P("col", "row"), P("row", "col"))
    gains, pair, gateup = (P(None, "col"), P("col", None), P("col", None, "row"))
    return jax.shard_map(
        functools.partial(on_device, (rows_on, lines)),
        mesh=split,
        in_specs=(
            tokens,
            tokens,
            P(("y", "core"), None),
            gains,
            narrow,
            pair,
            wide,
            gateup,
            wide,
            gains,
            gains,
            narrow,
            narrow,
            pair,
            pair,
            wide,
            wide,
            gateup,
            gateup,
            wide,
            wide,
        ),
        out_specs=(tokens, tokens)
        + (gains,) * 3
        + (narrow,) * 3
        + (pair,) * 3
        + (wide,) * 3
        + (gateup,) * 3
        + (wide,) * 3,
        check_vma=False,
    )
```

```python
import functools

import jax
import jax.numpy as jnp
from jax import lax
from jax.experimental import pallas as pl
from jax.experimental.pallas import tpu as pltpu
from jax.sharding import Mesh, PartitionSpec as P

D = 2048
HEADS = 32
KV_HEADS = 4
HEAD_DIM = 64
FF = 5632
STEP = 10

EPSILON = 1e-05
BETA_ONE = 0.9
BETA_TWO = 0.999
ADAM_EPS = 1e-08
MASKED = -1e30
SCORE_SCALE = HEAD_DIM ** (-0.5)
LANES = 128
VMEM_LIMIT = 48 * 1024 * 1024


def dot_nn(left, right):
    return lax.dot_general(left, right, (((1,), (0,)), ((), ())), preferred_element_type=jnp.float32)


def dot_nt(left, right):
    return lax.dot_general(left, right, (((1,), (1,)), ((), ())), preferred_element_type=jnp.float32)


def dot_tn(left, right):
    return lax.dot_general(left, right, (((0,), (0,)), ((), ())), preferred_element_type=jnp.float32)


def adamw_step(weight, gradient, moment, square, step_rate, decay_rate):
    moment_new = BETA_ONE * moment + (1.0 - BETA_ONE) * gradient
    square_new = BETA_TWO * square + (1.0 - BETA_TWO) * gradient * gradient
    fixed_one = moment_new / (1.0 - BETA_ONE**STEP)
    fixed_two = square_new / (1.0 - BETA_TWO**STEP)
    weight_new = weight - step_rate * (
        fixed_one / (jnp.sqrt(fixed_two) + ADAM_EPS) + decay_rate * weight
    )
    return (moment_new, square_new, weight_new)


def document_starts(segment_ids):
    places = jnp.arange(segment_ids.shape[0], dtype=jnp.int32)
    starts = jnp.concatenate([jnp.ones((1,), jnp.bool_), segment_ids[1:] != segment_ids[:-1]])
    return lax.cummax(jnp.where(starts, places, 0), axis=0)


def turn(values):
    lane = lax.broadcasted_iota(jnp.int32, values.shape, 1)
    ahead = pltpu.roll(values, LANES - HEAD_DIM // 2, 1)
    behind = pltpu.roll(values, HEAD_DIM // 2, 1)
    return jnp.where(lane % HEAD_DIM < HEAD_DIM // 2, -ahead, behind)


def take_chunk(rows_refs, held_ref):
    for at, ref in enumerate(rows_refs):

        @pl.when(pl.program_id(0) == at)
        def _(ref=ref):
            held_ref[...] = ref[...]


def project_kernel(slots, *refs):
    rows_refs, (weight_ref, cos_ref, sin_ref, query_ref, pair_ref, held_ref) = (refs[:slots], refs[slots:])
    take_chunk(rows_refs, held_ref)
    sums = dot_nn(held_ref[...], weight_ref[...])
    cosine, sine = cos_ref[...], sin_ref[...]
    width = query_ref.shape[1]
    lane = lax.broadcasted_iota(jnp.int32, cosine.shape, 1)
    for start in range(0, width, LANES):
        part = sums[:, start : start + LANES]
        turned = (part * cosine + turn(part) * sine).astype(jnp.bfloat16)
        query_ref[:, start : start + LANES] = turned * jnp.bfloat16(SCORE_SCALE)
    for which in range(2):
        part = sums[:, width + which * LANES : width + (which + 1) * LANES]
        is_key = (lane < HEAD_DIM) if which == 0 else (lane >= HEAD_DIM)
        turned = jnp.where(is_key, part * cosine + turn(part) * sine, part)
        pair_ref[:, which * LANES : (which + 1) * LANES] = turned.astype(jnp.bfloat16)


def project(chunks, weight, total, cosine, sine, width):
    slots = len(chunks)
    block, depth = chunks[0].shape
    rows = slots * block
    whole = pl.BlockSpec((block, depth), lambda i: (0, 0))
    return pl.pallas_call(
        functools.partial(project_kernel, slots),
        grid=(slots,),
        in_specs=[whole] * slots
        + [
            pl.BlockSpec((depth, total), lambda i: (0, 0)),
            pl.BlockSpec((block, LANES), lambda i: (i, 0)),
            pl.BlockSpec((block, LANES), lambda i: (i, 0)),
        ],
        out_specs=[
            pl.BlockSpec((block, width), lambda i: (i, 0)),
            pl.BlockSpec((block, total - width), lambda i: (i, 0)),
        ],
        out_shape=[
            jax.ShapeDtypeStruct((rows, width), jnp.bfloat16),
            jax.ShapeDtypeStruct((rows, total - width), jnp.bfloat16),
        ],
        scratch_shapes=[pltpu.VMEM((block, depth), jnp.bfloat16)],
        compiler_params=pltpu.CompilerParams(vmem_limit_bytes=VMEM_LIMIT),
        cost_estimate=pl.CostEstimate(
            flops=2 * rows * depth * total,
            bytes_accessed=(rows + total) * depth * 2,
            transcendentals=0,
        ),
        name="project",
    )(*chunks, weight, cosine, sine)


def widen_kernel(slots, *refs):
    rows_refs, (weight_ref, hidden_ref, factor_ref, silu_ref, held_ref) = (refs[:slots], refs[slots:])
    take_chunk(rows_refs, held_ref)
    sums = dot_nn(held_ref[...], weight_ref[...])
    width = hidden_ref.shape[1]
    gate, upward = (sums[:, :width], sums[:, width:])
    sigmoid = jax.nn.sigmoid(gate)
    silu = gate * sigmoid
    hidden_ref[...] = (silu * upward).astype(jnp.bfloat16)
    factor_ref[...] = (upward * sigmoid * (1.0 + gate * (1.0 - sigmoid))).astype(jnp.bfloat16)
    silu_ref[...] = silu.astype(jnp.bfloat16)


def widen(chunks, weight):
    slots = len(chunks)
    block, depth = chunks[0].shape
    width = weight.shape[1] // 2
    rows = slots * block
    once = pl.Buffered(1)
    return pl.pallas_call(
        functools.partial(widen_kernel, slots),
        grid=(slots,),
        in_specs=[pl.BlockSpec((block, depth), lambda i: (0, 0), pipeline_mode=once)] * slots
        + [pl.BlockSpec(weight.shape, lambda i: (0, 0), pipeline_mode=once)],
        out_specs=[pl.BlockSpec((block, width), lambda i: (i, 0))] * 3,
        out_shape=[jax.ShapeDtypeStruct((rows, width), jnp.bfloat16)] * 3,
        scratch_shapes=[pltpu.VMEM((block, depth), jnp.bfloat16)],
        compiler_params=pltpu.CompilerParams(vmem_limit_bytes=VMEM_LIMIT),
        cost_estimate=pl.CostEstimate(
            flops=4 * rows * depth * width,
            bytes_accessed=(rows + 2 * width) * depth * 2 + 6 * rows * width,
            transcendentals=rows * width,
        ),
        name="widen",
    )(*chunks, weight)


def widen_back_kernel(slots, kept, *refs):
    rows_refs, refs = (refs[:slots], refs[slots:])
    down_ref, gateup_ref, factor_ref, silu_ref = refs[:4]
    gate_ref, up_ref, partial_ref, held_ref = refs[4 + kept :]
    take_chunk(rows_refs, held_ref)
    grad_hidden = dot_nn(held_ref[...], down_ref[...])
    gate = (grad_hidden * factor_ref[...].astype(jnp.float32)).astype(jnp.bfloat16)
    up = (grad_hidden * silu_ref[...].astype(jnp.float32)).astype(jnp.bfloat16)
    gate_ref[...] = gate
    up_ref[...] = up
    both = jnp.concatenate([gate, up], axis=1)
    partial_ref[...] = dot_nt(both, gateup_ref[...]).astype(jnp.bfloat16)


def widen_back(chunks, down, gateup, factor, silu, first, kept):
    slots = len(chunks)
    block, depth = chunks[0].shape
    width = down.shape[1]
    once = pl.Buffered(1)
    tile = pl.BlockSpec((block, width), lambda i: (first + i, 0))
    return pl.pallas_call(
        functools.partial(widen_back_kernel, slots, len(kept)),
        grid=(slots,),
        in_specs=[pl.BlockSpec((block, depth), lambda i: (0, 0), pipeline_mode=once)] * slots
        + [
            pl.BlockSpec(down.shape, lambda i: (0, 0), pipeline_mode=once),
            pl.BlockSpec(gateup.shape, lambda i: (0, 0), pipeline_mode=once),
            tile,
            tile,
        ]
        + [pl.BlockSpec(memory_space=pl.ANY)] * len(kept),
        out_specs=[tile, tile, pl.BlockSpec((block, depth), lambda i: (i, 0))],
        out_shape=[jax.ShapeDtypeStruct(factor.shape, jnp.bfloat16)] * 2
        + [jax.ShapeDtypeStruct((slots * block, depth), jnp.bfloat16)],
        scratch_shapes=[pltpu.VMEM((block, depth), jnp.bfloat16)],
        input_output_aliases={slots + 4 + i: i for i in range(len(kept))},
        compiler_params=pltpu.CompilerParams(vmem_limit_bytes=VMEM_LIMIT),
        cost_estimate=pl.CostEstimate(
            flops=6 * slots * block * depth * width,
            bytes_accessed=3 * width * depth * 2 + 8 * slots * block * width,
            transcendentals=0,
        ),
        name="widen_back",
    )(*chunks, down, gateup, factor, silu, *kept)


def stack_heads(values):
    return jnp.concatenate(
        [values[:, start : start + LANES] for start in range(0, values.shape[1], LANES)], axis=0
    )


def block_of(meta_ref, chunk, step, parts, lines):
    base = chunk * (2 + parts)
    key_block = meta_ref[base + 1] - step
    slot = meta_ref[base + 2 + key_block // lines]
    own_line = meta_ref[pl.num_programs(0) * (2 + parts)]
    line = lax.rem(key_block, lines)
    return (key_block, slot, line, lax.rem(own_line - line + lines, lines))


def attend_kernel(parts, lines, meta_ref, query_ref, pair_ref, info_ref, out_ref, log_ref):
    chunk = pl.program_id(0)
    block = query_ref.shape[0]
    heads = query_ref.shape[1] // LANES
    stacked = stack_heads(query_ref[...])
    lane = lax.broadcasted_iota(jnp.int32, stacked.shape, 1)
    place = jnp.concatenate([info_ref[0, 0:1, :]] * heads, axis=1)
    start = jnp.concatenate([info_ref[0, 1:2, :]] * heads, axis=1)
    base = chunk * (2 + parts)
    steps = meta_ref[base + 1] - meta_ref[base] + 1
    width = heads * block
    outs = []
    for which in range(2):
        is_key = (lane < HEAD_DIM) if which == 0 else (lane >= HEAD_DIM)
        queries = jnp.where(is_key, stacked, jnp.zeros_like(stacked))

        def body(step, carry):
            peak, total, mixed = carry
            key_block, slot, at, _ = block_of(meta_ref, chunk, step, parts, lines)
            pair = pair_ref[at, slot, :, which * LANES : (which + 1) * LANES]
            scores = dot_nt(pair, queries)
            key_place = key_block * block + lax.broadcasted_iota(jnp.int32, (block, width), 0)
            scores = jnp.where((key_place <= place) & (key_place >= start), scores, MASKED)
            new_peak = jnp.maximum(peak, jnp.max(scores, axis=0, keepdims=True))
            weights = jnp.exp(scores - new_peak)
            shrink = jnp.exp(peak - new_peak)
            total = total * shrink + jnp.sum(weights, axis=0, keepdims=True)
            mixed = mixed * shrink + dot_tn(pair, weights.astype(jnp.bfloat16))
            return (new_peak, total, mixed)

        peak, total, mixed = lax.fori_loop(
            0,
            steps,
            body,
            (
                jnp.full((1, width), MASKED, jnp.float32),
                jnp.zeros((1, width), jnp.float32),
                jnp.zeros((LANES, width), jnp.float32),
            ),
        )
        log_ref[0, which : which + 1, :] = peak + jnp.log(total)
        outs.append(mixed / total)
    joined = jnp.concatenate([outs[1][:HEAD_DIM], outs[0][HEAD_DIM:]], axis=0)
    rows = joined.T.astype(jnp.bfloat16)
    for head in range(heads):
        out_ref[:, head * LANES : (head + 1) * LANES] = rows[head * block : (head + 1) * block]


def attend(meta, queries, pairs, info, parts):
    chunks, block = (info.shape[0], info.shape[2])
    width = queries.shape[1]
    heads = width // LANES
    lines = pairs.shape[0]
    steps = 3 * chunks
    return pl.pallas_call(
        functools.partial(attend_kernel, parts, lines),
        grid_spec=pltpu.PrefetchScalarGridSpec(
            num_scalar_prefetch=1,
            grid=(chunks,),
            in_specs=[
                pl.BlockSpec((block, width), lambda i, m: (i, 0)),
                pl.BlockSpec(pairs.shape, lambda i, m: (0, 0, 0, 0)),
                pl.BlockSpec((1, 2, block), lambda i, m: (i, 0, 0)),
            ],
            out_specs=[
                pl.BlockSpec((block, width), lambda i, m: (i, 0)),
                pl.BlockSpec((1, 2, heads * block), lambda i, m: (i, 0, 0)),
            ],
        ),
        out_shape=[
            jax.ShapeDtypeStruct(queries.shape, jnp.bfloat16),
            jax.ShapeDtypeStruct((chunks, 2, heads * block), jnp.float32),
        ],
        compiler_params=pltpu.CompilerParams(vmem_limit_bytes=VMEM_LIMIT),
        cost_estimate=pl.CostEstimate(
            flops=steps * 2 * 2 * 2 * heads * block * block * LANES,
            bytes_accessed=queries.size * 4 + pairs.size * 2,
            transcendentals=steps * 2 * heads * block * block,
        ),
        name="attend",
    )(meta, queries, pairs, info)


def attend_back_kernel(parts, lines, meta_ref, query_ref, *refs):
    pair_ref, grad_ref, mixed_ref, log_ref, info_ref, cos_ref, sin_ref, query_out = refs[:8]
    pair_outs = refs[8 : 8 + lines]
    sums = refs[8 + lines]
    chunk = pl.program_id(0)
    block = query_ref.shape[0]
    heads = query_ref.shape[1] // LANES

    @pl.when(chunk == 0)
    def _():
        sums[...] = jnp.zeros_like(sums)

    stacked = stack_heads(query_ref[...])
    stacked_grad = stack_heads(grad_ref[...])
    product = stacked_grad.astype(jnp.float32) * stack_heads(mixed_ref[...]).astype(jnp.float32)
    lane = lax.broadcasted_iota(jnp.int32, stacked.shape, 1)
    place = jnp.concatenate([info_ref[0, 0:1, :]] * heads, axis=1)
    start = jnp.concatenate([info_ref[0, 1:2, :]] * heads, axis=1)
    base = chunk * (2 + parts)
    steps = meta_ref[base + 1] - meta_ref[base] + 1
    width = heads * block
    grads = []
    for which in range(2):
        is_key = (lane < HEAD_DIM) if which == 0 else (lane >= HEAD_DIM)
        queries = jnp.where(is_key, stacked, jnp.zeros_like(stacked))
        grad = jnp.where(is_key, jnp.zeros_like(stacked_grad), stacked_grad)
        own = jnp.where(is_key, 0.0, product)
        centre = lax.dot_general(
            jnp.ones((8, LANES), jnp.float32),
            own,
            (((1,), (1,)), ((), ())),
            precision=lax.Precision.HIGHEST,
            preferred_element_type=jnp.float32,
        )[0:1]
        logs = log_ref[0, which : which + 1, :]

        def body(step, grad_query):
            key_block, slot, at, shift = block_of(meta_ref, chunk, step, parts, lines)
            columns = slice(which * LANES, (which + 1) * LANES)
            pair = pair_ref[at, slot, :, columns]
            scores = dot_nt(pair, queries)
            key_place = key_block * block + lax.broadcasted_iota(jnp.int32, (block, width), 0)
            scores = jnp.where((key_place <= place) & (key_place >= start), scores, MASKED)
            weights = jnp.exp(scores - logs)
            grad_scores = (weights * (dot_nt(pair, grad) - centre)).astype(jnp.bfloat16)
            sums[shift, slot, :, columns] += dot_nn(grad_scores, queries) + dot_nn(
                weights.astype(jnp.bfloat16), grad
            )
            return grad_query + dot_tn(pair, grad_scores)

        grads.append(lax.fori_loop(0, steps, body, jnp.zeros((LANES, width), jnp.float32)))
    joined = jnp.concatenate([grads[0][:HEAD_DIM], grads[1][HEAD_DIM:]], axis=0)
    rows = joined.T * SCORE_SCALE
    cosine, sine = cos_ref[...], sin_ref[...]
    for head in range(heads):
        part = rows[head * block : (head + 1) * block]
        back = part * cosine - turn(part) * sine
        query_out[:, head * LANES : (head + 1) * LANES] = back.astype(jnp.bfloat16)

    @pl.when(chunk == pl.num_programs(0) - 1)
    def _():
        for line in range(lines):
            pair_outs[line][...] = sums[line].astype(jnp.bfloat16)


def attend_back(meta, queries, pairs, grad_mixed, mixed, logs, info, cosine, sine, parts):
    chunks, block = (info.shape[0], info.shape[2])
    width = queries.shape[1]
    heads = width // LANES
    lines = pairs.shape[0]
    shape = pairs.shape[1:]
    steps = 3 * chunks
    wide = pl.BlockSpec((block, width), lambda i, m: (i, 0))
    table = pl.BlockSpec((block, LANES), lambda i, m: (i, 0))
    whole = pl.BlockSpec(shape, lambda i, m: (0, 0, 0))
    outs = pl.pallas_call(
        functools.partial(attend_back_kernel, parts, lines),
        grid_spec=pltpu.PrefetchScalarGridSpec(
            num_scalar_prefetch=1,
            grid=(chunks,),
            in_specs=[
                wide,
                pl.BlockSpec(pairs.shape, lambda i, m: (0, 0, 0, 0)),
                wide,
                wide,
                pl.BlockSpec((1, 2, heads * block), lambda i, m: (i, 0, 0)),
                pl.BlockSpec((1, 2, block), lambda i, m: (i, 0, 0)),
                table,
                table,
            ],
            out_specs=[wide] + [whole] * lines,
            scratch_shapes=[pltpu.VMEM(pairs.shape, jnp.float32)],
        ),
        out_shape=[jax.ShapeDtypeStruct(queries.shape, jnp.bfloat16)]
        + [jax.ShapeDtypeStruct(shape, jnp.bfloat16)] * lines,
        compiler_params=pltpu.CompilerParams(vmem_limit_bytes=VMEM_LIMIT),
        cost_estimate=pl.CostEstimate(
            flops=steps * 2 * 5 * 2 * heads * block * block * LANES,
            bytes_accessed=queries.size * 8 + 2 * pairs.size * 2,
            transcendentals=steps * 2 * heads * block * block,
        ),
        name="attend_back",
    )(
        meta,
        queries,
        pairs,
        grad_mixed,
        mixed,
        logs,
        info,
        cosine,
        sine,
    )
    return (outs[0], [out.reshape(chunks * block, 2 * LANES) for out in outs[1:]])


def pair_back_kernel(*refs):
    *part_refs, cos_ref, sin_ref, out_ref = refs
    cosine, sine = cos_ref[...], sin_ref[...]
    lane = lax.broadcasted_iota(jnp.int32, cosine.shape, 1)
    for which in range(2):
        columns = slice(which * LANES, (which + 1) * LANES)
        total = part_refs[0][:, columns].astype(jnp.float32)
        for ref in part_refs[1:]:
            total = total + ref[:, columns].astype(jnp.float32)
        is_key = (lane < HEAD_DIM) if which == 0 else (lane >= HEAD_DIM)
        total = jnp.where(is_key, total * cosine - turn(total) * sine, total)
        out_ref[:, columns] = total.astype(jnp.bfloat16)


def pair_back(parts, cosine, sine, block):
    rows, columns = parts[0].shape
    tile = pl.BlockSpec((block, columns), lambda i: (i, 0))
    table = pl.BlockSpec((block, LANES), lambda i: (i, 0))
    return pl.pallas_call(
        pair_back_kernel,
        grid=(rows // block,),
        in_specs=[tile] * len(parts) + [table, table],
        out_specs=tile,
        out_shape=jax.ShapeDtypeStruct((rows, columns), jnp.bfloat16),
        compiler_params=pltpu.CompilerParams(vmem_limit_bytes=VMEM_LIMIT),
        name="pair_back",
    )(*parts, cosine, sine)


def update(refs, index, gradient, rate):
    weight, moment, square = [ref[index] for ref in refs[:3]]
    moment_new, square_new, weight_new = adamw_step(weight, gradient, moment, square, rate, 0.1)
    for ref, value in zip(refs[3:], (moment_new, square_new, weight_new)):
        ref[index] = value


def chosen(meta_ref, grad_refs, at, rows, columns):
    own_y = meta_ref[0] == at
    first = pl.program_id(0) == 0
    near = jnp.where(first, grad_refs[0][rows, columns], grad_refs[2][rows, columns])
    far = jnp.where(first, grad_refs[1][rows, columns], grad_refs[3][rows, columns])
    return jnp.where(own_y, near, far).astype(jnp.float32)


def joint_update_kernel(meta_ref, *refs):
    grad_refs, query_refs, pair_refs = (refs[:4], refs[4:7] + refs[10:13], refs[7:10] + refs[13:16])
    groups = query_refs[0].shape[1] // (2 * LANES)
    every = slice(None)
    for at in range(2):
        for j in range(groups):
            gradient = chosen(meta_ref, grad_refs, at, every, slice(j * LANES, (j + 1) * LANES))
            place = slice((2 * j + at) * LANES, (2 * j + at + 1) * LANES)
            update(query_refs, (every, place), gradient, D ** (-0.5))
        for which in range(2):
            start = (groups + which) * LANES
            gradient = chosen(meta_ref, grad_refs, at, every, slice(start, start + LANES))
            if which == 1:
                gradient = pltpu.roll(gradient, HEAD_DIM, 1)
            place = slice((2 * at + which) * LANES, (2 * at + which + 1) * LANES)
            update(pair_refs, (every, place), gradient, D ** (-0.5))


def joint_update(meta, grads, query, pair):
    half = grads[0].shape[0]

    def rows_of(array):
        return pl.BlockSpec((half, array.shape[1]), lambda i, m: ((m[1] + i) % 2, 0))

    whole = pl.BlockSpec(grads[0].shape, lambda i, m: (0, 0))
    blocks = [rows_of(array) for array in (*query, *pair)]
    return pl.pallas_call(
        joint_update_kernel,
        grid_spec=pltpu.PrefetchScalarGridSpec(
            num_scalar_prefetch=1, grid=(2,), in_specs=[whole] * 4 + blocks, out_specs=blocks
        ),
        out_shape=[jax.ShapeDtypeStruct(array.shape, array.dtype) for array in (*query, *pair)],
        compiler_params=pltpu.CompilerParams(vmem_limit_bytes=VMEM_LIMIT),
        cost_estimate=pl.CostEstimate(
            flops=20 * (query[0].size + pair[0].size),
            bytes_accessed=24 * (query[0].size + pair[0].size),
            transcendentals=0,
        ),
        name="joint_update",
    )(meta, *grads, *query, *pair)


def turned_update_kernel(rate, swapped, meta_ref, *refs):
    grad_refs, weight_refs = (refs[:4], refs[4:10])
    at = pl.program_id(1)
    width = grad_refs[0].shape[1]
    every = slice(None)
    for j, start in enumerate(range(0, width, LANES)):
        strip = slice(start, min(start + LANES, width))
        gradient = chosen(meta_ref, grad_refs, at, every, strip).T
        if swapped:
            gradient = jnp.concatenate([gradient[HEAD_DIM:], gradient[:HEAD_DIM]], axis=0)
            index = (j, 0)
        else:
            index = (strip, every)
        update(weight_refs, index, gradient, rate)


def turned_update(meta, grads, weights, rate, swapped):
    half, width = grads[0].shape
    shape = weights[0].shape
    if swapped:
        weights = [w.reshape(width // LANES, 2, LANES, shape[1]) for w in weights]
        block = pl.BlockSpec(
            (width // LANES, 1, LANES, half), lambda i, at, m: (0, at, 0, (m[1] + i) % 2)
        )
    else:
        block = pl.BlockSpec((width, half), lambda i, at, m: (at, (m[1] + i) % 2))
    outs = pl.pallas_call(
        functools.partial(turned_update_kernel, rate, swapped),
        grid_spec=pltpu.PrefetchScalarGridSpec(
            num_scalar_prefetch=1,
            grid=(2, 2),
            in_specs=[pl.BlockSpec(grads[0].shape, lambda i, at, m: (0, 0))] * 4 + [block] * 3,
            out_specs=[block] * 3,
        ),
        out_shape=[jax.ShapeDtypeStruct(weights[0].shape, jnp.float32)] * 3,
        compiler_params=pltpu.CompilerParams(vmem_limit_bytes=VMEM_LIMIT),
        cost_estimate=pl.CostEstimate(
            flops=20 * weights[0].size, bytes_accessed=24 * weights[0].size, transcendentals=0
        ),
        name="turned_update",
    )(meta, *grads, *weights)
    return [out.reshape(shape) for out in outs]


def gateup_update_kernel(meta_ref, *refs):
    gate_refs, up_refs, weight_refs = (refs[:4], refs[4:8], refs[8:14])
    every = slice(None)
    gate, up = [
        jnp.concatenate([chosen(meta_ref, grads, at, every, every) for at in range(2)], axis=1)
        for grads in (gate_refs, up_refs)
    ]
    update(weight_refs, every, jnp.stack([gate, up], axis=1), D ** (-0.5))


def gateup_update(meta, gates, ups, weights, rows):
    half, width = gates[0].shape
    shape = weights[0].shape
    tiles = half // rows
    grad = pl.BlockSpec((rows, width), lambda i, j, m: (j, 0))
    block = pl.BlockSpec(
        (rows, 2, shape[2]), lambda i, j, m: (((m[1] + i) % 2) * tiles + j, 0, 0)
    )
    outs = pl.pallas_call(
        gateup_update_kernel,
        grid_spec=pltpu.PrefetchScalarGridSpec(
            num_scalar_prefetch=1,
            grid=(2, tiles),
            in_specs=[grad] * 8 + [block] * 3,
            out_specs=[block] * 3,
        ),
        out_shape=[jax.ShapeDtypeStruct(shape, jnp.float32)] * 3,
        compiler_params=pltpu.CompilerParams(vmem_limit_bytes=VMEM_LIMIT),
        cost_estimate=pl.CostEstimate(
            flops=20 * weights[0].size, bytes_accessed=28 * weights[0].size, transcendentals=0
        ),
        name="gateup_update",
    )(meta, *gates, *ups, *weights)
    return outs


def on_device(
    sizes,
    block_input,
    cotangent,
    segments,
    norm_gains,
    w_query,
    w_keyvalue,
    w_output,
    w_gateup,
    w_down,
    gains_moment,
    gains_square,
    query_moment,
    query_square,
    keyvalue_moment,
    keyvalue_square,
    output_moment,
    output_square,
    gateup_moment,
    gateup_square,
    down_moment,
    down_square,
):
    rows_on, lines = sizes
    y, core, row, line = [lax.axis_index(name) for name in ("y", "core", "row", "col")]
    length = segments.shape[1]
    block = block_input.shape[0] // lines
    wide = block_input.shape[1]
    half = wide // 2
    slots = 2 * rows_on
    per_row = w_query.shape[1] // (KV_HEADS * HEAD_DIM)
    query_width = per_row * LANES
    hidden_here = w_gateup.shape[2] // 2

    def shift(value, axis, size, by):
        return lax.ppermute(value, axis, [(i, (i + by) % size) for i in range(size)])

    def other_core(value):
        return lax.ppermute(value, "core", [(0, 1), (1, 0)])

    def other_y(value):
        return lax.ppermute(value, "y", [(0, 1), (1, 0)])

    def place_of(y_at, core_at, row_at):
        return (y_at * 2 + core_at) * rows_on + row_at

    first_pairs, second_pairs = ([], [])
    for y_at in range(2):
        for core_at in range(2):
            for row_at in range(rows_on):
                over_row = (
                    place_of(y_at, core_at, row_at),
                    place_of(y_at, core_at, (row_at + 1) % rows_on),
                )
                over_y = (place_of(y_at, core_at, row_at), place_of(1 - y_at, core_at, row_at))
                first_pairs.append(over_row if core_at == 0 else over_y)
                second_pairs.append(over_y if core_at == 0 else over_row)
    near = ("y", "core", "row")

    def gather_tokens(own):
        if rows_on == 2:
            first = lax.ppermute(own, near, first_pairs)
            second = lax.ppermute(own, near, second_pairs)
            third = lax.ppermute(first, near, second_pairs)
            return [own, first, second, third]
        parts = [own] + [shift(own, "row", rows_on, by) for by in range(1, rows_on)]
        return parts + [other_y(part) for part in parts]

    def reduce_tokens(rows_of, after_close=None, after_first=None, before_last=None):
        def same(value):
            return value

        after_close, after_first, before_last = [f or same for f in (after_close, after_first, before_last)]
        if rows_on == 2:
            far = rows_of(2, 4)
            third = lax.ppermute(far[block:], near, second_pairs)
            second = lax.ppermute(far[:block], near, second_pairs)
            close = after_close(rows_of(0, 2))
            key = (close[block:].astype(jnp.float32) + third.astype(jnp.float32)).astype(jnp.bfloat16)
            first = before_last(lax.ppermute(after_first(key), near, first_pairs))
            own = close[:block].astype(jnp.float32) + second.astype(jnp.float32)
            return own + first.astype(jnp.float32)
        partial = after_close(rows_of(0, slots))
        parts = [partial[i * block : (i + 1) * block] for i in range(slots)]
        sums = [
            parts[i].astype(jnp.float32) + other_y(parts[rows_on + i]).astype(jnp.float32)
            for i in range(rows_on)
        ]
        sums[0] = after_first(sums[0])
        total = sums[0]
        for by in range(1, rows_on):
            moved = shift(sums[by].astype(jnp.bfloat16), "row", rows_on, -by)
            total = total + moved.astype(jnp.float32)
        return before_last(total)

    def product(left, right):
        def rows_of(first, last):
            return dot_nt(left[first * block : last * block], right).astype(jnp.bfloat16)

        return rows_of

    if rows_on == 2:
        slot_y = [y, jnp.where(core == 0, y, 1 - y), jnp.where(core == 0, 1 - y, y), 1 - y]
        slot_row = [row, jnp.where(core == 0, 1 - row, row), jnp.where(core == 0, row, 1 - row), 1 - row]
    else:
        slot_y = [y] * rows_on + [1 - y] * rows_on
        slot_row = [(row - by) % rows_on for by in range(rows_on)] * 2

    def pick(parts, index):
        return lax.dynamic_index_in_dim(jnp.stack(parts), index, 0, keepdims=False)

    def tokens_sent(values):
        parts = []
        for by in range(lines):
            part = lax.dynamic_slice_in_dim(values, ((line + by) % lines) * block, block, 0)
            parts.append(part if by == 0 else shift(part, "col", lines, by))
        return parts

    def tokens_of(parts):
        blocks = [pick(parts, (line - at) % lines) for at in range(lines)]
        return jnp.concatenate([b[:, :half] for b in blocks] + [b[:, half:] for b in blocks], axis=1)

    def features_from_tokens(values):
        blocks = [
            jnp.concatenate(
                [
                    values[:, at * half : (at + 1) * half],
                    values[:, D // 2 + at * half : D // 2 + (at + 1) * half],
                ],
                axis=1,
            )
            for at in range(lines)
        ]
        parts = []
        for by in range(lines):
            part = pick(blocks, (line + by) % lines)
            parts.append(part if by == 0 else shift(part, "col", lines, by))
        return jnp.concatenate([pick(parts, (line - at) % lines) for at in range(lines)], axis=0)

    def half_rows(values):
        return lax.dynamic_slice_in_dim(values, core * half, half, 0)

    def half_columns(values):
        return lax.dynamic_slice_in_dim(values, core * half, half, 1)

    def gather_weight(piece):
        return lax.all_gather(piece, ("core", "col"), axis=0, tiled=True)

    query_rows = half_rows(w_query).astype(jnp.bfloat16)
    pair_rows = half_rows(w_keyvalue).astype(jnp.bfloat16)

    def joint_of(at):
        pieces = [
            query_rows[:, (2 * j + at) * LANES : (2 * j + at + 1) * LANES] for j in range(per_row)
        ]
        pair = pair_rows[:, at * 2 * LANES : (at + 1) * 2 * LANES]
        pieces += [
            pair[:, :LANES],
            pair[:, LANES + HEAD_DIM :],
            pair[:, LANES : LANES + HEAD_DIM],
        ]
        return jnp.concatenate(pieces, axis=1)

    joint_mine = jnp.where(y == 0, joint_of(0), joint_of(1))
    output_columns = half_columns(w_output).astype(jnp.bfloat16)

    def output_of(at):
        pieces = []
        for j in range(per_row):
            base = (2 * j + at) * LANES
            pieces += [
                output_columns[base + HEAD_DIM : base + LANES],
                output_columns[base : base + HEAD_DIM],
            ]
        return jnp.concatenate(pieces, axis=0)

    output_mine = jnp.where(y == 0, output_of(0), output_of(1)).T
    gateup_mine = lax.dynamic_slice(
        w_gateup, (core * half, 0, y * hidden_here), (half, 2, hidden_here)
    ).astype(jnp.bfloat16)
    gateup_mine = jnp.concatenate([gateup_mine[:, 0], gateup_mine[:, 1]], axis=1)
    down_mine = lax.dynamic_slice(
        w_down, (y * hidden_here, core * half), (hidden_here, half)
    ).astype(jnp.bfloat16).T

    gain_parts = [norm_gains] + [shift(norm_gains, "col", lines, by) for by in range(1, lines)]
    gain_blocks = [pick(gain_parts, (line - at) % lines) for at in range(lines)]
    gains = jnp.concatenate(
        [b[:, :half] for b in gain_blocks] + [b[:, half:] for b in gain_blocks], axis=1
    )

    own_starts = document_starts(segments[0])
    other_starts = document_starts(other_y(segments)[0])
    frequency = 10000.0 ** (-2.0 * jnp.arange(HEAD_DIM // 2, dtype=jnp.float32) / HEAD_DIM)
    starts, places, meta = ([], [], [])
    for slot in range(slots):
        begin = slot_row[slot] * (lines * block) + line * block
        of_chunk = lax.dynamic_slice_in_dim(
            jnp.where(slot_y[slot] == y, own_starts, other_starts), begin, block, 0
        )
        starts.append(of_chunk)
        places.append(begin + jnp.arange(block, dtype=jnp.int32))
        meta += [of_chunk[0] // block, begin // block]
        for row_at in range(rows_on):
            found = jnp.int32(0)
            for other in range(slots):
                same = (slot_y[other] == slot_y[slot]) & (slot_row[other] == row_at)
                found = found + jnp.where(same, other, 0)
            meta.append(found)
    meta = jnp.stack([jnp.asarray(m, jnp.int32) for m in meta + [line]])
    starts, places = (jnp.stack(starts), jnp.stack(places))
    info = jnp.stack([places, starts], axis=1)
    offsets = (places - starts).astype(jnp.float32).reshape(-1)
    phases = offsets[:, None] * jnp.tile(frequency, LANES // (HEAD_DIM // 2))[None, :]
    cosine, sine = (jnp.cos(phases), jnp.sin(phases))

    residual_low = tokens_of(tokens_sent(block_input))
    residual_low, joint_mine, output_mine = lax.optimization_barrier(
        (residual_low, joint_mine, output_mine)
    )
    first_weight = gather_weight(jnp.concatenate([joint_mine, output_mine], axis=1))
    joint_width = joint_mine.shape[1]
    joint_weight, output_weight = (first_weight[:, :joint_width], first_weight[:, joint_width:])
    residual = residual_low.astype(jnp.float32)
    scale_one = lax.rsqrt(jnp.mean(residual * residual, axis=1, keepdims=True) + EPSILON)
    normed_parts = gather_tokens((residual * scale_one * gains[0]).astype(jnp.bfloat16))
    queries, pair = project(normed_parts, first_weight, joint_width, cosine, sine, query_width)
    pairs = lax.all_gather(pair.reshape(slots, block, 2 * LANES), "col", axis=0, tiled=False)
    pairs, gateup_mine, down_mine = lax.optimization_barrier((pairs, gateup_mine, down_mine))
    gateup_weight = gather_weight(gateup_mine)
    down_weight = gather_weight(down_mine)
    mixed, logs = attend(meta, queries, pairs, info, rows_on)
    attn_sum = reduce_tokens(product(mixed, output_weight))
    attn_sum, late_cotangent = lax.optimization_barrier((attn_sum, cotangent))
    cot_parts = tokens_sent(late_cotangent)
    middle = residual + attn_sum
    scale_two = lax.rsqrt(jnp.mean(middle * middle, axis=1, keepdims=True) + EPSILON)
    two_parts = gather_tokens((middle * scale_two * gains[1]).astype(jnp.bfloat16))
    cot_low = tokens_of(cot_parts) + two_parts[-1][:1, :1] * jnp.bfloat16(0.0)
    cot_chunks = gather_tokens(cot_low)
    hidden, factor, silu_gate = widen(two_parts, gateup_weight)
    normed_two, cot = (jnp.concatenate(two_parts, axis=0), jnp.concatenate(cot_chunks, axis=0))

    def other_half(rows, grad):
        rows = lax.dynamic_slice_in_dim(rows, (1 - core) * (D // 2), D // 2, 1)
        return other_core(dot_tn(rows, grad).astype(jnp.bfloat16))

    def own_half(rows, grad, received):
        rows = lax.dynamic_slice_in_dim(rows, core * (D // 2), D // 2, 1)
        total = dot_tn(rows, grad) + received.astype(jnp.float32)
        return total.astype(jnp.bfloat16)

    def scatter(total):
        return lax.psum_scatter(total, "col", scatter_dimension=0, tiled=True)

    def collect(piece):
        near_y = other_y(piece)
        return [piece, near_y, other_core(piece), other_core(near_y)]

    down_total = own_half(cot, hidden, other_half(cot, hidden))
    down_total, down_weight = lax.optimization_barrier((down_total, down_weight))
    down_piece = scatter(down_total)
    work = {}

    def feed_back(first, last):
        work["grad_gate"], work["grad_up"], partial = widen_back(
            cot_chunks[first:last],
            down_weight,
            gateup_weight,
            factor,
            silu_gate,
            first,
            [work[name] for name in ("grad_gate", "grad_up") if name in work],
        )
        return partial

    def feed_others(close):
        close, rows, gate, up = lax.optimization_barrier(
            (close, normed_two, work["grad_gate"], work["grad_up"])
        )
        work["feed"] = (rows, gate, up, other_half(rows, gate), other_half(rows, up))
        return close

    def feed_owns(key):
        key, rows, gate, up, gate_other, up_other = lax.optimization_barrier((key, *work["feed"]))
        work["totals"] = (own_half(rows, gate, gate_other), own_half(rows, up, up_other))
        return key

    def feed_ends(first):
        first, *totals = lax.optimization_barrier((first, *work["totals"]))
        work["pieces"] = [scatter(total) for total in totals]
        return first

    grad_normed_two = reduce_tokens(feed_back, feed_others, feed_owns, feed_ends)
    gate_piece, up_piece = work["pieces"]

    def norm_back(values, scale, grad_normed, gain):
        scaled = grad_normed * gain
        total = jnp.sum(scaled * values, axis=1, keepdims=True)
        return scale * scaled - values * (scale**3 * total / D)

    grad_middle = cot_low.astype(jnp.float32) + norm_back(
        middle, scale_two, grad_normed_two, gains[1]
    )
    gain_two = jnp.sum(grad_normed_two * middle * scale_two, axis=0)

    grad_middle_low = grad_middle.astype(jnp.bfloat16)
    back = jnp.concatenate(gather_tokens(grad_middle_low), axis=0)
    grad_mixed = dot_nn(back, output_weight).astype(jnp.bfloat16)
    grad_query, grad_parts = attend_back(
        meta, queries, pairs, grad_mixed, mixed, logs, info, cosine, sine, rows_on
    )
    grad_parts = [grad_parts[0]] + [
        shift(grad_parts[by], "col", lines, -by) for by in range(1, lines)
    ]
    grad_query, late_hidden, back, mixed = lax.optimization_barrier((grad_query, hidden, back, mixed))
    output_total = own_half(back, mixed, other_half(back, mixed))

    def keys_arrive(key):
        key, work["output"], *work["grad_parts"] = lax.optimization_barrier(
            (key, output_total, *grad_parts)
        )
        return key

    ffn_sum = reduce_tokens(product(late_hidden, down_weight), None, keys_arrive)
    output_piece = scatter(work["output"])
    layer_output = features_from_tokens((middle + ffn_sum).astype(jnp.bfloat16))
    grad_keyvalue = pair_back(work["grad_parts"], cosine, sine, block)
    grad_joint = jnp.concatenate([grad_query, grad_keyvalue], axis=1)
    normed_one = jnp.concatenate(normed_parts, axis=0)
    meta_core = jnp.stack([y, core]).astype(jnp.int32)
    gateup_new = gateup_update(
        meta_core,
        collect(gate_piece),
        collect(up_piece),
        [w_gateup, gateup_moment, gateup_square],
        32,
    )

    def joint_others(close):
        close, rows, grad = lax.optimization_barrier((close, normed_one, grad_joint))
        work["joint"] = (rows, grad, other_half(rows, grad))
        return close

    def joint_owns(key):
        key, rows, grad, other = lax.optimization_barrier((key, *work["joint"]))
        work["joint_total"] = own_half(rows, grad, other)
        return key

    def joint_ends(first):
        first, total, *work["gateup"] = lax.optimization_barrier(
            (first, work["joint_total"], *gateup_new)
        )
        work["joint_piece"] = scatter(total)
        return first

    grad_normed_one = reduce_tokens(
        product(grad_joint, joint_weight), joint_others, joint_owns, joint_ends
    )
    joint_piece, gateup_new = (work["joint_piece"], work["gateup"])
    input_grad = grad_middle + norm_back(residual, scale_one, grad_normed_one, gains[0])
    gain_one = jnp.sum(grad_normed_one * residual * scale_one, axis=0)
    input_grad, layer_output = lax.optimization_barrier(
        (input_grad.astype(jnp.bfloat16), layer_output)
    )
    input_grad = features_from_tokens(input_grad).astype(jnp.float32)
    pair_piece = joint_piece[:, query_width:]
    pair_total = pair_piece.astype(jnp.float32)
    for by in range(1, rows_on):
        pair_total = pair_total + shift(pair_piece, "row", rows_on, by).astype(jnp.float32)
    joint_piece = jnp.concatenate(
        [joint_piece[:, :query_width], pair_total.astype(jnp.bfloat16)], axis=1
    )
    down_new = turned_update(
        meta_core, collect(down_piece), [w_down, down_moment, down_square], FF ** (-0.5), False
    )
    joint_new = joint_update(
        meta_core,
        collect(joint_piece),
        [w_query, query_moment, query_square],
        [w_keyvalue, keyvalue_moment, keyvalue_square],
    )
    output_new = turned_update(
        meta_core,
        collect(output_piece),
        [w_output, output_moment, output_square],
        (HEADS * HEAD_DIM // 64) ** (-0.5),
        True,
    )

    gain_sums = jnp.stack([gain_one, gain_two])
    blocks = [
        jnp.concatenate(
            [
                gain_sums[:, at * half : (at + 1) * half],
                gain_sums[:, D // 2 + at * half : D // 2 + (at + 1) * half],
            ],
            axis=1,
        )
        for at in range(lines)
    ]
    grad_gains = pick(blocks, line)
    for by in range(1, lines):
        grad_gains = grad_gains + shift(pick(blocks, (line + by) % lines), "col", lines, by)
    for axis, size in (("core", 2), ("y", 2), ("row", rows_on)):
        blocks_total = grad_gains
        for by in range(1, size):
            grad_gains = grad_gains + shift(blocks_total, axis, size, by)

    gains_new = adamw_step(norm_gains, grad_gains, gains_moment, gains_square, 0.6, 0.0)
    return (
        layer_output,
        input_grad,
        *gains_new,
        *joint_new,
        *output_new,
        *gateup_new,
        *down_new,
    )


def solution(mesh):
    dp, rows_on, lines = (mesh.shape["dp"], mesh.shape["row"], mesh.shape["col"])
    split = Mesh(mesh.devices.reshape(dp // 2, 2, rows_on, lines), ("y", "core", "row", "col"))
    tokens = P(("y", "core", "row"), "col")
    narrow, wide = (P("col", "row"), P("row", "col"))
    gains, pair, gateup = (P(None, "col"), P("col", None), P("col", None, "row"))
    return jax.shard_map(
        functools.partial(on_device, (rows_on, lines)),
        mesh=split,
        in_specs=(
            tokens,
            tokens,
            P(("y", "core"), None),
            gains,
            narrow,
            pair,
            wide,
            gateup,
            wide,
            gains,
            gains,
            narrow,
            narrow,
            pair,
            pair,
            wide,
            wide,
            gateup,
            gateup,
            wide,
            wide,
        ),
        out_specs=(tokens, tokens)
        + (gains,) * 3
        + (narrow,) * 3
        + (pair,) * 3
        + (wide,) * 3
        + (gateup,) * 3
        + (wide,) * 3,
        check_vma=False,
    )
```

```python
import functools

import jax
import jax.numpy as jnp
from jax import lax
from jax.experimental import pallas as pl
from jax.experimental.pallas import tpu as pltpu
from jax.sharding import Mesh, PartitionSpec as P

D = 2048
HEADS = 32
KV_HEADS = 4
HEAD_DIM = 64
FF = 5632
STEP = 10

EPSILON = 1e-05
BETA_ONE = 0.9
BETA_TWO = 0.999
ADAM_EPS = 1e-08
MASKED = -1e30
SCORE_SCALE = HEAD_DIM ** (-0.5)
LANES = 128
VMEM_LIMIT = 48 * 1024 * 1024


def dot_nn(left, right):
    return lax.dot_general(left, right, (((1,), (0,)), ((), ())), preferred_element_type=jnp.float32)


def dot_nt(left, right):
    return lax.dot_general(left, right, (((1,), (1,)), ((), ())), preferred_element_type=jnp.float32)


def dot_tn(left, right):
    return lax.dot_general(left, right, (((0,), (0,)), ((), ())), preferred_element_type=jnp.float32)


def adamw_step(weight, gradient, moment, square, step_rate, decay_rate):
    moment_new = BETA_ONE * moment + (1.0 - BETA_ONE) * gradient
    square_new = BETA_TWO * square + (1.0 - BETA_TWO) * gradient * gradient
    fixed_one = moment_new / (1.0 - BETA_ONE**STEP)
    fixed_two = square_new / (1.0 - BETA_TWO**STEP)
    weight_new = weight - step_rate * (
        fixed_one / (jnp.sqrt(fixed_two) + ADAM_EPS) + decay_rate * weight
    )
    return (moment_new, square_new, weight_new)


def document_starts(segment_ids):
    places = jnp.arange(segment_ids.shape[0], dtype=jnp.int32)
    starts = jnp.concatenate([jnp.ones((1,), jnp.bool_), segment_ids[1:] != segment_ids[:-1]])
    return lax.cummax(jnp.where(starts, places, 0), axis=0)


def turn(values):
    lane = lax.broadcasted_iota(jnp.int32, values.shape, 1)
    ahead = pltpu.roll(values, LANES - HEAD_DIM // 2, 1)
    behind = pltpu.roll(values, HEAD_DIM // 2, 1)
    return jnp.where(lane % HEAD_DIM < HEAD_DIM // 2, -ahead, behind)


def take_chunk(rows_refs, held_ref):
    for at, ref in enumerate(rows_refs):

        @pl.when(pl.program_id(0) == at)
        def _(ref=ref):
            held_ref[...] = ref[...]


def project_kernel(slots, *refs):
    rows_refs, (weight_ref, cos_ref, sin_ref, query_ref, pair_ref, held_ref) = (refs[:slots], refs[slots:])
    take_chunk(rows_refs, held_ref)
    sums = dot_nn(held_ref[...], weight_ref[...])
    cosine, sine = cos_ref[...], sin_ref[...]
    width = query_ref.shape[1]
    lane = lax.broadcasted_iota(jnp.int32, cosine.shape, 1)
    for start in range(0, width, LANES):
        part = sums[:, start : start + LANES]
        turned = (part * cosine + turn(part) * sine).astype(jnp.bfloat16)
        query_ref[:, start : start + LANES] = turned * jnp.bfloat16(SCORE_SCALE)
    for which in range(2):
        part = sums[:, width + which * LANES : width + (which + 1) * LANES]
        is_key = (lane < HEAD_DIM) if which == 0 else (lane >= HEAD_DIM)
        turned = jnp.where(is_key, part * cosine + turn(part) * sine, part)
        pair_ref[:, which * LANES : (which + 1) * LANES] = turned.astype(jnp.bfloat16)


def project(chunks, weight, total, cosine, sine, width):
    slots = len(chunks)
    block, depth = chunks[0].shape
    rows = slots * block
    whole = pl.BlockSpec((block, depth), lambda i: (0, 0))
    return pl.pallas_call(
        functools.partial(project_kernel, slots),
        grid=(slots,),
        in_specs=[whole] * slots
        + [
            pl.BlockSpec((depth, total), lambda i: (0, 0)),
            pl.BlockSpec((block, LANES), lambda i: (i, 0)),
            pl.BlockSpec((block, LANES), lambda i: (i, 0)),
        ],
        out_specs=[
            pl.BlockSpec((block, width), lambda i: (i, 0)),
            pl.BlockSpec((block, total - width), lambda i: (i, 0)),
        ],
        out_shape=[
            jax.ShapeDtypeStruct((rows, width), jnp.bfloat16),
            jax.ShapeDtypeStruct((rows, total - width), jnp.bfloat16),
        ],
        scratch_shapes=[pltpu.VMEM((block, depth), jnp.bfloat16)],
        compiler_params=pltpu.CompilerParams(vmem_limit_bytes=VMEM_LIMIT),
        cost_estimate=pl.CostEstimate(
            flops=2 * rows * depth * total,
            bytes_accessed=(rows + total) * depth * 2,
            transcendentals=0,
        ),
        name="project",
    )(*chunks, weight, cosine, sine)


def widen_kernel(slots, *refs):
    rows_refs, (weight_ref, hidden_ref, factor_ref, silu_ref, held_ref) = (refs[:slots], refs[slots:])
    take_chunk(rows_refs, held_ref)
    sums = dot_nn(held_ref[...], weight_ref[...])
    width = hidden_ref.shape[1]
    gate, upward = (sums[:, :width], sums[:, width:])
    sigmoid = jax.nn.sigmoid(gate)
    silu = gate * sigmoid
    hidden_ref[...] = (silu * upward).astype(jnp.bfloat16)
    factor_ref[...] = (upward * sigmoid * (1.0 + gate * (1.0 - sigmoid))).astype(jnp.bfloat16)
    silu_ref[...] = silu.astype(jnp.bfloat16)


def widen(chunks, weight):
    slots = len(chunks)
    block, depth = chunks[0].shape
    width = weight.shape[1] // 2
    rows = slots * block
    once = pl.Buffered(1)
    return pl.pallas_call(
        functools.partial(widen_kernel, slots),
        grid=(slots,),
        in_specs=[pl.BlockSpec((block, depth), lambda i: (0, 0), pipeline_mode=once)] * slots
        + [pl.BlockSpec(weight.shape, lambda i: (0, 0), pipeline_mode=once)],
        out_specs=[pl.BlockSpec((block, width), lambda i: (i, 0))] * 3,
        out_shape=[jax.ShapeDtypeStruct((rows, width), jnp.bfloat16)] * 3,
        scratch_shapes=[pltpu.VMEM((block, depth), jnp.bfloat16)],
        compiler_params=pltpu.CompilerParams(vmem_limit_bytes=VMEM_LIMIT),
        cost_estimate=pl.CostEstimate(
            flops=4 * rows * depth * width,
            bytes_accessed=(rows + 2 * width) * depth * 2 + 6 * rows * width,
            transcendentals=rows * width,
        ),
        name="widen",
    )(*chunks, weight)


def widen_back_kernel(slots, kept, *refs):
    rows_refs, refs = (refs[:slots], refs[slots:])
    down_ref, gateup_ref, factor_ref, silu_ref = refs[:4]
    gate_ref, up_ref, partial_ref, held_ref = refs[4 + kept :]
    take_chunk(rows_refs, held_ref)
    grad_hidden = dot_nn(held_ref[...], down_ref[...])
    gate = (grad_hidden * factor_ref[...].astype(jnp.float32)).astype(jnp.bfloat16)
    up = (grad_hidden * silu_ref[...].astype(jnp.float32)).astype(jnp.bfloat16)
    gate_ref[...] = gate
    up_ref[...] = up
    both = jnp.concatenate([gate, up], axis=1)
    partial_ref[...] = dot_nt(both, gateup_ref[...]).astype(jnp.bfloat16)


def widen_back(chunks, down, gateup, factor, silu, first, kept):
    slots = len(chunks)
    block, depth = chunks[0].shape
    width = down.shape[1]
    once = pl.Buffered(1)
    tile = pl.BlockSpec((block, width), lambda i: (first + i, 0))
    return pl.pallas_call(
        functools.partial(widen_back_kernel, slots, len(kept)),
        grid=(slots,),
        in_specs=[pl.BlockSpec((block, depth), lambda i: (0, 0), pipeline_mode=once)] * slots
        + [
            pl.BlockSpec(down.shape, lambda i: (0, 0), pipeline_mode=once),
            pl.BlockSpec(gateup.shape, lambda i: (0, 0), pipeline_mode=once),
            tile,
            tile,
        ]
        + [pl.BlockSpec(memory_space=pl.ANY)] * len(kept),
        out_specs=[tile, tile, pl.BlockSpec((block, depth), lambda i: (i, 0))],
        out_shape=[jax.ShapeDtypeStruct(factor.shape, jnp.bfloat16)] * 2
        + [jax.ShapeDtypeStruct((slots * block, depth), jnp.bfloat16)],
        scratch_shapes=[pltpu.VMEM((block, depth), jnp.bfloat16)],
        input_output_aliases={slots + 4 + i: i for i in range(len(kept))},
        compiler_params=pltpu.CompilerParams(vmem_limit_bytes=VMEM_LIMIT),
        cost_estimate=pl.CostEstimate(
            flops=6 * slots * block * depth * width,
            bytes_accessed=3 * width * depth * 2 + 8 * slots * block * width,
            transcendentals=0,
        ),
        name="widen_back",
    )(*chunks, down, gateup, factor, silu, *kept)


def stack_heads(values):
    return jnp.concatenate(
        [values[:, start : start + LANES] for start in range(0, values.shape[1], LANES)], axis=0
    )


def block_of(meta_ref, chunk, step, parts, lines):
    base = chunk * (2 + parts)
    key_block = meta_ref[base + 1] - step
    slot = meta_ref[base + 2 + key_block // lines]
    own_line = meta_ref[pl.num_programs(0) * (2 + parts)]
    line = lax.rem(key_block, lines)
    return (key_block, slot, line, lax.rem(own_line - line + lines, lines))


def attend_kernel(parts, lines, meta_ref, query_ref, pair_ref, info_ref, out_ref, log_ref):
    chunk = pl.program_id(0)
    block = query_ref.shape[0]
    heads = query_ref.shape[1] // LANES
    stacked = stack_heads(query_ref[...])
    lane = lax.broadcasted_iota(jnp.int32, stacked.shape, 1)
    place = jnp.concatenate([info_ref[0, 0:1, :]] * heads, axis=1)
    start = jnp.concatenate([info_ref[0, 1:2, :]] * heads, axis=1)
    base = chunk * (2 + parts)
    steps = meta_ref[base + 1] - meta_ref[base] + 1
    width = heads * block
    outs = []
    for which in range(2):
        is_key = (lane < HEAD_DIM) if which == 0 else (lane >= HEAD_DIM)
        queries = jnp.where(is_key, stacked, jnp.zeros_like(stacked))

        def body(step, carry):
            peak, total, mixed = carry
            key_block, slot, at, _ = block_of(meta_ref, chunk, step, parts, lines)
            pair = pair_ref[at, slot, :, which * LANES : (which + 1) * LANES]
            scores = dot_nt(pair, queries)
            key_place = key_block * block + lax.broadcasted_iota(jnp.int32, (block, width), 0)
            scores = jnp.where((key_place <= place) & (key_place >= start), scores, MASKED)
            new_peak = jnp.maximum(peak, jnp.max(scores, axis=0, keepdims=True))
            weights = jnp.exp(scores - new_peak)
            shrink = jnp.exp(peak - new_peak)
            total = total * shrink + jnp.sum(weights, axis=0, keepdims=True)
            mixed = mixed * shrink + dot_tn(pair, weights.astype(jnp.bfloat16))
            return (new_peak, total, mixed)

        peak, total, mixed = lax.fori_loop(
            0,
            steps,
            body,
            (
                jnp.full((1, width), MASKED, jnp.float32),
                jnp.zeros((1, width), jnp.float32),
                jnp.zeros((LANES, width), jnp.float32),
            ),
        )
        log_ref[0, which : which + 1, :] = peak + jnp.log(total)
        outs.append(mixed / total)
    joined = jnp.concatenate([outs[1][:HEAD_DIM], outs[0][HEAD_DIM:]], axis=0)
    rows = joined.T.astype(jnp.bfloat16)
    for head in range(heads):
        out_ref[:, head * LANES : (head + 1) * LANES] = rows[head * block : (head + 1) * block]


def attend(meta, queries, pairs, info, parts):
    chunks, block = (info.shape[0], info.shape[2])
    width = queries.shape[1]
    heads = width // LANES
    lines = pairs.shape[0]
    steps = 3 * chunks
    return pl.pallas_call(
        functools.partial(attend_kernel, parts, lines),
        grid_spec=pltpu.PrefetchScalarGridSpec(
            num_scalar_prefetch=1,
            grid=(chunks,),
            in_specs=[
                pl.BlockSpec((block, width), lambda i, m: (i, 0)),
                pl.BlockSpec(pairs.shape, lambda i, m: (0, 0, 0, 0)),
                pl.BlockSpec((1, 2, block), lambda i, m: (i, 0, 0)),
            ],
            out_specs=[
                pl.BlockSpec((block, width), lambda i, m: (i, 0)),
                pl.BlockSpec((1, 2, heads * block), lambda i, m: (i, 0, 0)),
            ],
        ),
        out_shape=[
            jax.ShapeDtypeStruct(queries.shape, jnp.bfloat16),
            jax.ShapeDtypeStruct((chunks, 2, heads * block), jnp.float32),
        ],
        compiler_params=pltpu.CompilerParams(vmem_limit_bytes=VMEM_LIMIT),
        cost_estimate=pl.CostEstimate(
            flops=steps * 2 * 2 * 2 * heads * block * block * LANES,
            bytes_accessed=queries.size * 4 + pairs.size * 2,
            transcendentals=steps * 2 * heads * block * block,
        ),
        name="attend",
    )(meta, queries, pairs, info)


def attend_back_kernel(parts, lines, meta_ref, query_ref, *refs):
    pair_ref, grad_ref, mixed_ref, log_ref, info_ref, cos_ref, sin_ref, query_out = refs[:8]
    pair_outs = refs[8 : 8 + lines]
    sums = refs[8 + lines]
    chunk = pl.program_id(0)
    block = query_ref.shape[0]
    heads = query_ref.shape[1] // LANES

    @pl.when(chunk == 0)
    def _():
        sums[...] = jnp.zeros_like(sums)

    stacked = stack_heads(query_ref[...])
    stacked_grad = stack_heads(grad_ref[...])
    product = stacked_grad.astype(jnp.float32) * stack_heads(mixed_ref[...]).astype(jnp.float32)
    lane = lax.broadcasted_iota(jnp.int32, stacked.shape, 1)
    place = jnp.concatenate([info_ref[0, 0:1, :]] * heads, axis=1)
    start = jnp.concatenate([info_ref[0, 1:2, :]] * heads, axis=1)
    base = chunk * (2 + parts)
    steps = meta_ref[base + 1] - meta_ref[base] + 1
    width = heads * block
    grads = []
    for which in range(2):
        is_key = (lane < HEAD_DIM) if which == 0 else (lane >= HEAD_DIM)
        queries = jnp.where(is_key, stacked, jnp.zeros_like(stacked))
        grad = jnp.where(is_key, jnp.zeros_like(stacked_grad), stacked_grad)
        own = jnp.where(is_key, 0.0, product)
        centre = lax.dot_general(
            jnp.ones((8, LANES), jnp.float32),
            own,
            (((1,), (1,)), ((), ())),
            precision=lax.Precision.HIGHEST,
            preferred_element_type=jnp.float32,
        )[0:1]
        logs = log_ref[0, which : which + 1, :]

        def body(step, grad_query):
            key_block, slot, at, shift = block_of(meta_ref, chunk, step, parts, lines)
            columns = slice(which * LANES, (which + 1) * LANES)
            pair = pair_ref[at, slot, :, columns]
            scores = dot_nt(pair, queries)
            key_place = key_block * block + lax.broadcasted_iota(jnp.int32, (block, width), 0)
            scores = jnp.where((key_place <= place) & (key_place >= start), scores, MASKED)
            weights = jnp.exp(scores - logs)
            grad_scores = (weights * (dot_nt(pair, grad) - centre)).astype(jnp.bfloat16)
            sums[shift, slot, :, columns] += dot_nn(grad_scores, queries) + dot_nn(
                weights.astype(jnp.bfloat16), grad
            )
            return grad_query + dot_tn(pair, grad_scores)

        grads.append(lax.fori_loop(0, steps, body, jnp.zeros((LANES, width), jnp.float32)))
    joined = jnp.concatenate([grads[0][:HEAD_DIM], grads[1][HEAD_DIM:]], axis=0)
    rows = joined.T * SCORE_SCALE
    cosine, sine = cos_ref[...], sin_ref[...]
    for head in range(heads):
        part = rows[head * block : (head + 1) * block]
        back = part * cosine - turn(part) * sine
        query_out[:, head * LANES : (head + 1) * LANES] = back.astype(jnp.bfloat16)

    @pl.when(chunk == pl.num_programs(0) - 1)
    def _():
        for line in range(lines):
            pair_outs[line][...] = sums[line].astype(jnp.bfloat16)


def attend_back(meta, queries, pairs, grad_mixed, mixed, logs, info, cosine, sine, parts):
    chunks, block = (info.shape[0], info.shape[2])
    width = queries.shape[1]
    heads = width // LANES
    lines = pairs.shape[0]
    shape = pairs.shape[1:]
    steps = 3 * chunks
    wide = pl.BlockSpec((block, width), lambda i, m: (i, 0))
    table = pl.BlockSpec((block, LANES), lambda i, m: (i, 0))
    whole = pl.BlockSpec(shape, lambda i, m: (0, 0, 0))
    outs = pl.pallas_call(
        functools.partial(attend_back_kernel, parts, lines),
        grid_spec=pltpu.PrefetchScalarGridSpec(
            num_scalar_prefetch=1,
            grid=(chunks,),
            in_specs=[
                wide,
                pl.BlockSpec(pairs.shape, lambda i, m: (0, 0, 0, 0)),
                wide,
                wide,
                pl.BlockSpec((1, 2, heads * block), lambda i, m: (i, 0, 0)),
                pl.BlockSpec((1, 2, block), lambda i, m: (i, 0, 0)),
                table,
                table,
            ],
            out_specs=[wide] + [whole] * lines,
            scratch_shapes=[pltpu.VMEM(pairs.shape, jnp.float32)],
        ),
        out_shape=[jax.ShapeDtypeStruct(queries.shape, jnp.bfloat16)]
        + [jax.ShapeDtypeStruct(shape, jnp.bfloat16)] * lines,
        compiler_params=pltpu.CompilerParams(vmem_limit_bytes=VMEM_LIMIT),
        cost_estimate=pl.CostEstimate(
            flops=steps * 2 * 5 * 2 * heads * block * block * LANES,
            bytes_accessed=queries.size * 8 + 2 * pairs.size * 2,
            transcendentals=steps * 2 * heads * block * block,
        ),
        name="attend_back",
    )(
        meta,
        queries,
        pairs,
        grad_mixed,
        mixed,
        logs,
        info,
        cosine,
        sine,
    )
    return (outs[0], [out.reshape(chunks * block, 2 * LANES) for out in outs[1:]])


def pair_back_kernel(*refs):
    *part_refs, cos_ref, sin_ref, out_ref = refs
    cosine, sine = cos_ref[...], sin_ref[...]
    lane = lax.broadcasted_iota(jnp.int32, cosine.shape, 1)
    for which in range(2):
        columns = slice(which * LANES, (which + 1) * LANES)
        total = part_refs[0][:, columns].astype(jnp.float32)
        for ref in part_refs[1:]:
            total = total + ref[:, columns].astype(jnp.float32)
        is_key = (lane < HEAD_DIM) if which == 0 else (lane >= HEAD_DIM)
        total = jnp.where(is_key, total * cosine - turn(total) * sine, total)
        out_ref[:, columns] = total.astype(jnp.bfloat16)


def pair_back(parts, cosine, sine, block):
    rows, columns = parts[0].shape
    tile = pl.BlockSpec((block, columns), lambda i: (i, 0))
    table = pl.BlockSpec((block, LANES), lambda i: (i, 0))
    return pl.pallas_call(
        pair_back_kernel,
        grid=(rows // block,),
        in_specs=[tile] * len(parts) + [table, table],
        out_specs=tile,
        out_shape=jax.ShapeDtypeStruct((rows, columns), jnp.bfloat16),
        compiler_params=pltpu.CompilerParams(vmem_limit_bytes=VMEM_LIMIT),
        name="pair_back",
    )(*parts, cosine, sine)


def update(refs, index, gradient, rate):
    weight, moment, square = [ref[index] for ref in refs[:3]]
    moment_new, square_new, weight_new = adamw_step(weight, gradient, moment, square, rate, 0.1)
    for ref, value in zip(refs[3:], (moment_new, square_new, weight_new)):
        ref[index] = value


def chosen(meta_ref, grad_refs, at, rows, columns):
    own_y = meta_ref[0] == at
    first = pl.program_id(0) == 0
    near = jnp.where(first, grad_refs[0][rows, columns], grad_refs[2][rows, columns])
    far = jnp.where(first, grad_refs[1][rows, columns], grad_refs[3][rows, columns])
    return jnp.where(own_y, near, far).astype(jnp.float32)


def joint_update_kernel(meta_ref, *refs):
    grad_refs, query_refs, pair_refs = (refs[:4], refs[4:7] + refs[10:13], refs[7:10] + refs[13:16])
    groups = query_refs[0].shape[1] // (2 * LANES)
    every = slice(None)
    for at in range(2):
        for j in range(groups):
            gradient = chosen(meta_ref, grad_refs, at, every, slice(j * LANES, (j + 1) * LANES))
            place = slice((2 * j + at) * LANES, (2 * j + at + 1) * LANES)
            update(query_refs, (every, place), gradient, D ** (-0.5))
        for which in range(2):
            start = (groups + which) * LANES
            gradient = chosen(meta_ref, grad_refs, at, every, slice(start, start + LANES))
            if which == 1:
                gradient = pltpu.roll(gradient, HEAD_DIM, 1)
            place = slice((2 * at + which) * LANES, (2 * at + which + 1) * LANES)
            update(pair_refs, (every, place), gradient, D ** (-0.5))


def joint_update(meta, grads, query, pair):
    half = grads[0].shape[0]

    def rows_of(array):
        return pl.BlockSpec((half, array.shape[1]), lambda i, m: ((m[1] + i) % 2, 0))

    whole = pl.BlockSpec(grads[0].shape, lambda i, m: (0, 0))
    blocks = [rows_of(array) for array in (*query, *pair)]
    return pl.pallas_call(
        joint_update_kernel,
        grid_spec=pltpu.PrefetchScalarGridSpec(
            num_scalar_prefetch=1, grid=(2,), in_specs=[whole] * 4 + blocks, out_specs=blocks
        ),
        out_shape=[jax.ShapeDtypeStruct(array.shape, array.dtype) for array in (*query, *pair)],
        compiler_params=pltpu.CompilerParams(vmem_limit_bytes=VMEM_LIMIT),
        cost_estimate=pl.CostEstimate(
            flops=20 * (query[0].size + pair[0].size),
            bytes_accessed=24 * (query[0].size + pair[0].size),
            transcendentals=0,
        ),
        name="joint_update",
    )(meta, *grads, *query, *pair)


def turned_update_kernel(rate, swapped, meta_ref, *refs):
    grad_refs, weight_refs = (refs[:4], refs[4:10])
    at = pl.program_id(1)
    width = grad_refs[0].shape[1]
    every = slice(None)
    for j, start in enumerate(range(0, width, LANES)):
        strip = slice(start, min(start + LANES, width))
        gradient = chosen(meta_ref, grad_refs, at, every, strip).T
        if swapped:
            gradient = jnp.concatenate([gradient[HEAD_DIM:], gradient[:HEAD_DIM]], axis=0)
            index = (j, 0)
        else:
            index = (strip, every)
        update(weight_refs, index, gradient, rate)


def turned_update(meta, grads, weights, rate, swapped):
    shape = weights[0].shape
    half, width = (shape[1] // 2, grads[0].shape[1])
    if swapped:
        weights = [w.reshape(width // LANES, 2, LANES, shape[1]) for w in weights]
        block = pl.BlockSpec(
            (width // LANES, 1, LANES, half), lambda i, at, m: (0, at, 0, (m[1] + i) % 2)
        )
    else:
        block = pl.BlockSpec((width, half), lambda i, at, m: (at, (m[1] + i) % 2))
    outs = pl.pallas_call(
        functools.partial(turned_update_kernel, rate, swapped),
        grid_spec=pltpu.PrefetchScalarGridSpec(
            num_scalar_prefetch=1,
            grid=(2, 2),
            in_specs=[pl.BlockSpec((half, width), lambda i, at, m: (0, 0))] * 4 + [block] * 3,
            out_specs=[block] * 3,
        ),
        out_shape=[jax.ShapeDtypeStruct(weights[0].shape, jnp.float32)] * 3,
        compiler_params=pltpu.CompilerParams(vmem_limit_bytes=VMEM_LIMIT),
        cost_estimate=pl.CostEstimate(
            flops=20 * weights[0].size, bytes_accessed=24 * weights[0].size, transcendentals=0
        ),
        name="turned_update",
    )(meta, *grads, *weights)
    return [out.reshape(shape) for out in outs]


def gateup_update_kernel(meta_ref, *refs):
    gate_refs, up_refs, weight_refs = (refs[:4], refs[4:8], refs[8:14])
    every = slice(None)
    gate, up = [
        jnp.concatenate([chosen(meta_ref, grads, at, every, every) for at in range(2)], axis=1)
        for grads in (gate_refs, up_refs)
    ]
    update(weight_refs, every, jnp.stack([gate, up], axis=1), D ** (-0.5))


def gateup_update(meta, shards, weights, rows):
    half, width = (shards[0].shape[0] // 3, shards[0].shape[1])
    shape = weights[0].shape
    tiles = half // rows
    gate = pl.BlockSpec((rows, width), lambda i, j, m: (tiles + j, 0))
    up = pl.BlockSpec((rows, width), lambda i, j, m: (2 * tiles + j, 0))
    block = pl.BlockSpec(
        (rows, 2, shape[2]), lambda i, j, m: (((m[1] + i) % 2) * tiles + j, 0, 0)
    )
    return pl.pallas_call(
        gateup_update_kernel,
        grid_spec=pltpu.PrefetchScalarGridSpec(
            num_scalar_prefetch=1,
            grid=(2, tiles),
            in_specs=[gate] * 4 + [up] * 4 + [block] * 3,
            out_specs=[block] * 3,
        ),
        out_shape=[jax.ShapeDtypeStruct(shape, jnp.float32)] * 3,
        compiler_params=pltpu.CompilerParams(vmem_limit_bytes=VMEM_LIMIT),
        cost_estimate=pl.CostEstimate(
            flops=20 * weights[0].size, bytes_accessed=28 * weights[0].size, transcendentals=0
        ),
        name="gateup_update",
    )(meta, *shards, *shards, *weights)


def on_device(
    sizes,
    block_input,
    cotangent,
    segments,
    norm_gains,
    w_query,
    w_keyvalue,
    w_output,
    w_gateup,
    w_down,
    gains_moment,
    gains_square,
    query_moment,
    query_square,
    keyvalue_moment,
    keyvalue_square,
    output_moment,
    output_square,
    gateup_moment,
    gateup_square,
    down_moment,
    down_square,
):
    rows_on, lines = sizes
    y, core, row, line = [lax.axis_index(name) for name in ("y", "core", "row", "col")]
    length = segments.shape[1]
    block = block_input.shape[0] // lines
    wide = block_input.shape[1]
    half = wide // 2
    slots = 2 * rows_on
    per_row = w_query.shape[1] // (KV_HEADS * HEAD_DIM)
    query_width = per_row * LANES
    hidden_here = w_gateup.shape[2] // 2

    def shift(value, axis, size, by):
        return lax.ppermute(value, axis, [(i, (i + by) % size) for i in range(size)])

    def other_core(value):
        return lax.ppermute(value, "core", [(0, 1), (1, 0)])

    def other_y(value):
        return lax.ppermute(value, "y", [(0, 1), (1, 0)])

    def place_of(y_at, core_at, row_at):
        return (y_at * 2 + core_at) * rows_on + row_at

    first_pairs, second_pairs = ([], [])
    for y_at in range(2):
        for core_at in range(2):
            for row_at in range(rows_on):
                over_row = (
                    place_of(y_at, core_at, row_at),
                    place_of(y_at, core_at, (row_at + 1) % rows_on),
                )
                over_y = (place_of(y_at, core_at, row_at), place_of(1 - y_at, core_at, row_at))
                first_pairs.append(over_row if core_at == 0 else over_y)
                second_pairs.append(over_y if core_at == 0 else over_row)
    near = ("y", "core", "row")

    def gather_tokens(own):
        if rows_on == 2:
            first = lax.ppermute(own, near, first_pairs)
            second = lax.ppermute(own, near, second_pairs)
            first, second = lax.optimization_barrier((first, second))
            third = lax.ppermute(first, near, second_pairs)
            return [own, first, second, third]
        parts = [own] + [shift(own, "row", rows_on, by) for by in range(1, rows_on)]
        return parts + [other_y(part) for part in parts]

    def reduce_tokens(
        rows_of, after_close=None, after_first=None, before_last=None, far_here=None, ready=None
    ):
        def same(value):
            return value

        after_close, after_first, before_last = [f or same for f in (after_close, after_first, before_last)]
        if rows_on == 2:
            far = rows_of(2, 4)
            if ready:
                far, close = ready((far, rows_of(0, 2)))
            third = lax.ppermute(far[block:], near, second_pairs)
            second = lax.ppermute(far[:block], near, second_pairs)
            if not ready:
                close = after_close(rows_of(0, 2))
            third, second = (far_here or lax.optimization_barrier)((third, second))
            key = (close[block:].astype(jnp.float32) + third.astype(jnp.float32)).astype(jnp.bfloat16)
            first = before_last(lax.ppermute(after_first(key), near, first_pairs))
            own = close[:block].astype(jnp.float32) + second.astype(jnp.float32)
            return own + first.astype(jnp.float32)
        partial = after_close(rows_of(0, slots))
        parts = [partial[i * block : (i + 1) * block] for i in range(slots)]
        sums = [
            parts[i].astype(jnp.float32) + other_y(parts[rows_on + i]).astype(jnp.float32)
            for i in range(rows_on)
        ]
        sums[0] = after_first(sums[0])
        total = sums[0]
        for by in range(1, rows_on):
            moved = shift(sums[by].astype(jnp.bfloat16), "row", rows_on, -by)
            total = total + moved.astype(jnp.float32)
        return before_last(total)

    def product(left, right):
        def rows_of(first, last):
            return dot_nt(left[first * block : last * block], right).astype(jnp.bfloat16)

        return rows_of

    if rows_on == 2:
        slot_y = [y, jnp.where(core == 0, y, 1 - y), jnp.where(core == 0, 1 - y, y), 1 - y]
        slot_row = [row, jnp.where(core == 0, 1 - row, row), jnp.where(core == 0, row, 1 - row), 1 - row]
    else:
        slot_y = [y] * rows_on + [1 - y] * rows_on
        slot_row = [(row - by) % rows_on for by in range(rows_on)] * 2

    def pick(parts, index):
        return lax.dynamic_index_in_dim(jnp.stack(parts), index, 0, keepdims=False)

    def tokens_sent(values):
        parts = []
        for by in range(lines):
            part = lax.dynamic_slice_in_dim(values, ((line + by) % lines) * block, block, 0)
            parts.append(part if by == 0 else shift(part, "col", lines, by))
        return parts

    def tokens_of(parts):
        blocks = [pick(parts, (line - at) % lines) for at in range(lines)]
        return jnp.concatenate([b[:, :half] for b in blocks] + [b[:, half:] for b in blocks], axis=1)

    def features_sent(values):
        blocks = [
            jnp.concatenate(
                [
                    values[:, at * half : (at + 1) * half],
                    values[:, D // 2 + at * half : D // 2 + (at + 1) * half],
                ],
                axis=1,
            )
            for at in range(lines)
        ]
        parts = []
        for by in range(lines):
            part = pick(blocks, (line + by) % lines)
            parts.append(part if by == 0 else shift(part, "col", lines, by))
        return parts

    def features_of(parts):
        return jnp.concatenate([pick(parts, (line - at) % lines) for at in range(lines)], axis=0)

    def half_rows(values):
        return lax.dynamic_slice_in_dim(values, core * half, half, 0)

    def half_columns(values):
        return lax.dynamic_slice_in_dim(values, core * half, half, 1)

    def gather_weight(piece):
        return lax.all_gather(piece, ("core", "col"), axis=0, tiled=True)

    query_rows = half_rows(w_query).astype(jnp.bfloat16)
    pair_rows = half_rows(w_keyvalue).astype(jnp.bfloat16)

    def joint_of(at):
        pieces = [
            query_rows[:, (2 * j + at) * LANES : (2 * j + at + 1) * LANES] for j in range(per_row)
        ]
        pair = pair_rows[:, at * 2 * LANES : (at + 1) * 2 * LANES]
        pieces += [
            pair[:, :LANES],
            pair[:, LANES + HEAD_DIM :],
            pair[:, LANES : LANES + HEAD_DIM],
        ]
        return jnp.concatenate(pieces, axis=1)

    joint_mine = jnp.where(y == 0, joint_of(0), joint_of(1))
    output_columns = half_columns(w_output).astype(jnp.bfloat16)

    def output_of(at):
        pieces = []
        for j in range(per_row):
            base = (2 * j + at) * LANES
            pieces += [
                output_columns[base + HEAD_DIM : base + LANES],
                output_columns[base : base + HEAD_DIM],
            ]
        return jnp.concatenate(pieces, axis=0)

    output_mine = jnp.where(y == 0, output_of(0), output_of(1)).T
    gateup_mine = lax.dynamic_slice(
        w_gateup, (core * half, 0, y * hidden_here), (half, 2, hidden_here)
    ).astype(jnp.bfloat16)
    gateup_mine = jnp.concatenate([gateup_mine[:, 0], gateup_mine[:, 1]], axis=1)
    down_mine = lax.dynamic_slice(
        w_down, (y * hidden_here, core * half), (hidden_here, half)
    ).astype(jnp.bfloat16).T

    gain_parts = [norm_gains] + [shift(norm_gains, "col", lines, by) for by in range(1, lines)]
    gain_blocks = [pick(gain_parts, (line - at) % lines) for at in range(lines)]
    gains = jnp.concatenate(
        [b[:, :half] for b in gain_blocks] + [b[:, half:] for b in gain_blocks], axis=1
    )

    own_starts = document_starts(segments[0])
    other_starts = document_starts(other_y(segments)[0])
    frequency = 10000.0 ** (-2.0 * jnp.arange(HEAD_DIM // 2, dtype=jnp.float32) / HEAD_DIM)
    starts, places, meta = ([], [], [])
    for slot in range(slots):
        begin = slot_row[slot] * (lines * block) + line * block
        of_chunk = lax.dynamic_slice_in_dim(
            jnp.where(slot_y[slot] == y, own_starts, other_starts), begin, block, 0
        )
        starts.append(of_chunk)
        places.append(begin + jnp.arange(block, dtype=jnp.int32))
        meta += [of_chunk[0] // block, begin // block]
        for row_at in range(rows_on):
            found = jnp.int32(0)
            for other in range(slots):
                same = (slot_y[other] == slot_y[slot]) & (slot_row[other] == row_at)
                found = found + jnp.where(same, other, 0)
            meta.append(found)
    meta = jnp.stack([jnp.asarray(m, jnp.int32) for m in meta + [line]])
    starts, places = (jnp.stack(starts), jnp.stack(places))
    info = jnp.stack([places, starts], axis=1)
    offsets = (places - starts).astype(jnp.float32).reshape(-1)
    phases = offsets[:, None] * jnp.tile(frequency, LANES // (HEAD_DIM // 2))[None, :]
    cosine, sine = (jnp.cos(phases), jnp.sin(phases))

    residual_low = tokens_of(tokens_sent(block_input))
    residual_low, late_cotangent, joint_mine, output_mine = lax.optimization_barrier(
        (residual_low, cotangent, joint_mine, output_mine)
    )
    cot_parts = tokens_sent(late_cotangent)
    first_weight = gather_weight(jnp.concatenate([joint_mine, output_mine], axis=1))
    joint_width = joint_mine.shape[1]
    joint_weight, output_weight = (first_weight[:, :joint_width], first_weight[:, joint_width:])
    residual = residual_low.astype(jnp.float32)
    scale_one = lax.rsqrt(jnp.mean(residual * residual, axis=1, keepdims=True) + EPSILON)
    normed_parts = gather_tokens((residual * scale_one * gains[0]).astype(jnp.bfloat16))
    normed_parts, cot_parts = lax.optimization_barrier((normed_parts, cot_parts))
    cot_low = tokens_of(cot_parts)
    cot_chunks = gather_tokens(cot_low)
    queries, pair = project(normed_parts, first_weight, joint_width, cosine, sine, query_width)
    pairs = lax.all_gather(pair.reshape(slots, block, 2 * LANES), "col", axis=0, tiled=False)
    pairs, cot_chunks, gateup_mine, down_mine = lax.optimization_barrier(
        (pairs, cot_chunks, gateup_mine, down_mine)
    )
    gateup_weight = gather_weight(gateup_mine)
    down_weight = gather_weight(down_mine)
    mixed, logs = attend(meta, queries, pairs, info, rows_on)
    attn_sum = reduce_tokens(product(mixed, output_weight))
    middle = residual + attn_sum
    scale_two = lax.rsqrt(jnp.mean(middle * middle, axis=1, keepdims=True) + EPSILON)
    two_parts = gather_tokens((middle * scale_two * gains[1]).astype(jnp.bfloat16))
    hidden, factor, silu_gate = widen(two_parts, gateup_weight)
    normed_two, cot = (jnp.concatenate(two_parts, axis=0), jnp.concatenate(cot_chunks, axis=0))

    def other_half(rows, grad):
        rows = lax.dynamic_slice_in_dim(rows, (1 - core) * (D // 2), D // 2, 1)
        return other_core(dot_tn(rows, grad).astype(jnp.bfloat16))

    def own_half(rows, grad, received):
        rows = lax.dynamic_slice_in_dim(rows, core * (D // 2), D // 2, 1)
        total = dot_tn(rows, grad) + received.astype(jnp.float32)
        return total.astype(jnp.bfloat16)

    def scatter(total):
        return lax.psum_scatter(total, "col", scatter_dimension=0, tiled=True)

    def collect(piece):
        near_y = other_y(piece)
        return [piece, near_y, other_core(piece), other_core(near_y)]

    down_total = own_half(cot, hidden, other_half(cot, hidden))
    down_total, down_weight = lax.optimization_barrier((down_total, down_weight))
    down_piece = scatter(down_total)
    work = {}

    def feed_back(first, last):
        work["grad_gate"], work["grad_up"], partial = widen_back(
            cot_chunks[first:last],
            down_weight,
            gateup_weight,
            factor,
            silu_gate,
            first,
            [work[name] for name in ("grad_gate", "grad_up") if name in work],
        )
        return partial

    def feed_others(close):
        close, rows, gate, up = lax.optimization_barrier(
            (close, normed_two, work["grad_gate"], work["grad_up"])
        )
        work["feed"] = (rows, gate, up, other_half(rows, gate), other_half(rows, up))
        return close

    def feed_owns(key):
        key, rows, gate, up, gate_other, up_other = lax.optimization_barrier((key, *work["feed"]))
        work["totals"] = (own_half(rows, gate, gate_other), own_half(rows, up, up_other))
        return key

    def feed_ends(first):
        first, work["down_piece"] = lax.optimization_barrier((first, down_piece))
        return first

    grad_normed_two = reduce_tokens(feed_back, feed_others, feed_owns, feed_ends)
    gate_piece, up_piece = [scatter(total) for total in work["totals"]]

    def norm_back(values, scale, grad_normed, gain):
        scaled = grad_normed * gain
        total = jnp.sum(scaled * values, axis=1, keepdims=True)
        return scale * scaled - values * (scale**3 * total / D)

    grad_middle = cot_low.astype(jnp.float32) + norm_back(
        middle, scale_two, grad_normed_two, gains[1]
    )
    gain_two = jnp.sum(grad_normed_two * middle * scale_two, axis=0)

    grad_middle_low, late_hidden = lax.optimization_barrier(
        (grad_middle.astype(jnp.bfloat16), hidden)
    )
    back = jnp.concatenate(gather_tokens(grad_middle_low), axis=0)

    def back_here(products):
        products, work["back"] = lax.optimization_barrier((products, back))
        return products

    def attention_back(far):
        here = work.get("back", back)
        grad_query, grad_parts = attend_back(
            meta,
            queries,
            pairs,
            dot_nn(here, output_weight).astype(jnp.bfloat16),
            mixed,
            logs,
            info,
            cosine,
            sine,
            rows_on,
        )
        work["grad_parts"] = [grad_parts[0]] + [
            shift(grad_parts[by], "col", lines, -by) for by in range(1, lines)
        ]
        names = ("grad_query", "gate_piece", "back", "mixed")
        far, *values = lax.optimization_barrier((far, grad_query, gate_piece, here, mixed))
        work.update(zip(names, values))
        return far

    def keys_arrive(first):
        first, work["grad_parts"] = lax.optimization_barrier((first, work["grad_parts"]))
        return first

    if rows_on == 2:
        ffn_sum = reduce_tokens(
            product(late_hidden, down_weight), None, None, keys_arrive, attention_back, back_here
        )
    else:
        ffn_sum = attention_back(reduce_tokens(product(late_hidden, down_weight)))
    grad_query, gate_piece, back, mixed = [
        work[name] for name in ("grad_query", "gate_piece", "back", "mixed")
    ]
    output_total = own_half(back, mixed, other_half(back, mixed))
    layer_output = features_of(features_sent((middle + ffn_sum).astype(jnp.bfloat16)))
    grad_keyvalue = pair_back(work["grad_parts"], cosine, sine, block)
    grad_joint = jnp.concatenate([grad_query, grad_keyvalue], axis=1)
    normed_one = jnp.concatenate(normed_parts, axis=0)
    def joint_others(close):
        close, up_done, work["output"], rows, grad = lax.optimization_barrier(
            (close, up_piece, output_total, normed_one, grad_joint)
        )
        work["feed_shards"] = collect(
            jnp.concatenate([work["down_piece"], gate_piece, up_done], axis=0)
        )
        work["joint"] = (rows, grad, other_half(rows, grad))
        return close

    def joint_owns(key):
        key, rows, grad, other = lax.optimization_barrier((key, *work["joint"]))
        work["joint_total"] = own_half(rows, grad, other)
        return key

    grad_normed_one = reduce_tokens(product(grad_joint, joint_weight), joint_others, joint_owns)
    joint_piece, output_piece = (scatter(work["joint_total"]), scatter(work["output"]))
    meta_core = jnp.stack([y, core]).astype(jnp.int32)
    gateup_new = gateup_update(
        meta_core, work["feed_shards"], [w_gateup, gateup_moment, gateup_square], 32
    )
    down_new = turned_update(
        meta_core,
        work["feed_shards"],
        [w_down, down_moment, down_square],
        FF ** (-0.5),
        False,
    )
    input_grad = grad_middle + norm_back(residual, scale_one, grad_normed_one, gains[0])
    gain_one = jnp.sum(grad_normed_one * residual * scale_one, axis=0)
    input_grad, layer_output = lax.optimization_barrier(
        (input_grad.astype(jnp.bfloat16), layer_output)
    )
    input_parts, gateup_new, down_new = lax.optimization_barrier(
        (features_sent(input_grad), gateup_new, down_new)
    )
    input_grad = features_of(input_parts).astype(jnp.float32)
    pair_piece = joint_piece[:, query_width:]
    pair_total = pair_piece.astype(jnp.float32)
    for by in range(1, rows_on):
        pair_total = pair_total + shift(pair_piece, "row", rows_on, by).astype(jnp.float32)
    joint_piece = jnp.concatenate(
        [joint_piece[:, :query_width], pair_total.astype(jnp.bfloat16)], axis=1
    )
    joint_new = joint_update(
        meta_core,
        collect(joint_piece),
        [w_query, query_moment, query_square],
        [w_keyvalue, keyvalue_moment, keyvalue_square],
    )
    output_new = turned_update(
        meta_core,
        collect(output_piece),
        [w_output, output_moment, output_square],
        (HEADS * HEAD_DIM // 64) ** (-0.5),
        True,
    )

    gain_sums = jnp.stack([gain_one, gain_two])
    blocks = [
        jnp.concatenate(
            [
                gain_sums[:, at * half : (at + 1) * half],
                gain_sums[:, D // 2 + at * half : D // 2 + (at + 1) * half],
            ],
            axis=1,
        )
        for at in range(lines)
    ]
    grad_gains = pick(blocks, line)
    for by in range(1, lines):
        grad_gains = grad_gains + shift(pick(blocks, (line + by) % lines), "col", lines, by)
    for axis, size in (("core", 2), ("y", 2), ("row", rows_on)):
        blocks_total = grad_gains
        for by in range(1, size):
            grad_gains = grad_gains + shift(blocks_total, axis, size, by)

    gains_new = adamw_step(norm_gains, grad_gains, gains_moment, gains_square, 0.6, 0.0)
    return (
        layer_output,
        input_grad,
        *gains_new,
        *joint_new,
        *output_new,
        *gateup_new,
        *down_new,
    )


def solution(mesh):
    dp, rows_on, lines = (mesh.shape["dp"], mesh.shape["row"], mesh.shape["col"])
    split = Mesh(mesh.devices.reshape(dp // 2, 2, rows_on, lines), ("y", "core", "row", "col"))
    tokens = P(("y", "core", "row"), "col")
    narrow, wide = (P("col", "row"), P("row", "col"))
    gains, pair, gateup = (P(None, "col"), P("col", None), P("col", None, "row"))
    return jax.shard_map(
        functools.partial(on_device, (rows_on, lines)),
        mesh=split,
        in_specs=(
            tokens,
            tokens,
            P(("y", "core"), None),
            gains,
            narrow,
            pair,
            wide,
            gateup,
            wide,
            gains,
            gains,
            narrow,
            narrow,
            pair,
            pair,
            wide,
            wide,
            gateup,
            gateup,
            wide,
            wide,
        ),
        out_specs=(tokens, tokens)
        + (gains,) * 3
        + (narrow,) * 3
        + (pair,) * 3
        + (wide,) * 3
        + (gateup,) * 3
        + (wide,) * 3,
        check_vma=False,
    )
```

```python
import functools

import jax
import jax.numpy as jnp
from jax import lax
from jax.experimental import pallas as pl
from jax.experimental.pallas import tpu as pltpu
from jax.sharding import Mesh, PartitionSpec as P

D = 2048
HEADS = 32
KV_HEADS = 4
HEAD_DIM = 64
FF = 5632
STEP = 10

EPSILON = 1e-05
BETA_ONE = 0.9
BETA_TWO = 0.999
ADAM_EPS = 1e-08
MASKED = -1e30
SCORE_SCALE = HEAD_DIM ** (-0.5)
LANES = 128
VMEM_LIMIT = 48 * 1024 * 1024


def dot_nn(left, right):
    return lax.dot_general(left, right, (((1,), (0,)), ((), ())), preferred_element_type=jnp.float32)


def dot_nt(left, right):
    return lax.dot_general(left, right, (((1,), (1,)), ((), ())), preferred_element_type=jnp.float32)


def dot_tn(left, right):
    return lax.dot_general(left, right, (((0,), (0,)), ((), ())), preferred_element_type=jnp.float32)


def adamw_step(weight, gradient, moment, square, step_rate, decay_rate):
    moment_new = BETA_ONE * moment + (1.0 - BETA_ONE) * gradient
    square_new = BETA_TWO * square + (1.0 - BETA_TWO) * gradient * gradient
    fixed_one = moment_new / (1.0 - BETA_ONE**STEP)
    fixed_two = square_new / (1.0 - BETA_TWO**STEP)
    weight_new = weight - step_rate * (
        fixed_one / (jnp.sqrt(fixed_two) + ADAM_EPS) + decay_rate * weight
    )
    return (moment_new, square_new, weight_new)


def document_starts(segment_ids):
    places = jnp.arange(segment_ids.shape[0], dtype=jnp.int32)
    starts = jnp.concatenate([jnp.ones((1,), jnp.bool_), segment_ids[1:] != segment_ids[:-1]])
    return lax.cummax(jnp.where(starts, places, 0), axis=0)


def turn(values):
    lane = lax.broadcasted_iota(jnp.int32, values.shape, 1)
    ahead = pltpu.roll(values, LANES - HEAD_DIM // 2, 1)
    behind = pltpu.roll(values, HEAD_DIM // 2, 1)
    return jnp.where(lane % HEAD_DIM < HEAD_DIM // 2, -ahead, behind)


def take_chunk(rows_refs, held_ref):
    for at, ref in enumerate(rows_refs):

        @pl.when(pl.program_id(0) == at)
        def _(ref=ref):
            held_ref[...] = ref[...]


def project_kernel(slots, *refs):
    rows_refs, (weight_ref, cos_ref, sin_ref, query_ref, pair_ref, held_ref) = (refs[:slots], refs[slots:])
    take_chunk(rows_refs, held_ref)
    sums = dot_nn(held_ref[...], weight_ref[...])
    cosine, sine = cos_ref[...], sin_ref[...]
    width = query_ref.shape[1]
    lane = lax.broadcasted_iota(jnp.int32, cosine.shape, 1)
    for start in range(0, width, LANES):
        part = sums[:, start : start + LANES]
        turned = (part * cosine + turn(part) * sine).astype(jnp.bfloat16)
        query_ref[:, start : start + LANES] = turned * jnp.bfloat16(SCORE_SCALE)
    for which in range(2):
        part = sums[:, width + which * LANES : width + (which + 1) * LANES]
        is_key = (lane < HEAD_DIM) if which == 0 else (lane >= HEAD_DIM)
        turned = jnp.where(is_key, part * cosine + turn(part) * sine, part)
        pair_ref[:, which * LANES : (which + 1) * LANES] = turned.astype(jnp.bfloat16)


def project(chunks, weight, total, cosine, sine, width):
    slots = len(chunks)
    block, depth = chunks[0].shape
    rows = slots * block
    whole = pl.BlockSpec((block, depth), lambda i: (0, 0))
    return pl.pallas_call(
        functools.partial(project_kernel, slots),
        grid=(slots,),
        in_specs=[whole] * slots
        + [
            pl.BlockSpec((depth, total), lambda i: (0, 0)),
            pl.BlockSpec((block, LANES), lambda i: (i, 0)),
            pl.BlockSpec((block, LANES), lambda i: (i, 0)),
        ],
        out_specs=[
            pl.BlockSpec((block, width), lambda i: (i, 0)),
            pl.BlockSpec((block, total - width), lambda i: (i, 0)),
        ],
        out_shape=[
            jax.ShapeDtypeStruct((rows, width), jnp.bfloat16),
            jax.ShapeDtypeStruct((rows, total - width), jnp.bfloat16),
        ],
        scratch_shapes=[pltpu.VMEM((block, depth), jnp.bfloat16)],
        compiler_params=pltpu.CompilerParams(vmem_limit_bytes=VMEM_LIMIT),
        cost_estimate=pl.CostEstimate(
            flops=2 * rows * depth * total,
            bytes_accessed=(rows + total) * depth * 2,
            transcendentals=0,
        ),
        name="project",
    )(*chunks, weight, cosine, sine)


def widen_kernel(slots, *refs):
    rows_refs, (weight_ref, hidden_ref, factor_ref, silu_ref, held_ref) = (refs[:slots], refs[slots:])
    take_chunk(rows_refs, held_ref)
    sums = dot_nn(held_ref[...], weight_ref[...])
    width = hidden_ref.shape[1]
    gate, upward = (sums[:, :width], sums[:, width:])
    sigmoid = jax.nn.sigmoid(gate)
    silu = gate * sigmoid
    hidden_ref[...] = (silu * upward).astype(jnp.bfloat16)
    factor_ref[...] = (upward * sigmoid * (1.0 + gate * (1.0 - sigmoid))).astype(jnp.bfloat16)
    silu_ref[...] = silu.astype(jnp.bfloat16)


def widen(chunks, weight):
    slots = len(chunks)
    block, depth = chunks[0].shape
    width = weight.shape[1] // 2
    rows = slots * block
    once = pl.Buffered(1)
    return pl.pallas_call(
        functools.partial(widen_kernel, slots),
        grid=(slots,),
        in_specs=[pl.BlockSpec((block, depth), lambda i: (0, 0), pipeline_mode=once)] * slots
        + [pl.BlockSpec(weight.shape, lambda i: (0, 0), pipeline_mode=once)],
        out_specs=[pl.BlockSpec((block, width), lambda i: (i, 0))] * 3,
        out_shape=[jax.ShapeDtypeStruct((rows, width), jnp.bfloat16)] * 3,
        scratch_shapes=[pltpu.VMEM((block, depth), jnp.bfloat16)],
        compiler_params=pltpu.CompilerParams(vmem_limit_bytes=VMEM_LIMIT),
        cost_estimate=pl.CostEstimate(
            flops=4 * rows * depth * width,
            bytes_accessed=(rows + 2 * width) * depth * 2 + 6 * rows * width,
            transcendentals=rows * width,
        ),
        name="widen",
    )(*chunks, weight)


def widen_back_kernel(slots, kept, *refs):
    rows_refs, refs = (refs[:slots], refs[slots:])
    down_ref, gateup_ref, factor_ref, silu_ref = refs[:4]
    gate_ref, up_ref, partial_ref, held_ref = refs[4 + kept :]
    take_chunk(rows_refs, held_ref)
    grad_hidden = dot_nn(held_ref[...], down_ref[...])
    gate = (grad_hidden * factor_ref[...].astype(jnp.float32)).astype(jnp.bfloat16)
    up = (grad_hidden * silu_ref[...].astype(jnp.float32)).astype(jnp.bfloat16)
    gate_ref[...] = gate
    up_ref[...] = up
    both = jnp.concatenate([gate, up], axis=1)
    partial_ref[...] = dot_nt(both, gateup_ref[...]).astype(jnp.bfloat16)


def widen_back(chunks, down, gateup, factor, silu, first, kept):
    slots = len(chunks)
    block, depth = chunks[0].shape
    width = down.shape[1]
    once = pl.Buffered(1)
    tile = pl.BlockSpec((block, width), lambda i: (first + i, 0))
    return pl.pallas_call(
        functools.partial(widen_back_kernel, slots, len(kept)),
        grid=(slots,),
        in_specs=[pl.BlockSpec((block, depth), lambda i: (0, 0), pipeline_mode=once)] * slots
        + [
            pl.BlockSpec(down.shape, lambda i: (0, 0), pipeline_mode=once),
            pl.BlockSpec(gateup.shape, lambda i: (0, 0), pipeline_mode=once),
            tile,
            tile,
        ]
        + [pl.BlockSpec(memory_space=pl.ANY)] * len(kept),
        out_specs=[tile, tile, pl.BlockSpec((block, depth), lambda i: (i, 0))],
        out_shape=[jax.ShapeDtypeStruct(factor.shape, jnp.bfloat16)] * 2
        + [jax.ShapeDtypeStruct((slots * block, depth), jnp.bfloat16)],
        scratch_shapes=[pltpu.VMEM((block, depth), jnp.bfloat16)],
        input_output_aliases={slots + 4 + i: i for i in range(len(kept))},
        compiler_params=pltpu.CompilerParams(vmem_limit_bytes=VMEM_LIMIT),
        cost_estimate=pl.CostEstimate(
            flops=6 * slots * block * depth * width,
            bytes_accessed=3 * width * depth * 2 + 8 * slots * block * width,
            transcendentals=0,
        ),
        name="widen_back",
    )(*chunks, down, gateup, factor, silu, *kept)


def stack_heads(values):
    return jnp.concatenate(
        [values[:, start : start + LANES] for start in range(0, values.shape[1], LANES)], axis=0
    )


def block_of(meta_ref, chunk, step, parts, lines):
    base = chunk * (2 + parts)
    key_block = meta_ref[base + 1] - step
    slot = meta_ref[base + 2 + key_block // lines]
    own_line = meta_ref[pl.num_programs(0) * (2 + parts)]
    line = lax.rem(key_block, lines)
    return (key_block, slot, line, lax.rem(own_line - line + lines, lines))


def attend_kernel(parts, lines, meta_ref, query_ref, pair_ref, info_ref, out_ref, log_ref):
    chunk = pl.program_id(0)
    block = query_ref.shape[0]
    heads = query_ref.shape[1] // LANES
    stacked = stack_heads(query_ref[...])
    lane = lax.broadcasted_iota(jnp.int32, stacked.shape, 1)
    place = jnp.concatenate([info_ref[0, 0:1, :]] * heads, axis=1)
    start = jnp.concatenate([info_ref[0, 1:2, :]] * heads, axis=1)
    base = chunk * (2 + parts)
    steps = meta_ref[base + 1] - meta_ref[base] + 1
    width = heads * block
    outs = []
    for which in range(2):
        is_key = (lane < HEAD_DIM) if which == 0 else (lane >= HEAD_DIM)
        queries = jnp.where(is_key, stacked, jnp.zeros_like(stacked))

        def body(step, carry):
            peak, total, mixed = carry
            key_block, slot, at, _ = block_of(meta_ref, chunk, step, parts, lines)
            pair = pair_ref[at, slot, :, which * LANES : (which + 1) * LANES]
            scores = dot_nt(pair, queries)
            key_place = key_block * block + lax.broadcasted_iota(jnp.int32, (block, width), 0)
            scores = jnp.where((key_place <= place) & (key_place >= start), scores, MASKED)
            new_peak = jnp.maximum(peak, jnp.max(scores, axis=0, keepdims=True))
            weights = jnp.exp(scores - new_peak)
            shrink = jnp.exp(peak - new_peak)
            total = total * shrink + jnp.sum(weights, axis=0, keepdims=True)
            mixed = mixed * shrink + dot_tn(pair, weights.astype(jnp.bfloat16))
            return (new_peak, total, mixed)

        peak, total, mixed = lax.fori_loop(
            0,
            steps,
            body,
            (
                jnp.full((1, width), MASKED, jnp.float32),
                jnp.zeros((1, width), jnp.float32),
                jnp.zeros((LANES, width), jnp.float32),
            ),
        )
        log_ref[0, which : which + 1, :] = peak + jnp.log(total)
        outs.append(mixed / total)
    joined = jnp.concatenate([outs[1][:HEAD_DIM], outs[0][HEAD_DIM:]], axis=0)
    rows = joined.T.astype(jnp.bfloat16)
    for head in range(heads):
        out_ref[:, head * LANES : (head + 1) * LANES] = rows[head * block : (head + 1) * block]


def attend(meta, queries, pairs, info, parts):
    chunks, block = (info.shape[0], info.shape[2])
    width = queries.shape[1]
    heads = width // LANES
    lines = pairs.shape[0]
    steps = 3 * chunks
    return pl.pallas_call(
        functools.partial(attend_kernel, parts, lines),
        grid_spec=pltpu.PrefetchScalarGridSpec(
            num_scalar_prefetch=1,
            grid=(chunks,),
            in_specs=[
                pl.BlockSpec((block, width), lambda i, m: (i, 0)),
                pl.BlockSpec(pairs.shape, lambda i, m: (0, 0, 0, 0)),
                pl.BlockSpec((1, 2, block), lambda i, m: (i, 0, 0)),
            ],
            out_specs=[
                pl.BlockSpec((block, width), lambda i, m: (i, 0)),
                pl.BlockSpec((1, 2, heads * block), lambda i, m: (i, 0, 0)),
            ],
        ),
        out_shape=[
            jax.ShapeDtypeStruct(queries.shape, jnp.bfloat16),
            jax.ShapeDtypeStruct((chunks, 2, heads * block), jnp.float32),
        ],
        compiler_params=pltpu.CompilerParams(vmem_limit_bytes=VMEM_LIMIT),
        cost_estimate=pl.CostEstimate(
            flops=steps * 2 * 2 * 2 * heads * block * block * LANES,
            bytes_accessed=queries.size * 4 + pairs.size * 2,
            transcendentals=steps * 2 * heads * block * block,
        ),
        name="attend",
    )(meta, queries, pairs, info)


def attend_back_kernel(parts, lines, meta_ref, query_ref, *refs):
    pair_ref, grad_ref, mixed_ref, log_ref, info_ref, cos_ref, sin_ref, query_out = refs[:8]
    pair_outs = refs[8 : 8 + lines]
    sums = refs[8 + lines]
    chunk = pl.program_id(0)
    block = query_ref.shape[0]
    heads = query_ref.shape[1] // LANES

    @pl.when(chunk == 0)
    def _():
        sums[...] = jnp.zeros_like(sums)

    stacked = stack_heads(query_ref[...])
    stacked_grad = stack_heads(grad_ref[...])
    product = stacked_grad.astype(jnp.float32) * stack_heads(mixed_ref[...]).astype(jnp.float32)
    lane = lax.broadcasted_iota(jnp.int32, stacked.shape, 1)
    place = jnp.concatenate([info_ref[0, 0:1, :]] * heads, axis=1)
    start = jnp.concatenate([info_ref[0, 1:2, :]] * heads, axis=1)
    base = chunk * (2 + parts)
    steps = meta_ref[base + 1] - meta_ref[base] + 1
    width = heads * block
    grads = []
    for which in range(2):
        is_key = (lane < HEAD_DIM) if which == 0 else (lane >= HEAD_DIM)
        queries = jnp.where(is_key, stacked, jnp.zeros_like(stacked))
        grad = jnp.where(is_key, jnp.zeros_like(stacked_grad), stacked_grad)
        own = jnp.where(is_key, 0.0, product)
        centre = lax.dot_general(
            jnp.ones((8, LANES), jnp.float32),
            own,
            (((1,), (1,)), ((), ())),
            precision=lax.Precision.HIGHEST,
            preferred_element_type=jnp.float32,
        )[0:1]
        logs = log_ref[0, which : which + 1, :]

        def body(step, grad_query):
            key_block, slot, at, shift = block_of(meta_ref, chunk, step, parts, lines)
            columns = slice(which * LANES, (which + 1) * LANES)
            pair = pair_ref[at, slot, :, columns]
            scores = dot_nt(pair, queries)
            key_place = key_block * block + lax.broadcasted_iota(jnp.int32, (block, width), 0)
            scores = jnp.where((key_place <= place) & (key_place >= start), scores, MASKED)
            weights = jnp.exp(scores - logs)
            grad_scores = (weights * (dot_nt(pair, grad) - centre)).astype(jnp.bfloat16)
            sums[shift, slot, :, columns] += dot_nn(grad_scores, queries) + dot_nn(
                weights.astype(jnp.bfloat16), grad
            )
            return grad_query + dot_tn(pair, grad_scores)

        grads.append(lax.fori_loop(0, steps, body, jnp.zeros((LANES, width), jnp.float32)))
    joined = jnp.concatenate([grads[0][:HEAD_DIM], grads[1][HEAD_DIM:]], axis=0)
    rows = joined.T * SCORE_SCALE
    cosine, sine = cos_ref[...], sin_ref[...]
    for head in range(heads):
        part = rows[head * block : (head + 1) * block]
        back = part * cosine - turn(part) * sine
        query_out[:, head * LANES : (head + 1) * LANES] = back.astype(jnp.bfloat16)

    @pl.when(chunk == pl.num_programs(0) - 1)
    def _():
        for line in range(lines):
            pair_outs[line][...] = sums[line].astype(jnp.bfloat16)


def attend_back(meta, queries, pairs, grad_mixed, mixed, logs, info, cosine, sine, parts):
    chunks, block = (info.shape[0], info.shape[2])
    width = queries.shape[1]
    heads = width // LANES
    lines = pairs.shape[0]
    shape = pairs.shape[1:]
    steps = 3 * chunks
    wide = pl.BlockSpec((block, width), lambda i, m: (i, 0))
    table = pl.BlockSpec((block, LANES), lambda i, m: (i, 0))
    whole = pl.BlockSpec(shape, lambda i, m: (0, 0, 0))
    outs = pl.pallas_call(
        functools.partial(attend_back_kernel, parts, lines),
        grid_spec=pltpu.PrefetchScalarGridSpec(
            num_scalar_prefetch=1,
            grid=(chunks,),
            in_specs=[
                wide,
                pl.BlockSpec(pairs.shape, lambda i, m: (0, 0, 0, 0)),
                wide,
                wide,
                pl.BlockSpec((1, 2, heads * block), lambda i, m: (i, 0, 0)),
                pl.BlockSpec((1, 2, block), lambda i, m: (i, 0, 0)),
                table,
                table,
            ],
            out_specs=[wide] + [whole] * lines,
            scratch_shapes=[pltpu.VMEM(pairs.shape, jnp.float32)],
        ),
        out_shape=[jax.ShapeDtypeStruct(queries.shape, jnp.bfloat16)]
        + [jax.ShapeDtypeStruct(shape, jnp.bfloat16)] * lines,
        compiler_params=pltpu.CompilerParams(vmem_limit_bytes=VMEM_LIMIT),
        cost_estimate=pl.CostEstimate(
            flops=steps * 2 * 5 * 2 * heads * block * block * LANES,
            bytes_accessed=queries.size * 8 + 2 * pairs.size * 2,
            transcendentals=steps * 2 * heads * block * block,
        ),
        name="attend_back",
    )(
        meta,
        queries,
        pairs,
        grad_mixed,
        mixed,
        logs,
        info,
        cosine,
        sine,
    )
    return (outs[0], [out.reshape(chunks * block, 2 * LANES) for out in outs[1:]])


def pair_back_kernel(*refs):
    *part_refs, cos_ref, sin_ref, out_ref = refs
    cosine, sine = cos_ref[...], sin_ref[...]
    lane = lax.broadcasted_iota(jnp.int32, cosine.shape, 1)
    for which in range(2):
        columns = slice(which * LANES, (which + 1) * LANES)
        total = part_refs[0][:, columns].astype(jnp.float32)
        for ref in part_refs[1:]:
            total = total + ref[:, columns].astype(jnp.float32)
        is_key = (lane < HEAD_DIM) if which == 0 else (lane >= HEAD_DIM)
        total = jnp.where(is_key, total * cosine - turn(total) * sine, total)
        out_ref[:, columns] = total.astype(jnp.bfloat16)


def pair_back(parts, cosine, sine, block):
    rows, columns = parts[0].shape
    tile = pl.BlockSpec((block, columns), lambda i: (i, 0))
    table = pl.BlockSpec((block, LANES), lambda i: (i, 0))
    return pl.pallas_call(
        pair_back_kernel,
        grid=(rows // block,),
        in_specs=[tile] * len(parts) + [table, table],
        out_specs=tile,
        out_shape=jax.ShapeDtypeStruct((rows, columns), jnp.bfloat16),
        compiler_params=pltpu.CompilerParams(vmem_limit_bytes=VMEM_LIMIT),
        name="pair_back",
    )(*parts, cosine, sine)


def update(refs, index, gradient, rate):
    weight, moment, square = [ref[index] for ref in refs[:3]]
    moment_new, square_new, weight_new = adamw_step(weight, gradient, moment, square, rate, 0.1)
    for ref, value in zip(refs[3:], (moment_new, square_new, weight_new)):
        ref[index] = value


def chosen(meta_ref, grad_refs, at, rows, columns):
    own_y = meta_ref[0] == at
    first = pl.program_id(0) == 0
    near = jnp.where(first, grad_refs[0][rows, columns], grad_refs[2][rows, columns])
    far = jnp.where(first, grad_refs[1][rows, columns], grad_refs[3][rows, columns])
    return jnp.where(own_y, near, far).astype(jnp.float32)


def joint_update_kernel(meta_ref, *refs):
    grad_refs, query_refs, pair_refs = (refs[:4], refs[4:7] + refs[10:13], refs[7:10] + refs[13:16])
    groups = query_refs[0].shape[1] // (2 * LANES)
    every = slice(None)
    for at in range(2):
        for j in range(groups):
            gradient = chosen(meta_ref, grad_refs, at, every, slice(j * LANES, (j + 1) * LANES))
            place = slice((2 * j + at) * LANES, (2 * j + at + 1) * LANES)
            update(query_refs, (every, place), gradient, D ** (-0.5))
        for which in range(2):
            start = (groups + which) * LANES
            gradient = chosen(meta_ref, grad_refs, at, every, slice(start, start + LANES))
            if which == 1:
                gradient = pltpu.roll(gradient, HEAD_DIM, 1)
            place = slice((2 * at + which) * LANES, (2 * at + which + 1) * LANES)
            update(pair_refs, (every, place), gradient, D ** (-0.5))


def joint_update(meta, grads, query, pair):
    half = grads[0].shape[0]

    def rows_of(array):
        return pl.BlockSpec((half, array.shape[1]), lambda i, m: ((m[1] + i) % 2, 0))

    whole = pl.BlockSpec(grads[0].shape, lambda i, m: (0, 0))
    blocks = [rows_of(array) for array in (*query, *pair)]
    return pl.pallas_call(
        joint_update_kernel,
        grid_spec=pltpu.PrefetchScalarGridSpec(
            num_scalar_prefetch=1, grid=(2,), in_specs=[whole] * 4 + blocks, out_specs=blocks
        ),
        out_shape=[jax.ShapeDtypeStruct(array.shape, array.dtype) for array in (*query, *pair)],
        compiler_params=pltpu.CompilerParams(vmem_limit_bytes=VMEM_LIMIT),
        cost_estimate=pl.CostEstimate(
            flops=20 * (query[0].size + pair[0].size),
            bytes_accessed=24 * (query[0].size + pair[0].size),
            transcendentals=0,
        ),
        name="joint_update",
    )(meta, *grads, *query, *pair)


def turned_update_kernel(rate, swapped, meta_ref, *refs):
    grad_refs, weight_refs = (refs[:4], refs[4:10])
    at = pl.program_id(1)
    width = grad_refs[0].shape[1]
    every = slice(None)
    for j, start in enumerate(range(0, width, LANES)):
        strip = slice(start, min(start + LANES, width))
        gradient = chosen(meta_ref, grad_refs, at, every, strip).T
        if swapped:
            gradient = jnp.concatenate([gradient[HEAD_DIM:], gradient[:HEAD_DIM]], axis=0)
            index = (j, 0)
        else:
            index = (strip, every)
        update(weight_refs, index, gradient, rate)


def turned_update(meta, grads, weights, rate, swapped):
    shape = weights[0].shape
    half, width = (shape[1] // 2, grads[0].shape[1])
    if swapped:
        weights = [w.reshape(width // LANES, 2, LANES, shape[1]) for w in weights]
        block = pl.BlockSpec(
            (width // LANES, 1, LANES, half), lambda i, at, m: (0, at, 0, (m[1] + i) % 2)
        )
    else:
        block = pl.BlockSpec((width, half), lambda i, at, m: (at, (m[1] + i) % 2))
    outs = pl.pallas_call(
        functools.partial(turned_update_kernel, rate, swapped),
        grid_spec=pltpu.PrefetchScalarGridSpec(
            num_scalar_prefetch=1,
            grid=(2, 2),
            in_specs=[pl.BlockSpec((half, width), lambda i, at, m: (0, 0))] * 4 + [block] * 3,
            out_specs=[block] * 3,
        ),
        out_shape=[jax.ShapeDtypeStruct(weights[0].shape, jnp.float32)] * 3,
        compiler_params=pltpu.CompilerParams(vmem_limit_bytes=VMEM_LIMIT),
        cost_estimate=pl.CostEstimate(
            flops=20 * weights[0].size, bytes_accessed=24 * weights[0].size, transcendentals=0
        ),
        name="turned_update",
    )(meta, *grads, *weights)
    return [out.reshape(shape) for out in outs]


def gateup_update_kernel(meta_ref, *refs):
    gate_refs, up_refs, weight_refs = (refs[:4], refs[4:8], refs[8:14])
    every = slice(None)
    gate, up = [
        jnp.concatenate([chosen(meta_ref, grads, at, every, every) for at in range(2)], axis=1)
        for grads in (gate_refs, up_refs)
    ]
    update(weight_refs, every, jnp.stack([gate, up], axis=1), D ** (-0.5))


def gateup_update(meta, gates, ups, weights, rows):
    half, width = ups[0].shape
    shape = weights[0].shape
    tiles = half // rows
    gate = pl.BlockSpec((rows, width), lambda i, j, m: (tiles + j, 0))
    up = pl.BlockSpec((rows, width), lambda i, j, m: (j, 0))
    block = pl.BlockSpec(
        (rows, 2, shape[2]), lambda i, j, m: (((m[1] + i) % 2) * tiles + j, 0, 0)
    )
    return pl.pallas_call(
        gateup_update_kernel,
        grid_spec=pltpu.PrefetchScalarGridSpec(
            num_scalar_prefetch=1,
            grid=(2, tiles),
            in_specs=[gate] * 4 + [up] * 4 + [block] * 3,
            out_specs=[block] * 3,
        ),
        out_shape=[jax.ShapeDtypeStruct(shape, jnp.float32)] * 3,
        compiler_params=pltpu.CompilerParams(vmem_limit_bytes=VMEM_LIMIT),
        cost_estimate=pl.CostEstimate(
            flops=20 * weights[0].size, bytes_accessed=28 * weights[0].size, transcendentals=0
        ),
        name="gateup_update",
    )(meta, *gates, *ups, *weights)


def on_device(
    sizes,
    block_input,
    cotangent,
    segments,
    norm_gains,
    w_query,
    w_keyvalue,
    w_output,
    w_gateup,
    w_down,
    gains_moment,
    gains_square,
    query_moment,
    query_square,
    keyvalue_moment,
    keyvalue_square,
    output_moment,
    output_square,
    gateup_moment,
    gateup_square,
    down_moment,
    down_square,
):
    rows_on, lines = sizes
    y, core, row, line = [lax.axis_index(name) for name in ("y", "core", "row", "col")]
    length = segments.shape[1]
    block = block_input.shape[0] // lines
    wide = block_input.shape[1]
    half = wide // 2
    slots = 2 * rows_on
    per_row = w_query.shape[1] // (KV_HEADS * HEAD_DIM)
    query_width = per_row * LANES
    hidden_here = w_gateup.shape[2] // 2

    def shift(value, axis, size, by):
        return lax.ppermute(value, axis, [(i, (i + by) % size) for i in range(size)])

    def other_core(value):
        return lax.ppermute(value, "core", [(0, 1), (1, 0)])

    def other_y(value):
        return lax.ppermute(value, "y", [(0, 1), (1, 0)])

    def place_of(y_at, core_at, row_at):
        return (y_at * 2 + core_at) * rows_on + row_at

    first_pairs, second_pairs = ([], [])
    for y_at in range(2):
        for core_at in range(2):
            for row_at in range(rows_on):
                over_row = (
                    place_of(y_at, core_at, row_at),
                    place_of(y_at, core_at, (row_at + 1) % rows_on),
                )
                over_y = (place_of(y_at, core_at, row_at), place_of(1 - y_at, core_at, row_at))
                first_pairs.append(over_row if core_at == 0 else over_y)
                second_pairs.append(over_y if core_at == 0 else over_row)
    near = ("y", "core", "row")

    def gather_tokens(own, beside=()):
        if rows_on == 2:
            first = lax.ppermute(own, near, first_pairs)
            second = lax.ppermute(own, near, second_pairs)
            first, second, *_ = lax.optimization_barrier((first, second, *beside))
            third = lax.ppermute(first, near, second_pairs)
            return [own, first, second, third]
        parts = [own] + [shift(own, "row", rows_on, by) for by in range(1, rows_on)]
        return parts + [other_y(part) for part in parts]

    def reduce_tokens(rows_of, middle=None, before_last=None, far_here=None, ready=None):
        def same(value):
            return value

        middle, before_last = (middle or same, before_last or same)
        if rows_on == 2:
            far = rows_of(2, 4)
            if ready:
                far, close = ready((far, rows_of(0, 2)))
            third = lax.ppermute(far[block:], near, second_pairs)
            second = lax.ppermute(far[:block], near, second_pairs)
            if not ready:
                close = rows_of(0, 2)
            third, second, close = (far_here or lax.optimization_barrier)((third, second, close))
            key = (close[block:].astype(jnp.float32) + third.astype(jnp.float32)).astype(jnp.bfloat16)
            first = before_last(lax.ppermute(middle(key), near, first_pairs))
            own = close[:block].astype(jnp.float32) + second.astype(jnp.float32)
            return own + first.astype(jnp.float32)
        partial = rows_of(0, slots)
        parts = [partial[i * block : (i + 1) * block] for i in range(slots)]
        sums = [
            parts[i].astype(jnp.float32) + other_y(parts[rows_on + i]).astype(jnp.float32)
            for i in range(rows_on)
        ]
        sums[0] = middle(sums[0])
        total = sums[0]
        for by in range(1, rows_on):
            moved = shift(sums[by].astype(jnp.bfloat16), "row", rows_on, -by)
            total = total + moved.astype(jnp.float32)
        return before_last(total)

    def product(left, right):
        def rows_of(first, last):
            return dot_nt(left[first * block : last * block], right).astype(jnp.bfloat16)

        return rows_of

    if rows_on == 2:
        slot_y = [y, jnp.where(core == 0, y, 1 - y), jnp.where(core == 0, 1 - y, y), 1 - y]
        slot_row = [row, jnp.where(core == 0, 1 - row, row), jnp.where(core == 0, row, 1 - row), 1 - row]
    else:
        slot_y = [y] * rows_on + [1 - y] * rows_on
        slot_row = [(row - by) % rows_on for by in range(rows_on)] * 2

    def pick(parts, index):
        return lax.dynamic_index_in_dim(jnp.stack(parts), index, 0, keepdims=False)

    def tokens_sent(values):
        parts = []
        for by in range(lines):
            part = lax.dynamic_slice_in_dim(values, ((line + by) % lines) * block, block, 0)
            parts.append(part if by == 0 else shift(part, "col", lines, by))
        return parts

    def tokens_of(parts):
        blocks = [pick(parts, (line - at) % lines) for at in range(lines)]
        return jnp.concatenate([b[:, :half] for b in blocks] + [b[:, half:] for b in blocks], axis=1)

    def features_sent(values):
        blocks = [
            jnp.concatenate(
                [
                    values[:, at * half : (at + 1) * half],
                    values[:, D // 2 + at * half : D // 2 + (at + 1) * half],
                ],
                axis=1,
            )
            for at in range(lines)
        ]
        parts = []
        for by in range(lines):
            part = pick(blocks, (line + by) % lines)
            parts.append(part if by == 0 else shift(part, "col", lines, by))
        return parts

    def features_of(parts):
        return jnp.concatenate([pick(parts, (line - at) % lines) for at in range(lines)], axis=0)

    def half_rows(values):
        return lax.dynamic_slice_in_dim(values, core * half, half, 0)

    def half_columns(values):
        return lax.dynamic_slice_in_dim(values, core * half, half, 1)

    def gather_weight(piece):
        return lax.all_gather(piece, ("core", "col"), axis=0, tiled=True)

    query_rows = half_rows(w_query).astype(jnp.bfloat16)
    pair_rows = half_rows(w_keyvalue).astype(jnp.bfloat16)

    def joint_of(at):
        pieces = [
            query_rows[:, (2 * j + at) * LANES : (2 * j + at + 1) * LANES] for j in range(per_row)
        ]
        pair = pair_rows[:, at * 2 * LANES : (at + 1) * 2 * LANES]
        pieces += [
            pair[:, :LANES],
            pair[:, LANES + HEAD_DIM :],
            pair[:, LANES : LANES + HEAD_DIM],
        ]
        return jnp.concatenate(pieces, axis=1)

    joint_mine = jnp.where(y == 0, joint_of(0), joint_of(1))
    output_columns = half_columns(w_output).astype(jnp.bfloat16)

    def output_of(at):
        pieces = []
        for j in range(per_row):
            base = (2 * j + at) * LANES
            pieces += [
                output_columns[base + HEAD_DIM : base + LANES],
                output_columns[base : base + HEAD_DIM],
            ]
        return jnp.concatenate(pieces, axis=0)

    output_mine = jnp.where(y == 0, output_of(0), output_of(1)).T
    gateup_mine = lax.dynamic_slice(
        w_gateup, (core * half, 0, y * hidden_here), (half, 2, hidden_here)
    ).astype(jnp.bfloat16)
    gateup_mine = jnp.concatenate([gateup_mine[:, 0], gateup_mine[:, 1]], axis=1)
    down_mine = lax.dynamic_slice(
        w_down, (y * hidden_here, core * half), (hidden_here, half)
    ).astype(jnp.bfloat16).T

    gain_parts = [norm_gains] + [shift(norm_gains, "col", lines, by) for by in range(1, lines)]
    gain_blocks = [pick(gain_parts, (line - at) % lines) for at in range(lines)]
    gains = jnp.concatenate(
        [b[:, :half] for b in gain_blocks] + [b[:, half:] for b in gain_blocks], axis=1
    )

    residual_low = tokens_of(tokens_sent(block_input))
    residual_low, late_cotangent, other_segments, joint_mine, output_mine = lax.optimization_barrier(
        (residual_low, cotangent, other_y(segments), joint_mine, output_mine)
    )

    own_starts = document_starts(segments[0])
    other_starts = document_starts(other_segments[0])
    frequency = 10000.0 ** (-2.0 * jnp.arange(HEAD_DIM // 2, dtype=jnp.float32) / HEAD_DIM)
    starts, places, meta = ([], [], [])
    for slot in range(slots):
        begin = slot_row[slot] * (lines * block) + line * block
        of_chunk = lax.dynamic_slice_in_dim(
            jnp.where(slot_y[slot] == y, own_starts, other_starts), begin, block, 0
        )
        starts.append(of_chunk)
        places.append(begin + jnp.arange(block, dtype=jnp.int32))
        meta += [of_chunk[0] // block, begin // block]
        for row_at in range(rows_on):
            found = jnp.int32(0)
            for other in range(slots):
                same = (slot_y[other] == slot_y[slot]) & (slot_row[other] == row_at)
                found = found + jnp.where(same, other, 0)
            meta.append(found)
    meta = jnp.stack([jnp.asarray(m, jnp.int32) for m in meta + [line]])
    starts, places = (jnp.stack(starts), jnp.stack(places))
    info = jnp.stack([places, starts], axis=1)
    offsets = (places - starts).astype(jnp.float32).reshape(-1)
    phases = offsets[:, None] * jnp.tile(frequency, LANES // (HEAD_DIM // 2))[None, :]
    cosine, sine = (jnp.cos(phases), jnp.sin(phases))

    cot_parts = tokens_sent(late_cotangent)
    first_weight = gather_weight(jnp.concatenate([joint_mine, output_mine], axis=1))
    joint_width = joint_mine.shape[1]
    joint_weight, output_weight = (first_weight[:, :joint_width], first_weight[:, joint_width:])
    residual = residual_low.astype(jnp.float32)
    scale_one = lax.rsqrt(jnp.mean(residual * residual, axis=1, keepdims=True) + EPSILON)
    normed_parts = gather_tokens((residual * scale_one * gains[0]).astype(jnp.bfloat16))
    normed_parts, cot_parts = lax.optimization_barrier((normed_parts, cot_parts))
    cot_low = tokens_of(cot_parts)
    cot_chunks = gather_tokens(cot_low)
    queries, pair = project(normed_parts, first_weight, joint_width, cosine, sine, query_width)
    pairs = lax.all_gather(pair.reshape(slots, block, 2 * LANES), "col", axis=0, tiled=False)
    pairs, cot_chunks, gateup_mine, down_mine = lax.optimization_barrier(
        (pairs, cot_chunks, gateup_mine, down_mine)
    )
    gateup_weight = gather_weight(gateup_mine)
    down_weight = gather_weight(down_mine)
    mixed, logs = attend(meta, queries, pairs, info, rows_on)
    attn_sum = reduce_tokens(product(mixed, output_weight))
    middle = residual + attn_sum
    scale_two = lax.rsqrt(jnp.mean(middle * middle, axis=1, keepdims=True) + EPSILON)
    two_parts = gather_tokens((middle * scale_two * gains[1]).astype(jnp.bfloat16))
    hidden, factor, silu_gate = widen(two_parts, gateup_weight)
    normed_two, cot = (jnp.concatenate(two_parts, axis=0), jnp.concatenate(cot_chunks, axis=0))

    def other_half(rows, grad):
        rows = lax.dynamic_slice_in_dim(rows, (1 - core) * (D // 2), D // 2, 1)
        return other_core(dot_tn(rows, grad).astype(jnp.bfloat16))

    def own_half(rows, grad, received):
        rows = lax.dynamic_slice_in_dim(rows, core * (D // 2), D // 2, 1)
        total = dot_tn(rows, grad) + received.astype(jnp.float32)
        return total.astype(jnp.bfloat16)

    def scatter(total):
        return lax.psum_scatter(total, "col", scatter_dimension=0, tiled=True)

    def collect(piece):
        near_y = other_y(piece)
        return [piece, near_y, other_core(piece), other_core(near_y)]

    down_total = own_half(cot, hidden, other_half(cot, hidden))
    down_total, down_weight = lax.optimization_barrier((down_total, down_weight))
    down_piece = scatter(down_total)
    work = {}

    def feed_back(first, last):
        work["grad_gate"], work["grad_up"], partial = widen_back(
            cot_chunks[first:last],
            down_weight,
            gateup_weight,
            factor,
            silu_gate,
            first,
            [work[name] for name in ("grad_gate", "grad_up") if name in work],
        )
        return partial

    def feed_others(key):
        key, rows, gate, up = lax.optimization_barrier(
            (key, normed_two, work["grad_gate"], work["grad_up"])
        )
        work["feed"] = (rows, gate, up, other_half(rows, gate), other_half(rows, up))
        return key

    def feed_owns(first):
        first, work["down_piece"], rows, gate, up, gate_other, up_other = lax.optimization_barrier(
            (first, down_piece, *work["feed"])
        )
        work["totals"] = (own_half(rows, gate, gate_other), own_half(rows, up, up_other))
        return first

    grad_normed_two = reduce_tokens(feed_back, feed_others, feed_owns)
    gate_piece, up_piece = [scatter(total) for total in work["totals"]]

    def norm_back(values, scale, grad_normed, gain):
        scaled = grad_normed * gain
        total = jnp.sum(scaled * values, axis=1, keepdims=True)
        return scale * scaled - values * (scale**3 * total / D)

    grad_middle = cot_low.astype(jnp.float32) + norm_back(
        middle, scale_two, grad_normed_two, gains[1]
    )
    gain_two = jnp.sum(grad_normed_two * middle * scale_two, axis=0)

    grad_middle_low, late_hidden = lax.optimization_barrier(
        (grad_middle.astype(jnp.bfloat16), hidden)
    )
    gate_total, up_total = work["totals"]
    back = jnp.concatenate(gather_tokens(grad_middle_low, (gate_total, up_total)), axis=0)

    def back_here(products):
        products, work["back"] = lax.optimization_barrier((products, back))
        return products

    def attention_back(far):
        here = work.get("back", back)
        grad_query, grad_parts = attend_back(
            meta,
            queries,
            pairs,
            dot_nn(here, output_weight).astype(jnp.bfloat16),
            mixed,
            logs,
            info,
            cosine,
            sine,
            rows_on,
        )
        work["grad_parts"] = [grad_parts[0]] + [
            shift(grad_parts[by], "col", lines, -by) for by in range(1, lines)
        ]
        names = ("grad_query", "gate_piece", "back", "mixed")
        far, *values = lax.optimization_barrier((far, grad_query, gate_piece, here, mixed))
        work.update(zip(names, values))
        return far

    def keys_arrive(first):
        first, work["grad_parts"], work["up_piece"] = lax.optimization_barrier(
            (first, work["grad_parts"], up_piece)
        )
        return first

    if rows_on == 2:
        ffn_sum = reduce_tokens(
            product(late_hidden, down_weight), None, keys_arrive, attention_back, back_here
        )
    else:
        ffn_sum = keys_arrive(attention_back(reduce_tokens(product(late_hidden, down_weight))))
    grad_query, gate_piece, back, mixed = [
        work[name] for name in ("grad_query", "gate_piece", "back", "mixed")
    ]
    output_total = own_half(back, mixed, other_half(back, mixed))
    output_parts = features_sent((middle + ffn_sum).astype(jnp.bfloat16))
    grad_keyvalue = pair_back(work["grad_parts"], cosine, sine, block)
    grad_joint = jnp.concatenate([grad_query, grad_keyvalue], axis=1)
    normed_one = jnp.concatenate(normed_parts, axis=0)
    meta_core = jnp.stack([y, core]).astype(jnp.int32)

    def joint_products(first, last):
        if first:
            return product(grad_joint, joint_weight)(first, last)
        work["shards"] = collect(jnp.concatenate([work["down_piece"], gate_piece], axis=0))
        down_new = turned_update(
            meta_core,
            work["shards"],
            [w_down, down_moment, down_square],
            FF ** (-0.5),
            False,
        )
        close, work["output"], work["down_new"] = lax.optimization_barrier(
            (product(grad_joint, joint_weight)(first, last), output_total, down_new)
        )
        return close

    def joint_others(key):
        key, rows, grad = lax.optimization_barrier((key, normed_one, grad_joint))
        work["joint"] = (rows, grad, other_half(rows, grad))
        work["output_piece"] = scatter(work["output"])
        return key

    def joint_owns(first):
        first, work["output_piece"], work["output_parts"], rows, grad, other = (
            lax.optimization_barrier((first, work["output_piece"], output_parts, *work["joint"]))
        )
        work["joint_total"] = own_half(rows, grad, other)
        return first

    grad_normed_one = reduce_tokens(joint_products, joint_others, joint_owns)
    joint_piece = scatter(work["joint_total"])
    gateup_new = gateup_update(
        meta_core,
        work["shards"],
        collect(work["up_piece"]),
        [w_gateup, gateup_moment, gateup_square],
        32,
    )
    input_grad = grad_middle + norm_back(residual, scale_one, grad_normed_one, gains[0])
    gain_one = jnp.sum(grad_normed_one * residual * scale_one, axis=0)
    input_parts, gateup_new = lax.optimization_barrier(
        (features_sent(input_grad.astype(jnp.bfloat16)), gateup_new)
    )
    layer_output = features_of(work["output_parts"])
    input_grad = features_of(input_parts).astype(jnp.float32)
    pair_piece = joint_piece[:, query_width:]
    pair_total = pair_piece.astype(jnp.float32)
    for by in range(1, rows_on):
        pair_total = pair_total + shift(pair_piece, "row", rows_on, by).astype(jnp.float32)
    joint_piece = jnp.concatenate(
        [joint_piece[:, :query_width], pair_total.astype(jnp.bfloat16)], axis=1
    )
    joint_new = joint_update(
        meta_core,
        collect(joint_piece),
        [w_query, query_moment, query_square],
        [w_keyvalue, keyvalue_moment, keyvalue_square],
    )
    output_new = turned_update(
        meta_core,
        collect(work["output_piece"]),
        [w_output, output_moment, output_square],
        (HEADS * HEAD_DIM // 64) ** (-0.5),
        True,
    )

    gain_sums = jnp.stack([gain_one, gain_two])
    blocks = [
        jnp.concatenate(
            [
                gain_sums[:, at * half : (at + 1) * half],
                gain_sums[:, D // 2 + at * half : D // 2 + (at + 1) * half],
            ],
            axis=1,
        )
        for at in range(lines)
    ]
    grad_gains = pick(blocks, line)
    for by in range(1, lines):
        grad_gains = grad_gains + shift(pick(blocks, (line + by) % lines), "col", lines, by)
    for axis, size in (("core", 2), ("y", 2), ("row", rows_on)):
        blocks_total = grad_gains
        for by in range(1, size):
            grad_gains = grad_gains + shift(blocks_total, axis, size, by)

    gains_new = adamw_step(norm_gains, grad_gains, gains_moment, gains_square, 0.6, 0.0)
    return (
        layer_output,
        input_grad,
        *gains_new,
        *joint_new,
        *output_new,
        *gateup_new,
        *work["down_new"],
    )


def solution(mesh):
    dp, rows_on, lines = (mesh.shape["dp"], mesh.shape["row"], mesh.shape["col"])
    split = Mesh(mesh.devices.reshape(dp // 2, 2, rows_on, lines), ("y", "core", "row", "col"))
    tokens = P(("y", "core", "row"), "col")
    narrow, wide = (P("col", "row"), P("row", "col"))
    gains, pair, gateup = (P(None, "col"), P("col", None), P("col", None, "row"))
    return jax.shard_map(
        functools.partial(on_device, (rows_on, lines)),
        mesh=split,
        in_specs=(
            tokens,
            tokens,
            P(("y", "core"), None),
            gains,
            narrow,
            pair,
            wide,
            gateup,
            wide,
            gains,
            gains,
            narrow,
            narrow,
            pair,
            pair,
            wide,
            wide,
            gateup,
            gateup,
            wide,
            wide,
        ),
        out_specs=(tokens, tokens)
        + (gains,) * 3
        + (narrow,) * 3
        + (pair,) * 3
        + (wide,) * 3
        + (gateup,) * 3
        + (wide,) * 3,
        check_vma=False,
    )
```

```python
import functools

import jax
import jax.numpy as jnp
from jax import lax
from jax.experimental import pallas as pl
from jax.experimental.pallas import tpu as pltpu
from jax.sharding import Mesh, PartitionSpec as P

D = 2048
HEADS = 32
KV_HEADS = 4
HEAD_DIM = 64
FF = 5632
STEP = 10

EPSILON = 1e-05
BETA_ONE = 0.9
BETA_TWO = 0.999
ADAM_EPS = 1e-08
MASKED = -1e30
SCORE_SCALE = HEAD_DIM ** (-0.5)
LANES = 128
VMEM_LIMIT = 48 * 1024 * 1024


def dot_nn(left, right):
    return lax.dot_general(left, right, (((1,), (0,)), ((), ())), preferred_element_type=jnp.float32)


def dot_nt(left, right):
    return lax.dot_general(left, right, (((1,), (1,)), ((), ())), preferred_element_type=jnp.float32)


def dot_tn(left, right):
    return lax.dot_general(left, right, (((0,), (0,)), ((), ())), preferred_element_type=jnp.float32)


def adamw_step(weight, gradient, moment, square, step_rate, decay_rate):
    moment_new = BETA_ONE * moment + (1.0 - BETA_ONE) * gradient
    square_new = BETA_TWO * square + (1.0 - BETA_TWO) * gradient * gradient
    fixed_one = moment_new / (1.0 - BETA_ONE**STEP)
    fixed_two = square_new / (1.0 - BETA_TWO**STEP)
    weight_new = weight - step_rate * (
        fixed_one / (jnp.sqrt(fixed_two) + ADAM_EPS) + decay_rate * weight
    )
    return (moment_new, square_new, weight_new)


def document_starts(segment_ids):
    places = jnp.arange(segment_ids.shape[0], dtype=jnp.int32)
    starts = jnp.concatenate([jnp.ones((1,), jnp.bool_), segment_ids[1:] != segment_ids[:-1]])
    return lax.cummax(jnp.where(starts, places, 0), axis=0)


def turn(values):
    lane = lax.broadcasted_iota(jnp.int32, values.shape, 1)
    ahead = pltpu.roll(values, LANES - HEAD_DIM // 2, 1)
    behind = pltpu.roll(values, HEAD_DIM // 2, 1)
    return jnp.where(lane % HEAD_DIM < HEAD_DIM // 2, -ahead, behind)


def take_chunk(rows_refs, held_ref):
    for at, ref in enumerate(rows_refs):

        @pl.when(pl.program_id(0) == at)
        def _(ref=ref):
            held_ref[...] = ref[...]


def project_kernel(slots, *refs):
    rows_refs, (weight_ref, cos_ref, sin_ref, query_ref, pair_ref, held_ref) = (refs[:slots], refs[slots:])
    take_chunk(rows_refs, held_ref)
    sums = dot_nn(held_ref[...], weight_ref[...])
    cosine, sine = cos_ref[...], sin_ref[...]
    width = query_ref.shape[1]
    lane = lax.broadcasted_iota(jnp.int32, cosine.shape, 1)
    for start in range(0, width, LANES):
        part = sums[:, start : start + LANES]
        turned = (part * cosine + turn(part) * sine).astype(jnp.bfloat16)
        query_ref[:, start : start + LANES] = turned * jnp.bfloat16(SCORE_SCALE)
    for which in range(2):
        part = sums[:, width + which * LANES : width + (which + 1) * LANES]
        is_key = (lane < HEAD_DIM) if which == 0 else (lane >= HEAD_DIM)
        turned = jnp.where(is_key, part * cosine + turn(part) * sine, part)
        pair_ref[:, which * LANES : (which + 1) * LANES] = turned.astype(jnp.bfloat16)


def project(chunks, weight, total, cosine, sine, width):
    slots = len(chunks)
    block, depth = chunks[0].shape
    rows = slots * block
    whole = pl.BlockSpec((block, depth), lambda i: (0, 0))
    return pl.pallas_call(
        functools.partial(project_kernel, slots),
        grid=(slots,),
        in_specs=[whole] * slots
        + [
            pl.BlockSpec((depth, total), lambda i: (0, 0)),
            pl.BlockSpec((block, LANES), lambda i: (i, 0)),
            pl.BlockSpec((block, LANES), lambda i: (i, 0)),
        ],
        out_specs=[
            pl.BlockSpec((block, width), lambda i: (i, 0)),
            pl.BlockSpec((block, total - width), lambda i: (i, 0)),
        ],
        out_shape=[
            jax.ShapeDtypeStruct((rows, width), jnp.bfloat16),
            jax.ShapeDtypeStruct((rows, total - width), jnp.bfloat16),
        ],
        scratch_shapes=[pltpu.VMEM((block, depth), jnp.bfloat16)],
        compiler_params=pltpu.CompilerParams(vmem_limit_bytes=VMEM_LIMIT),
        cost_estimate=pl.CostEstimate(
            flops=2 * rows * depth * total,
            bytes_accessed=(rows + total) * depth * 2,
            transcendentals=0,
        ),
        name="project",
    )(*chunks, weight, cosine, sine)


def widen_kernel(slots, *refs):
    rows_refs, (weight_ref, hidden_ref, factor_ref, silu_ref, held_ref) = (refs[:slots], refs[slots:])
    take_chunk(rows_refs, held_ref)
    sums = dot_nn(held_ref[...], weight_ref[...])
    width = hidden_ref.shape[1]
    gate, upward = (sums[:, :width], sums[:, width:])
    sigmoid = jax.nn.sigmoid(gate)
    silu = gate * sigmoid
    hidden_ref[...] = (silu * upward).astype(jnp.bfloat16)
    factor_ref[...] = (upward * sigmoid * (1.0 + gate * (1.0 - sigmoid))).astype(jnp.bfloat16)
    silu_ref[...] = silu.astype(jnp.bfloat16)


def widen(chunks, weight):
    slots = len(chunks)
    block, depth = chunks[0].shape
    width = weight.shape[1] // 2
    rows = slots * block
    once = pl.Buffered(1)
    return pl.pallas_call(
        functools.partial(widen_kernel, slots),
        grid=(slots,),
        in_specs=[pl.BlockSpec((block, depth), lambda i: (0, 0), pipeline_mode=once)] * slots
        + [pl.BlockSpec(weight.shape, lambda i: (0, 0), pipeline_mode=once)],
        out_specs=[pl.BlockSpec((block, width), lambda i: (i, 0))] * 3,
        out_shape=[jax.ShapeDtypeStruct((rows, width), jnp.bfloat16)] * 3,
        scratch_shapes=[pltpu.VMEM((block, depth), jnp.bfloat16)],
        compiler_params=pltpu.CompilerParams(vmem_limit_bytes=VMEM_LIMIT),
        cost_estimate=pl.CostEstimate(
            flops=4 * rows * depth * width,
            bytes_accessed=(rows + 2 * width) * depth * 2 + 6 * rows * width,
            transcendentals=rows * width,
        ),
        name="widen",
    )(*chunks, weight)


def widen_back_kernel(slots, kept, *refs):
    rows_refs, refs = (refs[:slots], refs[slots:])
    down_ref, gateup_ref, factor_ref, silu_ref = refs[:4]
    gate_ref, up_ref, partial_ref, held_ref = refs[4 + kept :]
    take_chunk(rows_refs, held_ref)
    grad_hidden = dot_nn(held_ref[...], down_ref[...])
    gate = (grad_hidden * factor_ref[...].astype(jnp.float32)).astype(jnp.bfloat16)
    up = (grad_hidden * silu_ref[...].astype(jnp.float32)).astype(jnp.bfloat16)
    gate_ref[...] = gate
    up_ref[...] = up
    both = jnp.concatenate([gate, up], axis=1)
    partial_ref[...] = dot_nt(both, gateup_ref[...]).astype(jnp.bfloat16)


def widen_back(chunks, down, gateup, factor, silu, first, kept):
    slots = len(chunks)
    block, depth = chunks[0].shape
    width = down.shape[1]
    once = pl.Buffered(1)
    tile = pl.BlockSpec((block, width), lambda i: (first + i, 0))
    return pl.pallas_call(
        functools.partial(widen_back_kernel, slots, len(kept)),
        grid=(slots,),
        in_specs=[pl.BlockSpec((block, depth), lambda i: (0, 0), pipeline_mode=once)] * slots
        + [
            pl.BlockSpec(down.shape, lambda i: (0, 0), pipeline_mode=once),
            pl.BlockSpec(gateup.shape, lambda i: (0, 0), pipeline_mode=once),
            tile,
            tile,
        ]
        + [pl.BlockSpec(memory_space=pl.ANY)] * len(kept),
        out_specs=[tile, tile, pl.BlockSpec((block, depth), lambda i: (i, 0))],
        out_shape=[jax.ShapeDtypeStruct(factor.shape, jnp.bfloat16)] * 2
        + [jax.ShapeDtypeStruct((slots * block, depth), jnp.bfloat16)],
        scratch_shapes=[pltpu.VMEM((block, depth), jnp.bfloat16)],
        input_output_aliases={slots + 4 + i: i for i in range(len(kept))},
        compiler_params=pltpu.CompilerParams(vmem_limit_bytes=VMEM_LIMIT),
        cost_estimate=pl.CostEstimate(
            flops=slots * block * depth * width,
            bytes_accessed=8 * slots * block * width,
            transcendentals=0,
        ),
        name="widen_back",
    )(*chunks, down, gateup, factor, silu, *kept)


def stack_heads(values):
    return jnp.concatenate(
        [values[:, start : start + LANES] for start in range(0, values.shape[1], LANES)], axis=0
    )


def block_of(meta_ref, chunk, step, parts, lines):
    base = chunk * (2 + parts)
    key_block = meta_ref[base + 1] - step
    slot = meta_ref[base + 2 + key_block // lines]
    own_line = meta_ref[pl.num_programs(0) * (2 + parts)]
    line = lax.rem(key_block, lines)
    return (key_block, slot, line, lax.rem(own_line - line + lines, lines))


def attend_kernel(parts, lines, meta_ref, query_ref, pair_ref, info_ref, out_ref, log_ref):
    chunk = pl.program_id(0)
    block = query_ref.shape[0]
    heads = query_ref.shape[1] // LANES
    stacked = stack_heads(query_ref[...])
    lane = lax.broadcasted_iota(jnp.int32, stacked.shape, 1)
    place = jnp.concatenate([info_ref[0, 0:1, :]] * heads, axis=1)
    start = jnp.concatenate([info_ref[0, 1:2, :]] * heads, axis=1)
    base = chunk * (2 + parts)
    steps = meta_ref[base + 1] - meta_ref[base] + 1
    width = heads * block
    outs = []
    for which in range(2):
        is_key = (lane < HEAD_DIM) if which == 0 else (lane >= HEAD_DIM)
        queries = jnp.where(is_key, stacked, jnp.zeros_like(stacked))

        def body(step, carry):
            peak, total, mixed = carry
            key_block, slot, at, _ = block_of(meta_ref, chunk, step, parts, lines)
            pair = pair_ref[at, slot, :, which * LANES : (which + 1) * LANES]
            scores = dot_nt(pair, queries)
            key_place = key_block * block + lax.broadcasted_iota(jnp.int32, (block, width), 0)
            scores = jnp.where((key_place <= place) & (key_place >= start), scores, MASKED)
            new_peak = jnp.maximum(peak, jnp.max(scores, axis=0, keepdims=True))
            weights = jnp.exp(scores - new_peak)
            shrink = jnp.exp(peak - new_peak)
            total = total * shrink + jnp.sum(weights, axis=0, keepdims=True)
            mixed = mixed * shrink + dot_tn(pair, weights.astype(jnp.bfloat16))
            return (new_peak, total, mixed)

        peak, total, mixed = lax.fori_loop(
            0,
            steps,
            body,
            (
                jnp.full((1, width), MASKED, jnp.float32),
                jnp.zeros((1, width), jnp.float32),
                jnp.zeros((LANES, width), jnp.float32),
            ),
        )
        log_ref[0, which : which + 1, :] = peak + jnp.log(total)
        outs.append(mixed / total)
    joined = jnp.concatenate([outs[1][:HEAD_DIM], outs[0][HEAD_DIM:]], axis=0)
    rows = joined.T.astype(jnp.bfloat16)
    for head in range(heads):
        out_ref[:, head * LANES : (head + 1) * LANES] = rows[head * block : (head + 1) * block]


def attend(meta, queries, pairs, info, parts):
    chunks, block = (info.shape[0], info.shape[2])
    width = queries.shape[1]
    heads = width // LANES
    lines = pairs.shape[0]
    steps = 3 * chunks
    return pl.pallas_call(
        functools.partial(attend_kernel, parts, lines),
        grid_spec=pltpu.PrefetchScalarGridSpec(
            num_scalar_prefetch=1,
            grid=(chunks,),
            in_specs=[
                pl.BlockSpec((block, width), lambda i, m: (i, 0)),
                pl.BlockSpec(pairs.shape, lambda i, m: (0, 0, 0, 0)),
                pl.BlockSpec((1, 2, block), lambda i, m: (i, 0, 0)),
            ],
            out_specs=[
                pl.BlockSpec((block, width), lambda i, m: (i, 0)),
                pl.BlockSpec((1, 2, heads * block), lambda i, m: (i, 0, 0)),
            ],
        ),
        out_shape=[
            jax.ShapeDtypeStruct(queries.shape, jnp.bfloat16),
            jax.ShapeDtypeStruct((chunks, 2, heads * block), jnp.float32),
        ],
        compiler_params=pltpu.CompilerParams(vmem_limit_bytes=VMEM_LIMIT),
        cost_estimate=pl.CostEstimate(
            flops=steps * 2 * 2 * 2 * heads * block * block * LANES,
            bytes_accessed=queries.size * 4 + pairs.size * 2,
            transcendentals=steps * 2 * heads * block * block,
        ),
        name="attend",
    )(meta, queries, pairs, info)


def attend_back_kernel(parts, lines, meta_ref, query_ref, *refs):
    pair_ref, grad_ref, mixed_ref, log_ref, info_ref, cos_ref, sin_ref, query_out = refs[:8]
    pair_outs = refs[8 : 8 + lines]
    sums = refs[8 + lines]
    chunk = pl.program_id(0)
    block = query_ref.shape[0]
    heads = query_ref.shape[1] // LANES

    @pl.when(chunk == 0)
    def _():
        sums[...] = jnp.zeros_like(sums)

    stacked = stack_heads(query_ref[...])
    stacked_grad = stack_heads(grad_ref[...])
    product = stacked_grad.astype(jnp.float32) * stack_heads(mixed_ref[...]).astype(jnp.float32)
    lane = lax.broadcasted_iota(jnp.int32, stacked.shape, 1)
    place = jnp.concatenate([info_ref[0, 0:1, :]] * heads, axis=1)
    start = jnp.concatenate([info_ref[0, 1:2, :]] * heads, axis=1)
    base = chunk * (2 + parts)
    steps = meta_ref[base + 1] - meta_ref[base] + 1
    width = heads * block
    grads = []
    for which in range(2):
        is_key = (lane < HEAD_DIM) if which == 0 else (lane >= HEAD_DIM)
        queries = jnp.where(is_key, stacked, jnp.zeros_like(stacked))
        grad = jnp.where(is_key, jnp.zeros_like(stacked_grad), stacked_grad)
        own = jnp.where(is_key, 0.0, product)
        centre = lax.dot_general(
            jnp.ones((8, LANES), jnp.float32),
            own,
            (((1,), (1,)), ((), ())),
            precision=lax.Precision.HIGHEST,
            preferred_element_type=jnp.float32,
        )[0:1]
        logs = log_ref[0, which : which + 1, :]

        def body(step, grad_query):
            key_block, slot, at, shift = block_of(meta_ref, chunk, step, parts, lines)
            columns = slice(which * LANES, (which + 1) * LANES)
            pair = pair_ref[at, slot, :, columns]
            scores = dot_nt(pair, queries)
            key_place = key_block * block + lax.broadcasted_iota(jnp.int32, (block, width), 0)
            scores = jnp.where((key_place <= place) & (key_place >= start), scores, MASKED)
            weights = jnp.exp(scores - logs)
            grad_scores = (weights * (dot_nt(pair, grad) - centre)).astype(jnp.bfloat16)
            sums[shift, slot, :, columns] += dot_nn(grad_scores, queries) + dot_nn(
                weights.astype(jnp.bfloat16), grad
            )
            return grad_query + dot_tn(pair, grad_scores)

        grads.append(lax.fori_loop(0, steps, body, jnp.zeros((LANES, width), jnp.float32)))
    joined = jnp.concatenate([grads[0][:HEAD_DIM], grads[1][HEAD_DIM:]], axis=0)
    rows = joined.T * SCORE_SCALE
    cosine, sine = cos_ref[...], sin_ref[...]
    for head in range(heads):
        part = rows[head * block : (head + 1) * block]
        back = part * cosine - turn(part) * sine
        query_out[:, head * LANES : (head + 1) * LANES] = back.astype(jnp.bfloat16)

    @pl.when(chunk == pl.num_programs(0) - 1)
    def _():
        for line in range(lines):
            pair_outs[line][...] = sums[line].astype(jnp.bfloat16)


def attend_back(meta, queries, pairs, grad_mixed, mixed, logs, info, cosine, sine, parts):
    chunks, block = (info.shape[0], info.shape[2])
    width = queries.shape[1]
    heads = width // LANES
    lines = pairs.shape[0]
    shape = pairs.shape[1:]
    steps = 3 * chunks
    wide = pl.BlockSpec((block, width), lambda i, m: (i, 0))
    table = pl.BlockSpec((block, LANES), lambda i, m: (i, 0))
    whole = pl.BlockSpec(shape, lambda i, m: (0, 0, 0))
    outs = pl.pallas_call(
        functools.partial(attend_back_kernel, parts, lines),
        grid_spec=pltpu.PrefetchScalarGridSpec(
            num_scalar_prefetch=1,
            grid=(chunks,),
            in_specs=[
                wide,
                pl.BlockSpec(pairs.shape, lambda i, m: (0, 0, 0, 0)),
                wide,
                wide,
                pl.BlockSpec((1, 2, heads * block), lambda i, m: (i, 0, 0)),
                pl.BlockSpec((1, 2, block), lambda i, m: (i, 0, 0)),
                table,
                table,
            ],
            out_specs=[wide] + [whole] * lines,
            scratch_shapes=[pltpu.VMEM(pairs.shape, jnp.float32)],
        ),
        out_shape=[jax.ShapeDtypeStruct(queries.shape, jnp.bfloat16)]
        + [jax.ShapeDtypeStruct(shape, jnp.bfloat16)] * lines,
        compiler_params=pltpu.CompilerParams(vmem_limit_bytes=VMEM_LIMIT),
        cost_estimate=pl.CostEstimate(
            flops=steps * 2 * 5 * 2 * heads * block * block * LANES,
            bytes_accessed=queries.size * 8 + 2 * pairs.size * 2,
            transcendentals=steps * 2 * heads * block * block,
        ),
        name="attend_back",
    )(
        meta,
        queries,
        pairs,
        grad_mixed,
        mixed,
        logs,
        info,
        cosine,
        sine,
    )
    return (outs[0], [out.reshape(chunks * block, 2 * LANES) for out in outs[1:]])


def pair_back_kernel(*refs):
    *part_refs, cos_ref, sin_ref, out_ref = refs
    cosine, sine = cos_ref[...], sin_ref[...]
    lane = lax.broadcasted_iota(jnp.int32, cosine.shape, 1)
    for which in range(2):
        columns = slice(which * LANES, (which + 1) * LANES)
        total = part_refs[0][:, columns].astype(jnp.float32)
        for ref in part_refs[1:]:
            total = total + ref[:, columns].astype(jnp.float32)
        is_key = (lane < HEAD_DIM) if which == 0 else (lane >= HEAD_DIM)
        total = jnp.where(is_key, total * cosine - turn(total) * sine, total)
        out_ref[:, columns] = total.astype(jnp.bfloat16)


def pair_back(parts, cosine, sine, block):
    rows, columns = parts[0].shape
    tile = pl.BlockSpec((block, columns), lambda i: (i, 0))
    table = pl.BlockSpec((block, LANES), lambda i: (i, 0))
    return pl.pallas_call(
        pair_back_kernel,
        grid=(rows // block,),
        in_specs=[tile] * len(parts) + [table, table],
        out_specs=tile,
        out_shape=jax.ShapeDtypeStruct((rows, columns), jnp.bfloat16),
        compiler_params=pltpu.CompilerParams(vmem_limit_bytes=VMEM_LIMIT),
        name="pair_back",
    )(*parts, cosine, sine)


def update(refs, index, gradient, rate):
    weight, moment, square = [ref[index] for ref in refs[:3]]
    moment_new, square_new, weight_new = adamw_step(weight, gradient, moment, square, rate, 0.1)
    for ref, value in zip(refs[3:], (moment_new, square_new, weight_new)):
        ref[index] = value


def chosen(meta_ref, grad_refs, at, rows, columns):
    own_y = meta_ref[0] == at
    first = pl.program_id(0) == 0
    near = jnp.where(first, grad_refs[0][rows, columns], grad_refs[2][rows, columns])
    far = jnp.where(first, grad_refs[1][rows, columns], grad_refs[3][rows, columns])
    return jnp.where(own_y, near, far).astype(jnp.float32)


def joint_update_kernel(meta_ref, *refs):
    grad_refs, query_refs, pair_refs = (refs[:4], refs[4:7] + refs[10:13], refs[7:10] + refs[13:16])
    groups = query_refs[0].shape[1] // (2 * LANES)
    every = slice(None)
    for at in range(2):
        for j in range(groups):
            gradient = chosen(meta_ref, grad_refs, at, every, slice(j * LANES, (j + 1) * LANES))
            place = slice((2 * j + at) * LANES, (2 * j + at + 1) * LANES)
            update(query_refs, (every, place), gradient, D ** (-0.5))
        for which in range(2):
            start = (groups + which) * LANES
            gradient = chosen(meta_ref, grad_refs, at, every, slice(start, start + LANES))
            if which == 1:
                gradient = pltpu.roll(gradient, HEAD_DIM, 1)
            place = slice((2 * at + which) * LANES, (2 * at + which + 1) * LANES)
            update(pair_refs, (every, place), gradient, D ** (-0.5))


def joint_update(meta, grads, query, pair):
    half = grads[0].shape[0]

    def rows_of(array):
        return pl.BlockSpec((half, array.shape[1]), lambda i, m: ((m[1] + i) % 2, 0))

    whole = pl.BlockSpec(grads[0].shape, lambda i, m: (0, 0))
    blocks = [rows_of(array) for array in (*query, *pair)]
    return pl.pallas_call(
        joint_update_kernel,
        grid_spec=pltpu.PrefetchScalarGridSpec(
            num_scalar_prefetch=1, grid=(2,), in_specs=[whole] * 4 + blocks, out_specs=blocks
        ),
        out_shape=[jax.ShapeDtypeStruct(array.shape, array.dtype) for array in (*query, *pair)],
        compiler_params=pltpu.CompilerParams(vmem_limit_bytes=VMEM_LIMIT),
        cost_estimate=pl.CostEstimate(
            flops=20 * (query[0].size + pair[0].size),
            bytes_accessed=24 * (query[0].size + pair[0].size),
            transcendentals=0,
        ),
        name="joint_update",
    )(meta, *grads, *query, *pair)


def turned_update_kernel(rate, swapped, meta_ref, *refs):
    grad_refs, weight_refs = (refs[:4], refs[4:10])
    at = pl.program_id(1)
    width = grad_refs[0].shape[1]
    every = slice(None)
    for j, start in enumerate(range(0, width, LANES)):
        strip = slice(start, min(start + LANES, width))
        gradient = chosen(meta_ref, grad_refs, at, every, strip).T
        if swapped:
            gradient = jnp.concatenate([gradient[HEAD_DIM:], gradient[:HEAD_DIM]], axis=0)
            index = (j, 0)
        else:
            index = (strip, every)
        update(weight_refs, index, gradient, rate)


def turned_update(meta, grads, weights, rate, swapped):
    shape = weights[0].shape
    half, width = (shape[1] // 2, grads[0].shape[1])
    if swapped:
        weights = [w.reshape(width // LANES, 2, LANES, shape[1]) for w in weights]
        block = pl.BlockSpec(
            (width // LANES, 1, LANES, half), lambda i, at, m: (0, at, 0, (m[1] + i) % 2)
        )
    else:
        block = pl.BlockSpec((width, half), lambda i, at, m: (at, (m[1] + i) % 2))
    outs = pl.pallas_call(
        functools.partial(turned_update_kernel, rate, swapped),
        grid_spec=pltpu.PrefetchScalarGridSpec(
            num_scalar_prefetch=1,
            grid=(2, 2),
            in_specs=[pl.BlockSpec((half, width), lambda i, at, m: (0, 0))] * 4 + [block] * 3,
            out_specs=[block] * 3,
        ),
        out_shape=[jax.ShapeDtypeStruct(weights[0].shape, jnp.float32)] * 3,
        compiler_params=pltpu.CompilerParams(vmem_limit_bytes=VMEM_LIMIT),
        cost_estimate=pl.CostEstimate(
            flops=20 * weights[0].size, bytes_accessed=24 * weights[0].size, transcendentals=0
        ),
        name="turned_update",
    )(meta, *grads, *weights)
    return [out.reshape(shape) for out in outs]


def gateup_update_kernel(meta_ref, *refs):
    gate_refs, up_refs, weight_refs = (refs[:4], refs[4:8], refs[8:14])
    every = slice(None)
    gate, up = [
        jnp.concatenate([chosen(meta_ref, grads, at, every, every) for at in range(2)], axis=1)
        for grads in (gate_refs, up_refs)
    ]
    update(weight_refs, every, jnp.stack([gate, up], axis=1), D ** (-0.5))


def gateup_update(meta, gates, ups, weights, rows):
    half, width = ups[0].shape
    shape = weights[0].shape
    tiles = half // rows
    gate = pl.BlockSpec((rows, width), lambda i, j, m: (tiles + j, 0))
    up = pl.BlockSpec((rows, width), lambda i, j, m: (j, 0))
    block = pl.BlockSpec(
        (rows, 2, shape[2]), lambda i, j, m: (((m[1] + i) % 2) * tiles + j, 0, 0)
    )
    return pl.pallas_call(
        gateup_update_kernel,
        grid_spec=pltpu.PrefetchScalarGridSpec(
            num_scalar_prefetch=1,
            grid=(2, tiles),
            in_specs=[gate] * 4 + [up] * 4 + [block] * 3,
            out_specs=[block] * 3,
        ),
        out_shape=[jax.ShapeDtypeStruct(shape, jnp.float32)] * 3,
        compiler_params=pltpu.CompilerParams(vmem_limit_bytes=VMEM_LIMIT),
        cost_estimate=pl.CostEstimate(
            flops=20 * weights[0].size, bytes_accessed=28 * weights[0].size, transcendentals=0
        ),
        name="gateup_update",
    )(meta, *gates, *ups, *weights)


def on_device(
    sizes,
    block_input,
    cotangent,
    segments,
    norm_gains,
    w_query,
    w_keyvalue,
    w_output,
    w_gateup,
    w_down,
    gains_moment,
    gains_square,
    query_moment,
    query_square,
    keyvalue_moment,
    keyvalue_square,
    output_moment,
    output_square,
    gateup_moment,
    gateup_square,
    down_moment,
    down_square,
):
    rows_on, lines = sizes
    y, core, row, line = [lax.axis_index(name) for name in ("y", "core", "row", "col")]
    length = segments.shape[1]
    block = block_input.shape[0] // lines
    wide = block_input.shape[1]
    half = wide // 2
    slots = 2 * rows_on
    per_row = w_query.shape[1] // (KV_HEADS * HEAD_DIM)
    query_width = per_row * LANES
    hidden_here = w_gateup.shape[2] // 2

    def shift(value, axis, size, by):
        return lax.ppermute(value, axis, [(i, (i + by) % size) for i in range(size)])

    def other_core(value):
        return lax.ppermute(value, "core", [(0, 1), (1, 0)])

    def other_y(value):
        return lax.ppermute(value, "y", [(0, 1), (1, 0)])

    def place_of(y_at, core_at, row_at):
        return (y_at * 2 + core_at) * rows_on + row_at

    first_pairs, second_pairs = ([], [])
    for y_at in range(2):
        for core_at in range(2):
            for row_at in range(rows_on):
                over_row = (
                    place_of(y_at, core_at, row_at),
                    place_of(y_at, core_at, (row_at + 1) % rows_on),
                )
                over_y = (place_of(y_at, core_at, row_at), place_of(1 - y_at, core_at, row_at))
                first_pairs.append(over_row if core_at == 0 else over_y)
                second_pairs.append(over_y if core_at == 0 else over_row)
    near = ("y", "core", "row")

    def gather_tokens(own, beside=()):
        if rows_on == 2:
            first = lax.ppermute(own, near, first_pairs)
            second = lax.ppermute(own, near, second_pairs)
            first, second, *_ = lax.optimization_barrier((first, second, *beside))
            third = lax.ppermute(first, near, second_pairs)
            return [own, first, second, third]
        parts = [own] + [shift(own, "row", rows_on, by) for by in range(1, rows_on)]
        return parts + [other_y(part) for part in parts]

    def reduce_tokens(rows_of, middle=None, before_last=None, far_here=None, ready=None):
        def same(value):
            return value

        middle, before_last = (middle or same, before_last or same)
        if rows_on == 2:
            far = rows_of(2, 4)
            if ready:
                far, close = ready((far, rows_of(0, 2)))
            third = lax.ppermute(far[block:], near, second_pairs)
            second = lax.ppermute(far[:block], near, second_pairs)
            if not ready:
                close = rows_of(0, 2)
            third, second, close = (far_here or lax.optimization_barrier)((third, second, close))
            key = (close[block:].astype(jnp.float32) + third.astype(jnp.float32)).astype(jnp.bfloat16)
            first = before_last(lax.ppermute(middle(key), near, first_pairs))
            own = close[:block].astype(jnp.float32) + second.astype(jnp.float32)
            return own + first.astype(jnp.float32)
        partial = rows_of(0, slots)
        parts = [partial[i * block : (i + 1) * block] for i in range(slots)]
        sums = [
            parts[i].astype(jnp.float32) + other_y(parts[rows_on + i]).astype(jnp.float32)
            for i in range(rows_on)
        ]
        sums[0] = middle(sums[0])
        total = sums[0]
        for by in range(1, rows_on):
            moved = shift(sums[by].astype(jnp.bfloat16), "row", rows_on, -by)
            total = total + moved.astype(jnp.float32)
        return before_last(total)

    def product(left, right):
        def rows_of(first, last):
            return dot_nt(left[first * block : last * block], right).astype(jnp.bfloat16)

        return rows_of

    if rows_on == 2:
        slot_y = [y, jnp.where(core == 0, y, 1 - y), jnp.where(core == 0, 1 - y, y), 1 - y]
        slot_row = [row, jnp.where(core == 0, 1 - row, row), jnp.where(core == 0, row, 1 - row), 1 - row]
    else:
        slot_y = [y] * rows_on + [1 - y] * rows_on
        slot_row = [(row - by) % rows_on for by in range(rows_on)] * 2

    def pick(parts, index):
        return lax.dynamic_index_in_dim(jnp.stack(parts), index, 0, keepdims=False)

    def tokens_sent(values):
        parts = []
        for by in range(lines):
            part = lax.dynamic_slice_in_dim(values, ((line + by) % lines) * block, block, 0)
            parts.append(part if by == 0 else shift(part, "col", lines, by))
        return parts

    def tokens_of(parts):
        blocks = [pick(parts, (line - at) % lines) for at in range(lines)]
        return jnp.concatenate([b[:, :half] for b in blocks] + [b[:, half:] for b in blocks], axis=1)

    def features_sent(values):
        blocks = [
            jnp.concatenate(
                [
                    values[:, at * half : (at + 1) * half],
                    values[:, D // 2 + at * half : D // 2 + (at + 1) * half],
                ],
                axis=1,
            )
            for at in range(lines)
        ]
        parts = []
        for by in range(lines):
            part = pick(blocks, (line + by) % lines)
            parts.append(part if by == 0 else shift(part, "col", lines, by))
        return parts

    def features_of(parts):
        return jnp.concatenate([pick(parts, (line - at) % lines) for at in range(lines)], axis=0)

    def half_rows(values):
        return lax.dynamic_slice_in_dim(values, core * half, half, 0)

    def half_columns(values):
        return lax.dynamic_slice_in_dim(values, core * half, half, 1)

    def gather_weight(piece):
        return lax.all_gather(piece, ("core", "col"), axis=0, tiled=True)

    query_rows = half_rows(w_query).astype(jnp.bfloat16)
    pair_rows = half_rows(w_keyvalue).astype(jnp.bfloat16)

    def joint_of(at):
        pieces = [
            query_rows[:, (2 * j + at) * LANES : (2 * j + at + 1) * LANES] for j in range(per_row)
        ]
        pair = pair_rows[:, at * 2 * LANES : (at + 1) * 2 * LANES]
        pieces += [
            pair[:, :LANES],
            pair[:, LANES + HEAD_DIM :],
            pair[:, LANES : LANES + HEAD_DIM],
        ]
        return jnp.concatenate(pieces, axis=1)

    joint_mine = jnp.where(y == 0, joint_of(0), joint_of(1))
    output_columns = half_columns(w_output).astype(jnp.bfloat16)

    def output_of(at):
        pieces = []
        for j in range(per_row):
            base = (2 * j + at) * LANES
            pieces += [
                output_columns[base + HEAD_DIM : base + LANES],
                output_columns[base : base + HEAD_DIM],
            ]
        return jnp.concatenate(pieces, axis=0)

    output_mine = jnp.where(y == 0, output_of(0), output_of(1)).T
    gateup_mine = lax.dynamic_slice(
        w_gateup, (core * half, 0, y * hidden_here), (half, 2, hidden_here)
    ).astype(jnp.bfloat16)
    gateup_mine = jnp.concatenate([gateup_mine[:, 0], gateup_mine[:, 1]], axis=1)
    down_mine = lax.dynamic_slice(
        w_down, (y * hidden_here, core * half), (hidden_here, half)
    ).astype(jnp.bfloat16).T

    gain_parts = [norm_gains] + [shift(norm_gains, "col", lines, by) for by in range(1, lines)]
    gain_blocks = [pick(gain_parts, (line - at) % lines) for at in range(lines)]
    gains = jnp.concatenate(
        [b[:, :half] for b in gain_blocks] + [b[:, half:] for b in gain_blocks], axis=1
    )

    residual_low = tokens_of(tokens_sent(block_input))
    residual_low, late_cotangent, other_segments, joint_mine, output_mine = lax.optimization_barrier(
        (residual_low, cotangent, other_y(segments), joint_mine, output_mine)
    )

    own_starts = document_starts(segments[0])
    other_starts = document_starts(other_segments[0])
    frequency = 10000.0 ** (-2.0 * jnp.arange(HEAD_DIM // 2, dtype=jnp.float32) / HEAD_DIM)
    slot_y, slot_row = (jnp.stack(slot_y).astype(jnp.int32), jnp.stack(slot_row).astype(jnp.int32))
    begins = slot_row * (lines * block) + line * block
    places = begins[:, None] + jnp.arange(block, dtype=jnp.int32)[None, :]
    both_starts = jnp.stack([own_starts, other_starts]).reshape(2, rows_on, lines, block)
    both_starts = lax.dynamic_index_in_dim(both_starts, line, 2, keepdims=False)
    starts = jnp.zeros((slots, block), jnp.int32)
    for which in range(2):
        for row_at in range(rows_on):
            here = ((slot_y != y) == bool(which)) & (slot_row == row_at)
            starts = jnp.where(here[:, None], both_starts[which, row_at][None, :], starts)
    same_y = slot_y[:, None] == slot_y[None, :]
    at_row = slot_row[None, :] == jnp.arange(rows_on, dtype=jnp.int32)[:, None]
    found = jnp.where(
        same_y[:, None, :] & at_row[None, :, :], jnp.arange(slots, dtype=jnp.int32), 0
    ).sum(axis=2)
    meta = jnp.concatenate(
        [(starts[:, :1] // block), (begins // block)[:, None], found.astype(jnp.int32)], axis=1
    )
    meta = jnp.concatenate([meta.reshape(-1), line[None].astype(jnp.int32)])
    info = jnp.stack([places, starts], axis=1)
    offsets = (places - starts).astype(jnp.float32).reshape(-1)
    phases = offsets[:, None] * jnp.tile(frequency, LANES // (HEAD_DIM // 2))[None, :]
    cosine, sine = (jnp.cos(phases), jnp.sin(phases))

    cot_parts = tokens_sent(late_cotangent)
    first_weight = gather_weight(jnp.concatenate([joint_mine, output_mine], axis=1))
    joint_width = joint_mine.shape[1]
    joint_weight, output_weight = (first_weight[:, :joint_width], first_weight[:, joint_width:])
    residual = residual_low.astype(jnp.float32)
    scale_one = lax.rsqrt(jnp.mean(residual * residual, axis=1, keepdims=True) + EPSILON)
    normed_parts = gather_tokens((residual * scale_one * gains[0]).astype(jnp.bfloat16))
    normed_parts, cot_parts = lax.optimization_barrier((normed_parts, cot_parts))
    cot_low = tokens_of(cot_parts)
    cot_chunks = gather_tokens(cot_low)
    queries, pair = project(normed_parts, first_weight, joint_width, cosine, sine, query_width)
    pairs = lax.all_gather(pair.reshape(slots, block, 2 * LANES), "col", axis=0, tiled=False)
    pairs, cot_chunks, gateup_mine, down_mine, meta, info = lax.optimization_barrier(
        (pairs, cot_chunks, gateup_mine, down_mine, meta, info)
    )
    gateup_weight = gather_weight(gateup_mine)
    down_weight = gather_weight(down_mine)
    mixed, logs = attend(meta, queries, pairs, info, rows_on)
    attn_sum = reduce_tokens(product(mixed, output_weight))
    middle = residual + attn_sum
    scale_two = lax.rsqrt(jnp.mean(middle * middle, axis=1, keepdims=True) + EPSILON)
    two_parts = gather_tokens((middle * scale_two * gains[1]).astype(jnp.bfloat16))
    hidden, factor, silu_gate = widen(two_parts, gateup_weight)
    normed_two, cot = (jnp.concatenate(two_parts, axis=0), jnp.concatenate(cot_chunks, axis=0))

    def other_half(rows, grad):
        rows = lax.dynamic_slice_in_dim(rows, (1 - core) * (D // 2), D // 2, 1)
        return dot_tn(rows, grad).astype(jnp.bfloat16)

    def own_half(rows, grad, received):
        rows = lax.dynamic_slice_in_dim(rows, core * (D // 2), D // 2, 1)
        total = dot_tn(rows, grad) + received.astype(jnp.float32)
        return total.astype(jnp.bfloat16)

    def scatter(total):
        return lax.psum_scatter(total, "col", scatter_dimension=0, tiled=True)

    def collect(piece):
        near_y = other_y(piece)
        return [piece, near_y, other_core(piece), other_core(near_y)]

    down_total = own_half(cot, hidden, other_core(other_half(cot, hidden)))
    down_total, down_weight = lax.optimization_barrier((down_total, down_weight))
    down_piece = scatter(down_total)
    work = {}

    def feed_back(first, last):
        work["grad_gate"], work["grad_up"], partial = widen_back(
            cot_chunks[first:last],
            down_weight,
            gateup_weight,
            factor,
            silu_gate,
            first,
            [work[name] for name in ("grad_gate", "grad_up") if name in work],
        )
        return partial

    def feed_others(key):
        gate, up = (work["grad_gate"], work["grad_up"])
        key, gate_other, up_other = lax.optimization_barrier(
            (key, other_half(normed_two, gate), other_half(normed_two, up))
        )
        work["feed"] = (normed_two, gate, up, other_core(gate_other), other_core(up_other))
        return key

    def feed_owns(first):
        first, work["down_piece"], rows, gate, up, gate_other, up_other = lax.optimization_barrier(
            (first, down_piece, *work["feed"])
        )
        work["totals"] = (own_half(rows, gate, gate_other), own_half(rows, up, up_other))
        return first

    grad_normed_two = reduce_tokens(feed_back, feed_others, feed_owns)
    gate_piece, up_piece = [scatter(total) for total in work["totals"]]

    def norm_back(values, scale, grad_normed, gain):
        scaled = grad_normed * gain
        total = jnp.sum(scaled * values, axis=1, keepdims=True)
        return scale * scaled - values * (scale**3 * total / D)

    grad_middle = cot_low.astype(jnp.float32) + norm_back(
        middle, scale_two, grad_normed_two, gains[1]
    )
    gain_two = jnp.sum(grad_normed_two * middle * scale_two, axis=0)

    grad_middle_low, late_hidden = lax.optimization_barrier(
        (grad_middle.astype(jnp.bfloat16), hidden)
    )
    gate_total, up_total = work["totals"]
    back = jnp.concatenate(gather_tokens(grad_middle_low, (gate_total, up_total)), axis=0)

    def back_here(products):
        products, work["back"] = lax.optimization_barrier((products, back))
        return products

    def attention_back(far):
        here = work.get("back", back)
        grad_query, grad_parts = attend_back(
            meta,
            queries,
            pairs,
            dot_nn(here, output_weight).astype(jnp.bfloat16),
            mixed,
            logs,
            info,
            cosine,
            sine,
            rows_on,
        )
        work["grad_parts"] = [grad_parts[0]] + [
            shift(grad_parts[by], "col", lines, -by) for by in range(1, lines)
        ]
        names = ("grad_query", "gate_piece", "back", "mixed")
        far, *values = lax.optimization_barrier((far, grad_query, gate_piece, here, mixed))
        work.update(zip(names, values))
        return far

    def keys_arrive(first):
        first, work["grad_parts"], work["up_piece"] = lax.optimization_barrier(
            (first, work["grad_parts"], up_piece)
        )
        return first

    if rows_on == 2:
        ffn_sum = reduce_tokens(
            product(late_hidden, down_weight), None, keys_arrive, attention_back, back_here
        )
    else:
        ffn_sum = keys_arrive(attention_back(reduce_tokens(product(late_hidden, down_weight))))
    grad_query, gate_piece, back, mixed = [
        work[name] for name in ("grad_query", "gate_piece", "back", "mixed")
    ]
    output_parts = features_sent((middle + ffn_sum).astype(jnp.bfloat16))
    grad_keyvalue = pair_back(work["grad_parts"], cosine, sine, block)
    grad_joint = jnp.concatenate([grad_query, grad_keyvalue], axis=1)
    normed_one = jnp.concatenate(normed_parts, axis=0)
    meta_core = jnp.stack([y, core]).astype(jnp.int32)

    def joint_products(first, last):
        if first:
            return product(grad_joint, joint_weight)(first, last)
        work["shards"] = collect(jnp.concatenate([work["down_piece"], gate_piece], axis=0))
        down_new = turned_update(
            meta_core,
            work["shards"],
            [w_down, down_moment, down_square],
            FF ** (-0.5),
            False,
        )
        output_total = own_half(back, mixed, other_core(other_half(back, mixed)))
        close, work["output"], work["down_new"] = lax.optimization_barrier(
            (product(grad_joint, joint_weight)(first, last), output_total, down_new)
        )
        return close

    def joint_others(key):
        key, work["output_parts"], other = lax.optimization_barrier(
            (key, output_parts, other_half(normed_one, grad_joint))
        )
        work["joint"] = (normed_one, grad_joint, other_core(other))
        work["output_piece"] = scatter(work["output"])
        return key

    def joint_owns(first):
        first, work["output_piece"], rows, grad, other = lax.optimization_barrier(
            (first, work["output_piece"], *work["joint"])
        )
        work["joint_total"] = own_half(rows, grad, other)
        return first

    grad_normed_one = reduce_tokens(joint_products, joint_others, joint_owns)
    joint_piece = scatter(work["joint_total"])
    gateup_new = gateup_update(
        meta_core,
        work["shards"],
        collect(work["up_piece"]),
        [w_gateup, gateup_moment, gateup_square],
        32,
    )
    input_grad = grad_middle + norm_back(residual, scale_one, grad_normed_one, gains[0])
    gain_one = jnp.sum(grad_normed_one * residual * scale_one, axis=0)
    joint_piece, input_parts, gateup_new = lax.optimization_barrier(
        (joint_piece, features_sent(input_grad.astype(jnp.bfloat16)), gateup_new)
    )
    layer_output = features_of(work["output_parts"])
    input_grad = features_of(input_parts).astype(jnp.float32)
    pair_piece = joint_piece[:, query_width:]
    pair_total = pair_piece.astype(jnp.float32)
    for by in range(1, rows_on):
        pair_total = pair_total + shift(pair_piece, "row", rows_on, by).astype(jnp.float32)
    joint_piece = jnp.concatenate(
        [joint_piece[:, :query_width], pair_total.astype(jnp.bfloat16)], axis=1
    )
    joint_new = joint_update(
        meta_core,
        collect(joint_piece),
        [w_query, query_moment, query_square],
        [w_keyvalue, keyvalue_moment, keyvalue_square],
    )
    output_new = turned_update(
        meta_core,
        collect(work["output_piece"]),
        [w_output, output_moment, output_square],
        (HEADS * HEAD_DIM // 64) ** (-0.5),
        True,
    )

    gain_sums = jnp.stack([gain_one, gain_two])
    blocks = [
        jnp.concatenate(
            [
                gain_sums[:, at * half : (at + 1) * half],
                gain_sums[:, D // 2 + at * half : D // 2 + (at + 1) * half],
            ],
            axis=1,
        )
        for at in range(lines)
    ]
    grad_gains = pick(blocks, line)
    for by in range(1, lines):
        grad_gains = grad_gains + shift(pick(blocks, (line + by) % lines), "col", lines, by)
    for axis, size in (("core", 2), ("y", 2), ("row", rows_on)):
        blocks_total = grad_gains
        for by in range(1, size):
            grad_gains = grad_gains + shift(blocks_total, axis, size, by)

    gains_new = adamw_step(norm_gains, grad_gains, gains_moment, gains_square, 0.6, 0.0)
    return (
        layer_output,
        input_grad,
        *gains_new,
        *joint_new,
        *output_new,
        *gateup_new,
        *work["down_new"],
    )


def solution(mesh):
    dp, rows_on, lines = (mesh.shape["dp"], mesh.shape["row"], mesh.shape["col"])
    split = Mesh(mesh.devices.reshape(dp // 2, 2, rows_on, lines), ("y", "core", "row", "col"))
    tokens = P(("y", "core", "row"), "col")
    narrow, wide = (P("col", "row"), P("row", "col"))
    gains, pair, gateup = (P(None, "col"), P("col", None), P("col", None, "row"))
    return jax.shard_map(
        functools.partial(on_device, (rows_on, lines)),
        mesh=split,
        in_specs=(
            tokens,
            tokens,
            P(("y", "core"), None),
            gains,
            narrow,
            pair,
            wide,
            gateup,
            wide,
            gains,
            gains,
            narrow,
            narrow,
            pair,
            pair,
            wide,
            wide,
            gateup,
            gateup,
            wide,
            wide,
        ),
        out_specs=(tokens, tokens)
        + (gains,) * 3
        + (narrow,) * 3
        + (pair,) * 3
        + (wide,) * 3
        + (gateup,) * 3
        + (wide,) * 3,
        check_vma=False,
    )
```

```python
import functools

import jax
import jax.numpy as jnp
from jax import lax
from jax.experimental import pallas as pl
from jax.experimental.pallas import tpu as pltpu
from jax.sharding import Mesh, PartitionSpec as P

D = 2048
HEADS = 32
KV_HEADS = 4
HEAD_DIM = 64
FF = 5632
STEP = 10

EPSILON = 1e-05
BETA_ONE = 0.9
BETA_TWO = 0.999
ADAM_EPS = 1e-08
MASKED = -1e30
SCORE_SCALE = HEAD_DIM ** (-0.5)
LANES = 128
VMEM_LIMIT = 48 * 1024 * 1024


def dot_nn(left, right):
    return lax.dot_general(left, right, (((1,), (0,)), ((), ())), preferred_element_type=jnp.float32)


def dot_nt(left, right):
    return lax.dot_general(left, right, (((1,), (1,)), ((), ())), preferred_element_type=jnp.float32)


def dot_tn(left, right):
    return lax.dot_general(left, right, (((0,), (0,)), ((), ())), preferred_element_type=jnp.float32)


def adamw_step(weight, gradient, moment, square, step_rate, decay_rate):
    moment_new = BETA_ONE * moment + (1.0 - BETA_ONE) * gradient
    square_new = BETA_TWO * square + (1.0 - BETA_TWO) * gradient * gradient
    fixed_one = moment_new / (1.0 - BETA_ONE**STEP)
    fixed_two = square_new / (1.0 - BETA_TWO**STEP)
    weight_new = weight - step_rate * (
        fixed_one / (jnp.sqrt(fixed_two) + ADAM_EPS) + decay_rate * weight
    )
    return (moment_new, square_new, weight_new)


def document_starts(segment_ids):
    places = jnp.arange(segment_ids.shape[0], dtype=jnp.int32)
    starts = jnp.concatenate([jnp.ones((1,), jnp.bool_), segment_ids[1:] != segment_ids[:-1]])
    return lax.cummax(jnp.where(starts, places, 0), axis=0)


def turn(values):
    lane = lax.broadcasted_iota(jnp.int32, values.shape, 1)
    ahead = pltpu.roll(values, LANES - HEAD_DIM // 2, 1)
    behind = pltpu.roll(values, HEAD_DIM // 2, 1)
    return jnp.where(lane % HEAD_DIM < HEAD_DIM // 2, -ahead, behind)


def take_chunk(rows_refs, held_ref):
    for at, ref in enumerate(rows_refs):

        @pl.when(pl.program_id(0) == at)
        def _(ref=ref):
            held_ref[...] = ref[...]


def project_kernel(slots, *refs):
    rows_refs, (weight_ref, cos_ref, sin_ref, query_ref, pair_ref, held_ref) = (refs[:slots], refs[slots:])
    take_chunk(rows_refs, held_ref)
    sums = dot_nn(held_ref[...], weight_ref[...])
    cosine, sine = cos_ref[...], sin_ref[...]
    width = query_ref.shape[1]
    lane = lax.broadcasted_iota(jnp.int32, cosine.shape, 1)
    for start in range(0, width, LANES):
        part = sums[:, start : start + LANES]
        turned = (part * cosine + turn(part) * sine).astype(jnp.bfloat16)
        query_ref[:, start : start + LANES] = turned * jnp.bfloat16(SCORE_SCALE)
    for which in range(2):
        part = sums[:, width + which * LANES : width + (which + 1) * LANES]
        is_key = (lane < HEAD_DIM) if which == 0 else (lane >= HEAD_DIM)
        turned = jnp.where(is_key, part * cosine + turn(part) * sine, part)
        pair_ref[:, which * LANES : (which + 1) * LANES] = turned.astype(jnp.bfloat16)


def project(chunks, weight, total, cosine, sine, width):
    slots = len(chunks)
    block, depth = chunks[0].shape
    rows = slots * block
    whole = pl.BlockSpec((block, depth), lambda i: (0, 0))
    return pl.pallas_call(
        functools.partial(project_kernel, slots),
        grid=(slots,),
        in_specs=[whole] * slots
        + [
            pl.BlockSpec((depth, total), lambda i: (0, 0)),
            pl.BlockSpec((block, LANES), lambda i: (i, 0)),
            pl.BlockSpec((block, LANES), lambda i: (i, 0)),
        ],
        out_specs=[
            pl.BlockSpec((block, width), lambda i: (i, 0)),
            pl.BlockSpec((block, total - width), lambda i: (i, 0)),
        ],
        out_shape=[
            jax.ShapeDtypeStruct((rows, width), jnp.bfloat16),
            jax.ShapeDtypeStruct((rows, total - width), jnp.bfloat16),
        ],
        scratch_shapes=[pltpu.VMEM((block, depth), jnp.bfloat16)],
        compiler_params=pltpu.CompilerParams(vmem_limit_bytes=VMEM_LIMIT),
        cost_estimate=pl.CostEstimate(
            flops=2 * rows * depth * total,
            bytes_accessed=(rows + total) * depth * 2,
            transcendentals=0,
        ),
        name="project",
    )(*chunks, weight, cosine, sine)


def widen_kernel(slots, *refs):
    rows_refs, (weight_ref, hidden_ref, factor_ref, silu_ref, held_ref) = (refs[:slots], refs[slots:])
    take_chunk(rows_refs, held_ref)
    sums = dot_nn(held_ref[...], weight_ref[...])
    width = hidden_ref.shape[1]
    gate, upward = (sums[:, :width], sums[:, width:])
    sigmoid = jax.nn.sigmoid(gate)
    silu = gate * sigmoid
    hidden_ref[...] = (silu * upward).astype(jnp.bfloat16)
    factor_ref[...] = (upward * sigmoid * (1.0 + gate * (1.0 - sigmoid))).astype(jnp.bfloat16)
    silu_ref[...] = silu.astype(jnp.bfloat16)


def widen(chunks, weight):
    slots = len(chunks)
    block, depth = chunks[0].shape
    width = weight.shape[1] // 2
    rows = slots * block
    once = pl.Buffered(1)
    return pl.pallas_call(
        functools.partial(widen_kernel, slots),
        grid=(slots,),
        in_specs=[pl.BlockSpec((block, depth), lambda i: (0, 0), pipeline_mode=once)] * slots
        + [pl.BlockSpec(weight.shape, lambda i: (0, 0), pipeline_mode=once)],
        out_specs=[pl.BlockSpec((block, width), lambda i: (i, 0))] * 3,
        out_shape=[jax.ShapeDtypeStruct((rows, width), jnp.bfloat16)] * 3,
        scratch_shapes=[pltpu.VMEM((block, depth), jnp.bfloat16)],
        compiler_params=pltpu.CompilerParams(vmem_limit_bytes=VMEM_LIMIT),
        cost_estimate=pl.CostEstimate(
            flops=4 * rows * depth * width,
            bytes_accessed=(rows + 2 * width) * depth * 2 + 6 * rows * width,
            transcendentals=rows * width,
        ),
        name="widen",
    )(*chunks, weight)


def widen_back_kernel(slots, kept, *refs):
    rows_refs, refs = (refs[:slots], refs[slots:])
    down_ref, gateup_ref, factor_ref, silu_ref = refs[:4]
    gate_ref, up_ref, partial_ref, held_ref = refs[4 + kept :]
    take_chunk(rows_refs, held_ref)
    grad_hidden = dot_nn(held_ref[...], down_ref[...])
    gate = (grad_hidden * factor_ref[...].astype(jnp.float32)).astype(jnp.bfloat16)
    up = (grad_hidden * silu_ref[...].astype(jnp.float32)).astype(jnp.bfloat16)
    gate_ref[...] = gate
    up_ref[...] = up
    both = jnp.concatenate([gate, up], axis=1)
    partial_ref[...] = dot_nt(both, gateup_ref[...]).astype(jnp.bfloat16)


def widen_back(chunks, down, gateup, factor, silu, first, kept):
    slots = len(chunks)
    block, depth = chunks[0].shape
    width = down.shape[1]
    once = pl.Buffered(1)
    tile = pl.BlockSpec((block, width), lambda i: (first + i, 0))
    return pl.pallas_call(
        functools.partial(widen_back_kernel, slots, len(kept)),
        grid=(slots,),
        in_specs=[pl.BlockSpec((block, depth), lambda i: (0, 0), pipeline_mode=once)] * slots
        + [
            pl.BlockSpec(down.shape, lambda i: (0, 0), pipeline_mode=once),
            pl.BlockSpec(gateup.shape, lambda i: (0, 0), pipeline_mode=once),
            tile,
            tile,
        ]
        + [pl.BlockSpec(memory_space=pl.ANY)] * len(kept),
        out_specs=[tile, tile, pl.BlockSpec((block, depth), lambda i: (i, 0))],
        out_shape=[jax.ShapeDtypeStruct(factor.shape, jnp.bfloat16)] * 2
        + [jax.ShapeDtypeStruct((slots * block, depth), jnp.bfloat16)],
        scratch_shapes=[pltpu.VMEM((block, depth), jnp.bfloat16)],
        input_output_aliases={slots + 4 + i: i for i in range(len(kept))},
        compiler_params=pltpu.CompilerParams(vmem_limit_bytes=VMEM_LIMIT),
        cost_estimate=pl.CostEstimate(
            flops=slots * block * depth * width,
            bytes_accessed=8 * slots * block * width,
            transcendentals=0,
        ),
        name="widen_back",
    )(*chunks, down, gateup, factor, silu, *kept)


def stack_heads(values):
    return jnp.concatenate(
        [values[:, start : start + LANES] for start in range(0, values.shape[1], LANES)], axis=0
    )


def block_of(meta_ref, chunk, step, parts, lines):
    base = chunk * (2 + parts)
    key_block = meta_ref[base + 1] - step
    slot = meta_ref[base + 2 + key_block // lines]
    own_line = meta_ref[pl.num_programs(0) * (2 + parts)]
    line = lax.rem(key_block, lines)
    return (key_block, slot, line, lax.rem(own_line - line + lines, lines))


def attend_kernel(parts, lines, meta_ref, query_ref, pair_ref, info_ref, out_ref, log_ref):
    chunk = pl.program_id(0)
    block = query_ref.shape[0]
    heads = query_ref.shape[1] // LANES
    stacked = stack_heads(query_ref[...])
    lane = lax.broadcasted_iota(jnp.int32, stacked.shape, 1)
    place = jnp.concatenate([info_ref[0, 0:1, :]] * heads, axis=1)
    start = jnp.concatenate([info_ref[0, 1:2, :]] * heads, axis=1)
    base = chunk * (2 + parts)
    steps = meta_ref[base + 1] - meta_ref[base] + 1
    width = heads * block
    key_lanes = lane < HEAD_DIM
    queries = [
        jnp.where(key_lanes if which == 0 else ~key_lanes, stacked, jnp.zeros_like(stacked))
        for which in range(2)
    ]

    def body(step, carry):
        key_block, slot, at, _ = block_of(meta_ref, chunk, step, parts, lines)
        key_place = key_block * block + lax.broadcasted_iota(jnp.int32, (block, width), 0)
        seen = (key_place <= place) & (key_place >= start)
        result = []
        for which in range(2):
            peak, total, mixed = carry[which]
            pair = pair_ref[at, slot, :, which * LANES : (which + 1) * LANES]
            scores = jnp.where(seen, dot_nt(pair, queries[which]), MASKED)
            new_peak = jnp.maximum(peak, jnp.max(scores, axis=0, keepdims=True))
            weights = jnp.exp(scores - new_peak)
            shrink = jnp.exp(peak - new_peak)
            total = total * shrink + jnp.sum(weights, axis=0, keepdims=True)
            mixed = mixed * shrink + dot_tn(pair, weights.astype(jnp.bfloat16))
            result.append((new_peak, total, mixed))
        return tuple(result)

    empty = (
        jnp.full((1, width), MASKED, jnp.float32),
        jnp.zeros((1, width), jnp.float32),
        jnp.zeros((LANES, width), jnp.float32),
    )
    outs = []
    for which, (peak, total, mixed) in enumerate(lax.fori_loop(0, steps, body, (empty, empty))):
        log_ref[0, which : which + 1, :] = peak + jnp.log(total)
        outs.append(mixed / total)
    joined = jnp.concatenate([outs[1][:HEAD_DIM], outs[0][HEAD_DIM:]], axis=0)
    rows = joined.T.astype(jnp.bfloat16)
    for head in range(heads):
        out_ref[:, head * LANES : (head + 1) * LANES] = rows[head * block : (head + 1) * block]


def attend(meta, queries, pairs, info, parts):
    chunks, block = (info.shape[0], info.shape[2])
    width = queries.shape[1]
    heads = width // LANES
    lines = pairs.shape[0]
    steps = 3 * chunks
    return pl.pallas_call(
        functools.partial(attend_kernel, parts, lines),
        grid_spec=pltpu.PrefetchScalarGridSpec(
            num_scalar_prefetch=1,
            grid=(chunks,),
            in_specs=[
                pl.BlockSpec((block, width), lambda i, m: (i, 0)),
                pl.BlockSpec(pairs.shape, lambda i, m: (0, 0, 0, 0)),
                pl.BlockSpec((1, 2, block), lambda i, m: (i, 0, 0)),
            ],
            out_specs=[
                pl.BlockSpec((block, width), lambda i, m: (i, 0)),
                pl.BlockSpec((1, 2, heads * block), lambda i, m: (i, 0, 0)),
            ],
        ),
        out_shape=[
            jax.ShapeDtypeStruct(queries.shape, jnp.bfloat16),
            jax.ShapeDtypeStruct((chunks, 2, heads * block), jnp.float32),
        ],
        compiler_params=pltpu.CompilerParams(vmem_limit_bytes=VMEM_LIMIT),
        cost_estimate=pl.CostEstimate(
            flops=steps * 2 * 2 * 2 * heads * block * block * LANES,
            bytes_accessed=queries.size * 4 + pairs.size * 2,
            transcendentals=steps * 2 * heads * block * block,
        ),
        name="attend",
    )(meta, queries, pairs, info)


def attend_back_kernel(parts, lines, meta_ref, query_ref, *refs):
    pair_ref, grad_ref, mixed_ref, log_ref, info_ref, cos_ref, sin_ref, query_out = refs[:8]
    pair_outs = refs[8 : 8 + lines]
    sums = refs[8 + lines]
    chunk = pl.program_id(0)
    block = query_ref.shape[0]
    heads = query_ref.shape[1] // LANES

    @pl.when(chunk == 0)
    def _():
        sums[...] = jnp.zeros_like(sums)

    stacked = stack_heads(query_ref[...])
    stacked_grad = stack_heads(grad_ref[...])
    product = stacked_grad.astype(jnp.float32) * stack_heads(mixed_ref[...]).astype(jnp.float32)
    lane = lax.broadcasted_iota(jnp.int32, stacked.shape, 1)
    place = jnp.concatenate([info_ref[0, 0:1, :]] * heads, axis=1)
    start = jnp.concatenate([info_ref[0, 1:2, :]] * heads, axis=1)
    base = chunk * (2 + parts)
    steps = meta_ref[base + 1] - meta_ref[base] + 1
    width = heads * block
    key_lanes = lane < HEAD_DIM
    queries, grad, centre, logs = ([], [], [], [])
    for which in range(2):
        is_key = key_lanes if which == 0 else ~key_lanes
        queries.append(jnp.where(is_key, stacked, jnp.zeros_like(stacked)))
        grad.append(jnp.where(is_key, jnp.zeros_like(stacked_grad), stacked_grad))
        own = jnp.where(is_key, 0.0, product)
        centre.append(
            lax.dot_general(
                jnp.ones((8, LANES), jnp.float32),
                own,
                (((1,), (1,)), ((), ())),
                precision=lax.Precision.HIGHEST,
                preferred_element_type=jnp.float32,
            )[0:1]
        )
        logs.append(log_ref[0, which : which + 1, :])

    def body(step, carry):
        key_block, slot, at, shift = block_of(meta_ref, chunk, step, parts, lines)
        key_place = key_block * block + lax.broadcasted_iota(jnp.int32, (block, width), 0)
        seen = (key_place <= place) & (key_place >= start)
        result = []
        for which in range(2):
            columns = slice(which * LANES, (which + 1) * LANES)
            pair = pair_ref[at, slot, :, columns]
            scores = jnp.where(seen, dot_nt(pair, queries[which]), MASKED)
            weights = jnp.exp(scores - logs[which])
            grad_weights = dot_nt(pair, grad[which]) - centre[which]
            grad_scores = (weights * grad_weights).astype(jnp.bfloat16)
            sums[shift, slot, :, columns] += dot_nn(grad_scores, queries[which]) + dot_nn(
                weights.astype(jnp.bfloat16), grad[which]
            )
            result.append(carry[which] + dot_tn(pair, grad_scores))
        return tuple(result)

    empty = jnp.zeros((LANES, width), jnp.float32)
    grads = lax.fori_loop(0, steps, body, (empty, empty))
    joined = jnp.concatenate([grads[0][:HEAD_DIM], grads[1][HEAD_DIM:]], axis=0)
    rows = joined.T * SCORE_SCALE
    cosine, sine = cos_ref[...], sin_ref[...]
    for head in range(heads):
        part = rows[head * block : (head + 1) * block]
        back = part * cosine - turn(part) * sine
        query_out[:, head * LANES : (head + 1) * LANES] = back.astype(jnp.bfloat16)

    @pl.when(chunk == pl.num_programs(0) - 1)
    def _():
        for line in range(lines):
            pair_outs[line][...] = sums[line].astype(jnp.bfloat16)


def attend_back(meta, queries, pairs, grad_mixed, mixed, logs, info, cosine, sine, parts):
    chunks, block = (info.shape[0], info.shape[2])
    width = queries.shape[1]
    heads = width // LANES
    lines = pairs.shape[0]
    shape = pairs.shape[1:]
    steps = 3 * chunks
    wide = pl.BlockSpec((block, width), lambda i, m: (i, 0))
    table = pl.BlockSpec((block, LANES), lambda i, m: (i, 0))
    whole = pl.BlockSpec(shape, lambda i, m: (0, 0, 0))
    outs = pl.pallas_call(
        functools.partial(attend_back_kernel, parts, lines),
        grid_spec=pltpu.PrefetchScalarGridSpec(
            num_scalar_prefetch=1,
            grid=(chunks,),
            in_specs=[
                wide,
                pl.BlockSpec(pairs.shape, lambda i, m: (0, 0, 0, 0)),
                wide,
                wide,
                pl.BlockSpec((1, 2, heads * block), lambda i, m: (i, 0, 0)),
                pl.BlockSpec((1, 2, block), lambda i, m: (i, 0, 0)),
                table,
                table,
            ],
            out_specs=[wide] + [whole] * lines,
            scratch_shapes=[pltpu.VMEM(pairs.shape, jnp.float32)],
        ),
        out_shape=[jax.ShapeDtypeStruct(queries.shape, jnp.bfloat16)]
        + [jax.ShapeDtypeStruct(shape, jnp.bfloat16)] * lines,
        compiler_params=pltpu.CompilerParams(vmem_limit_bytes=VMEM_LIMIT),
        cost_estimate=pl.CostEstimate(
            flops=steps * 2 * 5 * 2 * heads * block * block * LANES,
            bytes_accessed=queries.size * 8 + 2 * pairs.size * 2,
            transcendentals=steps * 2 * heads * block * block,
        ),
        name="attend_back",
    )(
        meta,
        queries,
        pairs,
        grad_mixed,
        mixed,
        logs,
        info,
        cosine,
        sine,
    )
    return (outs[0], [out.reshape(chunks * block, 2 * LANES) for out in outs[1:]])


def pair_back_kernel(*refs):
    *part_refs, cos_ref, sin_ref, out_ref = refs
    cosine, sine = cos_ref[...], sin_ref[...]
    lane = lax.broadcasted_iota(jnp.int32, cosine.shape, 1)
    for which in range(2):
        columns = slice(which * LANES, (which + 1) * LANES)
        total = part_refs[0][:, columns].astype(jnp.float32)
        for ref in part_refs[1:]:
            total = total + ref[:, columns].astype(jnp.float32)
        is_key = (lane < HEAD_DIM) if which == 0 else (lane >= HEAD_DIM)
        total = jnp.where(is_key, total * cosine - turn(total) * sine, total)
        out_ref[:, columns] = total.astype(jnp.bfloat16)


def pair_back(parts, cosine, sine, block):
    rows, columns = parts[0].shape
    tile = pl.BlockSpec((block, columns), lambda i: (i, 0))
    table = pl.BlockSpec((block, LANES), lambda i: (i, 0))
    return pl.pallas_call(
        pair_back_kernel,
        grid=(rows // block,),
        in_specs=[tile] * len(parts) + [table, table],
        out_specs=tile,
        out_shape=jax.ShapeDtypeStruct((rows, columns), jnp.bfloat16),
        compiler_params=pltpu.CompilerParams(vmem_limit_bytes=VMEM_LIMIT),
        name="pair_back",
    )(*parts, cosine, sine)


def update(refs, index, gradient, rate):
    weight, moment, square = [ref[index] for ref in refs[:3]]
    moment_new, square_new, weight_new = adamw_step(weight, gradient, moment, square, rate, 0.1)
    for ref, value in zip(refs[3:], (moment_new, square_new, weight_new)):
        ref[index] = value


def chosen(meta_ref, grad_refs, at, rows, columns):
    own_y = meta_ref[0] == at
    first = pl.program_id(0) == 0
    near = jnp.where(first, grad_refs[0][rows, columns], grad_refs[2][rows, columns])
    far = jnp.where(first, grad_refs[1][rows, columns], grad_refs[3][rows, columns])
    return jnp.where(own_y, near, far).astype(jnp.float32)


def joint_update_kernel(meta_ref, *refs):
    grad_refs, query_refs, pair_refs = (refs[:4], refs[4:7] + refs[10:13], refs[7:10] + refs[13:16])
    groups = query_refs[0].shape[1] // (2 * LANES)
    every = slice(None)
    for at in range(2):
        for j in range(groups):
            gradient = chosen(meta_ref, grad_refs, at, every, slice(j * LANES, (j + 1) * LANES))
            place = slice((2 * j + at) * LANES, (2 * j + at + 1) * LANES)
            update(query_refs, (every, place), gradient, D ** (-0.5))
        for which in range(2):
            start = (groups + which) * LANES
            gradient = chosen(meta_ref, grad_refs, at, every, slice(start, start + LANES))
            if which == 1:
                gradient = pltpu.roll(gradient, HEAD_DIM, 1)
            place = slice((2 * at + which) * LANES, (2 * at + which + 1) * LANES)
            update(pair_refs, (every, place), gradient, D ** (-0.5))


def joint_update(meta, grads, query, pair):
    half = grads[0].shape[0]

    def rows_of(array):
        return pl.BlockSpec((half, array.shape[1]), lambda i, m: ((m[1] + i) % 2, 0))

    whole = pl.BlockSpec(grads[0].shape, lambda i, m: (0, 0))
    blocks = [rows_of(array) for array in (*query, *pair)]
    return pl.pallas_call(
        joint_update_kernel,
        grid_spec=pltpu.PrefetchScalarGridSpec(
            num_scalar_prefetch=1, grid=(2,), in_specs=[whole] * 4 + blocks, out_specs=blocks
        ),
        out_shape=[jax.ShapeDtypeStruct(array.shape, array.dtype) for array in (*query, *pair)],
        compiler_params=pltpu.CompilerParams(vmem_limit_bytes=VMEM_LIMIT),
        cost_estimate=pl.CostEstimate(
            flops=20 * (query[0].size + pair[0].size),
            bytes_accessed=24 * (query[0].size + pair[0].size),
            transcendentals=0,
        ),
        name="joint_update",
    )(meta, *grads, *query, *pair)


def turned_update_kernel(rate, swapped, meta_ref, *refs):
    grad_refs, weight_refs = (refs[:4], refs[4:10])
    at = pl.program_id(1)
    width = grad_refs[0].shape[1]
    every = slice(None)
    for j, start in enumerate(range(0, width, LANES)):
        strip = slice(start, min(start + LANES, width))
        gradient = chosen(meta_ref, grad_refs, at, every, strip).T
        if swapped:
            gradient = jnp.concatenate([gradient[HEAD_DIM:], gradient[:HEAD_DIM]], axis=0)
            index = (j, 0)
        else:
            index = (strip, every)
        update(weight_refs, index, gradient, rate)


def turned_update(meta, grads, weights, rate, swapped):
    shape = weights[0].shape
    half, width = (shape[1] // 2, grads[0].shape[1])
    if swapped:
        weights = [w.reshape(width // LANES, 2, LANES, shape[1]) for w in weights]
        block = pl.BlockSpec(
            (width // LANES, 1, LANES, half), lambda i, at, m: (0, at, 0, (m[1] + i) % 2)
        )
    else:
        block = pl.BlockSpec((width, half), lambda i, at, m: (at, (m[1] + i) % 2))
    outs = pl.pallas_call(
        functools.partial(turned_update_kernel, rate, swapped),
        grid_spec=pltpu.PrefetchScalarGridSpec(
            num_scalar_prefetch=1,
            grid=(2, 2),
            in_specs=[pl.BlockSpec((half, width), lambda i, at, m: (0, 0))] * 4 + [block] * 3,
            out_specs=[block] * 3,
        ),
        out_shape=[jax.ShapeDtypeStruct(weights[0].shape, jnp.float32)] * 3,
        compiler_params=pltpu.CompilerParams(vmem_limit_bytes=VMEM_LIMIT),
        cost_estimate=pl.CostEstimate(
            flops=20 * weights[0].size, bytes_accessed=24 * weights[0].size, transcendentals=0
        ),
        name="turned_update",
    )(meta, *grads, *weights)
    return [out.reshape(shape) for out in outs]


def gateup_update_kernel(meta_ref, *refs):
    gate_refs, up_refs, weight_refs = (refs[:4], refs[4:8], refs[8:14])
    every = slice(None)
    gate, up = [
        jnp.concatenate([chosen(meta_ref, grads, at, every, every) for at in range(2)], axis=1)
        for grads in (gate_refs, up_refs)
    ]
    update(weight_refs, every, jnp.stack([gate, up], axis=1), D ** (-0.5))


def gateup_update(meta, gates, ups, weights, rows):
    half, width = ups[0].shape
    shape = weights[0].shape
    tiles = half // rows
    gate = pl.BlockSpec((rows, width), lambda i, j, m: (tiles + j, 0))
    up = pl.BlockSpec((rows, width), lambda i, j, m: (j, 0))
    block = pl.BlockSpec(
        (rows, 2, shape[2]), lambda i, j, m: (((m[1] + i) % 2) * tiles + j, 0, 0)
    )
    return pl.pallas_call(
        gateup_update_kernel,
        grid_spec=pltpu.PrefetchScalarGridSpec(
            num_scalar_prefetch=1,
            grid=(2, tiles),
            in_specs=[gate] * 4 + [up] * 4 + [block] * 3,
            out_specs=[block] * 3,
        ),
        out_shape=[jax.ShapeDtypeStruct(shape, jnp.float32)] * 3,
        compiler_params=pltpu.CompilerParams(vmem_limit_bytes=VMEM_LIMIT),
        cost_estimate=pl.CostEstimate(
            flops=20 * weights[0].size, bytes_accessed=28 * weights[0].size, transcendentals=0
        ),
        name="gateup_update",
    )(meta, *gates, *ups, *weights)


def on_device(
    sizes,
    block_input,
    cotangent,
    segments,
    norm_gains,
    w_query,
    w_keyvalue,
    w_output,
    w_gateup,
    w_down,
    gains_moment,
    gains_square,
    query_moment,
    query_square,
    keyvalue_moment,
    keyvalue_square,
    output_moment,
    output_square,
    gateup_moment,
    gateup_square,
    down_moment,
    down_square,
):
    rows_on, lines = sizes
    y, core, row, line = [lax.axis_index(name) for name in ("y", "core", "row", "col")]
    length = segments.shape[1]
    block = block_input.shape[0] // lines
    wide = block_input.shape[1]
    half = wide // 2
    slots = 2 * rows_on
    per_row = w_query.shape[1] // (KV_HEADS * HEAD_DIM)
    query_width = per_row * LANES
    hidden_here = w_gateup.shape[2] // 2

    def shift(value, axis, size, by):
        return lax.ppermute(value, axis, [(i, (i + by) % size) for i in range(size)])

    def other_core(value):
        return lax.ppermute(value, "core", [(0, 1), (1, 0)])

    def other_y(value):
        return lax.ppermute(value, "y", [(0, 1), (1, 0)])

    def place_of(y_at, core_at, row_at):
        return (y_at * 2 + core_at) * rows_on + row_at

    first_pairs, second_pairs = ([], [])
    for y_at in range(2):
        for core_at in range(2):
            for row_at in range(rows_on):
                over_row = (
                    place_of(y_at, core_at, row_at),
                    place_of(y_at, core_at, (row_at + 1) % rows_on),
                )
                over_y = (place_of(y_at, core_at, row_at), place_of(1 - y_at, core_at, row_at))
                first_pairs.append(over_row if core_at == 0 else over_y)
                second_pairs.append(over_y if core_at == 0 else over_row)
    near = ("y", "core", "row")

    def gather_tokens(own, beside=()):
        if rows_on == 2:
            first = lax.ppermute(own, near, first_pairs)
            second = lax.ppermute(own, near, second_pairs)
            first, second, *_ = lax.optimization_barrier((first, second, *beside))
            third = lax.ppermute(first, near, second_pairs)
            return [own, first, second, third]
        parts = [own] + [shift(own, "row", rows_on, by) for by in range(1, rows_on)]
        return parts + [other_y(part) for part in parts]

    def reduce_tokens(rows_of, middle=None, before_last=None, far_here=None, ready=None):
        def same(value):
            return value

        middle, before_last = (middle or same, before_last or same)
        if rows_on == 2:
            far = rows_of(2, 4)
            if ready:
                far, close = ready((far, rows_of(0, 2)))
            third = lax.ppermute(far[block:], near, second_pairs)
            second = lax.ppermute(far[:block], near, second_pairs)
            if not ready:
                close = rows_of(0, 2)
            third, second, close = (far_here or lax.optimization_barrier)((third, second, close))
            key = (close[block:].astype(jnp.float32) + third.astype(jnp.float32)).astype(jnp.bfloat16)
            first = before_last(lax.ppermute(middle(key), near, first_pairs))
            own = close[:block].astype(jnp.float32) + second.astype(jnp.float32)
            return own + first.astype(jnp.float32)
        partial = rows_of(0, slots)
        parts = [partial[i * block : (i + 1) * block] for i in range(slots)]
        sums = [
            parts[i].astype(jnp.float32) + other_y(parts[rows_on + i]).astype(jnp.float32)
            for i in range(rows_on)
        ]
        sums[0] = middle(sums[0])
        total = sums[0]
        for by in range(1, rows_on):
            moved = shift(sums[by].astype(jnp.bfloat16), "row", rows_on, -by)
            total = total + moved.astype(jnp.float32)
        return before_last(total)

    def product(left, right):
        def rows_of(first, last):
            return dot_nt(left[first * block : last * block], right).astype(jnp.bfloat16)

        return rows_of

    if rows_on == 2:
        slot_y = [y, jnp.where(core == 0, y, 1 - y), jnp.where(core == 0, 1 - y, y), 1 - y]
        slot_row = [row, jnp.where(core == 0, 1 - row, row), jnp.where(core == 0, row, 1 - row), 1 - row]
    else:
        slot_y = [y] * rows_on + [1 - y] * rows_on
        slot_row = [(row - by) % rows_on for by in range(rows_on)] * 2

    def pick(parts, index):
        return lax.dynamic_index_in_dim(jnp.stack(parts), index, 0, keepdims=False)

    def tokens_sent(values):
        parts = []
        for by in range(lines):
            part = lax.dynamic_slice_in_dim(values, ((line + by) % lines) * block, block, 0)
            parts.append(part if by == 0 else shift(part, "col", lines, by))
        return parts

    def tokens_of(parts):
        blocks = [pick(parts, (line - at) % lines) for at in range(lines)]
        return jnp.concatenate([b[:, :half] for b in blocks] + [b[:, half:] for b in blocks], axis=1)

    def features_sent(values):
        blocks = [
            jnp.concatenate(
                [
                    values[:, at * half : (at + 1) * half],
                    values[:, D // 2 + at * half : D // 2 + (at + 1) * half],
                ],
                axis=1,
            )
            for at in range(lines)
        ]
        parts = []
        for by in range(lines):
            part = pick(blocks, (line + by) % lines)
            parts.append(part if by == 0 else shift(part, "col", lines, by))
        return parts

    def features_of(parts):
        return jnp.concatenate([pick(parts, (line - at) % lines) for at in range(lines)], axis=0)

    def half_rows(values):
        return lax.dynamic_slice_in_dim(values, core * half, half, 0)

    def half_columns(values):
        return lax.dynamic_slice_in_dim(values, core * half, half, 1)

    def gather_weight(piece):
        return lax.all_gather(piece, ("core", "col"), axis=0, tiled=True)

    query_rows = half_rows(w_query).astype(jnp.bfloat16)
    pair_rows = half_rows(w_keyvalue).astype(jnp.bfloat16)

    def joint_of(at):
        pieces = [
            query_rows[:, (2 * j + at) * LANES : (2 * j + at + 1) * LANES] for j in range(per_row)
        ]
        pair = pair_rows[:, at * 2 * LANES : (at + 1) * 2 * LANES]
        pieces += [
            pair[:, :LANES],
            pair[:, LANES + HEAD_DIM :],
            pair[:, LANES : LANES + HEAD_DIM],
        ]
        return jnp.concatenate(pieces, axis=1)

    joint_mine = jnp.where(y == 0, joint_of(0), joint_of(1))
    output_columns = half_columns(w_output).astype(jnp.bfloat16)

    def output_of(at):
        pieces = []
        for j in range(per_row):
            base = (2 * j + at) * LANES
            pieces += [
                output_columns[base + HEAD_DIM : base + LANES],
                output_columns[base : base + HEAD_DIM],
            ]
        return jnp.concatenate(pieces, axis=0)

    output_mine = jnp.where(y == 0, output_of(0), output_of(1)).T
    gateup_mine = lax.dynamic_slice(
        w_gateup, (core * half, 0, y * hidden_here), (half, 2, hidden_here)
    ).astype(jnp.bfloat16)
    gateup_mine = jnp.concatenate([gateup_mine[:, 0], gateup_mine[:, 1]], axis=1)
    down_mine = lax.dynamic_slice(
        w_down, (y * hidden_here, core * half), (hidden_here, half)
    ).astype(jnp.bfloat16).T

    gain_parts = [norm_gains] + [shift(norm_gains, "col", lines, by) for by in range(1, lines)]
    gain_blocks = [pick(gain_parts, (line - at) % lines) for at in range(lines)]
    gains = jnp.concatenate(
        [b[:, :half] for b in gain_blocks] + [b[:, half:] for b in gain_blocks], axis=1
    )

    residual_low = tokens_of(tokens_sent(block_input))
    residual_low, late_cotangent, other_segments, joint_mine, output_mine = lax.optimization_barrier(
        (residual_low, cotangent, other_y(segments), joint_mine, output_mine)
    )

    own_starts = document_starts(segments[0])
    other_starts = document_starts(other_segments[0])
    frequency = 10000.0 ** (-2.0 * jnp.arange(HEAD_DIM // 2, dtype=jnp.float32) / HEAD_DIM)
    slot_y, slot_row = (jnp.stack(slot_y).astype(jnp.int32), jnp.stack(slot_row).astype(jnp.int32))
    begins = slot_row * (lines * block) + line * block
    places = begins[:, None] + jnp.arange(block, dtype=jnp.int32)[None, :]
    both_starts = jnp.stack([own_starts, other_starts]).reshape(2, rows_on, lines, block)
    both_starts = lax.dynamic_index_in_dim(both_starts, line, 2, keepdims=False)
    starts = jnp.zeros((slots, block), jnp.int32)
    for which in range(2):
        for row_at in range(rows_on):
            here = ((slot_y != y) == bool(which)) & (slot_row == row_at)
            starts = jnp.where(here[:, None], both_starts[which, row_at][None, :], starts)
    same_y = slot_y[:, None] == slot_y[None, :]
    at_row = slot_row[None, :] == jnp.arange(rows_on, dtype=jnp.int32)[:, None]
    found = jnp.where(
        same_y[:, None, :] & at_row[None, :, :], jnp.arange(slots, dtype=jnp.int32), 0
    ).sum(axis=2)
    meta = jnp.concatenate(
        [(starts[:, :1] // block), (begins // block)[:, None], found.astype(jnp.int32)], axis=1
    )
    meta = jnp.concatenate([meta.reshape(-1), line[None].astype(jnp.int32)])
    info = jnp.stack([places, starts], axis=1)
    offsets = (places - starts).astype(jnp.float32).reshape(-1)
    phases = offsets[:, None] * jnp.tile(frequency, LANES // (HEAD_DIM // 2))[None, :]
    cosine, sine = (jnp.cos(phases), jnp.sin(phases))

    cot_parts = tokens_sent(late_cotangent)
    first_weight = gather_weight(jnp.concatenate([joint_mine, output_mine], axis=1))
    joint_width = joint_mine.shape[1]
    joint_weight, output_weight = (first_weight[:, :joint_width], first_weight[:, joint_width:])
    residual = residual_low.astype(jnp.float32)
    scale_one = lax.rsqrt(jnp.mean(residual * residual, axis=1, keepdims=True) + EPSILON)
    normed_parts = gather_tokens((residual * scale_one * gains[0]).astype(jnp.bfloat16))
    normed_parts, cot_parts = lax.optimization_barrier((normed_parts, cot_parts))
    cot_low = tokens_of(cot_parts)
    cot_chunks = gather_tokens(cot_low)
    queries, pair = project(normed_parts, first_weight, joint_width, cosine, sine, query_width)
    pairs = lax.all_gather(pair.reshape(slots, block, 2 * LANES), "col", axis=0, tiled=False)
    pairs, cot_chunks, gateup_mine, down_mine, meta, info = lax.optimization_barrier(
        (pairs, cot_chunks, gateup_mine, down_mine, meta, info)
    )
    gateup_weight = gather_weight(gateup_mine)
    down_weight = gather_weight(down_mine)
    mixed, logs = attend(meta, queries, pairs, info, rows_on)
    attn_sum = reduce_tokens(product(mixed, output_weight))
    middle = residual + attn_sum
    scale_two = lax.rsqrt(jnp.mean(middle * middle, axis=1, keepdims=True) + EPSILON)
    two_parts = gather_tokens((middle * scale_two * gains[1]).astype(jnp.bfloat16))
    hidden, factor, silu_gate = widen(two_parts, gateup_weight)
    normed_two, cot = (jnp.concatenate(two_parts, axis=0), jnp.concatenate(cot_chunks, axis=0))

    def other_half(rows, grad):
        rows = lax.dynamic_slice_in_dim(rows, (1 - core) * (D // 2), D // 2, 1)
        return dot_tn(rows, grad).astype(jnp.bfloat16)

    def own_half(rows, grad, received):
        rows = lax.dynamic_slice_in_dim(rows, core * (D // 2), D // 2, 1)
        total = dot_tn(rows, grad) + received.astype(jnp.float32)
        return total.astype(jnp.bfloat16)

    def scatter(total):
        return lax.psum_scatter(total, "col", scatter_dimension=0, tiled=True)

    def collect(piece):
        near_y = other_y(piece)
        return [piece, near_y, other_core(piece), other_core(near_y)]

    down_total = own_half(cot, hidden, other_core(other_half(cot, hidden)))
    down_total, down_weight = lax.optimization_barrier((down_total, down_weight))
    down_piece = scatter(down_total)
    work = {}

    def feed_back(first, last):
        work["grad_gate"], work["grad_up"], partial = widen_back(
            cot_chunks[first:last],
            down_weight,
            gateup_weight,
            factor,
            silu_gate,
            first,
            [work[name] for name in ("grad_gate", "grad_up") if name in work],
        )
        return partial

    def feed_others(key):
        gate, up = (work["grad_gate"], work["grad_up"])
        key, work["down_piece"], gate_other, up_other = lax.optimization_barrier(
            (key, down_piece, other_half(normed_two, gate), other_half(normed_two, up))
        )
        work["feed"] = (normed_two, gate, up, other_core(gate_other), other_core(up_other))
        return key

    def feed_owns(first):
        rows, gate, up, gate_other, up_other = work["feed"]
        gate_total = own_half(rows, gate, gate_other)
        first, gate_total, rows, up, up_other = lax.optimization_barrier(
            (first, gate_total, rows, up, up_other)
        )
        work["totals"] = (gate_total, own_half(rows, up, up_other))
        return first

    grad_normed_two = reduce_tokens(feed_back, feed_others, feed_owns)
    gate_piece, up_piece = [scatter(total) for total in work["totals"]]

    def norm_back(values, scale, grad_normed, gain):
        scaled = grad_normed * gain
        total = jnp.sum(scaled * values, axis=1, keepdims=True)
        return scale * scaled - values * (scale**3 * total / D)

    grad_middle = cot_low.astype(jnp.float32) + norm_back(
        middle, scale_two, grad_normed_two, gains[1]
    )
    gain_two = jnp.sum(grad_normed_two * middle * scale_two, axis=0)

    grad_middle_low, late_hidden = lax.optimization_barrier(
        (grad_middle.astype(jnp.bfloat16), hidden)
    )
    gate_total, up_total = work["totals"]
    back = jnp.concatenate(gather_tokens(grad_middle_low, (gate_total, up_total)), axis=0)

    meta_core = jnp.stack([y, core]).astype(jnp.int32)

    def back_here(products):
        products, work["back"] = lax.optimization_barrier((products, back))
        return products

    def attention_back(far):
        here = work.get("back", back)
        grad_query, grad_parts = attend_back(
            meta,
            queries,
            pairs,
            dot_nn(here, output_weight).astype(jnp.bfloat16),
            mixed,
            logs,
            info,
            cosine,
            sine,
            rows_on,
        )
        work["grad_parts"] = [grad_parts[0]] + [
            shift(grad_parts[by], "col", lines, -by) for by in range(1, lines)
        ]
        names = ("grad_query", "gate_piece", "back", "mixed")
        far, *values = lax.optimization_barrier((far, grad_query, gate_piece, here, mixed))
        work.update(zip(names, values))
        return far

    def keys_arrive(first):
        first, work["grad_parts"], work["up_piece"] = lax.optimization_barrier(
            (first, work["grad_parts"], up_piece)
        )
        return first

    if rows_on == 2:
        ffn_sum = reduce_tokens(
            product(late_hidden, down_weight), None, keys_arrive, attention_back, back_here
        )
    else:
        ffn_sum = keys_arrive(attention_back(reduce_tokens(product(late_hidden, down_weight))))
    grad_query, gate_piece, back, mixed = [
        work[name] for name in ("grad_query", "gate_piece", "back", "mixed")
    ]
    output_parts = features_sent((middle + ffn_sum).astype(jnp.bfloat16))
    grad_keyvalue = pair_back(work["grad_parts"], cosine, sine, block)
    grad_joint = jnp.concatenate([grad_query, grad_keyvalue], axis=1)
    normed_one = jnp.concatenate(normed_parts, axis=0)

    def joint_products(first, last):
        if first:
            return product(grad_joint, joint_weight)(first, last)
        output_total = own_half(back, mixed, other_core(other_half(back, mixed)))
        shards = collect(jnp.concatenate([work["down_piece"], work["gate_piece"]], axis=0))
        close, work["output"], work["shards"] = lax.optimization_barrier(
            (product(grad_joint, joint_weight)(first, last), output_total, shards)
        )
        return close

    def joint_others(key):
        key, work["output_parts"], other = lax.optimization_barrier(
            (key, output_parts, other_half(normed_one, grad_joint))
        )
        work["joint"] = (normed_one, grad_joint, other_core(other))
        work["output_piece"] = scatter(work["output"])
        return key

    def joint_owns(first):
        down_new = turned_update(
            meta_core,
            work["shards"],
            [w_down, down_moment, down_square],
            FF ** (-0.5),
            False,
        )
        first, work["output_piece"], work["up_piece"], work["down_new"], rows, grad, other = (
            lax.optimization_barrier(
                (first, work["output_piece"], work["up_piece"], down_new, *work["joint"])
            )
        )
        work["joint_total"] = own_half(rows, grad, other)
        return first

    grad_normed_one = reduce_tokens(joint_products, joint_others, joint_owns)
    joint_piece = scatter(work["joint_total"])
    gateup_new = gateup_update(
        meta_core,
        work["shards"],
        collect(work["up_piece"]),
        [w_gateup, gateup_moment, gateup_square],
        32,
    )
    input_grad = grad_middle + norm_back(residual, scale_one, grad_normed_one, gains[0])
    gain_one = jnp.sum(grad_normed_one * residual * scale_one, axis=0)
    joint_piece, input_parts, gateup_new = lax.optimization_barrier(
        (joint_piece, features_sent(input_grad.astype(jnp.bfloat16)), gateup_new)
    )
    layer_output = features_of(work["output_parts"])
    input_grad = features_of(input_parts).astype(jnp.float32)
    pair_piece = joint_piece[:, query_width:]
    pair_total = pair_piece.astype(jnp.float32)
    for by in range(1, rows_on):
        pair_total = pair_total + shift(pair_piece, "row", rows_on, by).astype(jnp.float32)
    joint_piece = jnp.concatenate(
        [joint_piece[:, :query_width], pair_total.astype(jnp.bfloat16)], axis=1
    )
    joint_new = joint_update(
        meta_core,
        collect(joint_piece),
        [w_query, query_moment, query_square],
        [w_keyvalue, keyvalue_moment, keyvalue_square],
    )
    output_new = turned_update(
        meta_core,
        collect(work["output_piece"]),
        [w_output, output_moment, output_square],
        (HEADS * HEAD_DIM // 64) ** (-0.5),
        True,
    )

    gain_sums = jnp.stack([gain_one, gain_two])
    gain_sums, gateup_new = lax.optimization_barrier((gain_sums, gateup_new))
    blocks = [
        jnp.concatenate(
            [
                gain_sums[:, at * half : (at + 1) * half],
                gain_sums[:, D // 2 + at * half : D // 2 + (at + 1) * half],
            ],
            axis=1,
        )
        for at in range(lines)
    ]
    grad_gains = pick(blocks, line)
    for by in range(1, lines):
        grad_gains = grad_gains + shift(pick(blocks, (line + by) % lines), "col", lines, by)
    for axis, size in (("core", 2), ("y", 2), ("row", rows_on)):
        blocks_total = grad_gains
        for by in range(1, size):
            grad_gains = grad_gains + shift(blocks_total, axis, size, by)

    gains_new = adamw_step(norm_gains, grad_gains, gains_moment, gains_square, 0.6, 0.0)
    return (
        layer_output,
        input_grad,
        *gains_new,
        *joint_new,
        *output_new,
        *gateup_new,
        *work["down_new"],
    )


def solution(mesh):
    dp, rows_on, lines = (mesh.shape["dp"], mesh.shape["row"], mesh.shape["col"])
    split = Mesh(mesh.devices.reshape(dp // 2, 2, rows_on, lines), ("y", "core", "row", "col"))
    tokens = P(("y", "core", "row"), "col")
    narrow, wide = (P("col", "row"), P("row", "col"))
    gains, pair, gateup = (P(None, "col"), P("col", None), P("col", None, "row"))
    return jax.shard_map(
        functools.partial(on_device, (rows_on, lines)),
        mesh=split,
        in_specs=(
            tokens,
            tokens,
            P(("y", "core"), None),
            gains,
            narrow,
            pair,
            wide,
            gateup,
            wide,
            gains,
            gains,
            narrow,
            narrow,
            pair,
            pair,
            wide,
            wide,
            gateup,
            gateup,
            wide,
            wide,
        ),
        out_specs=(tokens, tokens)
        + (gains,) * 3
        + (narrow,) * 3
        + (pair,) * 3
        + (wide,) * 3
        + (gateup,) * 3
        + (wide,) * 3,
        check_vma=False,
    )
```

```python
import functools

import jax
import jax.numpy as jnp
from jax import lax
from jax.experimental import pallas as pl
from jax.experimental.pallas import tpu as pltpu
from jax.sharding import Mesh, PartitionSpec as P

D = 2048
HEADS = 32
KV_HEADS = 4
HEAD_DIM = 64
FF = 5632
STEP = 10

EPSILON = 1e-05
BETA_ONE = 0.9
BETA_TWO = 0.999
ADAM_EPS = 1e-08
MASKED = -1e30
SCORE_SCALE = HEAD_DIM ** (-0.5)
LANES = 128
VMEM_LIMIT = 48 * 1024 * 1024


def dot_nn(left, right):
    return lax.dot_general(left, right, (((1,), (0,)), ((), ())), preferred_element_type=jnp.float32)


def dot_nt(left, right):
    return lax.dot_general(left, right, (((1,), (1,)), ((), ())), preferred_element_type=jnp.float32)


def dot_tn(left, right):
    return lax.dot_general(left, right, (((0,), (0,)), ((), ())), preferred_element_type=jnp.float32)


def adamw_step(weight, gradient, moment, square, step_rate, decay_rate):
    moment_new = BETA_ONE * moment + (1.0 - BETA_ONE) * gradient
    square_new = BETA_TWO * square + (1.0 - BETA_TWO) * gradient * gradient
    fixed_one = moment_new / (1.0 - BETA_ONE**STEP)
    fixed_two = square_new / (1.0 - BETA_TWO**STEP)
    weight_new = weight - step_rate * (
        fixed_one / (jnp.sqrt(fixed_two) + ADAM_EPS) + decay_rate * weight
    )
    return (moment_new, square_new, weight_new)


def document_starts(segment_ids):
    places = jnp.arange(segment_ids.shape[0], dtype=jnp.int32)
    starts = jnp.concatenate([jnp.ones((1,), jnp.bool_), segment_ids[1:] != segment_ids[:-1]])
    return lax.cummax(jnp.where(starts, places, 0), axis=0)


def turn(values):
    lane = lax.broadcasted_iota(jnp.int32, values.shape, 1)
    ahead = pltpu.roll(values, LANES - HEAD_DIM // 2, 1)
    behind = pltpu.roll(values, HEAD_DIM // 2, 1)
    return jnp.where(lane % HEAD_DIM < HEAD_DIM // 2, -ahead, behind)


def take_chunk(rows_refs, held_ref):
    for at, ref in enumerate(rows_refs):

        @pl.when(pl.program_id(0) == at)
        def _(ref=ref):
            held_ref[...] = ref[...]


def project_kernel(slots, *refs):
    rows_refs, (weight_ref, cos_ref, sin_ref, query_ref, pair_ref, held_ref) = (refs[:slots], refs[slots:])
    take_chunk(rows_refs, held_ref)
    sums = dot_nn(held_ref[...], weight_ref[...])
    cosine, sine = cos_ref[...], sin_ref[...]
    width = query_ref.shape[1]
    lane = lax.broadcasted_iota(jnp.int32, cosine.shape, 1)
    for start in range(0, width, LANES):
        part = sums[:, start : start + LANES]
        turned = (part * cosine + turn(part) * sine).astype(jnp.bfloat16)
        query_ref[:, start : start + LANES] = turned * jnp.bfloat16(SCORE_SCALE)
    for which in range(2):
        part = sums[:, width + which * LANES : width + (which + 1) * LANES]
        is_key = (lane < HEAD_DIM) if which == 0 else (lane >= HEAD_DIM)
        turned = jnp.where(is_key, part * cosine + turn(part) * sine, part)
        pair_ref[:, which * LANES : (which + 1) * LANES] = turned.astype(jnp.bfloat16)


def project(chunks, weight, total, cosine, sine, width):
    slots = len(chunks)
    block, depth = chunks[0].shape
    rows = slots * block
    whole = pl.BlockSpec((block, depth), lambda i: (0, 0))
    return pl.pallas_call(
        functools.partial(project_kernel, slots),
        grid=(slots,),
        in_specs=[whole] * slots
        + [
            pl.BlockSpec((depth, total), lambda i: (0, 0)),
            pl.BlockSpec((block, LANES), lambda i: (i, 0)),
            pl.BlockSpec((block, LANES), lambda i: (i, 0)),
        ],
        out_specs=[
            pl.BlockSpec((block, width), lambda i: (i, 0)),
            pl.BlockSpec((block, total - width), lambda i: (i, 0)),
        ],
        out_shape=[
            jax.ShapeDtypeStruct((rows, width), jnp.bfloat16),
            jax.ShapeDtypeStruct((rows, total - width), jnp.bfloat16),
        ],
        scratch_shapes=[pltpu.VMEM((block, depth), jnp.bfloat16)],
        compiler_params=pltpu.CompilerParams(vmem_limit_bytes=VMEM_LIMIT),
        cost_estimate=pl.CostEstimate(
            flops=2 * rows * depth * total,
            bytes_accessed=(rows + total) * depth * 2,
            transcendentals=0,
        ),
        name="project",
    )(*chunks, weight, cosine, sine)


def widen_kernel(slots, *refs):
    rows_refs, (weight_ref, hidden_ref, factor_ref, silu_ref, held_ref) = (refs[:slots], refs[slots:])
    take_chunk(rows_refs, held_ref)
    sums = dot_nn(held_ref[...], weight_ref[...])
    width = hidden_ref.shape[1]
    gate, upward = (sums[:, :width], sums[:, width:])
    sigmoid = jax.nn.sigmoid(gate)
    silu = gate * sigmoid
    hidden_ref[...] = (silu * upward).astype(jnp.bfloat16)
    factor_ref[...] = (upward * sigmoid * (1.0 + gate * (1.0 - sigmoid))).astype(jnp.bfloat16)
    silu_ref[...] = silu.astype(jnp.bfloat16)


def widen(chunks, weight):
    slots = len(chunks)
    block, depth = chunks[0].shape
    width = weight.shape[1] // 2
    rows = slots * block
    once = pl.Buffered(1)
    return pl.pallas_call(
        functools.partial(widen_kernel, slots),
        grid=(slots,),
        in_specs=[pl.BlockSpec((block, depth), lambda i: (0, 0), pipeline_mode=once)] * slots
        + [pl.BlockSpec(weight.shape, lambda i: (0, 0), pipeline_mode=once)],
        out_specs=[pl.BlockSpec((block, width), lambda i: (i, 0))] * 3,
        out_shape=[jax.ShapeDtypeStruct((rows, width), jnp.bfloat16)] * 3,
        scratch_shapes=[pltpu.VMEM((block, depth), jnp.bfloat16)],
        compiler_params=pltpu.CompilerParams(vmem_limit_bytes=VMEM_LIMIT),
        cost_estimate=pl.CostEstimate(
            flops=4 * rows * depth * width,
            bytes_accessed=(rows + 2 * width) * depth * 2 + 6 * rows * width,
            transcendentals=rows * width,
        ),
        name="widen",
    )(*chunks, weight)


def widen_back_kernel(slots, kept, *refs):
    rows_refs, refs = (refs[:slots], refs[slots:])
    down_ref, gateup_ref, factor_ref, silu_ref = refs[:4]
    gate_ref, up_ref, partial_ref, held_ref = refs[4 + kept :]
    take_chunk(rows_refs, held_ref)
    grad_hidden = dot_nn(held_ref[...], down_ref[...])
    gate = (grad_hidden * factor_ref[...].astype(jnp.float32)).astype(jnp.bfloat16)
    up = (grad_hidden * silu_ref[...].astype(jnp.float32)).astype(jnp.bfloat16)
    gate_ref[...] = gate
    up_ref[...] = up
    both = jnp.concatenate([gate, up], axis=1)
    partial_ref[...] = dot_nt(both, gateup_ref[...]).astype(jnp.bfloat16)


def widen_back(chunks, down, gateup, factor, silu, first, kept):
    slots = len(chunks)
    block, depth = chunks[0].shape
    width = down.shape[1]
    once = pl.Buffered(1)
    tile = pl.BlockSpec((block, width), lambda i: (first + i, 0))
    return pl.pallas_call(
        functools.partial(widen_back_kernel, slots, len(kept)),
        grid=(slots,),
        in_specs=[pl.BlockSpec((block, depth), lambda i: (0, 0), pipeline_mode=once)] * slots
        + [
            pl.BlockSpec(down.shape, lambda i: (0, 0), pipeline_mode=once),
            pl.BlockSpec(gateup.shape, lambda i: (0, 0), pipeline_mode=once),
            tile,
            tile,
        ]
        + [pl.BlockSpec(memory_space=pl.ANY)] * len(kept),
        out_specs=[tile, tile, pl.BlockSpec((block, depth), lambda i: (i, 0))],
        out_shape=[jax.ShapeDtypeStruct(factor.shape, jnp.bfloat16)] * 2
        + [jax.ShapeDtypeStruct((slots * block, depth), jnp.bfloat16)],
        scratch_shapes=[pltpu.VMEM((block, depth), jnp.bfloat16)],
        input_output_aliases={slots + 4 + i: i for i in range(len(kept))},
        compiler_params=pltpu.CompilerParams(vmem_limit_bytes=VMEM_LIMIT),
        cost_estimate=pl.CostEstimate(
            flops=slots * block * depth * width,
            bytes_accessed=8 * slots * block * width,
            transcendentals=0,
        ),
        name="widen_back",
    )(*chunks, down, gateup, factor, silu, *kept)


def stack_heads(values):
    return jnp.concatenate(
        [values[:, start : start + LANES] for start in range(0, values.shape[1], LANES)], axis=0
    )


def block_of(meta_ref, chunk, step, parts, lines):
    base = chunk * (2 + parts)
    key_block = meta_ref[base + 1] - step
    slot = meta_ref[base + 2 + key_block // lines]
    own_line = meta_ref[pl.num_programs(0) * (2 + parts)]
    line = lax.rem(key_block, lines)
    return (key_block, slot, line, lax.rem(own_line - line + lines, lines))


def attend_kernel(parts, lines, meta_ref, query_ref, pair_ref, info_ref, out_ref, log_ref):
    chunk = pl.program_id(0)
    block = query_ref.shape[0]
    heads = query_ref.shape[1] // LANES
    stacked = stack_heads(query_ref[...])
    lane = lax.broadcasted_iota(jnp.int32, stacked.shape, 1)
    place = jnp.concatenate([info_ref[0, 0:1, :]] * heads, axis=1)
    start = jnp.concatenate([info_ref[0, 1:2, :]] * heads, axis=1)
    base = chunk * (2 + parts)
    steps = meta_ref[base + 1] - meta_ref[base] + 1
    width = heads * block
    key_lanes = lane < HEAD_DIM
    queries = [
        jnp.where(key_lanes if which == 0 else ~key_lanes, stacked, jnp.zeros_like(stacked))
        for which in range(2)
    ]

    def body(step, carry):
        key_block, slot, at, _ = block_of(meta_ref, chunk, step, parts, lines)
        key_place = key_block * block + lax.broadcasted_iota(jnp.int32, (block, width), 0)
        seen = (key_place <= place) & (key_place >= start)
        result = []
        for which in range(2):
            peak, total, mixed = carry[which]
            pair = pair_ref[at, slot, :, which * LANES : (which + 1) * LANES]
            scores = jnp.where(seen, dot_nt(pair, queries[which]), MASKED)
            new_peak = jnp.maximum(peak, jnp.max(scores, axis=0, keepdims=True))
            weights = jnp.exp(scores - new_peak)
            shrink = jnp.exp(peak - new_peak)
            total = total * shrink + jnp.sum(weights, axis=0, keepdims=True)
            mixed = mixed * shrink + dot_tn(pair, weights.astype(jnp.bfloat16))
            result.append((new_peak, total, mixed))
        return tuple(result)

    empty = (
        jnp.full((1, width), MASKED, jnp.float32),
        jnp.zeros((1, width), jnp.float32),
        jnp.zeros((LANES, width), jnp.float32),
    )
    outs = []
    for which, (peak, total, mixed) in enumerate(lax.fori_loop(0, steps, body, (empty, empty))):
        log_ref[0, which : which + 1, :] = peak + jnp.log(total)
        outs.append(mixed / total)
    joined = jnp.concatenate([outs[1][:HEAD_DIM], outs[0][HEAD_DIM:]], axis=0)
    rows = joined.T.astype(jnp.bfloat16)
    for head in range(heads):
        out_ref[:, head * LANES : (head + 1) * LANES] = rows[head * block : (head + 1) * block]


def attend(meta, queries, pairs, info, parts):
    chunks, block = (info.shape[0], info.shape[2])
    width = queries.shape[1]
    heads = width // LANES
    lines = pairs.shape[0]
    steps = 3 * chunks
    return pl.pallas_call(
        functools.partial(attend_kernel, parts, lines),
        grid_spec=pltpu.PrefetchScalarGridSpec(
            num_scalar_prefetch=1,
            grid=(chunks,),
            in_specs=[
                pl.BlockSpec((block, width), lambda i, m: (i, 0)),
                pl.BlockSpec(pairs.shape, lambda i, m: (0, 0, 0, 0)),
                pl.BlockSpec((1, 2, block), lambda i, m: (i, 0, 0)),
            ],
            out_specs=[
                pl.BlockSpec((block, width), lambda i, m: (i, 0)),
                pl.BlockSpec((1, 2, heads * block), lambda i, m: (i, 0, 0)),
            ],
        ),
        out_shape=[
            jax.ShapeDtypeStruct(queries.shape, jnp.bfloat16),
            jax.ShapeDtypeStruct((chunks, 2, heads * block), jnp.float32),
        ],
        compiler_params=pltpu.CompilerParams(vmem_limit_bytes=VMEM_LIMIT),
        cost_estimate=pl.CostEstimate(
            flops=steps * 2 * 2 * 2 * heads * block * block * LANES,
            bytes_accessed=queries.size * 4 + pairs.size * 2,
            transcendentals=steps * 2 * heads * block * block,
        ),
        name="attend",
    )(meta, queries, pairs, info)


def attend_back_kernel(parts, lines, meta_ref, query_ref, *refs):
    pair_ref, grad_ref, mixed_ref, log_ref, info_ref, cos_ref, sin_ref, query_out = refs[:8]
    pair_outs = refs[8 : 8 + lines]
    sums = refs[8 + lines]
    chunk = pl.program_id(0)
    block = query_ref.shape[0]
    heads = query_ref.shape[1] // LANES

    @pl.when(chunk == 0)
    def _():
        sums[...] = jnp.zeros_like(sums)

    stacked = stack_heads(query_ref[...])
    stacked_grad = stack_heads(grad_ref[...])
    product = stacked_grad.astype(jnp.float32) * stack_heads(mixed_ref[...]).astype(jnp.float32)
    lane = lax.broadcasted_iota(jnp.int32, stacked.shape, 1)
    place = jnp.concatenate([info_ref[0, 0:1, :]] * heads, axis=1)
    start = jnp.concatenate([info_ref[0, 1:2, :]] * heads, axis=1)
    base = chunk * (2 + parts)
    steps = meta_ref[base + 1] - meta_ref[base] + 1
    width = heads * block
    key_lanes = lane < HEAD_DIM
    queries, grad, centre, logs = ([], [], [], [])
    for which in range(2):
        is_key = key_lanes if which == 0 else ~key_lanes
        queries.append(jnp.where(is_key, stacked, jnp.zeros_like(stacked)))
        grad.append(jnp.where(is_key, jnp.zeros_like(stacked_grad), stacked_grad))
        own = jnp.where(is_key, 0.0, product)
        centre.append(
            lax.dot_general(
                jnp.ones((8, LANES), jnp.float32),
                own,
                (((1,), (1,)), ((), ())),
                precision=lax.Precision.HIGHEST,
                preferred_element_type=jnp.float32,
            )[0:1]
        )
        logs.append(log_ref[0, which : which + 1, :])

    def body(step, carry):
        key_block, slot, at, shift = block_of(meta_ref, chunk, step, parts, lines)
        key_place = key_block * block + lax.broadcasted_iota(jnp.int32, (block, width), 0)
        seen = (key_place <= place) & (key_place >= start)
        result = []
        for which in range(2):
            columns = slice(which * LANES, (which + 1) * LANES)
            pair = pair_ref[at, slot, :, columns]
            scores = jnp.where(seen, dot_nt(pair, queries[which]), MASKED)
            weights = jnp.exp(scores - logs[which])
            grad_weights = dot_nt(pair, grad[which]) - centre[which]
            grad_scores = (weights * grad_weights).astype(jnp.bfloat16)
            sums[shift, slot, :, columns] += dot_nn(grad_scores, queries[which]) + dot_nn(
                weights.astype(jnp.bfloat16), grad[which]
            )
            result.append(carry[which] + dot_tn(pair, grad_scores))
        return tuple(result)

    empty = jnp.zeros((LANES, width), jnp.float32)
    grads = lax.fori_loop(0, steps, body, (empty, empty))
    joined = jnp.concatenate([grads[0][:HEAD_DIM], grads[1][HEAD_DIM:]], axis=0)
    rows = joined.T * SCORE_SCALE
    cosine, sine = cos_ref[...], sin_ref[...]
    for head in range(heads):
        part = rows[head * block : (head + 1) * block]
        back = part * cosine - turn(part) * sine
        query_out[:, head * LANES : (head + 1) * LANES] = back.astype(jnp.bfloat16)

    @pl.when(chunk == pl.num_programs(0) - 1)
    def _():
        for line in range(lines):
            pair_outs[line][...] = sums[line].astype(jnp.bfloat16)


def attend_back(meta, queries, pairs, grad_mixed, mixed, logs, info, cosine, sine, parts):
    chunks, block = (info.shape[0], info.shape[2])
    width = queries.shape[1]
    heads = width // LANES
    lines = pairs.shape[0]
    shape = pairs.shape[1:]
    steps = 3 * chunks
    wide = pl.BlockSpec((block, width), lambda i, m: (i, 0))
    table = pl.BlockSpec((block, LANES), lambda i, m: (i, 0))
    whole = pl.BlockSpec(shape, lambda i, m: (0, 0, 0))
    outs = pl.pallas_call(
        functools.partial(attend_back_kernel, parts, lines),
        grid_spec=pltpu.PrefetchScalarGridSpec(
            num_scalar_prefetch=1,
            grid=(chunks,),
            in_specs=[
                wide,
                pl.BlockSpec(pairs.shape, lambda i, m: (0, 0, 0, 0)),
                wide,
                wide,
                pl.BlockSpec((1, 2, heads * block), lambda i, m: (i, 0, 0)),
                pl.BlockSpec((1, 2, block), lambda i, m: (i, 0, 0)),
                table,
                table,
            ],
            out_specs=[wide] + [whole] * lines,
            scratch_shapes=[pltpu.VMEM(pairs.shape, jnp.float32)],
        ),
        out_shape=[jax.ShapeDtypeStruct(queries.shape, jnp.bfloat16)]
        + [jax.ShapeDtypeStruct(shape, jnp.bfloat16)] * lines,
        compiler_params=pltpu.CompilerParams(vmem_limit_bytes=VMEM_LIMIT),
        cost_estimate=pl.CostEstimate(
            flops=steps * 2 * 5 * 2 * heads * block * block * LANES,
            bytes_accessed=queries.size * 8 + 2 * pairs.size * 2,
            transcendentals=steps * 2 * heads * block * block,
        ),
        name="attend_back",
    )(
        meta,
        queries,
        pairs,
        grad_mixed,
        mixed,
        logs,
        info,
        cosine,
        sine,
    )
    return (outs[0], [out.reshape(chunks * block, 2 * LANES) for out in outs[1:]])


def pair_back_kernel(*refs):
    *part_refs, cos_ref, sin_ref, out_ref = refs
    cosine, sine = cos_ref[...], sin_ref[...]
    lane = lax.broadcasted_iota(jnp.int32, cosine.shape, 1)
    for which in range(2):
        columns = slice(which * LANES, (which + 1) * LANES)
        total = part_refs[0][:, columns].astype(jnp.float32)
        for ref in part_refs[1:]:
            total = total + ref[:, columns].astype(jnp.float32)
        is_key = (lane < HEAD_DIM) if which == 0 else (lane >= HEAD_DIM)
        total = jnp.where(is_key, total * cosine - turn(total) * sine, total)
        out_ref[:, columns] = total.astype(jnp.bfloat16)


def pair_back(parts, cosine, sine, block):
    rows, columns = parts[0].shape
    tile = pl.BlockSpec((block, columns), lambda i: (i, 0))
    table = pl.BlockSpec((block, LANES), lambda i: (i, 0))
    return pl.pallas_call(
        pair_back_kernel,
        grid=(rows // block,),
        in_specs=[tile] * len(parts) + [table, table],
        out_specs=tile,
        out_shape=jax.ShapeDtypeStruct((rows, columns), jnp.bfloat16),
        compiler_params=pltpu.CompilerParams(vmem_limit_bytes=VMEM_LIMIT),
        name="pair_back",
    )(*parts, cosine, sine)


def update(refs, index, gradient, rate):
    weight, moment, square = [ref[index] for ref in refs[:3]]
    moment_new, square_new, weight_new = adamw_step(weight, gradient, moment, square, rate, 0.1)
    for ref, value in zip(refs[3:], (moment_new, square_new, weight_new)):
        ref[index] = value


def chosen(meta_ref, grad_refs, at, rows, columns):
    own_y = meta_ref[0] == at
    first = pl.program_id(0) == 0
    near = jnp.where(first, grad_refs[0][rows, columns], grad_refs[2][rows, columns])
    far = jnp.where(first, grad_refs[1][rows, columns], grad_refs[3][rows, columns])
    return jnp.where(own_y, near, far).astype(jnp.float32)


def joint_update_kernel(meta_ref, *refs):
    grad_refs, query_refs, pair_refs = (refs[:4], refs[4:7] + refs[10:13], refs[7:10] + refs[13:16])
    groups = query_refs[0].shape[1] // (2 * LANES)
    every = slice(None)
    for at in range(2):
        for j in range(groups):
            gradient = chosen(meta_ref, grad_refs, at, every, slice(j * LANES, (j + 1) * LANES))
            place = slice((2 * j + at) * LANES, (2 * j + at + 1) * LANES)
            update(query_refs, (every, place), gradient, D ** (-0.5))
        for which in range(2):
            start = (groups + which) * LANES
            gradient = chosen(meta_ref, grad_refs, at, every, slice(start, start + LANES))
            if which == 1:
                gradient = pltpu.roll(gradient, HEAD_DIM, 1)
            place = slice((2 * at + which) * LANES, (2 * at + which + 1) * LANES)
            update(pair_refs, (every, place), gradient, D ** (-0.5))


def joint_update(meta, grads, query, pair):
    half = grads[0].shape[0]

    def rows_of(array):
        return pl.BlockSpec((half, array.shape[1]), lambda i, m: ((m[1] + i) % 2, 0))

    whole = pl.BlockSpec(grads[0].shape, lambda i, m: (0, 0))
    blocks = [rows_of(array) for array in (*query, *pair)]
    return pl.pallas_call(
        joint_update_kernel,
        grid_spec=pltpu.PrefetchScalarGridSpec(
            num_scalar_prefetch=1, grid=(2,), in_specs=[whole] * 4 + blocks, out_specs=blocks
        ),
        out_shape=[jax.ShapeDtypeStruct(array.shape, array.dtype) for array in (*query, *pair)],
        compiler_params=pltpu.CompilerParams(vmem_limit_bytes=VMEM_LIMIT),
        cost_estimate=pl.CostEstimate(
            flops=20 * (query[0].size + pair[0].size),
            bytes_accessed=24 * (query[0].size + pair[0].size),
            transcendentals=0,
        ),
        name="joint_update",
    )(meta, *grads, *query, *pair)


def turned_update_kernel(rate, swapped, meta_ref, *refs):
    grad_refs, weight_refs = (refs[:4], refs[4:10])
    at = pl.program_id(1)
    width = grad_refs[0].shape[1]
    every = slice(None)
    for j, start in enumerate(range(0, width, LANES)):
        strip = slice(start, min(start + LANES, width))
        gradient = chosen(meta_ref, grad_refs, at, every, strip).T
        if swapped:
            gradient = jnp.concatenate([gradient[HEAD_DIM:], gradient[:HEAD_DIM]], axis=0)
            index = (j, 0)
        else:
            index = (strip, every)
        update(weight_refs, index, gradient, rate)


def turned_update(meta, grads, weights, rate, swapped):
    shape = weights[0].shape
    half, width = (shape[1] // 2, grads[0].shape[1])
    if swapped:
        weights = [w.reshape(width // LANES, 2, LANES, shape[1]) for w in weights]
        block = pl.BlockSpec(
            (width // LANES, 1, LANES, half), lambda i, at, m: (0, at, 0, (m[1] + i) % 2)
        )
    else:
        block = pl.BlockSpec((width, half), lambda i, at, m: (at, (m[1] + i) % 2))
    outs = pl.pallas_call(
        functools.partial(turned_update_kernel, rate, swapped),
        grid_spec=pltpu.PrefetchScalarGridSpec(
            num_scalar_prefetch=1,
            grid=(2, 2),
            in_specs=[pl.BlockSpec((half, width), lambda i, at, m: (0, 0))] * 4 + [block] * 3,
            out_specs=[block] * 3,
        ),
        out_shape=[jax.ShapeDtypeStruct(weights[0].shape, jnp.float32)] * 3,
        compiler_params=pltpu.CompilerParams(vmem_limit_bytes=VMEM_LIMIT),
        cost_estimate=pl.CostEstimate(
            flops=20 * weights[0].size, bytes_accessed=24 * weights[0].size, transcendentals=0
        ),
        name="turned_update",
    )(meta, *grads, *weights)
    return [out.reshape(shape) for out in outs]


def gateup_update_kernel(meta_ref, *refs):
    gate_refs, up_refs, weight_refs = (refs[:4], refs[4:8], refs[8:14])
    every = slice(None)
    gate, up = [
        jnp.concatenate([chosen(meta_ref, grads, at, every, every) for at in range(2)], axis=1)
        for grads in (gate_refs, up_refs)
    ]
    update(weight_refs, every, jnp.stack([gate, up], axis=1), D ** (-0.5))


def gateup_update(meta, gates, ups, weights, rows):
    half, width = ups[0].shape
    shape = weights[0].shape
    tiles = half // rows
    gate = pl.BlockSpec((rows, width), lambda i, j, m: (tiles + j, 0))
    up = pl.BlockSpec((rows, width), lambda i, j, m: (j, 0))
    block = pl.BlockSpec(
        (rows, 2, shape[2]), lambda i, j, m: (((m[1] + i) % 2) * tiles + j, 0, 0)
    )
    return pl.pallas_call(
        gateup_update_kernel,
        grid_spec=pltpu.PrefetchScalarGridSpec(
            num_scalar_prefetch=1,
            grid=(2, tiles),
            in_specs=[gate] * 4 + [up] * 4 + [block] * 3,
            out_specs=[block] * 3,
        ),
        out_shape=[jax.ShapeDtypeStruct(shape, jnp.float32)] * 3,
        compiler_params=pltpu.CompilerParams(vmem_limit_bytes=VMEM_LIMIT),
        cost_estimate=pl.CostEstimate(
            flops=20 * weights[0].size, bytes_accessed=28 * weights[0].size, transcendentals=0
        ),
        name="gateup_update",
    )(meta, *gates, *ups, *weights)


def on_device(
    sizes,
    block_input,
    cotangent,
    segments,
    norm_gains,
    w_query,
    w_keyvalue,
    w_output,
    w_gateup,
    w_down,
    gains_moment,
    gains_square,
    query_moment,
    query_square,
    keyvalue_moment,
    keyvalue_square,
    output_moment,
    output_square,
    gateup_moment,
    gateup_square,
    down_moment,
    down_square,
):
    rows_on, lines = sizes
    y, core, row, line = [lax.axis_index(name) for name in ("y", "core", "row", "col")]
    length = segments.shape[1]
    block = block_input.shape[0] // lines
    wide = block_input.shape[1]
    half = wide // 2
    slots = 2 * rows_on
    per_row = w_query.shape[1] // (KV_HEADS * HEAD_DIM)
    query_width = per_row * LANES
    hidden_here = w_gateup.shape[2] // 2

    def shift(value, axis, size, by):
        return lax.ppermute(value, axis, [(i, (i + by) % size) for i in range(size)])

    def other_core(value):
        return lax.ppermute(value, "core", [(0, 1), (1, 0)])

    def other_y(value):
        return lax.ppermute(value, "y", [(0, 1), (1, 0)])

    def place_of(y_at, core_at, row_at):
        return (y_at * 2 + core_at) * rows_on + row_at

    first_pairs, second_pairs = ([], [])
    for y_at in range(2):
        for core_at in range(2):
            for row_at in range(rows_on):
                over_row = (
                    place_of(y_at, core_at, row_at),
                    place_of(y_at, core_at, (row_at + 1) % rows_on),
                )
                over_y = (place_of(y_at, core_at, row_at), place_of(1 - y_at, core_at, row_at))
                first_pairs.append(over_row if core_at == 0 else over_y)
                second_pairs.append(over_y if core_at == 0 else over_row)
    near = ("y", "core", "row")

    def gather_tokens(own, beside=()):
        if rows_on == 2:
            first = lax.ppermute(own, near, first_pairs)
            second = lax.ppermute(own, near, second_pairs)
            first, second, *_ = lax.optimization_barrier((first, second, *beside))
            third = lax.ppermute(first, near, second_pairs)
            return [own, first, second, third]
        parts = [own] + [shift(own, "row", rows_on, by) for by in range(1, rows_on)]
        return parts + [other_y(part) for part in parts]

    def reduce_tokens(rows_of, middle=None, before_last=None, far_here=None, ready=None):
        def same(value):
            return value

        middle, before_last = (middle or same, before_last or same)
        if rows_on == 2:
            far = rows_of(2, 4)
            if ready:
                far, close = ready((far, rows_of(0, 2)))
            third = lax.ppermute(far[block:], near, second_pairs)
            second = lax.ppermute(far[:block], near, second_pairs)
            if not ready:
                close = rows_of(0, 2)
            third, second, close = (far_here or lax.optimization_barrier)((third, second, close))
            key = (close[block:].astype(jnp.float32) + third.astype(jnp.float32)).astype(jnp.bfloat16)
            first = before_last(lax.ppermute(middle(key), near, first_pairs))
            own = close[:block].astype(jnp.float32) + second.astype(jnp.float32)
            return own + first.astype(jnp.float32)
        partial = rows_of(0, slots)
        parts = [partial[i * block : (i + 1) * block] for i in range(slots)]
        sums = [
            parts[i].astype(jnp.float32) + other_y(parts[rows_on + i]).astype(jnp.float32)
            for i in range(rows_on)
        ]
        sums[0] = middle(sums[0])
        total = sums[0]
        for by in range(1, rows_on):
            moved = shift(sums[by].astype(jnp.bfloat16), "row", rows_on, -by)
            total = total + moved.astype(jnp.float32)
        return before_last(total)

    def product(left, right):
        def rows_of(first, last):
            return dot_nt(left[first * block : last * block], right).astype(jnp.bfloat16)

        return rows_of

    if rows_on == 2:
        slot_y = [y, jnp.where(core == 0, y, 1 - y), jnp.where(core == 0, 1 - y, y), 1 - y]
        slot_row = [row, jnp.where(core == 0, 1 - row, row), jnp.where(core == 0, row, 1 - row), 1 - row]
    else:
        slot_y = [y] * rows_on + [1 - y] * rows_on
        slot_row = [(row - by) % rows_on for by in range(rows_on)] * 2

    def pick(parts, index):
        return lax.dynamic_index_in_dim(jnp.stack(parts), index, 0, keepdims=False)

    def tokens_sent(values):
        parts = []
        for by in range(lines):
            part = lax.dynamic_slice_in_dim(values, ((line + by) % lines) * block, block, 0)
            parts.append(part if by == 0 else shift(part, "col", lines, by))
        return parts

    def tokens_of(parts):
        blocks = [pick(parts, (line - at) % lines) for at in range(lines)]
        return jnp.concatenate([b[:, :half] for b in blocks] + [b[:, half:] for b in blocks], axis=1)

    def features_sent(values):
        blocks = [
            jnp.concatenate(
                [
                    values[:, at * half : (at + 1) * half],
                    values[:, D // 2 + at * half : D // 2 + (at + 1) * half],
                ],
                axis=1,
            )
            for at in range(lines)
        ]
        parts = []
        for by in range(lines):
            part = pick(blocks, (line + by) % lines)
            parts.append(part if by == 0 else shift(part, "col", lines, by))
        return parts

    def features_of(parts):
        return jnp.concatenate([pick(parts, (line - at) % lines) for at in range(lines)], axis=0)

    def half_rows(values):
        return lax.dynamic_slice_in_dim(values, core * half, half, 0)

    def half_columns(values):
        return lax.dynamic_slice_in_dim(values, core * half, half, 1)

    def gather_weight(piece):
        return lax.all_gather(piece, ("core", "col"), axis=0, tiled=True)

    query_rows = half_rows(w_query).astype(jnp.bfloat16)
    pair_rows = half_rows(w_keyvalue).astype(jnp.bfloat16)

    def joint_of(at):
        pieces = [
            query_rows[:, (2 * j + at) * LANES : (2 * j + at + 1) * LANES] for j in range(per_row)
        ]
        pair = pair_rows[:, at * 2 * LANES : (at + 1) * 2 * LANES]
        pieces += [
            pair[:, :LANES],
            pair[:, LANES + HEAD_DIM :],
            pair[:, LANES : LANES + HEAD_DIM],
        ]
        return jnp.concatenate(pieces, axis=1)

    joint_mine = jnp.where(y == 0, joint_of(0), joint_of(1))
    output_columns = half_columns(w_output).astype(jnp.bfloat16)

    def output_of(at):
        pieces = []
        for j in range(per_row):
            base = (2 * j + at) * LANES
            pieces += [
                output_columns[base + HEAD_DIM : base + LANES],
                output_columns[base : base + HEAD_DIM],
            ]
        return jnp.concatenate(pieces, axis=0)

    output_mine = jnp.where(y == 0, output_of(0), output_of(1)).T
    gateup_mine = lax.dynamic_slice(
        w_gateup, (core * half, 0, y * hidden_here), (half, 2, hidden_here)
    ).astype(jnp.bfloat16)
    gateup_mine = jnp.concatenate([gateup_mine[:, 0], gateup_mine[:, 1]], axis=1)
    down_mine = lax.dynamic_slice(
        w_down, (y * hidden_here, core * half), (hidden_here, half)
    ).astype(jnp.bfloat16).T

    gain_parts = [norm_gains] + [shift(norm_gains, "col", lines, by) for by in range(1, lines)]
    gain_blocks = [pick(gain_parts, (line - at) % lines) for at in range(lines)]
    gains = jnp.concatenate(
        [b[:, :half] for b in gain_blocks] + [b[:, half:] for b in gain_blocks], axis=1
    )

    residual_low = tokens_of(tokens_sent(block_input))
    residual_low, late_cotangent, other_segments, joint_mine, output_mine = lax.optimization_barrier(
        (residual_low, cotangent, other_y(segments), joint_mine, output_mine)
    )

    own_starts = document_starts(segments[0])
    other_starts = document_starts(other_segments[0])
    frequency = 10000.0 ** (-2.0 * jnp.arange(HEAD_DIM // 2, dtype=jnp.float32) / HEAD_DIM)
    slot_y, slot_row = (jnp.stack(slot_y).astype(jnp.int32), jnp.stack(slot_row).astype(jnp.int32))
    begins = slot_row * (lines * block) + line * block
    places = begins[:, None] + jnp.arange(block, dtype=jnp.int32)[None, :]
    both_starts = jnp.stack([own_starts, other_starts]).reshape(2, rows_on, lines, block)
    both_starts = lax.dynamic_index_in_dim(both_starts, line, 2, keepdims=False)
    starts = jnp.zeros((slots, block), jnp.int32)
    for which in range(2):
        for row_at in range(rows_on):
            here = ((slot_y != y) == bool(which)) & (slot_row == row_at)
            starts = jnp.where(here[:, None], both_starts[which, row_at][None, :], starts)
    same_y = slot_y[:, None] == slot_y[None, :]
    at_row = slot_row[None, :] == jnp.arange(rows_on, dtype=jnp.int32)[:, None]
    found = jnp.where(
        same_y[:, None, :] & at_row[None, :, :], jnp.arange(slots, dtype=jnp.int32), 0
    ).sum(axis=2)
    meta = jnp.concatenate(
        [(starts[:, :1] // block), (begins // block)[:, None], found.astype(jnp.int32)], axis=1
    )
    meta = jnp.concatenate([meta.reshape(-1), line[None].astype(jnp.int32)])
    info = jnp.stack([places, starts], axis=1)
    offsets = (places - starts).astype(jnp.float32).reshape(-1)
    phases = offsets[:, None] * jnp.tile(frequency, LANES // (HEAD_DIM // 2))[None, :]
    cosine, sine = (jnp.cos(phases), jnp.sin(phases))

    cot_parts = tokens_sent(late_cotangent)
    first_weight = gather_weight(jnp.concatenate([joint_mine, output_mine], axis=1))
    joint_width = joint_mine.shape[1]
    joint_weight, output_weight = (first_weight[:, :joint_width], first_weight[:, joint_width:])
    residual = residual_low.astype(jnp.float32)
    scale_one = lax.rsqrt(jnp.mean(residual * residual, axis=1, keepdims=True) + EPSILON)
    normed_parts = gather_tokens((residual * scale_one * gains[0]).astype(jnp.bfloat16))
    normed_parts, cot_parts = lax.optimization_barrier((normed_parts, cot_parts))
    cot_low = tokens_of(cot_parts)
    cot_chunks = gather_tokens(cot_low)
    queries, pair = project(normed_parts, first_weight, joint_width, cosine, sine, query_width)
    pairs = lax.all_gather(pair.reshape(slots, block, 2 * LANES), "col", axis=0, tiled=False)
    pairs, cot_chunks, gateup_mine, down_mine, meta, info = lax.optimization_barrier(
        (pairs, cot_chunks, gateup_mine, down_mine, meta, info)
    )
    gateup_weight = gather_weight(gateup_mine)
    down_weight = gather_weight(down_mine)
    mixed, logs = attend(meta, queries, pairs, info, rows_on)
    attn_sum = reduce_tokens(product(mixed, output_weight))
    middle = residual + attn_sum
    scale_two = lax.rsqrt(jnp.mean(middle * middle, axis=1, keepdims=True) + EPSILON)
    two_parts = gather_tokens((middle * scale_two * gains[1]).astype(jnp.bfloat16))
    hidden, factor, silu_gate = widen(two_parts, gateup_weight)
    normed_two, cot = (jnp.concatenate(two_parts, axis=0), jnp.concatenate(cot_chunks, axis=0))

    def other_half(rows, grad):
        rows = lax.dynamic_slice_in_dim(rows, (1 - core) * (D // 2), D // 2, 1)
        return dot_tn(rows, grad).astype(jnp.bfloat16)

    def own_half(rows, grad, received):
        rows = lax.dynamic_slice_in_dim(rows, core * (D // 2), D // 2, 1)
        total = dot_tn(rows, grad) + received.astype(jnp.float32)
        return total.astype(jnp.bfloat16)

    def scatter(total):
        return lax.psum_scatter(total, "col", scatter_dimension=0, tiled=True)

    def collect(piece):
        near_y = other_y(piece)
        return [piece, near_y, other_core(piece), other_core(near_y)]

    down_total = own_half(cot, hidden, other_core(other_half(cot, hidden)))
    down_total, down_weight = lax.optimization_barrier((down_total, down_weight))
    down_piece = scatter(down_total)
    work = {}

    def feed_back(first, last):
        work["grad_gate"], work["grad_up"], partial = widen_back(
            cot_chunks[first:last],
            down_weight,
            gateup_weight,
            factor,
            silu_gate,
            first,
            [work[name] for name in ("grad_gate", "grad_up") if name in work],
        )
        return partial

    def feed_others(key):
        gate, up = (work["grad_gate"], work["grad_up"])
        key, work["down_piece"], gate_other, up_other = lax.optimization_barrier(
            (key, down_piece, other_half(normed_two, gate), other_half(normed_two, up))
        )
        work["feed"] = (normed_two, gate, up, other_core(gate_other), other_core(up_other))
        return key

    def feed_owns(first):
        rows, gate, up, gate_other, up_other = work["feed"]
        gate_total = own_half(rows, gate, gate_other)
        first, gate_total, rows, up, up_other = lax.optimization_barrier(
            (first, gate_total, rows, up, up_other)
        )
        work["totals"] = (gate_total, own_half(rows, up, up_other))
        return first

    grad_normed_two = reduce_tokens(feed_back, feed_others, feed_owns)
    gate_piece, up_piece = [scatter(total) for total in work["totals"]]

    def norm_back(values, scale, grad_normed, gain):
        scaled = grad_normed * gain
        total = jnp.sum(scaled * values, axis=1, keepdims=True)
        return scale * scaled - values * (scale**3 * total / D)

    grad_middle = cot_low.astype(jnp.float32) + norm_back(
        middle, scale_two, grad_normed_two, gains[1]
    )
    gain_two = jnp.sum(grad_normed_two * middle * scale_two, axis=0)

    grad_middle_low, late_hidden = lax.optimization_barrier(
        (grad_middle.astype(jnp.bfloat16), hidden)
    )
    gate_total, up_total = work["totals"]
    back = jnp.concatenate(gather_tokens(grad_middle_low, (gate_total, up_total)), axis=0)

    meta_core = jnp.stack([y, core]).astype(jnp.int32)

    def back_here(products):
        products, work["back"] = lax.optimization_barrier((products, back))
        return products

    def attention_back(far):
        here = work.get("back", back)
        grad_query, grad_parts = attend_back(
            meta,
            queries,
            pairs,
            dot_nn(here, output_weight).astype(jnp.bfloat16),
            mixed,
            logs,
            info,
            cosine,
            sine,
            rows_on,
        )
        work["grad_parts"] = [grad_parts[0]] + [
            shift(grad_parts[by], "col", lines, -by) for by in range(1, lines)
        ]
        names = ("grad_query", "gate_piece", "back", "mixed")
        far, *values = lax.optimization_barrier((far, grad_query, gate_piece, here, mixed))
        work.update(zip(names, values))
        return far

    def keys_arrive(first):
        first, work["grad_parts"], work["up_piece"] = lax.optimization_barrier(
            (first, work["grad_parts"], up_piece)
        )
        return first

    if rows_on == 2:
        ffn_sum = reduce_tokens(
            product(late_hidden, down_weight), None, keys_arrive, attention_back, back_here
        )
    else:
        ffn_sum = keys_arrive(attention_back(reduce_tokens(product(late_hidden, down_weight))))
    grad_query, gate_piece, back, mixed = [
        work[name] for name in ("grad_query", "gate_piece", "back", "mixed")
    ]
    output_parts = features_sent((middle + ffn_sum).astype(jnp.bfloat16))
    grad_keyvalue = pair_back(work["grad_parts"], cosine, sine, block)
    grad_joint = jnp.concatenate([grad_query, grad_keyvalue], axis=1)
    normed_one = jnp.concatenate(normed_parts, axis=0)

    def joint_products(first, last):
        if first:
            return product(grad_joint, joint_weight)(first, last)
        output_total = own_half(back, mixed, other_core(other_half(back, mixed)))
        shards = collect(jnp.concatenate([work["down_piece"], work["gate_piece"]], axis=0))
        close, work["output"], work["shards"], work["up_shards"] = lax.optimization_barrier(
            (
                product(grad_joint, joint_weight)(first, last),
                output_total,
                shards,
                collect(work["up_piece"]),
            )
        )
        return close

    def joint_others(key):
        key, other = lax.optimization_barrier((key, other_half(normed_one, grad_joint)))
        work["joint"] = (normed_one, grad_joint, other_core(other))
        work["output_piece"] = scatter(work["output"])
        return key

    def joint_owns(first):
        down_new = turned_update(
            meta_core,
            work["shards"],
            [w_down, down_moment, down_square],
            FF ** (-0.5),
            False,
        )
        names = ("output_piece", "output_parts", "down_new", "up_shards")
        first, rows, grad, other, *values = lax.optimization_barrier(
            (
                first,
                *work["joint"],
                work["output_piece"],
                output_parts,
                down_new,
                work["up_shards"],
            )
        )
        work.update(zip(names, values))
        work["joint_total"] = own_half(rows, grad, other)
        return first

    grad_normed_one = reduce_tokens(joint_products, joint_others, joint_owns)
    joint_piece = scatter(work["joint_total"])
    gateup_new = gateup_update(
        meta_core,
        work["shards"],
        work["up_shards"],
        [w_gateup, gateup_moment, gateup_square],
        32,
    )
    input_grad = grad_middle + norm_back(residual, scale_one, grad_normed_one, gains[0])
    gain_one = jnp.sum(grad_normed_one * residual * scale_one, axis=0)
    joint_piece, input_parts, gateup_new = lax.optimization_barrier(
        (joint_piece, features_sent(input_grad.astype(jnp.bfloat16)), gateup_new)
    )
    layer_output = features_of(work["output_parts"])
    input_grad = features_of(input_parts).astype(jnp.float32)
    pair_piece = joint_piece[:, query_width:]
    pair_total = pair_piece.astype(jnp.float32)
    for by in range(1, rows_on):
        pair_total = pair_total + shift(pair_piece, "row", rows_on, by).astype(jnp.float32)
    joint_piece = jnp.concatenate(
        [joint_piece[:, :query_width], pair_total.astype(jnp.bfloat16)], axis=1
    )
    joint_new = joint_update(
        meta_core,
        collect(joint_piece),
        [w_query, query_moment, query_square],
        [w_keyvalue, keyvalue_moment, keyvalue_square],
    )
    output_new = turned_update(
        meta_core,
        collect(work["output_piece"]),
        [w_output, output_moment, output_square],
        (HEADS * HEAD_DIM // 64) ** (-0.5),
        True,
    )

    gain_sums = jnp.stack([gain_one, gain_two])
    gain_sums, gateup_new = lax.optimization_barrier((gain_sums, gateup_new))
    blocks = [
        jnp.concatenate(
            [
                gain_sums[:, at * half : (at + 1) * half],
                gain_sums[:, D // 2 + at * half : D // 2 + (at + 1) * half],
            ],
            axis=1,
        )
        for at in range(lines)
    ]
    grad_gains = pick(blocks, line)
    for by in range(1, lines):
        grad_gains = grad_gains + shift(pick(blocks, (line + by) % lines), "col", lines, by)
    for axis, size in (("core", 2), ("y", 2), ("row", rows_on)):
        blocks_total = grad_gains
        for by in range(1, size):
            grad_gains = grad_gains + shift(blocks_total, axis, size, by)

    gains_new = adamw_step(norm_gains, grad_gains, gains_moment, gains_square, 0.6, 0.0)
    return (
        layer_output,
        input_grad,
        *gains_new,
        *joint_new,
        *output_new,
        *gateup_new,
        *work["down_new"],
    )


def solution(mesh):
    dp, rows_on, lines = (mesh.shape["dp"], mesh.shape["row"], mesh.shape["col"])
    split = Mesh(mesh.devices.reshape(dp // 2, 2, rows_on, lines), ("y", "core", "row", "col"))
    tokens = P(("y", "core", "row"), "col")
    narrow, wide = (P("col", "row"), P("row", "col"))
    gains, pair, gateup = (P(None, "col"), P("col", None), P("col", None, "row"))
    return jax.shard_map(
        functools.partial(on_device, (rows_on, lines)),
        mesh=split,
        in_specs=(
            tokens,
            tokens,
            P(("y", "core"), None),
            gains,
            narrow,
            pair,
            wide,
            gateup,
            wide,
            gains,
            gains,
            narrow,
            narrow,
            pair,
            pair,
            wide,
            wide,
            gateup,
            gateup,
            wide,
            wide,
        ),
        out_specs=(tokens, tokens)
        + (gains,) * 3
        + (narrow,) * 3
        + (pair,) * 3
        + (wide,) * 3
        + (gateup,) * 3
        + (wide,) * 3,
        check_vma=False,
    )
```

```python
import functools

import jax
import jax.numpy as jnp
from jax import lax
from jax.experimental import pallas as pl
from jax.experimental.pallas import tpu as pltpu
from jax.sharding import Mesh, PartitionSpec as P

D = 2048
HEADS = 32
KV_HEADS = 4
HEAD_DIM = 64
FF = 5632
STEP = 10

EPSILON = 1e-05
BETA_ONE = 0.9
BETA_TWO = 0.999
ADAM_EPS = 1e-08
MASKED = -1e30
SCORE_SCALE = HEAD_DIM ** (-0.5)
LANES = 128
VMEM_LIMIT = 48 * 1024 * 1024


def dot_nn(left, right):
    return lax.dot_general(left, right, (((1,), (0,)), ((), ())), preferred_element_type=jnp.float32)


def dot_nt(left, right):
    return lax.dot_general(left, right, (((1,), (1,)), ((), ())), preferred_element_type=jnp.float32)


def dot_tn(left, right):
    return lax.dot_general(left, right, (((0,), (0,)), ((), ())), preferred_element_type=jnp.float32)


def adamw_step(weight, gradient, moment, square, step_rate, decay_rate):
    moment_new = BETA_ONE * moment + (1.0 - BETA_ONE) * gradient
    square_new = BETA_TWO * square + (1.0 - BETA_TWO) * gradient * gradient
    fixed_one = moment_new / (1.0 - BETA_ONE**STEP)
    fixed_two = square_new / (1.0 - BETA_TWO**STEP)
    weight_new = weight - step_rate * (
        fixed_one / (jnp.sqrt(fixed_two) + ADAM_EPS) + decay_rate * weight
    )
    return (moment_new, square_new, weight_new)


def document_starts(segment_ids):
    places = jnp.arange(segment_ids.shape[0], dtype=jnp.int32)
    starts = jnp.concatenate([jnp.ones((1,), jnp.bool_), segment_ids[1:] != segment_ids[:-1]])
    return lax.cummax(jnp.where(starts, places, 0), axis=0)


def turn(values):
    lane = lax.broadcasted_iota(jnp.int32, values.shape, 1)
    ahead = pltpu.roll(values, LANES - HEAD_DIM // 2, 1)
    behind = pltpu.roll(values, HEAD_DIM // 2, 1)
    return jnp.where(lane % HEAD_DIM < HEAD_DIM // 2, -ahead, behind)


def take_chunk(rows_refs, held_ref):
    for at, ref in enumerate(rows_refs):

        @pl.when(pl.program_id(0) == at)
        def _(ref=ref):
            held_ref[...] = ref[...]


def project_kernel(slots, *refs):
    rows_refs, (weight_ref, cos_ref, sin_ref, query_ref, pair_ref, held_ref) = (refs[:slots], refs[slots:])
    take_chunk(rows_refs, held_ref)
    sums = dot_nn(held_ref[...], weight_ref[...])
    cosine, sine = cos_ref[...], sin_ref[...]
    width = query_ref.shape[1]
    lane = lax.broadcasted_iota(jnp.int32, cosine.shape, 1)
    for start in range(0, width, LANES):
        part = sums[:, start : start + LANES]
        turned = (part * cosine + turn(part) * sine).astype(jnp.bfloat16)
        query_ref[:, start : start + LANES] = turned * jnp.bfloat16(SCORE_SCALE)
    for which in range(2):
        part = sums[:, width + which * LANES : width + (which + 1) * LANES]
        is_key = (lane < HEAD_DIM) if which == 0 else (lane >= HEAD_DIM)
        turned = jnp.where(is_key, part * cosine + turn(part) * sine, part)
        pair_ref[:, which * LANES : (which + 1) * LANES] = turned.astype(jnp.bfloat16)


def project(chunks, weight, total, cosine, sine, width):
    slots = len(chunks)
    block, depth = chunks[0].shape
    rows = slots * block
    whole = pl.BlockSpec((block, depth), lambda i: (0, 0))
    return pl.pallas_call(
        functools.partial(project_kernel, slots),
        grid=(slots,),
        in_specs=[whole] * slots
        + [
            pl.BlockSpec((depth, total), lambda i: (0, 0)),
            pl.BlockSpec((block, LANES), lambda i: (i, 0)),
            pl.BlockSpec((block, LANES), lambda i: (i, 0)),
        ],
        out_specs=[
            pl.BlockSpec((block, width), lambda i: (i, 0)),
            pl.BlockSpec((block, total - width), lambda i: (i, 0)),
        ],
        out_shape=[
            jax.ShapeDtypeStruct((rows, width), jnp.bfloat16),
            jax.ShapeDtypeStruct((rows, total - width), jnp.bfloat16),
        ],
        scratch_shapes=[pltpu.VMEM((block, depth), jnp.bfloat16)],
        compiler_params=pltpu.CompilerParams(vmem_limit_bytes=VMEM_LIMIT),
        cost_estimate=pl.CostEstimate(
            flops=2 * rows * depth * total,
            bytes_accessed=(rows + total) * depth * 2,
            transcendentals=0,
        ),
        name="project",
    )(*chunks, weight, cosine, sine)


def widen_kernel(slots, *refs):
    rows_refs, (weight_ref, hidden_ref, factor_ref, silu_ref, held_ref) = (refs[:slots], refs[slots:])
    take_chunk(rows_refs, held_ref)
    sums = dot_nn(held_ref[...], weight_ref[...])
    width = hidden_ref.shape[1]
    gate, upward = (sums[:, :width], sums[:, width:])
    sigmoid = jax.nn.sigmoid(gate)
    silu = gate * sigmoid
    hidden_ref[...] = (silu * upward).astype(jnp.bfloat16)
    factor_ref[...] = (upward * sigmoid * (1.0 + gate * (1.0 - sigmoid))).astype(jnp.bfloat16)
    silu_ref[...] = silu.astype(jnp.bfloat16)


def widen(chunks, weight):
    slots = len(chunks)
    block, depth = chunks[0].shape
    width = weight.shape[1] // 2
    rows = slots * block
    once = pl.Buffered(1)
    return pl.pallas_call(
        functools.partial(widen_kernel, slots),
        grid=(slots,),
        in_specs=[pl.BlockSpec((block, depth), lambda i: (0, 0), pipeline_mode=once)] * slots
        + [pl.BlockSpec(weight.shape, lambda i: (0, 0), pipeline_mode=once)],
        out_specs=[pl.BlockSpec((block, width), lambda i: (i, 0))] * 3,
        out_shape=[jax.ShapeDtypeStruct((rows, width), jnp.bfloat16)] * 3,
        scratch_shapes=[pltpu.VMEM((block, depth), jnp.bfloat16)],
        compiler_params=pltpu.CompilerParams(vmem_limit_bytes=VMEM_LIMIT),
        cost_estimate=pl.CostEstimate(
            flops=4 * rows * depth * width,
            bytes_accessed=(rows + 2 * width) * depth * 2 + 6 * rows * width,
            transcendentals=rows * width,
        ),
        name="widen",
    )(*chunks, weight)


def widen_back_kernel(slots, kept, *refs):
    rows_refs, refs = (refs[:slots], refs[slots:])
    down_ref, gateup_ref, factor_ref, silu_ref = refs[:4]
    gate_ref, up_ref, partial_ref, held_ref = refs[4 + kept :]
    take_chunk(rows_refs, held_ref)
    grad_hidden = dot_nn(held_ref[...], down_ref[...])
    gate = (grad_hidden * factor_ref[...].astype(jnp.float32)).astype(jnp.bfloat16)
    up = (grad_hidden * silu_ref[...].astype(jnp.float32)).astype(jnp.bfloat16)
    gate_ref[...] = gate
    up_ref[...] = up
    both = jnp.concatenate([gate, up], axis=1)
    partial_ref[...] = dot_nt(both, gateup_ref[...]).astype(jnp.bfloat16)


def widen_back(chunks, down, gateup, factor, silu, first, kept):
    slots = len(chunks)
    block, depth = chunks[0].shape
    width = down.shape[1]
    once = pl.Buffered(1)
    tile = pl.BlockSpec((block, width), lambda i: (first + i, 0))
    return pl.pallas_call(
        functools.partial(widen_back_kernel, slots, len(kept)),
        grid=(slots,),
        in_specs=[pl.BlockSpec((block, depth), lambda i: (0, 0), pipeline_mode=once)] * slots
        + [
            pl.BlockSpec(down.shape, lambda i: (0, 0), pipeline_mode=once),
            pl.BlockSpec(gateup.shape, lambda i: (0, 0), pipeline_mode=once),
            tile,
            tile,
        ]
        + [pl.BlockSpec(memory_space=pl.ANY)] * len(kept),
        out_specs=[tile, tile, pl.BlockSpec((block, depth), lambda i: (i, 0))],
        out_shape=[jax.ShapeDtypeStruct(factor.shape, jnp.bfloat16)] * 2
        + [jax.ShapeDtypeStruct((slots * block, depth), jnp.bfloat16)],
        scratch_shapes=[pltpu.VMEM((block, depth), jnp.bfloat16)],
        input_output_aliases={slots + 4 + i: i for i in range(len(kept))},
        compiler_params=pltpu.CompilerParams(vmem_limit_bytes=VMEM_LIMIT),
        cost_estimate=pl.CostEstimate(
            flops=slots * block * depth * width,
            bytes_accessed=8 * slots * block * width,
            transcendentals=0,
        ),
        name="widen_back",
    )(*chunks, down, gateup, factor, silu, *kept)


def stack_heads(values):
    return jnp.concatenate(
        [values[:, start : start + LANES] for start in range(0, values.shape[1], LANES)], axis=0
    )


def block_of(meta_ref, chunk, step, parts, lines):
    base = chunk * (2 + parts)
    key_block = meta_ref[base + 1] - step
    slot = meta_ref[base + 2 + key_block // lines]
    own_line = meta_ref[pl.num_programs(0) * (2 + parts)]
    line = lax.rem(key_block, lines)
    return (key_block, slot, line, lax.rem(own_line - line + lines, lines))


def attend_kernel(parts, lines, meta_ref, query_ref, pair_ref, info_ref, out_ref, log_ref):
    chunk = pl.program_id(0)
    block = query_ref.shape[0]
    heads = query_ref.shape[1] // LANES
    stacked = stack_heads(query_ref[...])
    lane = lax.broadcasted_iota(jnp.int32, stacked.shape, 1)
    place = jnp.concatenate([info_ref[0, 0:1, :]] * heads, axis=1)
    start = jnp.concatenate([info_ref[0, 1:2, :]] * heads, axis=1)
    base = chunk * (2 + parts)
    steps = meta_ref[base + 1] - meta_ref[base] + 1
    width = heads * block
    key_lanes = lane < HEAD_DIM
    queries = [
        jnp.where(key_lanes if which == 0 else ~key_lanes, stacked, jnp.zeros_like(stacked))
        for which in range(2)
    ]

    def body(step, carry):
        key_block, slot, at, _ = block_of(meta_ref, chunk, step, parts, lines)
        key_place = key_block * block + lax.broadcasted_iota(jnp.int32, (block, width), 0)
        seen = (key_place <= place) & (key_place >= start)
        result = []
        for which in range(2):
            peak, total, mixed = carry[which]
            pair = pair_ref[at, slot, :, which * LANES : (which + 1) * LANES]
            scores = jnp.where(seen, dot_nt(pair, queries[which]), MASKED)
            new_peak = jnp.maximum(peak, jnp.max(scores, axis=0, keepdims=True))
            weights = jnp.exp(scores - new_peak)
            shrink = jnp.exp(peak - new_peak)
            total = total * shrink + jnp.sum(weights, axis=0, keepdims=True)
            mixed = mixed * shrink + dot_tn(pair, weights.astype(jnp.bfloat16))
            result.append((new_peak, total, mixed))
        return tuple(result)

    empty = (
        jnp.full((1, width), MASKED, jnp.float32),
        jnp.zeros((1, width), jnp.float32),
        jnp.zeros((LANES, width), jnp.float32),
    )
    outs = []
    for which, (peak, total, mixed) in enumerate(lax.fori_loop(0, steps, body, (empty, empty))):
        log_ref[0, which : which + 1, :] = peak + jnp.log(total)
        outs.append(mixed / total)
    joined = jnp.concatenate([outs[1][:HEAD_DIM], outs[0][HEAD_DIM:]], axis=0)
    rows = joined.T.astype(jnp.bfloat16)
    for head in range(heads):
        out_ref[:, head * LANES : (head + 1) * LANES] = rows[head * block : (head + 1) * block]


def attend(meta, queries, pairs, info, parts):
    chunks, block = (info.shape[0], info.shape[2])
    width = queries.shape[1]
    heads = width // LANES
    lines = pairs.shape[0]
    steps = 3 * chunks
    return pl.pallas_call(
        functools.partial(attend_kernel, parts, lines),
        grid_spec=pltpu.PrefetchScalarGridSpec(
            num_scalar_prefetch=1,
            grid=(chunks,),
            in_specs=[
                pl.BlockSpec((block, width), lambda i, m: (i, 0)),
                pl.BlockSpec(pairs.shape, lambda i, m: (0, 0, 0, 0)),
                pl.BlockSpec((1, 2, block), lambda i, m: (i, 0, 0)),
            ],
            out_specs=[
                pl.BlockSpec((block, width), lambda i, m: (i, 0)),
                pl.BlockSpec((1, 2, heads * block), lambda i, m: (i, 0, 0)),
            ],
        ),
        out_shape=[
            jax.ShapeDtypeStruct(queries.shape, jnp.bfloat16),
            jax.ShapeDtypeStruct((chunks, 2, heads * block), jnp.float32),
        ],
        compiler_params=pltpu.CompilerParams(vmem_limit_bytes=VMEM_LIMIT),
        cost_estimate=pl.CostEstimate(
            flops=steps * 2 * 2 * 2 * heads * block * block * LANES,
            bytes_accessed=queries.size * 4 + pairs.size * 2,
            transcendentals=steps * 2 * heads * block * block,
        ),
        name="attend",
    )(meta, queries, pairs, info)


def attend_back_kernel(parts, lines, meta_ref, query_ref, *refs):
    pair_ref, grad_ref, mixed_ref, log_ref, info_ref, cos_ref, sin_ref, query_out = refs[:8]
    pair_outs = refs[8 : 8 + lines]
    sums = refs[8 + lines]
    chunk = pl.program_id(0)
    block = query_ref.shape[0]
    heads = query_ref.shape[1] // LANES

    @pl.when(chunk == 0)
    def _():
        sums[...] = jnp.zeros_like(sums)

    stacked = stack_heads(query_ref[...])
    stacked_grad = stack_heads(grad_ref[...])
    product = stacked_grad.astype(jnp.float32) * stack_heads(mixed_ref[...]).astype(jnp.float32)
    lane = lax.broadcasted_iota(jnp.int32, stacked.shape, 1)
    place = jnp.concatenate([info_ref[0, 0:1, :]] * heads, axis=1)
    start = jnp.concatenate([info_ref[0, 1:2, :]] * heads, axis=1)
    base = chunk * (2 + parts)
    steps = meta_ref[base + 1] - meta_ref[base] + 1
    width = heads * block
    key_lanes = lane < HEAD_DIM
    queries, grad, centre, logs = ([], [], [], [])
    for which in range(2):
        is_key = key_lanes if which == 0 else ~key_lanes
        queries.append(jnp.where(is_key, stacked, jnp.zeros_like(stacked)))
        grad.append(jnp.where(is_key, jnp.zeros_like(stacked_grad), stacked_grad))
        own = jnp.where(is_key, 0.0, product)
        centre.append(
            lax.dot_general(
                jnp.ones((8, LANES), jnp.float32),
                own,
                (((1,), (1,)), ((), ())),
                precision=lax.Precision.HIGHEST,
                preferred_element_type=jnp.float32,
            )[0:1]
        )
        logs.append(log_ref[0, which : which + 1, :])

    def body(step, carry):
        key_block, slot, at, shift = block_of(meta_ref, chunk, step, parts, lines)
        key_place = key_block * block + lax.broadcasted_iota(jnp.int32, (block, width), 0)
        seen = (key_place <= place) & (key_place >= start)
        result = []
        for which in range(2):
            columns = slice(which * LANES, (which + 1) * LANES)
            pair = pair_ref[at, slot, :, columns]
            scores = jnp.where(seen, dot_nt(pair, queries[which]), MASKED)
            weights = jnp.exp(scores - logs[which])
            grad_weights = dot_nt(pair, grad[which]) - centre[which]
            grad_scores = (weights * grad_weights).astype(jnp.bfloat16)
            sums[shift, slot, :, columns] += dot_nn(grad_scores, queries[which]) + dot_nn(
                weights.astype(jnp.bfloat16), grad[which]
            )
            result.append(carry[which] + dot_tn(pair, grad_scores))
        return tuple(result)

    empty = jnp.zeros((LANES, width), jnp.float32)
    grads = lax.fori_loop(0, steps, body, (empty, empty))
    joined = jnp.concatenate([grads[0][:HEAD_DIM], grads[1][HEAD_DIM:]], axis=0)
    rows = joined.T * SCORE_SCALE
    cosine, sine = cos_ref[...], sin_ref[...]
    for head in range(heads):
        part = rows[head * block : (head + 1) * block]
        back = part * cosine - turn(part) * sine
        query_out[:, head * LANES : (head + 1) * LANES] = back.astype(jnp.bfloat16)

    @pl.when(chunk == pl.num_programs(0) - 1)
    def _():
        for line in range(lines):
            pair_outs[line][...] = sums[line].astype(jnp.bfloat16)


def attend_back(meta, queries, pairs, grad_mixed, mixed, logs, info, cosine, sine, parts):
    chunks, block = (info.shape[0], info.shape[2])
    width = queries.shape[1]
    heads = width // LANES
    lines = pairs.shape[0]
    shape = pairs.shape[1:]
    steps = 3 * chunks
    wide = pl.BlockSpec((block, width), lambda i, m: (i, 0))
    table = pl.BlockSpec((block, LANES), lambda i, m: (i, 0))
    whole = pl.BlockSpec(shape, lambda i, m: (0, 0, 0))
    outs = pl.pallas_call(
        functools.partial(attend_back_kernel, parts, lines),
        grid_spec=pltpu.PrefetchScalarGridSpec(
            num_scalar_prefetch=1,
            grid=(chunks,),
            in_specs=[
                wide,
                pl.BlockSpec(pairs.shape, lambda i, m: (0, 0, 0, 0)),
                wide,
                wide,
                pl.BlockSpec((1, 2, heads * block), lambda i, m: (i, 0, 0)),
                pl.BlockSpec((1, 2, block), lambda i, m: (i, 0, 0)),
                table,
                table,
            ],
            out_specs=[wide] + [whole] * lines,
            scratch_shapes=[pltpu.VMEM(pairs.shape, jnp.float32)],
        ),
        out_shape=[jax.ShapeDtypeStruct(queries.shape, jnp.bfloat16)]
        + [jax.ShapeDtypeStruct(shape, jnp.bfloat16)] * lines,
        compiler_params=pltpu.CompilerParams(vmem_limit_bytes=VMEM_LIMIT),
        cost_estimate=pl.CostEstimate(
            flops=steps * 2 * 5 * 2 * heads * block * block * LANES,
            bytes_accessed=queries.size * 8 + 2 * pairs.size * 2,
            transcendentals=steps * 2 * heads * block * block,
        ),
        name="attend_back",
    )(
        meta,
        queries,
        pairs,
        grad_mixed,
        mixed,
        logs,
        info,
        cosine,
        sine,
    )
    return (outs[0], [out.reshape(chunks * block, 2 * LANES) for out in outs[1:]])


def pair_back_kernel(*refs):
    *part_refs, cos_ref, sin_ref, out_ref = refs
    cosine, sine = cos_ref[...], sin_ref[...]
    lane = lax.broadcasted_iota(jnp.int32, cosine.shape, 1)
    for which in range(2):
        columns = slice(which * LANES, (which + 1) * LANES)
        total = part_refs[0][:, columns].astype(jnp.float32)
        for ref in part_refs[1:]:
            total = total + ref[:, columns].astype(jnp.float32)
        is_key = (lane < HEAD_DIM) if which == 0 else (lane >= HEAD_DIM)
        total = jnp.where(is_key, total * cosine - turn(total) * sine, total)
        out_ref[:, columns] = total.astype(jnp.bfloat16)


def pair_back(parts, cosine, sine, block):
    rows, columns = parts[0].shape
    tile = pl.BlockSpec((block, columns), lambda i: (i, 0))
    table = pl.BlockSpec((block, LANES), lambda i: (i, 0))
    return pl.pallas_call(
        pair_back_kernel,
        grid=(rows // block,),
        in_specs=[tile] * len(parts) + [table, table],
        out_specs=tile,
        out_shape=jax.ShapeDtypeStruct((rows, columns), jnp.bfloat16),
        compiler_params=pltpu.CompilerParams(vmem_limit_bytes=VMEM_LIMIT),
        name="pair_back",
    )(*parts, cosine, sine)


def update(refs, index, gradient, rate):
    weight, moment, square = [ref[index] for ref in refs[:3]]
    moment_new, square_new, weight_new = adamw_step(weight, gradient, moment, square, rate, 0.1)
    for ref, value in zip(refs[3:], (moment_new, square_new, weight_new)):
        ref[index] = value


def chosen(meta_ref, grad_refs, at, rows, columns):
    own_y = meta_ref[0] == at
    first = pl.program_id(0) == 0
    near = jnp.where(first, grad_refs[0][rows, columns], grad_refs[2][rows, columns])
    far = jnp.where(first, grad_refs[1][rows, columns], grad_refs[3][rows, columns])
    return jnp.where(own_y, near, far).astype(jnp.float32)


def joint_update_kernel(meta_ref, *refs):
    grad_refs, query_refs, pair_refs = (refs[:4], refs[4:7] + refs[10:13], refs[7:10] + refs[13:16])
    groups = query_refs[0].shape[1] // (2 * LANES)
    every = slice(None)
    for at in range(2):
        for j in range(groups):
            gradient = chosen(meta_ref, grad_refs, at, every, slice(j * LANES, (j + 1) * LANES))
            place = slice((2 * j + at) * LANES, (2 * j + at + 1) * LANES)
            update(query_refs, (every, place), gradient, D ** (-0.5))
        for which in range(2):
            start = (groups + which) * LANES
            gradient = chosen(meta_ref, grad_refs, at, every, slice(start, start + LANES))
            if which == 1:
                gradient = pltpu.roll(gradient, HEAD_DIM, 1)
            place = slice((2 * at + which) * LANES, (2 * at + which + 1) * LANES)
            update(pair_refs, (every, place), gradient, D ** (-0.5))


def joint_update(meta, grads, query, pair):
    half = grads[0].shape[0]

    def rows_of(array):
        return pl.BlockSpec((half, array.shape[1]), lambda i, m: ((m[1] + i) % 2, 0))

    whole = pl.BlockSpec(grads[0].shape, lambda i, m: (0, 0))
    blocks = [rows_of(array) for array in (*query, *pair)]
    return pl.pallas_call(
        joint_update_kernel,
        grid_spec=pltpu.PrefetchScalarGridSpec(
            num_scalar_prefetch=1, grid=(2,), in_specs=[whole] * 4 + blocks, out_specs=blocks
        ),
        out_shape=[jax.ShapeDtypeStruct(array.shape, array.dtype) for array in (*query, *pair)],
        compiler_params=pltpu.CompilerParams(vmem_limit_bytes=VMEM_LIMIT),
        cost_estimate=pl.CostEstimate(
            flops=20 * (query[0].size + pair[0].size),
            bytes_accessed=24 * (query[0].size + pair[0].size),
            transcendentals=0,
        ),
        name="joint_update",
    )(meta, *grads, *query, *pair)


def turned_update_kernel(rate, swapped, meta_ref, *refs):
    grad_refs, weight_refs = (refs[:4], refs[4:10])
    at = pl.program_id(1)
    width = grad_refs[0].shape[1]
    every = slice(None)
    for j, start in enumerate(range(0, width, LANES)):
        strip = slice(start, min(start + LANES, width))
        gradient = chosen(meta_ref, grad_refs, at, every, strip).T
        if swapped:
            gradient = jnp.concatenate([gradient[HEAD_DIM:], gradient[:HEAD_DIM]], axis=0)
            index = (j, 0)
        else:
            index = (strip, every)
        update(weight_refs, index, gradient, rate)


def turned_update(meta, grads, weights, rate, swapped):
    shape = weights[0].shape
    half, width = (shape[1] // 2, grads[0].shape[1])
    if swapped:
        weights = [w.reshape(width // LANES, 2, LANES, shape[1]) for w in weights]
        block = pl.BlockSpec(
            (width // LANES, 1, LANES, half), lambda i, at, m: (0, at, 0, (m[1] + i) % 2)
        )
    else:
        block = pl.BlockSpec((width, half), lambda i, at, m: (at, (m[1] + i) % 2))
    outs = pl.pallas_call(
        functools.partial(turned_update_kernel, rate, swapped),
        grid_spec=pltpu.PrefetchScalarGridSpec(
            num_scalar_prefetch=1,
            grid=(2, 2),
            in_specs=[pl.BlockSpec((half, width), lambda i, at, m: (0, 0))] * 4 + [block] * 3,
            out_specs=[block] * 3,
        ),
        out_shape=[jax.ShapeDtypeStruct(weights[0].shape, jnp.float32)] * 3,
        compiler_params=pltpu.CompilerParams(vmem_limit_bytes=VMEM_LIMIT),
        cost_estimate=pl.CostEstimate(
            flops=20 * weights[0].size, bytes_accessed=24 * weights[0].size, transcendentals=0
        ),
        name="turned_update",
    )(meta, *grads, *weights)
    return [out.reshape(shape) for out in outs]


def gateup_update_kernel(meta_ref, *refs):
    gate_refs, up_refs, weight_refs = (refs[:4], refs[4:8], refs[8:14])
    every = slice(None)
    gate, up = [
        jnp.concatenate([chosen(meta_ref, grads, at, every, every) for at in range(2)], axis=1)
        for grads in (gate_refs, up_refs)
    ]
    update(weight_refs, every, jnp.stack([gate, up], axis=1), D ** (-0.5))


def gateup_update(meta, gates, ups, weights, rows):
    half, width = ups[0].shape
    shape = weights[0].shape
    tiles = half // rows
    gate = pl.BlockSpec((rows, width), lambda i, j, m: (tiles + j, 0))
    up = pl.BlockSpec((rows, width), lambda i, j, m: (j, 0))
    block = pl.BlockSpec(
        (rows, 2, shape[2]), lambda i, j, m: (((m[1] + i) % 2) * tiles + j, 0, 0)
    )
    return pl.pallas_call(
        gateup_update_kernel,
        grid_spec=pltpu.PrefetchScalarGridSpec(
            num_scalar_prefetch=1,
            grid=(2, tiles),
            in_specs=[gate] * 4 + [up] * 4 + [block] * 3,
            out_specs=[block] * 3,
        ),
        out_shape=[jax.ShapeDtypeStruct(shape, jnp.float32)] * 3,
        compiler_params=pltpu.CompilerParams(vmem_limit_bytes=VMEM_LIMIT),
        cost_estimate=pl.CostEstimate(
            flops=20 * weights[0].size, bytes_accessed=28 * weights[0].size, transcendentals=0
        ),
        name="gateup_update",
    )(meta, *gates, *ups, *weights)


def on_device(
    sizes,
    block_input,
    cotangent,
    segments,
    norm_gains,
    w_query,
    w_keyvalue,
    w_output,
    w_gateup,
    w_down,
    gains_moment,
    gains_square,
    query_moment,
    query_square,
    keyvalue_moment,
    keyvalue_square,
    output_moment,
    output_square,
    gateup_moment,
    gateup_square,
    down_moment,
    down_square,
):
    rows_on, lines = sizes
    y, core, row, line = [lax.axis_index(name) for name in ("y", "core", "row", "col")]
    length = segments.shape[1]
    block = block_input.shape[0] // lines
    wide = block_input.shape[1]
    half = wide // 2
    slots = 2 * rows_on
    per_row = w_query.shape[1] // (KV_HEADS * HEAD_DIM)
    query_width = per_row * LANES
    hidden_here = w_gateup.shape[2] // 2

    def shift(value, axis, size, by):
        return lax.ppermute(value, axis, [(i, (i + by) % size) for i in range(size)])

    def other_core(value):
        return lax.ppermute(value, "core", [(0, 1), (1, 0)])

    def other_y(value):
        return lax.ppermute(value, "y", [(0, 1), (1, 0)])

    def place_of(y_at, core_at, row_at):
        return (y_at * 2 + core_at) * rows_on + row_at

    first_pairs, second_pairs = ([], [])
    for y_at in range(2):
        for core_at in range(2):
            for row_at in range(rows_on):
                over_row = (
                    place_of(y_at, core_at, row_at),
                    place_of(y_at, core_at, (row_at + 1) % rows_on),
                )
                over_y = (place_of(y_at, core_at, row_at), place_of(1 - y_at, core_at, row_at))
                first_pairs.append(over_row if core_at == 0 else over_y)
                second_pairs.append(over_y if core_at == 0 else over_row)
    near = ("y", "core", "row")

    def gather_tokens(own, beside=()):
        if rows_on == 2:
            first = lax.ppermute(own, near, first_pairs)
            second = lax.ppermute(own, near, second_pairs)
            first, second, *_ = lax.optimization_barrier((first, second, *beside))
            third = lax.ppermute(first, near, second_pairs)
            return [own, first, second, third]
        parts = [own] + [shift(own, "row", rows_on, by) for by in range(1, rows_on)]
        return parts + [other_y(part) for part in parts]

    def reduce_tokens(rows_of, middle=None, before_last=None, far_here=None, ready=None):
        def same(value):
            return value

        middle, before_last = (middle or same, before_last or same)
        if rows_on == 2:
            far = rows_of(2, 4)
            if ready:
                far, close = ready((far, rows_of(0, 2)))
            third = lax.ppermute(far[block:], near, second_pairs)
            second = lax.ppermute(far[:block], near, second_pairs)
            if not ready:
                close = rows_of(0, 2)
            third, second, close = (far_here or lax.optimization_barrier)((third, second, close))
            key = (close[block:].astype(jnp.float32) + third.astype(jnp.float32)).astype(jnp.bfloat16)
            first = before_last(lax.ppermute(middle(key), near, first_pairs))
            own = close[:block].astype(jnp.float32) + second.astype(jnp.float32)
            return own + first.astype(jnp.float32)
        partial = rows_of(0, slots)
        parts = [partial[i * block : (i + 1) * block] for i in range(slots)]
        sums = [
            parts[i].astype(jnp.float32) + other_y(parts[rows_on + i]).astype(jnp.float32)
            for i in range(rows_on)
        ]
        sums[0] = middle(sums[0])
        total = sums[0]
        for by in range(1, rows_on):
            moved = shift(sums[by].astype(jnp.bfloat16), "row", rows_on, -by)
            total = total + moved.astype(jnp.float32)
        return before_last(total)

    def product(left, right):
        def rows_of(first, last):
            return dot_nt(left[first * block : last * block], right).astype(jnp.bfloat16)

        return rows_of

    if rows_on == 2:
        slot_y = [y, jnp.where(core == 0, y, 1 - y), jnp.where(core == 0, 1 - y, y), 1 - y]
        slot_row = [row, jnp.where(core == 0, 1 - row, row), jnp.where(core == 0, row, 1 - row), 1 - row]
    else:
        slot_y = [y] * rows_on + [1 - y] * rows_on
        slot_row = [(row - by) % rows_on for by in range(rows_on)] * 2

    def pick(parts, index):
        return lax.dynamic_index_in_dim(jnp.stack(parts), index, 0, keepdims=False)

    def tokens_sent(values):
        parts = []
        for by in range(lines):
            part = lax.dynamic_slice_in_dim(values, ((line + by) % lines) * block, block, 0)
            parts.append(part if by == 0 else shift(part, "col", lines, by))
        return parts

    def tokens_of(parts):
        blocks = [pick(parts, (line - at) % lines) for at in range(lines)]
        return jnp.concatenate([b[:, :half] for b in blocks] + [b[:, half:] for b in blocks], axis=1)

    def features_sent(values):
        blocks = [
            jnp.concatenate(
                [
                    values[:, at * half : (at + 1) * half],
                    values[:, D // 2 + at * half : D // 2 + (at + 1) * half],
                ],
                axis=1,
            )
            for at in range(lines)
        ]
        parts = []
        for by in range(lines):
            part = pick(blocks, (line + by) % lines)
            parts.append(part if by == 0 else shift(part, "col", lines, by))
        return parts

    def features_of(parts):
        return jnp.concatenate([pick(parts, (line - at) % lines) for at in range(lines)], axis=0)

    def half_rows(values):
        return lax.dynamic_slice_in_dim(values, core * half, half, 0)

    def half_columns(values):
        return lax.dynamic_slice_in_dim(values, core * half, half, 1)

    def gather_weight(piece):
        return lax.all_gather(piece, ("core", "col"), axis=0, tiled=True)

    query_rows = half_rows(w_query).astype(jnp.bfloat16)
    pair_rows = half_rows(w_keyvalue).astype(jnp.bfloat16)

    def joint_of(at):
        pieces = [
            query_rows[:, (2 * j + at) * LANES : (2 * j + at + 1) * LANES] for j in range(per_row)
        ]
        pair = pair_rows[:, at * 2 * LANES : (at + 1) * 2 * LANES]
        pieces += [
            pair[:, :LANES],
            pair[:, LANES + HEAD_DIM :],
            pair[:, LANES : LANES + HEAD_DIM],
        ]
        return jnp.concatenate(pieces, axis=1)

    joint_mine = jnp.where(y == 0, joint_of(0), joint_of(1))
    output_columns = half_columns(w_output).astype(jnp.bfloat16)

    def output_of(at):
        pieces = []
        for j in range(per_row):
            base = (2 * j + at) * LANES
            pieces += [
                output_columns[base + HEAD_DIM : base + LANES],
                output_columns[base : base + HEAD_DIM],
            ]
        return jnp.concatenate(pieces, axis=0)

    output_mine = jnp.where(y == 0, output_of(0), output_of(1)).T
    gateup_mine = lax.dynamic_slice(
        w_gateup, (core * half, 0, y * hidden_here), (half, 2, hidden_here)
    ).astype(jnp.bfloat16)
    gateup_mine = jnp.concatenate([gateup_mine[:, 0], gateup_mine[:, 1]], axis=1)
    down_mine = lax.dynamic_slice(
        w_down, (y * hidden_here, core * half), (hidden_here, half)
    ).astype(jnp.bfloat16).T

    gain_parts = [norm_gains] + [shift(norm_gains, "col", lines, by) for by in range(1, lines)]
    gain_blocks = [pick(gain_parts, (line - at) % lines) for at in range(lines)]
    gains = jnp.concatenate(
        [b[:, :half] for b in gain_blocks] + [b[:, half:] for b in gain_blocks], axis=1
    )

    residual_low = tokens_of(tokens_sent(block_input))
    residual_low, late_cotangent, other_segments, joint_mine, output_mine = lax.optimization_barrier(
        (residual_low, cotangent, other_y(segments), joint_mine, output_mine)
    )

    own_starts = document_starts(segments[0])
    other_starts = document_starts(other_segments[0])
    frequency = 10000.0 ** (-2.0 * jnp.arange(HEAD_DIM // 2, dtype=jnp.float32) / HEAD_DIM)
    slot_y, slot_row = (jnp.stack(slot_y).astype(jnp.int32), jnp.stack(slot_row).astype(jnp.int32))
    begins = slot_row * (lines * block) + line * block
    places = begins[:, None] + jnp.arange(block, dtype=jnp.int32)[None, :]
    both_starts = jnp.stack([own_starts, other_starts]).reshape(2, rows_on, lines, block)
    both_starts = lax.dynamic_index_in_dim(both_starts, line, 2, keepdims=False)
    starts = jnp.zeros((slots, block), jnp.int32)
    for which in range(2):
        for row_at in range(rows_on):
            here = ((slot_y != y) == bool(which)) & (slot_row == row_at)
            starts = jnp.where(here[:, None], both_starts[which, row_at][None, :], starts)
    same_y = slot_y[:, None] == slot_y[None, :]
    at_row = slot_row[None, :] == jnp.arange(rows_on, dtype=jnp.int32)[:, None]
    found = jnp.where(
        same_y[:, None, :] & at_row[None, :, :], jnp.arange(slots, dtype=jnp.int32), 0
    ).sum(axis=2)
    meta = jnp.concatenate(
        [(starts[:, :1] // block), (begins // block)[:, None], found.astype(jnp.int32)], axis=1
    )
    meta = jnp.concatenate([meta.reshape(-1), line[None].astype(jnp.int32)])
    info = jnp.stack([places, starts], axis=1)
    offsets = (places - starts).astype(jnp.float32).reshape(-1)
    phases = offsets[:, None] * jnp.tile(frequency, LANES // (HEAD_DIM // 2))[None, :]
    cosine, sine = (jnp.cos(phases), jnp.sin(phases))

    cot_parts = tokens_sent(late_cotangent)
    first_weight = gather_weight(jnp.concatenate([joint_mine, output_mine], axis=1))
    joint_width = joint_mine.shape[1]
    joint_weight, output_weight = (first_weight[:, :joint_width], first_weight[:, joint_width:])
    residual = residual_low.astype(jnp.float32)
    scale_one = lax.rsqrt(jnp.mean(residual * residual, axis=1, keepdims=True) + EPSILON)
    normed_parts = gather_tokens((residual * scale_one * gains[0]).astype(jnp.bfloat16))
    normed_parts, cot_parts = lax.optimization_barrier((normed_parts, cot_parts))
    cot_low = tokens_of(cot_parts)
    cot_chunks = gather_tokens(cot_low)
    queries, pair = project(normed_parts, first_weight, joint_width, cosine, sine, query_width)
    pairs = lax.all_gather(pair.reshape(slots, block, 2 * LANES), "col", axis=0, tiled=False)
    pairs, cot_chunks, gateup_mine, down_mine, meta, info = lax.optimization_barrier(
        (pairs, cot_chunks, gateup_mine, down_mine, meta, info)
    )
    gateup_weight = gather_weight(gateup_mine)
    down_weight = gather_weight(down_mine)
    mixed, logs = attend(meta, queries, pairs, info, rows_on)
    attn_sum = reduce_tokens(product(mixed, output_weight))
    middle = residual + attn_sum
    scale_two = lax.rsqrt(jnp.mean(middle * middle, axis=1, keepdims=True) + EPSILON)
    two_parts = gather_tokens((middle * scale_two * gains[1]).astype(jnp.bfloat16))
    hidden, factor, silu_gate = widen(two_parts, gateup_weight)
    normed_two, cot = (jnp.concatenate(two_parts, axis=0), jnp.concatenate(cot_chunks, axis=0))

    def other_half(rows, grad):
        rows = lax.dynamic_slice_in_dim(rows, (1 - core) * (D // 2), D // 2, 1)
        return dot_tn(rows, grad).astype(jnp.bfloat16)

    def own_half(rows, grad, received):
        rows = lax.dynamic_slice_in_dim(rows, core * (D // 2), D // 2, 1)
        total = dot_tn(rows, grad) + received.astype(jnp.float32)
        return total.astype(jnp.bfloat16)

    def scatter(total):
        return lax.psum_scatter(total, "col", scatter_dimension=0, tiled=True)

    def collect(piece):
        near_y = other_y(piece)
        return [piece, near_y, other_core(piece), other_core(near_y)]

    down_total = own_half(cot, hidden, other_core(other_half(cot, hidden)))
    down_total, down_weight = lax.optimization_barrier((down_total, down_weight))
    down_piece = scatter(down_total)
    work = {}

    def feed_back(first, last):
        work["grad_gate"], work["grad_up"], partial = widen_back(
            cot_chunks[first:last],
            down_weight,
            gateup_weight,
            factor,
            silu_gate,
            first,
            [work[name] for name in ("grad_gate", "grad_up") if name in work],
        )
        return partial

    def feed_others(key):
        gate, up = (work["grad_gate"], work["grad_up"])
        key, work["down_piece"], gate_other, up_other = lax.optimization_barrier(
            (key, down_piece, other_half(normed_two, gate), other_half(normed_two, up))
        )
        work["feed"] = (normed_two, gate, up, other_core(gate_other), other_core(up_other))
        return key

    def feed_owns(first):
        rows, gate, up, gate_other, up_other = work["feed"]
        gate_total = own_half(rows, gate, gate_other)
        first, gate_total, rows, up, up_other = lax.optimization_barrier(
            (first, gate_total, rows, up, up_other)
        )
        work["totals"] = (gate_total, own_half(rows, up, up_other))
        return first

    grad_normed_two = reduce_tokens(feed_back, feed_others, feed_owns)
    gate_piece, up_piece = [scatter(total) for total in work["totals"]]

    def norm_back(values, scale, grad_normed, gain):
        scaled = grad_normed * gain
        total = jnp.sum(scaled * values, axis=1, keepdims=True)
        return scale * scaled - values * (scale**3 * total / D)

    grad_middle = cot_low.astype(jnp.float32) + norm_back(
        middle, scale_two, grad_normed_two, gains[1]
    )
    gain_two = jnp.sum(grad_normed_two * middle * scale_two, axis=0)

    grad_middle_low, late_hidden = lax.optimization_barrier(
        (grad_middle.astype(jnp.bfloat16), hidden)
    )
    gate_total, up_total = work["totals"]
    back = jnp.concatenate(gather_tokens(grad_middle_low, (gate_total, up_total)), axis=0)

    meta_core = jnp.stack([y, core]).astype(jnp.int32)

    def back_here(products):
        products, work["back"] = lax.optimization_barrier((products, back))
        return products

    def attention_back(far):
        here = work.get("back", back)
        grad_query, grad_parts = attend_back(
            meta,
            queries,
            pairs,
            dot_nn(here, output_weight).astype(jnp.bfloat16),
            mixed,
            logs,
            info,
            cosine,
            sine,
            rows_on,
        )
        work["grad_parts"] = [grad_parts[0]] + [
            shift(grad_parts[by], "col", lines, -by) for by in range(1, lines)
        ]
        names = ("grad_query", "gate_piece", "back", "mixed")
        far, *values = lax.optimization_barrier((far, grad_query, gate_piece, here, mixed))
        work.update(zip(names, values))
        return far

    def keys_arrive(first):
        first, work["grad_parts"], work["up_piece"] = lax.optimization_barrier(
            (first, work["grad_parts"], up_piece)
        )
        return first

    if rows_on == 2:
        ffn_sum = reduce_tokens(
            product(late_hidden, down_weight), None, keys_arrive, attention_back, back_here
        )
    else:
        ffn_sum = keys_arrive(attention_back(reduce_tokens(product(late_hidden, down_weight))))
    grad_query, gate_piece, back, mixed = [
        work[name] for name in ("grad_query", "gate_piece", "back", "mixed")
    ]
    output_parts = features_sent((middle + ffn_sum).astype(jnp.bfloat16))
    grad_keyvalue = pair_back(work["grad_parts"], cosine, sine, block)
    grad_joint = jnp.concatenate([grad_query, grad_keyvalue], axis=1)
    normed_one = jnp.concatenate(normed_parts, axis=0)

    def joint_products(first, last):
        if first:
            return product(grad_joint, joint_weight)(first, last)
        output_total = own_half(back, mixed, other_core(other_half(back, mixed)))
        shards = collect(jnp.concatenate([work["down_piece"], work["gate_piece"]], axis=0))
        names = ("output", "shards", "up_shards")
        close, *values = lax.optimization_barrier(
            (
                product(grad_joint, joint_weight)(first, last),
                output_total,
                shards,
                collect(work["up_piece"]),
            )
        )
        work.update(zip(names, values))
        return close

    def joint_others(key):
        key, other = lax.optimization_barrier((key, other_half(normed_one, grad_joint)))
        work["joint"] = (normed_one, grad_joint, other_core(other))
        work["output_piece"] = scatter(work["output"])
        return key

    def joint_owns(first):
        down_new = turned_update(
            meta_core,
            work["shards"],
            [w_down, down_moment, down_square],
            FF ** (-0.5),
            False,
        )
        names = ("output_piece", "down_new", "up_shards")
        first, rows, grad, other, *values = lax.optimization_barrier(
            (
                first,
                *work["joint"],
                work["output_piece"],
                down_new,
                work["up_shards"],
            )
        )
        work.update(zip(names, values))
        work["joint_total"] = own_half(rows, grad, other)
        return first

    grad_normed_one = reduce_tokens(joint_products, joint_others, joint_owns)
    joint_piece = scatter(work["joint_total"])
    gateup_new = gateup_update(
        meta_core,
        work["shards"],
        work["up_shards"],
        [w_gateup, gateup_moment, gateup_square],
        32,
    )
    input_grad = grad_middle + norm_back(residual, scale_one, grad_normed_one, gains[0])
    gain_one = jnp.sum(grad_normed_one * residual * scale_one, axis=0)
    gain_sums = jnp.stack([gain_one, gain_two])
    gain_blocks = [
        jnp.concatenate(
            [
                gain_sums[:, at * half : (at + 1) * half],
                gain_sums[:, D // 2 + at * half : D // 2 + (at + 1) * half],
            ],
            axis=1,
        )
        for at in range(lines)
    ]
    gain_parts = [pick(gain_blocks, line)] + [
        shift(pick(gain_blocks, (line + by) % lines), "col", lines, by) for by in range(1, lines)
    ]
    joint_piece, input_grad, gateup_new, output_parts, gain_parts = lax.optimization_barrier(
        (joint_piece, input_grad.astype(jnp.bfloat16), gateup_new, output_parts, gain_parts)
    )
    grad_gains = sum(gain_parts[1:], gain_parts[0])
    for axis, size in (("core", 2), ("y", 2), ("row", rows_on)):
        own_gains = grad_gains
        for by in range(1, size):
            grad_gains = grad_gains + shift(own_gains, axis, size, by)
    input_parts = features_sent(input_grad)
    layer_output = features_of(output_parts)
    input_grad = features_of(input_parts).astype(jnp.float32)
    pair_piece = joint_piece[:, query_width:]
    pair_total = pair_piece.astype(jnp.float32)
    for by in range(1, rows_on):
        pair_total = pair_total + shift(pair_piece, "row", rows_on, by).astype(jnp.float32)
    joint_piece = jnp.concatenate(
        [joint_piece[:, :query_width], pair_total.astype(jnp.bfloat16)], axis=1
    )
    joint_new = joint_update(
        meta_core,
        collect(joint_piece),
        [w_query, query_moment, query_square],
        [w_keyvalue, keyvalue_moment, keyvalue_square],
    )
    output_new = turned_update(
        meta_core,
        collect(work["output_piece"]),
        [w_output, output_moment, output_square],
        (HEADS * HEAD_DIM // 64) ** (-0.5),
        True,
    )

    gains_new = adamw_step(norm_gains, grad_gains, gains_moment, gains_square, 0.6, 0.0)
    return (
        layer_output,
        input_grad,
        *gains_new,
        *joint_new,
        *output_new,
        *gateup_new,
        *work["down_new"],
    )


def solution(mesh):
    dp, rows_on, lines = (mesh.shape["dp"], mesh.shape["row"], mesh.shape["col"])
    split = Mesh(mesh.devices.reshape(dp // 2, 2, rows_on, lines), ("y", "core", "row", "col"))
    tokens = P(("y", "core", "row"), "col")
    narrow, wide = (P("col", "row"), P("row", "col"))
    gains, pair, gateup = (P(None, "col"), P("col", None), P("col", None, "row"))
    return jax.shard_map(
        functools.partial(on_device, (rows_on, lines)),
        mesh=split,
        in_specs=(
            tokens,
            tokens,
            P(("y", "core"), None),
            gains,
            narrow,
            pair,
            wide,
            gateup,
            wide,
            gains,
            gains,
            narrow,
            narrow,
            pair,
            pair,
            wide,
            wide,
            gateup,
            gateup,
            wide,
            wide,
        ),
        out_specs=(tokens, tokens)
        + (gains,) * 3
        + (narrow,) * 3
        + (pair,) * 3
        + (wide,) * 3
        + (gateup,) * 3
        + (wide,) * 3,
        check_vma=False,
    )
```

```python
import functools

import jax
import jax.numpy as jnp
from jax import lax
from jax.experimental import pallas as pl
from jax.experimental.pallas import tpu as pltpu
from jax.sharding import Mesh, PartitionSpec as P

D = 2048
HEADS = 32
KV_HEADS = 4
HEAD_DIM = 64
FF = 5632
STEP = 10

EPSILON = 1e-05
BETA_ONE = 0.9
BETA_TWO = 0.999
ADAM_EPS = 1e-08
MASKED = -1e30
SCORE_SCALE = HEAD_DIM ** (-0.5)
LANES = 128
VMEM_LIMIT = 48 * 1024 * 1024


def dot_nn(left, right):
    return lax.dot_general(left, right, (((1,), (0,)), ((), ())), preferred_element_type=jnp.float32)


def dot_nt(left, right):
    return lax.dot_general(left, right, (((1,), (1,)), ((), ())), preferred_element_type=jnp.float32)


def dot_tn(left, right):
    return lax.dot_general(left, right, (((0,), (0,)), ((), ())), preferred_element_type=jnp.float32)


def adamw_step(weight, gradient, moment, square, step_rate, decay_rate):
    moment_new = BETA_ONE * moment + (1.0 - BETA_ONE) * gradient
    square_new = BETA_TWO * square + (1.0 - BETA_TWO) * gradient * gradient
    fixed_one = moment_new / (1.0 - BETA_ONE**STEP)
    fixed_two = square_new / (1.0 - BETA_TWO**STEP)
    weight_new = weight - step_rate * (
        fixed_one / (jnp.sqrt(fixed_two) + ADAM_EPS) + decay_rate * weight
    )
    return (moment_new, square_new, weight_new)


def document_starts(segment_ids):
    places = jnp.arange(segment_ids.shape[0], dtype=jnp.int32)
    starts = jnp.concatenate([jnp.ones((1,), jnp.bool_), segment_ids[1:] != segment_ids[:-1]])
    return lax.cummax(jnp.where(starts, places, 0), axis=0)


def turn(values):
    lane = lax.broadcasted_iota(jnp.int32, values.shape, 1)
    ahead = pltpu.roll(values, LANES - HEAD_DIM // 2, 1)
    behind = pltpu.roll(values, HEAD_DIM // 2, 1)
    return jnp.where(lane % HEAD_DIM < HEAD_DIM // 2, -ahead, behind)


def take_chunk(rows_refs, held_ref):
    for at, ref in enumerate(rows_refs):

        @pl.when(pl.program_id(0) == at)
        def _(ref=ref):
            held_ref[...] = ref[...]


def project_kernel(slots, *refs):
    rows_refs, (weight_ref, cos_ref, sin_ref, query_ref, pair_ref, held_ref) = (refs[:slots], refs[slots:])
    take_chunk(rows_refs, held_ref)
    sums = dot_nn(held_ref[...], weight_ref[...])
    cosine, sine = cos_ref[...], sin_ref[...]
    width = query_ref.shape[1]
    lane = lax.broadcasted_iota(jnp.int32, cosine.shape, 1)
    for start in range(0, width, LANES):
        part = sums[:, start : start + LANES]
        turned = (part * cosine + turn(part) * sine).astype(jnp.bfloat16)
        query_ref[:, start : start + LANES] = turned * jnp.bfloat16(SCORE_SCALE)
    for which in range(2):
        part = sums[:, width + which * LANES : width + (which + 1) * LANES]
        is_key = (lane < HEAD_DIM) if which == 0 else (lane >= HEAD_DIM)
        turned = jnp.where(is_key, part * cosine + turn(part) * sine, part)
        pair_ref[:, which * LANES : (which + 1) * LANES] = turned.astype(jnp.bfloat16)


def project(chunks, weight, total, cosine, sine, width):
    slots = len(chunks)
    block, depth = chunks[0].shape
    rows = slots * block
    whole = pl.BlockSpec((block, depth), lambda i: (0, 0))
    return pl.pallas_call(
        functools.partial(project_kernel, slots),
        grid=(slots,),
        in_specs=[whole] * slots
        + [
            pl.BlockSpec((depth, total), lambda i: (0, 0)),
            pl.BlockSpec((block, LANES), lambda i: (i, 0)),
            pl.BlockSpec((block, LANES), lambda i: (i, 0)),
        ],
        out_specs=[
            pl.BlockSpec((block, width), lambda i: (i, 0)),
            pl.BlockSpec((block, total - width), lambda i: (i, 0)),
        ],
        out_shape=[
            jax.ShapeDtypeStruct((rows, width), jnp.bfloat16),
            jax.ShapeDtypeStruct((rows, total - width), jnp.bfloat16),
        ],
        scratch_shapes=[pltpu.VMEM((block, depth), jnp.bfloat16)],
        compiler_params=pltpu.CompilerParams(vmem_limit_bytes=VMEM_LIMIT),
        cost_estimate=pl.CostEstimate(
            flops=2 * rows * depth * total,
            bytes_accessed=(rows + total) * depth * 2,
            transcendentals=0,
        ),
        name="project",
    )(*chunks, weight, cosine, sine)


def widen_kernel(slots, *refs):
    rows_refs, (weight_ref, hidden_ref, factor_ref, silu_ref, held_ref) = (refs[:slots], refs[slots:])
    take_chunk(rows_refs, held_ref)
    sums = dot_nn(held_ref[...], weight_ref[...])
    width = hidden_ref.shape[1]
    gate, upward = (sums[:, :width], sums[:, width:])
    sigmoid = jax.nn.sigmoid(gate)
    silu = gate * sigmoid
    hidden_ref[...] = (silu * upward).astype(jnp.bfloat16)
    factor_ref[...] = (upward * sigmoid * (1.0 + gate * (1.0 - sigmoid))).astype(jnp.bfloat16)
    silu_ref[...] = silu.astype(jnp.bfloat16)


def widen(chunks, weight):
    slots = len(chunks)
    block, depth = chunks[0].shape
    width = weight.shape[1] // 2
    rows = slots * block
    once = pl.Buffered(1)
    return pl.pallas_call(
        functools.partial(widen_kernel, slots),
        grid=(slots,),
        in_specs=[pl.BlockSpec((block, depth), lambda i: (0, 0), pipeline_mode=once)] * slots
        + [pl.BlockSpec(weight.shape, lambda i: (0, 0), pipeline_mode=once)],
        out_specs=[pl.BlockSpec((block, width), lambda i: (i, 0))] * 3,
        out_shape=[jax.ShapeDtypeStruct((rows, width), jnp.bfloat16)] * 3,
        scratch_shapes=[pltpu.VMEM((block, depth), jnp.bfloat16)],
        compiler_params=pltpu.CompilerParams(vmem_limit_bytes=VMEM_LIMIT),
        cost_estimate=pl.CostEstimate(
            flops=4 * rows * depth * width,
            bytes_accessed=(rows + 2 * width) * depth * 2 + 6 * rows * width,
            transcendentals=rows * width,
        ),
        name="widen",
    )(*chunks, weight)


def widen_back_kernel(slots, kept, *refs):
    rows_refs, refs = (refs[:slots], refs[slots:])
    down_ref, gateup_ref, factor_ref, silu_ref = refs[:4]
    gate_ref, up_ref, partial_ref, held_ref = refs[4 + kept :]
    take_chunk(rows_refs, held_ref)
    grad_hidden = dot_nn(held_ref[...], down_ref[...])
    gate = (grad_hidden * factor_ref[...].astype(jnp.float32)).astype(jnp.bfloat16)
    up = (grad_hidden * silu_ref[...].astype(jnp.float32)).astype(jnp.bfloat16)
    gate_ref[...] = gate
    up_ref[...] = up
    both = jnp.concatenate([gate, up], axis=1)
    partial_ref[...] = dot_nt(both, gateup_ref[...]).astype(jnp.bfloat16)


def widen_back(chunks, down, gateup, factor, silu, first, kept):
    slots = len(chunks)
    block, depth = chunks[0].shape
    width = down.shape[1]
    once = pl.Buffered(1)
    tile = pl.BlockSpec((block, width), lambda i: (first + i, 0))
    return pl.pallas_call(
        functools.partial(widen_back_kernel, slots, len(kept)),
        grid=(slots,),
        in_specs=[pl.BlockSpec((block, depth), lambda i: (0, 0), pipeline_mode=once)] * slots
        + [
            pl.BlockSpec(down.shape, lambda i: (0, 0), pipeline_mode=once),
            pl.BlockSpec(gateup.shape, lambda i: (0, 0), pipeline_mode=once),
            tile,
            tile,
        ]
        + [pl.BlockSpec(memory_space=pl.ANY)] * len(kept),
        out_specs=[tile, tile, pl.BlockSpec((block, depth), lambda i: (i, 0))],
        out_shape=[jax.ShapeDtypeStruct(factor.shape, jnp.bfloat16)] * 2
        + [jax.ShapeDtypeStruct((slots * block, depth), jnp.bfloat16)],
        scratch_shapes=[pltpu.VMEM((block, depth), jnp.bfloat16)],
        input_output_aliases={slots + 4 + i: i for i in range(len(kept))},
        compiler_params=pltpu.CompilerParams(vmem_limit_bytes=VMEM_LIMIT),
        cost_estimate=pl.CostEstimate(
            flops=slots * block * depth * width,
            bytes_accessed=8 * slots * block * width,
            transcendentals=0,
        ),
        name="widen_back",
    )(*chunks, down, gateup, factor, silu, *kept)


def stack_heads(values):
    return jnp.concatenate(
        [values[:, start : start + LANES] for start in range(0, values.shape[1], LANES)], axis=0
    )


def block_of(meta_ref, chunk, step, parts, lines):
    base = chunk * (2 + parts)
    key_block = meta_ref[base + 1] - step
    slot = meta_ref[base + 2 + key_block // lines]
    own_line = meta_ref[pl.num_programs(0) * (2 + parts)]
    line = lax.rem(key_block, lines)
    return (key_block, slot, line, lax.rem(own_line - line + lines, lines))


def attend_kernel(parts, lines, meta_ref, query_ref, pair_ref, info_ref, out_ref, log_ref):
    chunk = pl.program_id(0)
    block = query_ref.shape[0]
    heads = query_ref.shape[1] // LANES
    stacked = stack_heads(query_ref[...])
    lane = lax.broadcasted_iota(jnp.int32, stacked.shape, 1)
    place = jnp.concatenate([info_ref[0, 0:1, :]] * heads, axis=1)
    start = jnp.concatenate([info_ref[0, 1:2, :]] * heads, axis=1)
    base = chunk * (2 + parts)
    steps = meta_ref[base + 1] - meta_ref[base] + 1
    width = heads * block
    key_lanes = lane < HEAD_DIM
    queries = [
        jnp.where(key_lanes if which == 0 else ~key_lanes, stacked, jnp.zeros_like(stacked))
        for which in range(2)
    ]

    def body(step, carry):
        key_block, slot, at, _ = block_of(meta_ref, chunk, step, parts, lines)
        key_place = key_block * block + lax.broadcasted_iota(jnp.int32, (block, width), 0)
        seen = (key_place <= place) & (key_place >= start)
        result = []
        for which in range(2):
            peak, total, mixed = carry[which]
            pair = pair_ref[at, slot, :, which * LANES : (which + 1) * LANES]
            scores = jnp.where(seen, dot_nt(pair, queries[which]), MASKED)
            new_peak = jnp.maximum(peak, jnp.max(scores, axis=0, keepdims=True))
            weights = jnp.exp(scores - new_peak)
            shrink = jnp.exp(peak - new_peak)
            total = total * shrink + jnp.sum(weights, axis=0, keepdims=True)
            mixed = mixed * shrink + dot_tn(pair, weights.astype(jnp.bfloat16))
            result.append((new_peak, total, mixed))
        return tuple(result)

    empty = (
        jnp.full((1, width), MASKED, jnp.float32),
        jnp.zeros((1, width), jnp.float32),
        jnp.zeros((LANES, width), jnp.float32),
    )
    outs = []
    for which, (peak, total, mixed) in enumerate(lax.fori_loop(0, steps, body, (empty, empty))):
        log_ref[0, which : which + 1, :] = peak + jnp.log(total)
        outs.append(mixed / total)
    joined = jnp.concatenate([outs[1][:HEAD_DIM], outs[0][HEAD_DIM:]], axis=0)
    rows = joined.T.astype(jnp.bfloat16)
    for head in range(heads):
        out_ref[:, head * LANES : (head + 1) * LANES] = rows[head * block : (head + 1) * block]


def attend(meta, queries, pairs, info, parts):
    chunks, block = (info.shape[0], info.shape[2])
    width = queries.shape[1]
    heads = width // LANES
    lines = pairs.shape[0]
    steps = 3 * chunks
    return pl.pallas_call(
        functools.partial(attend_kernel, parts, lines),
        grid_spec=pltpu.PrefetchScalarGridSpec(
            num_scalar_prefetch=1,
            grid=(chunks,),
            in_specs=[
                pl.BlockSpec((block, width), lambda i, m: (i, 0)),
                pl.BlockSpec(pairs.shape, lambda i, m: (0, 0, 0, 0)),
                pl.BlockSpec((1, 2, block), lambda i, m: (i, 0, 0)),
            ],
            out_specs=[
                pl.BlockSpec((block, width), lambda i, m: (i, 0)),
                pl.BlockSpec((1, 2, heads * block), lambda i, m: (i, 0, 0)),
            ],
        ),
        out_shape=[
            jax.ShapeDtypeStruct(queries.shape, jnp.bfloat16),
            jax.ShapeDtypeStruct((chunks, 2, heads * block), jnp.float32),
        ],
        compiler_params=pltpu.CompilerParams(vmem_limit_bytes=VMEM_LIMIT),
        cost_estimate=pl.CostEstimate(
            flops=steps * 2 * 2 * 2 * heads * block * block * LANES,
            bytes_accessed=queries.size * 4 + pairs.size * 2,
            transcendentals=steps * 2 * heads * block * block,
        ),
        name="attend",
    )(meta, queries, pairs, info)


def attend_back_kernel(parts, lines, meta_ref, query_ref, *refs):
    pair_ref, grad_ref, mixed_ref, log_ref, info_ref, cos_ref, sin_ref, query_out = refs[:8]
    pair_outs = refs[8 : 8 + lines]
    sums = refs[8 + lines]
    chunk = pl.program_id(0)
    block = query_ref.shape[0]
    heads = query_ref.shape[1] // LANES

    @pl.when(chunk == 0)
    def _():
        sums[...] = jnp.zeros_like(sums)

    stacked = stack_heads(query_ref[...])
    stacked_grad = stack_heads(grad_ref[...])
    product = stacked_grad.astype(jnp.float32) * stack_heads(mixed_ref[...]).astype(jnp.float32)
    lane = lax.broadcasted_iota(jnp.int32, stacked.shape, 1)
    place = jnp.concatenate([info_ref[0, 0:1, :]] * heads, axis=1)
    start = jnp.concatenate([info_ref[0, 1:2, :]] * heads, axis=1)
    base = chunk * (2 + parts)
    steps = meta_ref[base + 1] - meta_ref[base] + 1
    width = heads * block
    key_lanes = lane < HEAD_DIM
    queries, grad, centre, logs = ([], [], [], [])
    for which in range(2):
        is_key = key_lanes if which == 0 else ~key_lanes
        queries.append(jnp.where(is_key, stacked, jnp.zeros_like(stacked)))
        grad.append(jnp.where(is_key, jnp.zeros_like(stacked_grad), stacked_grad))
        own = jnp.where(is_key, 0.0, product)
        centre.append(
            lax.dot_general(
                jnp.ones((8, LANES), jnp.float32),
                own,
                (((1,), (1,)), ((), ())),
                precision=lax.Precision.HIGHEST,
                preferred_element_type=jnp.float32,
            )[0:1]
        )
        logs.append(log_ref[0, which : which + 1, :])

    def body(step, carry):
        key_block, slot, at, shift = block_of(meta_ref, chunk, step, parts, lines)
        key_place = key_block * block + lax.broadcasted_iota(jnp.int32, (block, width), 0)
        seen = (key_place <= place) & (key_place >= start)
        result = []
        for which in range(2):
            columns = slice(which * LANES, (which + 1) * LANES)
            pair = pair_ref[at, slot, :, columns]
            scores = jnp.where(seen, dot_nt(pair, queries[which]), MASKED)
            weights = jnp.exp(scores - logs[which])
            grad_weights = dot_nt(pair, grad[which]) - centre[which]
            grad_scores = (weights * grad_weights).astype(jnp.bfloat16)
            sums[shift, slot, :, columns] += dot_nn(grad_scores, queries[which]) + dot_nn(
                weights.astype(jnp.bfloat16), grad[which]
            )
            result.append(carry[which] + dot_tn(pair, grad_scores))
        return tuple(result)

    empty = jnp.zeros((LANES, width), jnp.float32)
    grads = lax.fori_loop(0, steps, body, (empty, empty))
    joined = jnp.concatenate([grads[0][:HEAD_DIM], grads[1][HEAD_DIM:]], axis=0)
    rows = joined.T * SCORE_SCALE
    cosine, sine = cos_ref[...], sin_ref[...]
    for head in range(heads):
        part = rows[head * block : (head + 1) * block]
        back = part * cosine - turn(part) * sine
        query_out[:, head * LANES : (head + 1) * LANES] = back.astype(jnp.bfloat16)

    @pl.when(chunk == pl.num_programs(0) - 1)
    def _():
        for line in range(lines):
            pair_outs[line][...] = sums[line].astype(jnp.bfloat16)


def attend_back(meta, queries, pairs, grad_mixed, mixed, logs, info, cosine, sine, parts):
    chunks, block = (info.shape[0], info.shape[2])
    width = queries.shape[1]
    heads = width // LANES
    lines = pairs.shape[0]
    shape = pairs.shape[1:]
    steps = 3 * chunks
    wide = pl.BlockSpec((block, width), lambda i, m: (i, 0))
    table = pl.BlockSpec((block, LANES), lambda i, m: (i, 0))
    whole = pl.BlockSpec(shape, lambda i, m: (0, 0, 0))
    outs = pl.pallas_call(
        functools.partial(attend_back_kernel, parts, lines),
        grid_spec=pltpu.PrefetchScalarGridSpec(
            num_scalar_prefetch=1,
            grid=(chunks,),
            in_specs=[
                wide,
                pl.BlockSpec(pairs.shape, lambda i, m: (0, 0, 0, 0)),
                wide,
                wide,
                pl.BlockSpec((1, 2, heads * block), lambda i, m: (i, 0, 0)),
                pl.BlockSpec((1, 2, block), lambda i, m: (i, 0, 0)),
                table,
                table,
            ],
            out_specs=[wide] + [whole] * lines,
            scratch_shapes=[pltpu.VMEM(pairs.shape, jnp.float32)],
        ),
        out_shape=[jax.ShapeDtypeStruct(queries.shape, jnp.bfloat16)]
        + [jax.ShapeDtypeStruct(shape, jnp.bfloat16)] * lines,
        compiler_params=pltpu.CompilerParams(vmem_limit_bytes=VMEM_LIMIT),
        cost_estimate=pl.CostEstimate(
            flops=steps * 2 * 5 * 2 * heads * block * block * LANES,
            bytes_accessed=queries.size * 8 + 2 * pairs.size * 2,
            transcendentals=steps * 2 * heads * block * block,
        ),
        name="attend_back",
    )(
        meta,
        queries,
        pairs,
        grad_mixed,
        mixed,
        logs,
        info,
        cosine,
        sine,
    )
    return (outs[0], [out.reshape(chunks * block, 2 * LANES) for out in outs[1:]])


def pair_back_kernel(*refs):
    *part_refs, cos_ref, sin_ref, out_ref = refs
    cosine, sine = cos_ref[...], sin_ref[...]
    lane = lax.broadcasted_iota(jnp.int32, cosine.shape, 1)
    for which in range(2):
        columns = slice(which * LANES, (which + 1) * LANES)
        total = part_refs[0][:, columns].astype(jnp.float32)
        for ref in part_refs[1:]:
            total = total + ref[:, columns].astype(jnp.float32)
        is_key = (lane < HEAD_DIM) if which == 0 else (lane >= HEAD_DIM)
        total = jnp.where(is_key, total * cosine - turn(total) * sine, total)
        out_ref[:, columns] = total.astype(jnp.bfloat16)


def pair_back(parts, cosine, sine, block):
    rows, columns = parts[0].shape
    tile = pl.BlockSpec((block, columns), lambda i: (i, 0))
    table = pl.BlockSpec((block, LANES), lambda i: (i, 0))
    return pl.pallas_call(
        pair_back_kernel,
        grid=(rows // block,),
        in_specs=[tile] * len(parts) + [table, table],
        out_specs=tile,
        out_shape=jax.ShapeDtypeStruct((rows, columns), jnp.bfloat16),
        compiler_params=pltpu.CompilerParams(vmem_limit_bytes=VMEM_LIMIT),
        name="pair_back",
    )(*parts, cosine, sine)


def update(refs, index, gradient, rate):
    weight, moment, square = [ref[index] for ref in refs[:3]]
    moment_new, square_new, weight_new = adamw_step(weight, gradient, moment, square, rate, 0.1)
    for ref, value in zip(refs[3:], (moment_new, square_new, weight_new)):
        ref[index] = value


def chosen(meta_ref, grad_refs, at, rows, columns):
    own_y = meta_ref[0] == at
    first = pl.program_id(0) == 0
    near = jnp.where(first, grad_refs[0][rows, columns], grad_refs[2][rows, columns])
    far = jnp.where(first, grad_refs[1][rows, columns], grad_refs[3][rows, columns])
    return jnp.where(own_y, near, far).astype(jnp.float32)


def joint_update_kernel(meta_ref, *refs):
    grad_refs, query_refs, pair_refs = (refs[:4], refs[4:7] + refs[10:13], refs[7:10] + refs[13:16])
    groups = query_refs[0].shape[1] // (2 * LANES)
    every = slice(None)
    for at in range(2):
        for j in range(groups):
            gradient = chosen(meta_ref, grad_refs, at, every, slice(j * LANES, (j + 1) * LANES))
            place = slice((2 * j + at) * LANES, (2 * j + at + 1) * LANES)
            update(query_refs, (every, place), gradient, D ** (-0.5))
        for which in range(2):
            start = (groups + which) * LANES
            gradient = chosen(meta_ref, grad_refs, at, every, slice(start, start + LANES))
            if which == 1:
                gradient = pltpu.roll(gradient, HEAD_DIM, 1)
            place = slice((2 * at + which) * LANES, (2 * at + which + 1) * LANES)
            update(pair_refs, (every, place), gradient, D ** (-0.5))


def joint_update(meta, grads, query, pair):
    half = grads[0].shape[0]

    def rows_of(array):
        return pl.BlockSpec((half, array.shape[1]), lambda i, m: ((m[1] + i) % 2, 0))

    whole = pl.BlockSpec(grads[0].shape, lambda i, m: (0, 0))
    blocks = [rows_of(array) for array in (*query, *pair)]
    return pl.pallas_call(
        joint_update_kernel,
        grid_spec=pltpu.PrefetchScalarGridSpec(
            num_scalar_prefetch=1, grid=(2,), in_specs=[whole] * 4 + blocks, out_specs=blocks
        ),
        out_shape=[jax.ShapeDtypeStruct(array.shape, array.dtype) for array in (*query, *pair)],
        compiler_params=pltpu.CompilerParams(vmem_limit_bytes=VMEM_LIMIT),
        cost_estimate=pl.CostEstimate(
            flops=20 * (query[0].size + pair[0].size),
            bytes_accessed=24 * (query[0].size + pair[0].size),
            transcendentals=0,
        ),
        name="joint_update",
    )(meta, *grads, *query, *pair)


def turned_update_kernel(rate, swapped, meta_ref, *refs):
    grad_refs, weight_refs = (refs[:4], refs[4:10])
    at = pl.program_id(1)
    width = grad_refs[0].shape[1]
    every = slice(None)
    for j, start in enumerate(range(0, width, LANES)):
        strip = slice(start, min(start + LANES, width))
        gradient = chosen(meta_ref, grad_refs, at, every, strip).T
        if swapped:
            gradient = jnp.concatenate([gradient[HEAD_DIM:], gradient[:HEAD_DIM]], axis=0)
            index = (j, 0)
        else:
            index = (strip, every)
        update(weight_refs, index, gradient, rate)


def turned_update(meta, grads, weights, rate, swapped):
    shape = weights[0].shape
    half, width = (shape[1] // 2, grads[0].shape[1])
    if swapped:
        weights = [w.reshape(width // LANES, 2, LANES, shape[1]) for w in weights]
        block = pl.BlockSpec(
            (width // LANES, 1, LANES, half), lambda i, at, m: (0, at, 0, (m[1] + i) % 2)
        )
    else:
        block = pl.BlockSpec((width, half), lambda i, at, m: (at, (m[1] + i) % 2))
    outs = pl.pallas_call(
        functools.partial(turned_update_kernel, rate, swapped),
        grid_spec=pltpu.PrefetchScalarGridSpec(
            num_scalar_prefetch=1,
            grid=(2, 2),
            in_specs=[pl.BlockSpec((half, width), lambda i, at, m: (0, 0))] * 4 + [block] * 3,
            out_specs=[block] * 3,
        ),
        out_shape=[jax.ShapeDtypeStruct(weights[0].shape, jnp.float32)] * 3,
        compiler_params=pltpu.CompilerParams(vmem_limit_bytes=VMEM_LIMIT),
        cost_estimate=pl.CostEstimate(
            flops=20 * weights[0].size, bytes_accessed=24 * weights[0].size, transcendentals=0
        ),
        name="turned_update",
    )(meta, *grads, *weights)
    return [out.reshape(shape) for out in outs]


def gateup_update_kernel(meta_ref, *refs):
    gate_refs, up_refs, weight_refs = (refs[:4], refs[4:8], refs[8:14])
    every = slice(None)
    gate, up = [
        jnp.concatenate([chosen(meta_ref, grads, at, every, every) for at in range(2)], axis=1)
        for grads in (gate_refs, up_refs)
    ]
    update(weight_refs, every, jnp.stack([gate, up], axis=1), D ** (-0.5))


def gateup_update(meta, gates, ups, weights, rows):
    half, width = ups[0].shape
    shape = weights[0].shape
    tiles = half // rows
    gate = pl.BlockSpec((rows, width), lambda i, j, m: (tiles + j, 0))
    up = pl.BlockSpec((rows, width), lambda i, j, m: (j, 0))
    block = pl.BlockSpec(
        (rows, 2, shape[2]), lambda i, j, m: (((m[1] + i) % 2) * tiles + j, 0, 0)
    )
    return pl.pallas_call(
        gateup_update_kernel,
        grid_spec=pltpu.PrefetchScalarGridSpec(
            num_scalar_prefetch=1,
            grid=(2, tiles),
            in_specs=[gate] * 4 + [up] * 4 + [block] * 3,
            out_specs=[block] * 3,
        ),
        out_shape=[jax.ShapeDtypeStruct(shape, jnp.float32)] * 3,
        compiler_params=pltpu.CompilerParams(vmem_limit_bytes=VMEM_LIMIT),
        cost_estimate=pl.CostEstimate(
            flops=20 * weights[0].size, bytes_accessed=4 * weights[0].size, transcendentals=0
        ),
        name="gateup_update",
    )(meta, *gates, *ups, *weights)


def on_device(
    sizes,
    block_input,
    cotangent,
    segments,
    norm_gains,
    w_query,
    w_keyvalue,
    w_output,
    w_gateup,
    w_down,
    gains_moment,
    gains_square,
    query_moment,
    query_square,
    keyvalue_moment,
    keyvalue_square,
    output_moment,
    output_square,
    gateup_moment,
    gateup_square,
    down_moment,
    down_square,
):
    rows_on, lines = sizes
    y, core, row, line = [lax.axis_index(name) for name in ("y", "core", "row", "col")]
    length = segments.shape[1]
    block = block_input.shape[0] // lines
    wide = block_input.shape[1]
    half = wide // 2
    slots = 2 * rows_on
    per_row = w_query.shape[1] // (KV_HEADS * HEAD_DIM)
    query_width = per_row * LANES
    hidden_here = w_gateup.shape[2] // 2

    def shift(value, axis, size, by):
        return lax.ppermute(value, axis, [(i, (i + by) % size) for i in range(size)])

    def other_core(value):
        return lax.ppermute(value, "core", [(0, 1), (1, 0)])

    def other_y(value):
        return lax.ppermute(value, "y", [(0, 1), (1, 0)])

    def place_of(y_at, core_at, row_at):
        return (y_at * 2 + core_at) * rows_on + row_at

    first_pairs, second_pairs = ([], [])
    for y_at in range(2):
        for core_at in range(2):
            for row_at in range(rows_on):
                over_row = (
                    place_of(y_at, core_at, row_at),
                    place_of(y_at, core_at, (row_at + 1) % rows_on),
                )
                over_y = (place_of(y_at, core_at, row_at), place_of(1 - y_at, core_at, row_at))
                first_pairs.append(over_row if core_at == 0 else over_y)
                second_pairs.append(over_y if core_at == 0 else over_row)
    near = ("y", "core", "row")

    def gather_tokens(own, beside=()):
        if rows_on == 2:
            first = lax.ppermute(own, near, first_pairs)
            second = lax.ppermute(own, near, second_pairs)
            first, second, *_ = lax.optimization_barrier((first, second, *beside))
            third = lax.ppermute(first, near, second_pairs)
            return [own, first, second, third]
        parts = [own] + [shift(own, "row", rows_on, by) for by in range(1, rows_on)]
        return parts + [other_y(part) for part in parts]

    def reduce_tokens(rows_of, middle=None, before_last=None, far_here=None, ready=None):
        def same(value):
            return value

        middle, before_last = (middle or same, before_last or same)
        if rows_on == 2:
            far = rows_of(2, 4)
            if ready:
                far, close = ready((far, rows_of(0, 2)))
            third = lax.ppermute(far[block:], near, second_pairs)
            second = lax.ppermute(far[:block], near, second_pairs)
            if not ready:
                close = rows_of(0, 2)
            third, second, close = (far_here or lax.optimization_barrier)((third, second, close))
            key = (close[block:].astype(jnp.float32) + third.astype(jnp.float32)).astype(jnp.bfloat16)
            first = before_last(lax.ppermute(middle(key), near, first_pairs))
            own = close[:block].astype(jnp.float32) + second.astype(jnp.float32)
            return own + first.astype(jnp.float32)
        partial = rows_of(0, slots)
        parts = [partial[i * block : (i + 1) * block] for i in range(slots)]
        sums = [
            parts[i].astype(jnp.float32) + other_y(parts[rows_on + i]).astype(jnp.float32)
            for i in range(rows_on)
        ]
        sums[0] = middle(sums[0])
        total = sums[0]
        for by in range(1, rows_on):
            moved = shift(sums[by].astype(jnp.bfloat16), "row", rows_on, -by)
            total = total + moved.astype(jnp.float32)
        return before_last(total)

    def product(left, right):
        def rows_of(first, last):
            return dot_nt(left[first * block : last * block], right).astype(jnp.bfloat16)

        return rows_of

    if rows_on == 2:
        slot_y = [y, jnp.where(core == 0, y, 1 - y), jnp.where(core == 0, 1 - y, y), 1 - y]
        slot_row = [row, jnp.where(core == 0, 1 - row, row), jnp.where(core == 0, row, 1 - row), 1 - row]
    else:
        slot_y = [y] * rows_on + [1 - y] * rows_on
        slot_row = [(row - by) % rows_on for by in range(rows_on)] * 2

    def pick(parts, index):
        return lax.dynamic_index_in_dim(jnp.stack(parts), index, 0, keepdims=False)

    def tokens_sent(values):
        parts = []
        for by in range(lines):
            part = lax.dynamic_slice_in_dim(values, ((line + by) % lines) * block, block, 0)
            parts.append(part if by == 0 else shift(part, "col", lines, by))
        return parts

    def tokens_of(parts):
        blocks = [pick(parts, (line - at) % lines) for at in range(lines)]
        return jnp.concatenate([b[:, :half] for b in blocks] + [b[:, half:] for b in blocks], axis=1)

    def features_sent(values):
        blocks = [
            jnp.concatenate(
                [
                    values[:, at * half : (at + 1) * half],
                    values[:, D // 2 + at * half : D // 2 + (at + 1) * half],
                ],
                axis=1,
            )
            for at in range(lines)
        ]
        parts = []
        for by in range(lines):
            part = pick(blocks, (line + by) % lines)
            parts.append(part if by == 0 else shift(part, "col", lines, by))
        return parts

    def features_of(parts):
        return jnp.concatenate([pick(parts, (line - at) % lines) for at in range(lines)], axis=0)

    def half_rows(values):
        return lax.dynamic_slice_in_dim(values, core * half, half, 0)

    def half_columns(values):
        return lax.dynamic_slice_in_dim(values, core * half, half, 1)

    def gather_weight(piece):
        return lax.all_gather(piece, ("core", "col"), axis=0, tiled=True)

    query_rows = half_rows(w_query).astype(jnp.bfloat16)
    pair_rows = half_rows(w_keyvalue).astype(jnp.bfloat16)

    def joint_of(at):
        pieces = [
            query_rows[:, (2 * j + at) * LANES : (2 * j + at + 1) * LANES] for j in range(per_row)
        ]
        pair = pair_rows[:, at * 2 * LANES : (at + 1) * 2 * LANES]
        pieces += [
            pair[:, :LANES],
            pair[:, LANES + HEAD_DIM :],
            pair[:, LANES : LANES + HEAD_DIM],
        ]
        return jnp.concatenate(pieces, axis=1)

    joint_mine = jnp.where(y == 0, joint_of(0), joint_of(1))
    output_columns = half_columns(w_output).astype(jnp.bfloat16)

    def output_of(at):
        pieces = []
        for j in range(per_row):
            base = (2 * j + at) * LANES
            pieces += [
                output_columns[base + HEAD_DIM : base + LANES],
                output_columns[base : base + HEAD_DIM],
            ]
        return jnp.concatenate(pieces, axis=0)

    output_mine = jnp.where(y == 0, output_of(0), output_of(1)).T
    gateup_mine = lax.dynamic_slice(
        w_gateup, (core * half, 0, y * hidden_here), (half, 2, hidden_here)
    ).astype(jnp.bfloat16)
    gateup_mine = jnp.concatenate([gateup_mine[:, 0], gateup_mine[:, 1]], axis=1)
    down_mine = lax.dynamic_slice(
        w_down, (y * hidden_here, core * half), (hidden_here, half)
    ).astype(jnp.bfloat16).T

    gain_parts = [norm_gains] + [shift(norm_gains, "col", lines, by) for by in range(1, lines)]
    gain_blocks = [pick(gain_parts, (line - at) % lines) for at in range(lines)]
    gains = jnp.concatenate(
        [b[:, :half] for b in gain_blocks] + [b[:, half:] for b in gain_blocks], axis=1
    )

    residual_low = tokens_of(tokens_sent(block_input))
    residual_low, late_cotangent, other_segments, joint_mine, output_mine = lax.optimization_barrier(
        (residual_low, cotangent, other_y(segments), joint_mine, output_mine)
    )

    own_starts = document_starts(segments[0])
    other_starts = document_starts(other_segments[0])
    frequency = 10000.0 ** (-2.0 * jnp.arange(HEAD_DIM // 2, dtype=jnp.float32) / HEAD_DIM)
    slot_y, slot_row = (jnp.stack(slot_y).astype(jnp.int32), jnp.stack(slot_row).astype(jnp.int32))
    begins = slot_row * (lines * block) + line * block
    places = begins[:, None] + jnp.arange(block, dtype=jnp.int32)[None, :]
    both_starts = jnp.stack([own_starts, other_starts]).reshape(2, rows_on, lines, block)
    both_starts = lax.dynamic_index_in_dim(both_starts, line, 2, keepdims=False)
    starts = jnp.zeros((slots, block), jnp.int32)
    for which in range(2):
        for row_at in range(rows_on):
            here = ((slot_y != y) == bool(which)) & (slot_row == row_at)
            starts = jnp.where(here[:, None], both_starts[which, row_at][None, :], starts)
    same_y = slot_y[:, None] == slot_y[None, :]
    at_row = slot_row[None, :] == jnp.arange(rows_on, dtype=jnp.int32)[:, None]
    found = jnp.where(
        same_y[:, None, :] & at_row[None, :, :], jnp.arange(slots, dtype=jnp.int32), 0
    ).sum(axis=2)
    meta = jnp.concatenate(
        [(starts[:, :1] // block), (begins // block)[:, None], found.astype(jnp.int32)], axis=1
    )
    meta = jnp.concatenate([meta.reshape(-1), line[None].astype(jnp.int32)])
    info = jnp.stack([places, starts], axis=1)
    offsets = (places - starts).astype(jnp.float32).reshape(-1)
    phases = offsets[:, None] * jnp.tile(frequency, LANES // (HEAD_DIM // 2))[None, :]
    cosine, sine = (jnp.cos(phases), jnp.sin(phases))

    cot_parts = tokens_sent(late_cotangent)
    first_weight = gather_weight(jnp.concatenate([joint_mine, output_mine], axis=1))
    joint_width = joint_mine.shape[1]
    joint_weight, output_weight = (first_weight[:, :joint_width], first_weight[:, joint_width:])
    residual = residual_low.astype(jnp.float32)
    scale_one = lax.rsqrt(jnp.mean(residual * residual, axis=1, keepdims=True) + EPSILON)
    normed_parts = gather_tokens((residual * scale_one * gains[0]).astype(jnp.bfloat16))
    normed_parts, cot_parts = lax.optimization_barrier((normed_parts, cot_parts))
    cot_low = tokens_of(cot_parts)
    cot_chunks = gather_tokens(cot_low)
    queries, pair = project(normed_parts, first_weight, joint_width, cosine, sine, query_width)
    pairs = lax.all_gather(pair.reshape(slots, block, 2 * LANES), "col", axis=0, tiled=False)
    pairs, cot_chunks, gateup_mine, down_mine, meta, info = lax.optimization_barrier(
        (pairs, cot_chunks, gateup_mine, down_mine, meta, info)
    )
    gateup_weight = gather_weight(gateup_mine)
    down_weight = gather_weight(down_mine)
    mixed, logs = attend(meta, queries, pairs, info, rows_on)
    attn_sum = reduce_tokens(product(mixed, output_weight))
    middle = residual + attn_sum
    scale_two = lax.rsqrt(jnp.mean(middle * middle, axis=1, keepdims=True) + EPSILON)
    two_parts = gather_tokens((middle * scale_two * gains[1]).astype(jnp.bfloat16))
    hidden, factor, silu_gate = widen(two_parts, gateup_weight)
    normed_two, cot = (jnp.concatenate(two_parts, axis=0), jnp.concatenate(cot_chunks, axis=0))

    def other_half(rows, grad):
        rows = lax.dynamic_slice_in_dim(rows, (1 - core) * (D // 2), D // 2, 1)
        return dot_tn(rows, grad).astype(jnp.bfloat16)

    def own_half(rows, grad, received):
        rows = lax.dynamic_slice_in_dim(rows, core * (D // 2), D // 2, 1)
        total = dot_tn(rows, grad) + received.astype(jnp.float32)
        return total.astype(jnp.bfloat16)

    def scatter(total):
        return lax.psum_scatter(total, "col", scatter_dimension=0, tiled=True)

    def collect(piece):
        near_y = other_y(piece)
        return [piece, near_y, other_core(piece), other_core(near_y)]

    down_total = own_half(cot, hidden, other_core(other_half(cot, hidden)))
    down_total, down_weight = lax.optimization_barrier((down_total, down_weight))
    down_piece = scatter(down_total)
    work = {}

    def feed_back(first, last):
        work["grad_gate"], work["grad_up"], partial = widen_back(
            cot_chunks[first:last],
            down_weight,
            gateup_weight,
            factor,
            silu_gate,
            first,
            [work[name] for name in ("grad_gate", "grad_up") if name in work],
        )
        return partial

    def feed_others(key):
        gate, up = (work["grad_gate"], work["grad_up"])
        key, work["down_piece"], gate_other, up_other = lax.optimization_barrier(
            (key, down_piece, other_half(normed_two, gate), other_half(normed_two, up))
        )
        work["feed"] = (normed_two, gate, up, other_core(gate_other), other_core(up_other))
        return key

    def feed_owns(first):
        rows, gate, up, gate_other, up_other = work["feed"]
        gate_total = own_half(rows, gate, gate_other)
        first, gate_total, rows, up, up_other = lax.optimization_barrier(
            (first, gate_total, rows, up, up_other)
        )
        work["totals"] = (gate_total, own_half(rows, up, up_other))
        return first

    grad_normed_two = reduce_tokens(feed_back, feed_others, feed_owns)
    gate_piece, up_piece = [scatter(total) for total in work["totals"]]

    def norm_back(values, scale, grad_normed, gain):
        scaled = grad_normed * gain
        total = jnp.sum(scaled * values, axis=1, keepdims=True)
        return scale * scaled - values * (scale**3 * total / D)

    grad_middle = cot_low.astype(jnp.float32) + norm_back(
        middle, scale_two, grad_normed_two, gains[1]
    )
    gain_two = jnp.sum(grad_normed_two * middle * scale_two, axis=0)

    grad_middle_low, late_hidden = lax.optimization_barrier(
        (grad_middle.astype(jnp.bfloat16), hidden)
    )
    gate_total, up_total = work["totals"]
    back = jnp.concatenate(gather_tokens(grad_middle_low, (gate_total, up_total)), axis=0)

    meta_core = jnp.stack([y, core]).astype(jnp.int32)

    def back_here(products):
        products, work["back"] = lax.optimization_barrier((products, back))
        return products

    def attention_back(far):
        here = work.get("back", back)
        grad_query, grad_parts = attend_back(
            meta,
            queries,
            pairs,
            dot_nn(here, output_weight).astype(jnp.bfloat16),
            mixed,
            logs,
            info,
            cosine,
            sine,
            rows_on,
        )
        work["grad_parts"] = [grad_parts[0]] + [
            shift(grad_parts[by], "col", lines, -by) for by in range(1, lines)
        ]
        names = ("grad_query", "gate_piece", "back", "mixed")
        far, *values = lax.optimization_barrier((far, grad_query, gate_piece, here, mixed))
        work.update(zip(names, values))
        return far

    def keys_arrive(first):
        first, work["grad_parts"], work["up_piece"] = lax.optimization_barrier(
            (first, work["grad_parts"], up_piece)
        )
        return first

    if rows_on == 2:
        ffn_sum = reduce_tokens(
            product(late_hidden, down_weight), None, keys_arrive, attention_back, back_here
        )
    else:
        ffn_sum = keys_arrive(attention_back(reduce_tokens(product(late_hidden, down_weight))))
    grad_query, gate_piece, back, mixed = [
        work[name] for name in ("grad_query", "gate_piece", "back", "mixed")
    ]
    output_parts = features_sent((middle + ffn_sum).astype(jnp.bfloat16))
    grad_keyvalue = pair_back(work["grad_parts"], cosine, sine, block)
    grad_joint = jnp.concatenate([grad_query, grad_keyvalue], axis=1)
    normed_one = jnp.concatenate(normed_parts, axis=0)

    def joint_products(first, last):
        if first:
            return product(grad_joint, joint_weight)(first, last)
        output_total = own_half(back, mixed, other_core(other_half(back, mixed)))
        shards = collect(jnp.concatenate([work["down_piece"], work["gate_piece"]], axis=0))
        names = ("output", "shards", "up_shards")
        close, *values = lax.optimization_barrier(
            (
                product(grad_joint, joint_weight)(first, last),
                output_total,
                shards,
                collect(work["up_piece"]),
            )
        )
        work.update(zip(names, values))
        return close

    def joint_others(key):
        key, other = lax.optimization_barrier((key, other_half(normed_one, grad_joint)))
        work["joint"] = (normed_one, grad_joint, other_core(other))
        work["output_piece"] = scatter(work["output"])
        return key

    def joint_owns(first):
        down_new = turned_update(
            meta_core,
            work["shards"],
            [w_down, down_moment, down_square],
            FF ** (-0.5),
            False,
        )
        names = ("output_piece", "down_new", "up_shards")
        first, rows, grad, other, *values = lax.optimization_barrier(
            (
                first,
                *work["joint"],
                work["output_piece"],
                down_new,
                work["up_shards"],
            )
        )
        work.update(zip(names, values))
        work["joint_total"] = own_half(rows, grad, other)
        return first

    grad_normed_one = reduce_tokens(joint_products, joint_others, joint_owns)
    joint_total, up_shards = lax.optimization_barrier((work["joint_total"], work["up_shards"]))
    joint_piece = scatter(joint_total)
    gateup_new = gateup_update(
        meta_core,
        work["shards"],
        up_shards,
        [w_gateup, gateup_moment, gateup_square],
        32,
    )
    input_grad = grad_middle + norm_back(residual, scale_one, grad_normed_one, gains[0])
    gain_one = jnp.sum(grad_normed_one * residual * scale_one, axis=0)
    gain_sums = jnp.stack([gain_one, gain_two])
    gain_blocks = [
        jnp.concatenate(
            [
                gain_sums[:, at * half : (at + 1) * half],
                gain_sums[:, D // 2 + at * half : D // 2 + (at + 1) * half],
            ],
            axis=1,
        )
        for at in range(lines)
    ]
    gain_parts = [pick(gain_blocks, line)] + [
        shift(pick(gain_blocks, (line + by) % lines), "col", lines, by) for by in range(1, lines)
    ]
    output_shards = collect(work["output_piece"])
    joint_piece, input_grad, gateup_new, output_parts, output_shards = lax.optimization_barrier(
        (joint_piece, input_grad.astype(jnp.bfloat16), gateup_new, output_parts, output_shards)
    )
    gain_parts, output_shards = lax.optimization_barrier((gain_parts, output_shards))
    grad_gains = sum(gain_parts[1:], gain_parts[0])
    for axis, size in (("core", 2), ("y", 2), ("row", rows_on)):
        own_gains = grad_gains
        for by in range(1, size):
            grad_gains = grad_gains + shift(own_gains, axis, size, by)
    input_parts = features_sent(input_grad)
    layer_output = features_of(output_parts)
    input_grad = features_of(input_parts).astype(jnp.float32)
    pair_piece = joint_piece[:, query_width:]
    pair_total = pair_piece.astype(jnp.float32)
    for by in range(1, rows_on):
        pair_total = pair_total + shift(pair_piece, "row", rows_on, by).astype(jnp.float32)
    joint_piece = jnp.concatenate(
        [joint_piece[:, :query_width], pair_total.astype(jnp.bfloat16)], axis=1
    )
    joint_new = joint_update(
        meta_core,
        collect(joint_piece),
        [w_query, query_moment, query_square],
        [w_keyvalue, keyvalue_moment, keyvalue_square],
    )
    output_new = turned_update(
        meta_core,
        output_shards,
        [w_output, output_moment, output_square],
        (HEADS * HEAD_DIM // 64) ** (-0.5),
        True,
    )

    gains_new = adamw_step(norm_gains, grad_gains, gains_moment, gains_square, 0.6, 0.0)
    return (
        layer_output,
        input_grad,
        *gains_new,
        *joint_new,
        *output_new,
        *gateup_new,
        *work["down_new"],
    )


def solution(mesh):
    dp, rows_on, lines = (mesh.shape["dp"], mesh.shape["row"], mesh.shape["col"])
    split = Mesh(mesh.devices.reshape(dp // 2, 2, rows_on, lines), ("y", "core", "row", "col"))
    tokens = P(("y", "core", "row"), "col")
    narrow, wide = (P("col", "row"), P("row", "col"))
    gains, pair, gateup = (P(None, "col"), P("col", None), P("col", None, "row"))
    return jax.shard_map(
        functools.partial(on_device, (rows_on, lines)),
        mesh=split,
        in_specs=(
            tokens,
            tokens,
            P(("y", "core"), None),
            gains,
            narrow,
            pair,
            wide,
            gateup,
            wide,
            gains,
            gains,
            narrow,
            narrow,
            pair,
            pair,
            wide,
            wide,
            gateup,
            gateup,
            wide,
            wide,
        ),
        out_specs=(tokens, tokens)
        + (gains,) * 3
        + (narrow,) * 3
        + (pair,) * 3
        + (wide,) * 3
        + (gateup,) * 3
        + (wide,) * 3,
        check_vma=False,
    )
```
